32 devices in a mesh: rep: 4 (over x, core), fsdp: 8 (over z, y).
Axes of the slice: x: 2, y: 2, z: 4, core: 2. Of those that a mesh axis runs over, the one named last changes fastest.
Arguments:
- tokens: bfloat16 [32, 1024, 2048], P(('rep', 'fsdp')), may hold values from -6 to 6
- target: bfloat16 [32, 1024, 2048], P(('rep', 'fsdp')), may hold values from -6 to 6
- doc_lengths: int32 [32, 4], P(('rep', 'fsdp')), may hold values from 1 to 512, 1024 in all within a row
- corpus_ids: int32 [32, 1024], P(('rep', 'fsdp')), may hold values from 0 to 7
- corpus_weights: int32 [8], replicated, may hold values from 1 to 5
- w_in: float32 [2048, 3584], P('fsdp'), may hold values from -0.125 to 0.125
- w_out: float32 [2, 1024, 2048], P(None, 'fsdp'), may hold values from -0.375 to 0.375
- gains: float32 [2, 2048], P(None, 'fsdp'), may hold values from 0.5 to 1.5
- first_in: float32 [4, 2048, 3584], P('rep', 'fsdp'), may hold values from -40 to 40
- first_out: float32 [4, 2, 1024, 2048], P('rep', None, 'fsdp'), may hold values from -40 to 40
- first_gains: float32 [4, 2, 2048], P('rep', None, 'fsdp'), may hold values from -40 to 40
- second_in: float32 [4, 2048, 3584], P('rep', 'fsdp'), may hold values from 163.84 to 655.36
- second_out: float32 [4, 2, 1024, 2048], P('rep', None, 'fsdp'), may hold values from 163.84 to 655.36
- second_gains: float32 [4, 2, 2048], P('rep', None, 'fsdp'), may hold values from 163.84 to 655.36
- outer_in: float32 [2048, 3584], P('fsdp'), may hold values from -0.0625 to 0.0625
- outer_out: float32 [2, 1024, 2048], P(None, 'fsdp'), may hold values from -0.1875 to 0.1875
- outer_gains: float32 [2, 2048], P(None, 'fsdp'), may hold values from -3 to 3
Outputs:
- activations: bfloat16 [32, 1024, 2048], P(('rep', 'fsdp'))
- input_grad: bfloat16 [32, 1024, 2048], P(('rep', 'fsdp'))
- grad_in: float32 [4, 2048, 3584], P('rep', 'fsdp')
- grad_out: float32 [4, 2, 1024, 2048], P('rep', None, 'fsdp')
- grad_gains: float32 [4, 2, 2048], P('rep', None, 'fsdp')
- first_in_new: float32 [4, 2048, 3584], P('rep', 'fsdp')
- first_out_new: float32 [4, 2, 1024, 2048], P('rep', None, 'fsdp')
- first_gains_new: float32 [4, 2, 2048], P('rep', None, 'fsdp')
- second_in_new: float32 [4, 2048, 3584], P('rep', 'fsdp')
- second_out_new: float32 [4, 2, 1024, 2048], P('rep', None, 'fsdp')
- second_gains_new: float32 [4, 2, 2048], P('rep', None, 'fsdp')
- diff_in: float32 [2048, 3584], P('fsdp')
- diff_out: float32 [2, 1024, 2048], P(None, 'fsdp')
- diff_gains: float32 [2, 2048], P(None, 'fsdp')
- outer_in_new: float32 [2048, 3584], P('fsdp')
- outer_out_new: float32 [2, 1024, 2048], P(None, 'fsdp')
- outer_gains_new: float32 [2, 2048], P(None, 'fsdp')
- new_in: float32 [2048, 3584], P('fsdp')
- new_out: float32 [2, 1024, 2048], P(None, 'fsdp')
- new_gains: float32 [2, 2048], P(None, 'fsdp')
- copy_in: bfloat16 [2048, 3584], P('fsdp')
- copy_out: bfloat16 [2, 1024, 2048], P(None, 'fsdp')
- copy_gains: bfloat16 [2, 2048], P(None, 'fsdp')
The draws below stay inside these ranges and needn't reach their ends.
Inputs may be any that keep to these rules, and one draw needn't show every extreme that they name: `doc_lengths`: each row's lengths sum to 1024.
All inputs are finite; a program needn't handle non-finite values.
Results may differ from the reference program's by a relative error of at most 0.023.
Values may be sent and summed in bfloat16 or wider, within the bound.
A program may use at most 448 MiB of HBM per device.

```python
import math
import jax
import jax.numpy as jnp
import numpy as np
from jax import lax

D = 2048
H = 16
HD = 64
KVH = 4
FF = 1024
LEN = 1024
NDOC = 4
NCORP = 8
STEP = 10
ROWS = 32
WIN = 3584
N_REP = 4
N_FSDP = 8


def place_ends(array, own_key, low, largest):
    index_at = [jax.random.randint(jax.random.fold_in(own_key, axis), (), 0, length) for axis, length in enumerate(array.shape)]
    widest = array.shape.index(max(array.shape))
    neighbour = index_at[:widest] + [(index_at[widest] + 1) % array.shape[widest]] + index_at[widest + 1:]
    return array.at[tuple(index_at)].set(low).at[tuple(neighbour)].set(largest)


def level_of(stream_key, extent, split, least, top_value):
    level = 1.0
    for axis_at, shards_of in split:
        draws = jax.random.uniform(jax.random.fold_in(jax.random.fold_in(stream_key, 6), axis_at), (shards_of,), jnp.float32, least / len(split), top_value / len(split))
        level = level * jnp.repeat(jnp.exp(draws), extent[axis_at] // shards_of).reshape((-1,) + (1,) * (len(extent) - 1 - axis_at))
    return level


def length_profile(amount, total, bound, slope):
    weights = [(1 << 20) // math.isqrt(standing ** slope) + 1 for standing in range(2, amount + 1)]
    surplus, holding = total - bound - (amount - 1), [1] * (amount - 1)
    while surplus > 0:
        movable = [i for i in range(amount - 1) if holding[i] < bound]
        whole, budget = sum([weights[i] for i in movable]), surplus
        for i in movable:
            addition = min(bound - holding[i], max(1, budget * weights[i] // whole), surplus)
            holding[i] = holding[i] + addition
            surplus = surplus - addition
    return np.array([bound] + holding)


def uneven(rng, count, total, bound, lean):
    if count == 2:
        one = jax.random.randint(rng, (), max(1, total - bound), min(bound, total - 1) + 1)
        return jnp.stack([one, total - one])
    sizes = jnp.asarray(length_profile(count, total, bound, lean), jnp.int32)
    couples = (count - 1) // 2
    source_of, receiver = sizes[1:1 + 2 * couples:2], sizes[2:2 + 2 * couples:2]
    slack = jnp.minimum(source_of - 1, bound - receiver)
    moved = jax.random.randint(jax.random.fold_in(rng, 1), (couples,), 0, 1 << 20) % (slack + 1)
    sizes = sizes.at[1:1 + 2 * couples:2].set(source_of - moved).at[2:2 + 2 * couples:2].set(receiver + moved)
    return sizes[jax.random.permutation(jax.random.fold_in(rng, 2), count)]


def centred(rng, shape, scale, most, shards=(), held_as=jnp.bfloat16):
    level = level_of(rng, shape, shards, -0.22, 0.18) if shards else 1.0
    values = jax.random.normal(rng, shape, jnp.float32) * scale * level
    return jnp.minimum(jnp.maximum(values, -most), most).astype(held_as)


def setup_inputs(seed: int = 0) -> dict:
    splits = jax.random.split(jax.random.key(seed), 18)
    tokens = centred(splits[0], (ROWS, LEN, D), 1.0, 6.0, ((0, 32),))
    target = centred(splits[1], (ROWS, LEN, D), 1.0, 6.0, ((0, 32),))
    doc_lengths = jax.vmap(lambda own: uneven(own, NDOC, LEN, LEN // 2, 2))(jax.random.split(splits[2], ROWS)).reshape((ROWS, NDOC)).astype(jnp.int32)
    corpus_ids = place_ends(jax.random.randint(splits[3], (ROWS, LEN), 0, NCORP), jax.random.fold_in(splits[3], 1), 0, NCORP - 1).astype(jnp.int32)
    corpus_weights = place_ends(jax.random.randint(splits[4], (NCORP,), 1, 6), jax.random.fold_in(splits[4], 1), 1, 5).astype(jnp.int32)
    w_in = centred(splits[5], (D, WIN), D ** -0.5, 0.125, ((0, 8),), jnp.float32)
    w_out = centred(splits[6], (2, FF, D), (FF // 4) ** -0.5, 0.375, ((1, 8),), jnp.float32)
    gains = jnp.clip(1.0 + 0.1 * jax.random.normal(splits[7], (2, D), jnp.float32), 0.5, 1.5)
    first_in = centred(splits[8], (N_REP, D, WIN), (0.07 * (LEN * N_FSDP) ** 0.5), 40.0, ((0, 4), (1, 8)), jnp.float32)
    first_out = centred(splits[9], (N_REP, 2, FF, D), (0.07 * (LEN * N_FSDP) ** 0.5), 40.0, ((0, 4), (2, 8)), jnp.float32)
    first_gains = centred(splits[10], (N_REP, 2, D), (0.07 * (LEN * N_FSDP) ** 0.5), 40.0, ((0, 4), (2, 8)), jnp.float32)
    second_in = jnp.clip(jnp.exp(math.log(655.36) - 1.3862944 * jax.random.uniform(splits[11], (N_REP, D, WIN), jnp.float32) ** level_of(splits[11], (N_REP, D, WIN), ((0, 4), (1, 8)), -0.2, 0.2)), 163.84, 655.36)
    second_out = jnp.clip(jnp.exp(math.log(655.36) - 1.3862944 * jax.random.uniform(splits[12], (N_REP, 2, FF, D), jnp.float32) ** level_of(splits[12], (N_REP, 2, FF, D), ((0, 4), (2, 8)), -0.2, 0.2)), 163.84, 655.36)
    second_gains = jnp.clip(jnp.exp(math.log(655.36) - 1.3862944 * jax.random.uniform(splits[13], (N_REP, 2, D), jnp.float32) ** level_of(splits[13], (N_REP, 2, D), ((0, 4), (2, 8)), -0.2, 0.2)), 163.84, 655.36)
    outer_in = centred(splits[14], (D, WIN), 0.01, 0.0625, ((0, 8),), jnp.float32)
    outer_out = centred(splits[15], (2, FF, D), 0.03, 0.1875, ((1, 8),), jnp.float32)
    outer_gains = centred(splits[16], (2, D), 0.5, 3.0, ((1, 8),), jnp.float32)
    return {"tokens": tokens, "target": target, "doc_lengths": doc_lengths, "corpus_ids": corpus_ids, "corpus_weights": corpus_weights, "w_in": w_in, "w_out": w_out, "gains": gains, "first_in": first_in, "first_out": first_out, "first_gains": first_gains, "second_in": second_in, "second_out": second_out, "second_gains": second_gains, "outer_in": outer_in, "outer_out": outer_out, "outer_gains": outer_gains}


norm_eps = 1e-06
beta_first = 0.9
beta_second = 0.95
adam_eps = 1e-08
decay_rate = 0.1
rate_in = 0.02
rate_out = 0.08
rate_gains = 1.2
outer_decay = 0.5
outer_rate = 0.7
masked_score = -1e+30

@jax.custom_vjp
def low(v):
    return lax.optimization_barrier(v.astype(jnp.bfloat16)).astype(jnp.float32)

@jax.custom_vjp
def low_back(v):
    return v

def low_keep(v):
    return (low(v), None)

def low_pass(kept, grad):
    return (grad,)

def back_keep(v):
    return (v, None)

def back_low(kept, grad):
    return (low(grad),)
low.defvjp(low_keep, low_pass)
low_back.defvjp(back_keep, back_low)

def norm_scale(values, gain):
    inverse = lax.rsqrt(lax.optimization_barrier(jnp.mean(values * values, axis=-1, keepdims=True)) + norm_eps)
    return values * inverse * gain

def doc_mask(lengths):
    doc_ends = jnp.cumsum(lengths).astype(jnp.int32)
    position = jnp.arange(LEN, dtype=jnp.int32)
    doc_index = lax.optimization_barrier(jnp.sum((position[:, None] >= doc_ends[None, :]).astype(jnp.int32), axis=1))
    return (doc_index[:, None] == doc_index[None, :]) & (position[:, None] >= position[None, :])

def forward(row_input, weight_in, weight_out, gain_pair, allowed):
    highest = lax.Precision.HIGHEST
    weight_in = low(weight_in)
    weight_out = low(weight_out)
    gain_pair = low(gain_pair)
    group_size = H // KVH
    query_cols = H * HD
    key_cols = KVH * HD
    attn_cols = query_cols + 2 * key_cols
    first = low(norm_scale(row_input, gain_pair[0]))
    packed = low(low_back(jnp.dot(first, weight_in[:, :attn_cols], precision=highest)))
    queries = packed[:, :query_cols].reshape(LEN, KVH, group_size, HD)
    key_heads = packed[:, query_cols:query_cols + key_cols].reshape(LEN, KVH, HD)
    value_heads = packed[:, query_cols + key_cols:].reshape(LEN, KVH, HD)
    scores = low_back(jnp.einsum('qkgd,skd->kgqs', queries, key_heads, precision=highest) * HD ** (-0.5))
    scores = jnp.where(allowed, scores, masked_score)
    attn_probs = low(jax.nn.softmax(scores, axis=-1))
    mixed = jnp.einsum('kgqs,skd->qkgd', attn_probs, value_heads, precision=highest).reshape(LEN, query_cols)
    mixed = low(low_back(mixed))
    middle = row_input + low_back(jnp.dot(mixed, weight_out[0], precision=highest))
    second = low(norm_scale(middle, gain_pair[1]))
    both = low_back(jnp.dot(second, weight_in[:, attn_cols:], precision=highest))
    hidden = low(jax.nn.silu(both[:, :FF]) * both[:, FF:])
    return middle + low_back(jnp.dot(hidden, weight_out[1], precision=highest))

def adam_step(grad, first, second, weight, rate):
    first_new = beta_first * first + (1.0 - beta_first) * grad
    second_new = beta_second * second + (1.0 - beta_second) * grad * grad
    ratio = first_new / (1.0 - beta_first ** STEP) / (jnp.sqrt(second_new / (1.0 - beta_second ** STEP)) + adam_eps)
    local = weight - rate * (ratio + decay_rate * weight)
    return (first_new, second_new, weight - local)

def outer_step(delta_sum, momentum, weight, groups):
    average = delta_sum / groups
    momentum_new = outer_decay * momentum + average
    weight_new = weight - outer_rate * (average + outer_decay * momentum_new)
    return (average, momentum_new, weight_new)

def reference(tokens, target, doc_lengths, corpus_ids, corpus_weights, w_in, w_out, gains, first_in, first_out, first_gains, second_in, second_out, second_gains, outer_in, outer_out, outer_gains):
    table = corpus_weights.astype(jnp.float32) / 4.0
    corpus_range = jnp.arange(NCORP, dtype=jnp.int32)

    def group_pass(group):
        group_tokens, group_target, group_lengths, group_ids = group
        zeros = (jnp.zeros_like(w_in), jnp.zeros_like(w_out), jnp.zeros_like(gains))

        def row_pass(carry, row):
            row_tokens, row_target, row_lengths, row_ids = row
            allowed = doc_mask(row_lengths)
            token_weight = lax.optimization_barrier(jnp.sum(jnp.where(row_ids[:, None] == corpus_range[None, :], table[None, :], 0.0), axis=1))
            cotangent = token_weight[:, None] * row_target.astype(jnp.float32)

            def run(row_input, weight_in, weight_out, gain_pair):
                return forward(row_input, weight_in, weight_out, gain_pair, allowed)
            result, pull = jax.vjp(run, row_tokens.astype(jnp.float32), w_in, w_out, gains)
            d_input, d_in, d_out, d_gains = pull(cotangent)
            carry = (carry[0] + d_in, carry[1] + d_out, carry[2] + d_gains)
            return (carry, (result.astype(jnp.bfloat16), d_input.astype(jnp.bfloat16)))
        return lax.scan(row_pass, zeros, (group_tokens, group_target, group_lengths, group_ids))
    sums, rows_out = lax.map(group_pass, (tokens.reshape(N_REP, N_FSDP, LEN, D), target.reshape(N_REP, N_FSDP, LEN, D), doc_lengths.reshape(N_REP, N_FSDP, NDOC), corpus_ids.reshape(N_REP, N_FSDP, LEN)))
    grad_in, grad_out, grad_gains = sums
    activations = rows_out[0].reshape(ROWS, LEN, D)
    input_grad = rows_out[1].reshape(ROWS, LEN, D)
    first_in_new, second_in_new, delta_in = adam_step(grad_in, first_in, second_in, w_in[None], rate_in)
    first_out_new, second_out_new, delta_out = adam_step(grad_out, first_out, second_out, w_out[None], rate_out)
    first_gains_new, second_gains_new, delta_gains = adam_step(grad_gains, first_gains, second_gains, gains[None], rate_gains)
    diff_in, outer_in_new, new_in = outer_step(lax.optimization_barrier(jnp.sum(delta_in, axis=0)), outer_in, w_in, N_REP)
    diff_out, outer_out_new, new_out = outer_step(lax.optimization_barrier(jnp.sum(delta_out, axis=0)), outer_out, w_out, N_REP)
    diff_gains, outer_gains_new, new_gains = outer_step(lax.optimization_barrier(jnp.sum(delta_gains, axis=0)), outer_gains, gains, N_REP)
    return (activations, input_grad, grad_in, grad_out, grad_gains, first_in_new, first_out_new, first_gains_new, second_in_new, second_out_new, second_gains_new, diff_in, diff_out, diff_gains, outer_in_new, outer_out_new, outer_gains_new, new_in, new_out, new_gains, new_in.astype(jnp.bfloat16), new_out.astype(jnp.bfloat16), new_gains.astype(jnp.bfloat16))
```

```python
import functools
import jax
import jax.numpy as jnp
from jax import lax
from jax.experimental import pallas as pl
from jax.experimental.pallas import tpu as pltpu
from jax.sharding import PartitionSpec as P

H = 16
HD = 64
KVH = 4
FF = 1024
LEN = 1024
NCORP = 8
f32 = jnp.float32
bf16 = jnp.bfloat16
norm_eps = 1e-06
BQ = 256
NT = (((1,), (1,)), ((), ()))
TN = (((0,), (0,)), ((), ()))


def mm(a, b, dims=(((1,), (0,)), ((), ()))):
    return lax.dot_general(a, b, dims, preferred_element_type=f32)


def params(**kw):
    return pltpu.CompilerParams(vmem_limit_bytes=60 << 20, **kw)


def one(shape, index):
    return pl.BlockSpec(shape, index, pipeline_mode=pl.Buffered(1))


def qkv_kernel(x_ref, g_ref, w_ref, first_ref, packed_ref):
    x = x_ref[...].astype(f32)
    r = lax.rsqrt(jnp.mean(x * x, axis=-1, keepdims=True) + norm_eps)
    first = (x * r * g_ref[0:1, :]).astype(bf16)
    first_ref[...] = first
    packed_ref[...] = mm(first, w_ref[...]).astype(bf16)


def qkv(x, gains, w):
    rows, width = x.shape
    cols = w.shape[1]
    return pl.pallas_call(
        qkv_kernel,
        grid=(rows // BQ,),
        in_specs=[
            pl.BlockSpec((BQ, width), lambda i: (i, 0)),
            one(gains.shape, lambda i: (0, 0)),
            one((width, cols), lambda i: (0, 0)),
        ],
        out_specs=[
            pl.BlockSpec((BQ, width), lambda i: (i, 0)),
            pl.BlockSpec((BQ, cols), lambda i: (i, 0)),
        ],
        out_shape=[
            jax.ShapeDtypeStruct((rows, width), bf16),
            jax.ShapeDtypeStruct((rows, cols), bf16),
        ],
        compiler_params=params(),
        cost_estimate=pl.CostEstimate(
            flops=2 * rows * width * cols, bytes_accessed=rows * width * 4 + width * cols * 2, transcendentals=0
        ),
        name="norm_qkv",
    )(x, gains, w)


def doc_start(lengths_ref, position):
    end = jnp.int32(0)
    start = jnp.zeros_like(position)
    for j in range(lengths_ref.shape[0]):
        end = end + lengths_ref[j]
        start = jnp.where(position >= end, end, start)
    return start


def key_blocks(lengths_ref, i):
    first_row = i * BQ
    return i + 1 - doc_start(lengths_ref, first_row) // BQ


def max_blocks():
    return LEN // (2 * BQ) + 1


def attn_kernel(len_ref, q_ref, k_ref, v_ref, o_ref, lse_ref):
    i = pl.program_id(0)
    count = key_blocks(len_ref, i)
    row = i * BQ + lax.broadcasted_iota(jnp.int32, (BQ, 1), 0)
    start = doc_start(len_ref, row)
    lane = lax.broadcasted_iota(jnp.int32, (BQ, 128), 1)
    for nb in range(1, max_blocks() + 1):

        @pl.when(count == nb)
        def _():
            span = nb * BQ
            base = pl.multiple_of((i - (nb - 1)) * BQ, BQ)
            col = base + lax.broadcasted_iota(jnp.int32, (BQ, span), 1)
            bias = jnp.where((col >= start) & (col <= row), 0.0, -1e30)
            k2 = k_ref[pl.ds(base, span), :]
            v2 = v_ref[pl.ds(base, span), :]
            tile = jnp.zeros((BQ, 128), f32)
            outs = []
            for kv in range(2):
                k = k2[:, kv * HD : (kv + 1) * HD]
                v = v2[:, kv * HD : (kv + 1) * HD]
                for g in range(H // KVH):
                    h = kv * (H // KVH) + g
                    q = q_ref[:, h * HD : (h + 1) * HD] * jnp.asarray(HD**-0.5, bf16)
                    s = mm(q, k, NT) + bias
                    m = jnp.max(s, axis=-1, keepdims=True)
                    e = jnp.exp(s - m)
                    total = jnp.sum(e, axis=-1, keepdims=True)
                    o = mm(e.astype(bf16), v) * (1.0 / total)
                    outs.append(o.astype(bf16))
                    tile = jnp.where(lane == h, m + jnp.log(total), tile)
            o_ref[...] = jnp.concatenate(outs, axis=1)
            lse_ref[...] = tile.T[0:8, :]


def attention(lengths, packed):
    qw = H // 2 * HD
    kcol = H * HD // 128
    vcol = kcol + KVH * HD // 128
    return pl.pallas_call(
        attn_kernel,
        grid_spec=pltpu.PrefetchScalarGridSpec(
            num_scalar_prefetch=1,
            grid=(LEN // BQ, 2),
            in_specs=[
                pl.BlockSpec((BQ, qw), lambda i, p, s: (i, p)),
                pl.BlockSpec((LEN, 128), lambda i, p, s: (0, kcol + p)),
                pl.BlockSpec((LEN, 128), lambda i, p, s: (0, vcol + p)),
            ],
            out_specs=[
                pl.BlockSpec((BQ, qw), lambda i, p, s: (i, p)),
                pl.BlockSpec((8, BQ), lambda i, p, s: (p, i)),
            ],
        ),
        out_shape=[
            jax.ShapeDtypeStruct((LEN, H * HD), bf16),
            jax.ShapeDtypeStruct((H, LEN), f32),
        ],
        compiler_params=params(),
        cost_estimate=pl.CostEstimate(flops=4 * H * LEN * LEN * HD * 4, bytes_accessed=1 << 24, transcendentals=0),
        name="attention",
    )(lengths, packed, packed, packed)


def attn_back_kernel(len_ref, q_ref, k_ref, v_ref, d_ref, o_ref, lse_ref, dq_ref, dk_ref, dv_ref, dk_acc, dv_acc):
    i = pl.program_id(1)
    count = key_blocks(len_ref, i)
    row = i * BQ + lax.broadcasted_iota(jnp.int32, (1, BQ), 1)
    start = doc_start(len_ref, row)
    lane = lax.broadcasted_iota(jnp.int32, (BQ, 128), 1)
    group = H // KVH
    scale = jnp.asarray(HD**-0.5, bf16)

    @pl.when(i == 0)
    def _():
        dk_acc[...] = jnp.zeros_like(dk_acc)
        dv_acc[...] = jnp.zeros_like(dv_acc)

    tile = jnp.zeros((BQ, 128), f32)
    for h in range(2 * group):
        cols = slice(h * HD, (h + 1) * HD)
        dot = jnp.sum(d_ref[:, cols].astype(f32) * o_ref[:, cols].astype(f32), axis=-1, keepdims=True)
        tile = jnp.where(lane == h, dot, tile)
    inner = tile.T
    for nb in range(1, max_blocks() + 1):

        @pl.when(count == nb)
        def _():
            span = nb * BQ
            base = pl.multiple_of((i - (nb - 1)) * BQ, BQ)
            key = base + lax.broadcasted_iota(jnp.int32, (span, BQ), 0)
            bias = jnp.where((key >= start) & (key <= row), 0.0, -1e30)
            k2 = k_ref[pl.ds(base, span), :]
            v2 = v_ref[pl.ds(base, span), :]
            dks, dvs = [], []
            for kv in range(2):
                k = k2[:, kv * HD : (kv + 1) * HD]
                v = v2[:, kv * HD : (kv + 1) * HD]
                dk = dv = None
                dqs = []
                for g in range(group):
                    h = kv * group + g
                    cols = slice(h * HD, (h + 1) * HD)
                    q = q_ref[:, cols] * scale
                    d = d_ref[:, cols]
                    s = mm(k, q, NT) + bias
                    p = jnp.exp(s - lse_ref[h : h + 1, :])
                    dp = mm(v, d, NT)
                    ds = (p * (dp - inner[h : h + 1, :])).astype(bf16)
                    dv_h = mm(p.astype(bf16), d)
                    dk_h = mm(ds, q)
                    dv = dv_h if dv is None else dv + dv_h
                    dk = dk_h if dk is None else dk + dk_h
                    dqs.append(mm(k, ds, TN))
                dq = jnp.concatenate(dqs, axis=0) * (HD**-0.5)
                dq_ref[:, kv * group * HD : (kv + 1) * group * HD] = dq.T.astype(bf16)
                dks.append(dk)
                dvs.append(dv)
            dk_acc[pl.ds(base, span), :] += jnp.concatenate(dks, axis=1)
            dv_acc[pl.ds(base, span), :] += jnp.concatenate(dvs, axis=1)

    @pl.when(i == pl.num_programs(1) - 1)
    def _():
        dk_ref[...] = dk_acc[...].astype(bf16)
        dv_ref[...] = dv_acc[...].astype(bf16)


def attention_back(lengths, packed, d_mixed, mixed, lse):
    qw = H // 2 * HD
    kcol = H * HD // 128
    vcol = kcol + KVH * HD // 128
    return pl.pallas_call(
        attn_back_kernel,
        grid_spec=pltpu.PrefetchScalarGridSpec(
            num_scalar_prefetch=1,
            grid=(2, LEN // BQ),
            in_specs=[
                pl.BlockSpec((BQ, qw), lambda p, i, s: (i, p)),
                pl.BlockSpec((LEN, 128), lambda p, i, s: (0, kcol + p)),
                pl.BlockSpec((LEN, 128), lambda p, i, s: (0, vcol + p)),
                pl.BlockSpec((BQ, qw), lambda p, i, s: (i, p)),
                pl.BlockSpec((BQ, qw), lambda p, i, s: (i, p)),
                pl.BlockSpec((8, BQ), lambda p, i, s: (p, i)),
            ],
            out_specs=[
                pl.BlockSpec((BQ, qw), lambda p, i, s: (i, p)),
                pl.BlockSpec((LEN, 128), lambda p, i, s: (0, p)),
                pl.BlockSpec((LEN, 128), lambda p, i, s: (0, p)),
            ],
            scratch_shapes=[pltpu.VMEM((LEN, 128), f32), pltpu.VMEM((LEN, 128), f32)],
        ),
        out_shape=[
            jax.ShapeDtypeStruct((LEN, H * HD), bf16),
            jax.ShapeDtypeStruct((LEN, KVH * HD), bf16),
            jax.ShapeDtypeStruct((LEN, KVH * HD), bf16),
        ],
        compiler_params=params(),
        cost_estimate=pl.CostEstimate(flops=10 * H * LEN * LEN * HD * 4, bytes_accessed=1 << 24, transcendentals=0),
        name="attention_back",
    )(lengths, packed, packed, packed, d_mixed, mixed, lse)


def token_weight(table_ref, ids):
    weight = jnp.zeros(ids.shape, f32)
    for j in range(table_ref.shape[0]):
        weight = jnp.where(ids == j, table_ref[j].astype(f32) * 0.25, weight)
    return weight


def ffn_kernel(table_ref, x_ref, mixed_ref, t_ref, ids_ref, g_ref, proj_ref, wf_ref, down_ref,
               middle_ref, second_ref, hidden_ref, dboth_ref, dy_ref):
    middle = x_ref[...].astype(f32) + mm(mixed_ref[...], proj_ref[...])
    middle_ref[...] = middle
    r = lax.rsqrt(jnp.mean(middle * middle, axis=-1, keepdims=True) + norm_eps)
    second = (middle * r * g_ref[1:2, :]).astype(bf16)
    second_ref[...] = second
    dy = (token_weight(table_ref, ids_ref[...]) * t_ref[...].astype(f32)).astype(bf16)
    dy_ref[...] = dy
    step = 512
    for c in range(0, FF, step):
        gate = mm(second, wf_ref[:, c : c + step])
        up = mm(second, wf_ref[:, FF + c : FF + c + step])
        dh = mm(dy, down_ref[c : c + step, :], NT)
        sig = jax.nn.sigmoid(gate)
        silu = gate * sig
        hidden_ref[:, c : c + step] = (silu * up).astype(bf16)
        dboth_ref[:, c : c + step] = (dh * up * sig * (1.0 + gate * (1.0 - sig))).astype(bf16)
        dboth_ref[:, FF + c : FF + c + step] = (dh * silu).astype(bf16)


def ffn(table, x, mixed, target, ids, gains, proj, wf, down):
    width = x.shape[1]
    rowb = lambda n: pl.BlockSpec((BQ, n), lambda i, s: (i, 0))
    whole = lambda a: one(a.shape, lambda i, s: (0, 0))
    return pl.pallas_call(
        ffn_kernel,
        grid_spec=pltpu.PrefetchScalarGridSpec(
            num_scalar_prefetch=1,
            grid=(LEN // BQ,),
            in_specs=[rowb(width), rowb(H * HD), rowb(width), rowb(1), whole(gains), whole(proj), whole(wf), whole(down)],
            out_specs=[rowb(width), rowb(width), rowb(FF), rowb(2 * FF), rowb(width)],
        ),
        out_shape=[
            jax.ShapeDtypeStruct((LEN, width), f32),
            jax.ShapeDtypeStruct((LEN, width), bf16),
            jax.ShapeDtypeStruct((LEN, FF), bf16),
            jax.ShapeDtypeStruct((LEN, 2 * FF), bf16),
            jax.ShapeDtypeStruct((LEN, width), bf16),
        ],
        compiler_params=params(),
        cost_estimate=pl.CostEstimate(flops=2 * LEN * width * FF * 4, bytes_accessed=40 << 20, transcendentals=0),
        name="ffn",
    )(table, x, mixed, target, ids, gains, proj, wf, down)


def mid_kernel(table_ref, middle_ref, hidden_ref, dboth_ref, t_ref, ids_ref, g_ref, proj_ref, wf_ref, down_ref,
               act_ref, dmid_ref, dlow_ref, dmix_ref, gain_ref):
    middle = middle_ref[...]
    act_ref[...] = (middle + mm(hidden_ref[...], down_ref[...])).astype(bf16)
    r = lax.rsqrt(jnp.mean(middle * middle, axis=-1, keepdims=True) + norm_eps)
    n2 = middle * r
    ds2 = mm(dboth_ref[...], wf_ref[...], NT)
    prod = ds2 * n2
    part = jnp.sum(prod.reshape(BQ // 8, 8, prod.shape[1]), axis=0)

    @pl.when(pl.program_id(0) == 0)
    def _():
        gain_ref[...] = jnp.zeros_like(gain_ref)

    gain_ref[...] += part
    g = g_ref[1:2, :]
    e2 = ds2 * g
    dy = token_weight(table_ref, ids_ref[...]) * t_ref[...].astype(f32)
    dmid = dy + r * (e2 - n2 * jnp.mean(prod * g, axis=-1, keepdims=True))
    dmid_ref[...] = dmid
    low = dmid.astype(bf16)
    dlow_ref[...] = low
    dmix_ref[...] = mm(low, proj_ref[...], NT).astype(bf16)


def mid(table, middle, hidden, dboth, target, ids, gains, proj, wf, down):
    width = middle.shape[1]
    rowb = lambda n: pl.BlockSpec((BQ, n), lambda i, s: (i, 0))
    whole = lambda a: one(a.shape, lambda i, s: (0, 0))
    return pl.pallas_call(
        mid_kernel,
        grid_spec=pltpu.PrefetchScalarGridSpec(
            num_scalar_prefetch=1,
            grid=(LEN // BQ,),
            in_specs=[rowb(width), rowb(FF), rowb(2 * FF), rowb(width), rowb(1), whole(gains), whole(proj), whole(wf), whole(down)],
            out_specs=[rowb(width), rowb(width), rowb(width), rowb(H * HD), pl.BlockSpec((8, width), lambda i, s: (0, 0))],
        ),
        out_shape=[
            jax.ShapeDtypeStruct((LEN, width), bf16),
            jax.ShapeDtypeStruct((LEN, width), f32),
            jax.ShapeDtypeStruct((LEN, width), bf16),
            jax.ShapeDtypeStruct((LEN, H * HD), bf16),
            jax.ShapeDtypeStruct((8, width), f32),
        ],
        compiler_params=params(),
        cost_estimate=pl.CostEstimate(flops=2 * LEN * width * FF * 4, bytes_accessed=40 << 20, transcendentals=0),
        name="mid",
    )(table, middle, hidden, dboth, target, ids, gains, proj, wf, down)


def input_kernel(x_ref, dmid_ref, dq_ref, dk_ref, dv_ref, g_ref, w_ref, out_ref, gain_ref):
    x = x_ref[...].astype(f32)
    r = lax.rsqrt(jnp.mean(x * x, axis=-1, keepdims=True) + norm_eps)
    n1 = x * r
    q, k = H * HD, H * HD + KVH * HD
    ds1 = mm(dq_ref[...], w_ref[:, :q], NT) + mm(dk_ref[...], w_ref[:, q:k], NT) + mm(dv_ref[...], w_ref[:, k:], NT)
    prod = ds1 * n1
    part = jnp.sum(prod.reshape(BQ // 8, 8, prod.shape[1]), axis=0)

    @pl.when(pl.program_id(0) == 0)
    def _():
        gain_ref[...] = jnp.zeros_like(gain_ref)

    gain_ref[...] += part
    g = g_ref[0:1, :]
    out = dmid_ref[...] + r * (ds1 * g - n1 * jnp.mean(prod * g, axis=-1, keepdims=True))
    out_ref[...] = out.astype(bf16)


def input_back(x, dmid, dq, dk, dv, gains, w):
    width = x.shape[1]
    rowb = lambda n: pl.BlockSpec((BQ, n), lambda i: (i, 0))
    whole = lambda a: one(a.shape, lambda i: (0, 0))
    return pl.pallas_call(
        input_kernel,
        grid=(LEN // BQ,),
        in_specs=[rowb(width), rowb(width), rowb(H * HD), rowb(KVH * HD), rowb(KVH * HD), whole(gains), whole(w)],
        out_specs=[rowb(width), pl.BlockSpec((8, width), lambda i: (0, 0))],
        out_shape=[jax.ShapeDtypeStruct((LEN, width), bf16), jax.ShapeDtypeStruct((8, width), f32)],
        compiler_params=params(),
        cost_estimate=pl.CostEstimate(flops=2 * LEN * width * 1536, bytes_accessed=24 << 20, transcendentals=0),
        name="input_back",
    )(x, dmid, dq, dk, dv, gains, w)


def grad_kernel(pick_ref, a_ref, *refs):
    out_ref = refs[-1]
    b_refs = refs[:-1]
    add_ref = None
    if len(b_refs) > 1 and len(b_refs[-1].shape) == 3:
        add_ref, b_refs = b_refs[-1], b_refs[:-1]
    col = 0
    a = a_ref[...]
    for b_ref in b_refs:
        n = b_ref.shape[1]
        g = mm(a, b_ref[...], TN)
        if add_ref is not None:
            g = g + add_ref[0, :, col : col + n].astype(f32)
        out_ref[0, :, col : col + n] = g.astype(bf16)
        col += n


def grad_rows(pick, a, bs, rows, add=None, name="grad"):
    cols = sum(width for _, _, width in bs)
    count = pick.shape[0]
    specs = [pl.BlockSpec((LEN, rows), lambda j, p: (0, p[j]))]
    specs += [one((LEN, width), functools.partial(lambda at, j, p: (0, at), at)) for _, at, width in bs]
    ops = [a, *(b for b, _, _ in bs)]
    if add is not None:
        specs.append(pl.BlockSpec((1, rows, cols), lambda j, p: (j, 0, 0)))
        ops.append(add)
    return pl.pallas_call(
        grad_kernel,
        grid_spec=pltpu.PrefetchScalarGridSpec(
            num_scalar_prefetch=1,
            grid=(count,),
            in_specs=specs,
            out_specs=pl.BlockSpec((1, rows, cols), lambda j, p: (j, 0, 0)),
        ),
        out_shape=jax.ShapeDtypeStruct((count, rows, cols), bf16),
        compiler_params=params(),
        cost_estimate=pl.CostEstimate(flops=2 * LEN * rows * count * cols, bytes_accessed=12 << 20, transcendentals=0),
        name=name,
    )(pick, *ops)


def flip_pairs(n):
    return [(i, i ^ 1) for i in range(n)]


def add_low(a, b):
    return (a.astype(f32) + b.astype(f32)).astype(a.dtype)


def line_sum(blocks, z, line):
    right = left = None
    for step in range(1, line):
        at_right = jnp.clip(line - step + z, 0, line - 1)
        at_left = jnp.clip(z - line + step, 0, line - 1)
        to_right = lax.dynamic_index_in_dim(blocks, at_right, 0, keepdims=False)
        to_left = lax.dynamic_index_in_dim(blocks, at_left, 0, keepdims=False)
        if right is not None:
            to_right = add_low(to_right, right)
            to_left = add_low(to_left, left)
        pairs = [(k * 2 + y, k * 2 + 2 + y) for k in range(step) for y in range(2)]
        last = 2 * line - 1
        right = lax.ppermute(to_right, "fsdp", pairs)
        left = lax.ppermute(to_left, "fsdp", [(last - a, last - b) for a, b in pairs])
    return right, left


beta_first = 0.9
beta_second = 0.95
adam_eps = 1e-08
decay_rate = 0.1
outer_decay = 0.5
outer_rate = 0.7
STEP = 10


def adam_step(grad, first, second, weight, rate):
    first_new = beta_first * first + (1.0 - beta_first) * grad
    second_new = beta_second * second + (1.0 - beta_second) * grad * grad
    ratio = first_new / (1.0 - beta_first**STEP) / (jnp.sqrt(second_new / (1.0 - beta_second**STEP)) + adam_eps)
    local = weight - rate * (ratio + decay_rate * weight)
    return first_new, second_new, weight - local


def outer_step(delta_sum, momentum, weight, groups):
    average = delta_sum / groups
    momentum_new = outer_decay * momentum + average
    return average, momentum_new, weight - outer_rate * (average + outer_decay * momentum_new)


def adam_kernel(place_ref, own_ref, *refs, terms, rate):
    refs = list(refs)
    more = [refs.pop(0) for _ in range(terms)]
    first_ref, second_ref, w_ref = refs[:3]
    grad_ref, first_new_ref, second_new_ref, keep_ref, send_ref = refs[-5:]
    grad = own_ref[0].astype(f32)
    for term in more:
        grad = grad + term[...].astype(f32)
    first_new, second_new, delta = adam_step(grad, first_ref[...], second_ref[...], w_ref[...], rate)
    grad_ref[...] = grad
    first_new_ref[...] = first_new
    second_new_ref[...] = second_new
    half = delta.shape[0] // 2
    low = delta.astype(bf16)
    core = place_ref[1]

    @pl.when(core == 0)
    def _():
        keep_ref[...] = low[:half]
        send_ref[...] = low[half:]

    @pl.when(core != 0)
    def _():
        keep_ref[...] = low[half:]
        send_ref[...] = low[:half]


def adam_piece(place, own, terms, first, second, w, held, rows, row_at, col_at, cols, tile, rate):
    at = lambda j, p: (row_at // rows, col_at // tile + j)
    piece = pl.BlockSpec((rows, tile), lambda j, p: (0, j))
    half = pl.BlockSpec((rows // 2, tile), lambda j, p: (0, j))
    state = pl.BlockSpec((rows, tile), at)
    full = jax.ShapeDtypeStruct(first.shape, f32)
    low = jax.ShapeDtypeStruct((rows // 2, cols), bf16)
    specs = [pl.BlockSpec((1, rows, tile), lambda j, p: (p[0], 0, j))] + [piece] * len(terms) + [state] * 3
    ops = [own, *terms, first, second, w]
    aliases = {}
    if held is not None:
        aliases = {1 + len(ops) + k: k for k in range(3)}
        ops += list(held)
        specs += [pl.BlockSpec(memory_space=pl.ANY)] * 3
    out = pl.pallas_call(
        functools.partial(adam_kernel, terms=len(terms), rate=rate),
        grid_spec=pltpu.PrefetchScalarGridSpec(
            num_scalar_prefetch=1,
            grid=(cols // tile,),
            in_specs=specs,
            out_specs=[state, state, state, half, half],
        ),
        out_shape=[full, full, full, low, low],
        input_output_aliases=aliases,
        compiler_params=params(),
        cost_estimate=pl.CostEstimate(flops=0, bytes_accessed=rows * cols * 28, transcendentals=0),
        name="adam",
    )(place, *ops)
    return out[:3], out[3], out[4]


def outer_kernel(place_ref, keep_ref, other_ref, outer_ref, w_ref, *refs, groups):
    diff_ref, outer_new_ref, new_ref, copy_ref = refs[-4:]
    core = place_ref[1]
    half = keep_ref.shape[0]

    def write(rows, total_ref):
        average, momentum, weight = outer_step(total_ref[...].astype(f32), outer_ref[rows, :], w_ref[rows, :], groups)
        diff_ref[rows, :] = average
        outer_new_ref[rows, :] = momentum
        new_ref[rows, :] = weight
        copy_ref[rows, :] = weight.astype(bf16)

    @pl.when(core == 0)
    def _():
        write(slice(0, half), keep_ref)
        write(slice(half, 2 * half), other_ref)

    @pl.when(core != 0)
    def _():
        write(slice(0, half), other_ref)
        write(slice(half, 2 * half), keep_ref)


def outer_piece(place, keep, other, outer, w, held, rows, row_at, col_at, cols, tile, groups):
    half = pl.BlockSpec((rows // 2, tile), lambda j, p: (0, j))
    state = pl.BlockSpec((rows, tile), lambda j, p: (row_at // rows, col_at // tile + j))
    full = jax.ShapeDtypeStruct(outer.shape, f32)
    specs = [half, half, state, state]
    ops = [keep, other, outer, w]
    aliases = {}
    if held is not None:
        aliases = {1 + len(ops) + k: k for k in range(4)}
        ops += list(held)
        specs += [pl.BlockSpec(memory_space=pl.ANY)] * 4
    return pl.pallas_call(
        functools.partial(outer_kernel, groups=groups),
        grid_spec=pltpu.PrefetchScalarGridSpec(
            num_scalar_prefetch=1, grid=(cols // tile,), in_specs=specs, out_specs=[state] * 4
        ),
        out_shape=[full, full, full, jax.ShapeDtypeStruct(outer.shape, bf16)],
        input_output_aliases=aliases,
        compiler_params=params(),
        cost_estimate=pl.CostEstimate(flops=0, bytes_accessed=rows * cols * 24, transcendentals=0),
        name="outer",
    )(place, *ops)


def rep_sum(keep, send, rep):
    pair = flip_pairs(rep)
    part = add_low(keep, lax.ppermute(send, "rep", pair))
    for hop in range(1, (rep - 1).bit_length()):
        part = add_low(part, lax.ppermute(part, "rep", [(i, i ^ (1 << hop)) for i in range(rep)]))
    return part, lax.ppermute(part, "rep", pair)


def gather_kernel(*refs, count, line, shares):
    ins, outs = refs[:count], refs[count : 2 * count]
    send, recv, local = refs[2 * count :]
    r, f = lax.axis_index("rep"), lax.axis_index("fsdp")
    x, core, z, y = r // 2, r % 2, f // 2, f % 2
    to_y = (r, f + 1 - 2 * y)
    to_x = (r + 2 - 4 * x, f)
    to_core = (r + 1 - 2 * core, f)
    barrier = pltpu.get_barrier_semaphore()
    greet = lambda to: pl.semaphore_signal(barrier, inc=1, device_id=to, device_id_type=pl.DeviceIdType.MESH)
    for to in (to_y, to_x, to_core):
        greet(to)
    pl.when(z > 0)(lambda: greet((r, f - 2)))
    pl.when(z < line - 1)(lambda: greet((r, f + 2)))
    pl.semaphore_wait(barrier, 3 + jnp.where(z > 0, 1, 0) + jnp.where(z < line - 1, 1, 0))

    def item(side, d):
        return 0 if d == 0 else 2 * d - 1 + (side > 0)

    def exists(side, d):
        return None if d == 0 else (z - d >= 0 if side < 0 else z + d < line)

    def guard(cond, fn):
        if cond is None:
            fn()
        else:
            pl.when(cond)(fn)

    def rows_of(m):
        rows = ins[m].shape[0]
        half = rows // 2
        return half, shares[m]

    def copy(src, dst, stage, m, k, to):
        return pltpu.make_async_remote_copy(
            src_ref=src, dst_ref=dst, send_sem=send.at[stage, m, k], recv_sem=recv.at[stage, m, k],
            device_id=to, device_id_type=pl.DeviceIdType.MESH,
        )

    def portion(m):
        half, bx = rows_of(m)
        return pl.ds(pl.multiple_of(core * half + x * bx, 16), half - bx)

    def line_copy(m, side, d):
        plane = z - (d - 1) if side < 0 else z + (d - 1)
        to = (r, f + 2) if side < 0 else (r, f - 2)
        rows = portion(m)
        dst = outs[m].at[plane * 2 + y, rows, :]
        src = ins[m].at[rows, :] if d == 1 else dst
        return copy(src, dst, 0, m, item(side, d), to)

    def line_arrival(m, side, d):
        plane = z - d if side < 0 else z + d
        dst = outs[m].at[plane * 2 + y, portion(m), :]
        return copy(dst, dst, 0, m, item(side, d), to_y)

    def y_copy(m, side, d):
        plane = z + side * d
        dst = outs[m].at[plane * 2 + y, portion(m), :]
        return copy(ins[m].at[portion(m), :] if d == 0 else dst, dst, 1, m, item(side, d), to_y)

    def x_copy(m, side, d):
        half, bx = rows_of(m)
        rows = pl.ds(pl.multiple_of(core * half + x * (half - bx), 16), bx)
        return both_copy(m, side, d, rows, 2, to_x)

    def core_copy(m, side, d):
        half, _ = rows_of(m)
        rows = pl.ds(pl.multiple_of(core * half, 16), half)
        return both_copy(m, side, d, rows, 3, to_core)

    def both_copy(m, side, d, rows, stage, to):
        if d == 0:
            ref = outs[m].at[pl.ds(z * 2 + 1 - y, 1), rows, :]
        else:
            ref = outs[m].at[pl.ds((z + side * d) * 2, 2), rows, :]
        return copy(ref, ref, stage, m, item(side, d), to)

    sides = lambda d: (1,) if d == 0 else (-1, 1)
    order = []
    for m in range(count):
        blocks = [[(m, s, d) for s in sides(d)] for d in range(line)]
        if m == 0:
            order += blocks[0] + blocks[1]
        else:
            order += blocks[1]
        if m + 1 < count:
            order += [(m + 1, 1, 0)]
        for block in blocks[2:]:
            order += block

    def line_stage(m, side, d):
        if d > 0:
            line_arrival(m, side, d).wait_recv()
        if d == 0:
            pl.when(z < line - 1)(lambda: line_copy(m, -1, 1).start())
            pl.when(z > 0)(lambda: line_copy(m, 1, 1).start())
        elif d < line - 1:
            onward = z < line - 1 if side < 0 else z > 0
            pl.when(onward)(lambda: line_copy(m, side, d + 1).start())
        y_copy(m, side, d).start()

    def y_stage(m, side, d):
        y_copy(m, side, d).wait_recv()
        x_copy(m, side, d).start()

    def x_stage(m, side, d):
        x_copy(m, side, d).wait_recv()
        core_copy(m, side, d).start()

    stages = (line_stage, y_stage, x_stage)
    for m in range(count):
        pltpu.make_async_copy(ins[m], outs[m].at[f], local.at[m]).start()
    for k in range(len(order) + len(stages) - 1):
        for lag, stage in enumerate(stages):
            if 0 <= k - lag < len(order):
                it = order[k - lag]
                guard(exists(*it[1:]), functools.partial(stage, *it))
    for it in order:
        m, side, d = it

        def finish():
            core_copy(m, side, d).wait()
            x_copy(m, side, d).wait_send()
            y_copy(m, side, d).wait_send()

        guard(exists(side, d), finish)
        if d > 0:
            sent = z - (d - 1) >= 0 if side < 0 else z + (d - 1) < line
            onward = z < line - 1 if side < 0 else z > 0
            pl.when(sent & onward)(lambda: line_copy(m, side, d).wait_send())
    for m in range(count):
        pltpu.make_async_copy(ins[m], outs[m].at[f], local.at[m]).wait()


def gather(shards, n, shares):
    count = len(shards)
    items = n - 1
    return pl.pallas_call(
        functools.partial(gather_kernel, count=count, line=n // 2, shares=shares),
        out_shape=[jax.ShapeDtypeStruct((n, *a.shape), a.dtype) for a in shards],
        in_specs=[pl.BlockSpec(memory_space=pl.ANY)] * count,
        out_specs=[pl.BlockSpec(memory_space=pl.ANY)] * count,
        scratch_shapes=[
            pltpu.SemaphoreType.DMA((4, count, items)),
            pltpu.SemaphoreType.DMA((4, count, items)),
            pltpu.SemaphoreType.DMA((count,)),
        ],
        compiler_params=pltpu.CompilerParams(collective_id=0, has_side_effects=True),
        cost_estimate=pl.CostEstimate(flops=0, bytes_accessed=200 << 20, transcendentals=0),
        name="gather",
    )(*shards)


def by_neighbours(n, rep):
    return n == 8 and rep == 4


def all_weights(w_in, w_out, gains, n, rep):
    split = H * HD + 2 * KVH * HD
    low_in, low_out = w_in.astype(bf16), w_out.astype(bf16)
    low_gains = jnp.pad(gains.astype(bf16), ((0, 62), (0, 0)))
    shards = [low_gains, low_in[:, :split], low_out[0], low_in[:, split:], low_out[1]]
    if by_neighbours(n, rep):
        full = gather(shards, n, (16, 48, 16, 48, 32))
    else:
        full = [lax.all_gather(a, "fsdp") for a in shards]
    gain_full = full[0][:, :8].astype(f32).transpose(1, 0, 2).reshape(8, -1)
    return [gain_full] + [a.reshape(-1, a.shape[-1]) for a in full[1:]]


rate_in = 0.02
rate_out = 0.08
rate_gains = 1.2


def body(
    tokens,
    target,
    doc_lengths,
    corpus_ids,
    corpus_weights,
    w_in,
    w_out,
    gains,
    first_in,
    first_out,
    first_gains,
    second_in,
    second_out,
    second_gains,
    outer_in,
    outer_out,
    outer_gains,
):
    n, rep = lax.axis_size("fsdp"), lax.axis_size("rep")
    line = n // 2
    f, r = lax.axis_index("fsdp"), lax.axis_index("rep")
    z, y = f // 2, f % 2
    direct = by_neighbours(n, rep)
    place = jnp.stack([z if direct else 0 * z, r % 2, y if direct else 0 * y]).astype(jnp.int32)
    rows_in, rows_out = w_in.shape[0], w_out.shape[1]
    gain_full, wq, proj, wf, down = all_weights(w_in, w_out, gains, n, rep)
    x, tgt, lengths = tokens[0], target[0], doc_lengths[0]
    ids = corpus_ids[0][:, None]

    first_low, packed = qkv(x, gain_full, wq)
    mixed, lse = attention(lengths, packed)
    middle, second_low, hidden, d_both, dy = ffn(corpus_weights, x, mixed, tgt, ids, gain_full, proj, wf, down)

    every = jnp.arange(line, dtype=jnp.int32)
    ours, theirs = every * 2 + y, every * 2 + 1 - y
    flip = flip_pairs(n)

    def by_library(a, bs, name):
        block = 2 * BQ if a.shape[1] % (2 * BQ) == 0 else BQ
        every_row = jnp.arange(a.shape[1] // block, dtype=jnp.int32)
        total = grad_rows(every_row, a, bs, block, name=name)
        return lax.psum_scatter(total.reshape(a.shape[1], -1), "fsdp", scatter_dimension=0, tiled=True)[None], ()

    def pair_first(a, bs, rows, name):
        if not direct:
            return by_library(a, bs, name)
        away = grad_rows(theirs, a, bs, rows, name=name + "_send")
        came = lax.ppermute(away, "fsdp", flip)
        total = grad_rows(ours, a, bs, rows, add=came, name=name + "_keep")
        return total, line_sum(total, z, line)

    def line_first(a, bs, rows, name):
        if not direct:
            return by_library(a, bs, name)
        total = grad_rows(every, a, bs, 2 * rows, name=name)
        right, left = line_sum(total, z, line)
        mine = lax.dynamic_index_in_dim(total, z, 0, keepdims=False)
        mine = (mine.astype(f32) + right.astype(f32) + left.astype(f32)).astype(bf16).reshape(2, rows, -1)
        came = lax.ppermute(lax.dynamic_index_in_dim(mine, 1 - y, 0, keepdims=False), "fsdp", flip)
        return mine, (came,)

    gate_sum = pair_first(second_low, [(d_both, 0, FF)], rows_in, "grad_gate")
    down_sum = line_first(hidden, [(dy, 0, dy.shape[1])], rows_out, "grad_down")
    up_sum = pair_first(second_low, [(d_both, 1, FF)], rows_in, "grad_up")
    activations, d_mid, d_low, d_mix, gain_two = mid(
        corpus_weights, middle, hidden, d_both, tgt, ids, gain_full, proj, wf, down
    )
    proj_sum = pair_first(mixed, [(d_low, 0, d_low.shape[1])], rows_out, "grad_proj")
    dq, dk, dv = attention_back(lengths, packed, d_mix, mixed, lse)
    q_sum = pair_first(first_low, [(dq, 0, H * HD)], rows_in, "grad_q")
    kv_sum = pair_first(first_low, [(dk, 0, KVH * HD), (dv, 0, KVH * HD)], rows_in, "grad_kv")
    input_grad, gain_one = input_back(x, d_mid, dq, dk, dv, gain_full, wq)

    by_y = place.at[0].set(place[2])
    flat = lambda a: a.reshape(-1, a.shape[-1])

    def weight_steps(pieces, first, second, w, outer, rate):
        grads = steps = None
        for spot, ((own, terms), rows, row_at, col_at, cols, tile) in pieces:
            grads, keep, send = adam_piece(
                spot, own, terms, first, second, w, grads, rows, row_at, col_at, cols, tile, rate
            )
            keep, other = rep_sum(keep, send, rep)
            steps = outer_piece(place, keep, other, outer, w, steps, rows, row_at, col_at, cols, tile, rep)
        return grads, steps

    qw, kvw = H * HD, 2 * KVH * HD
    in_pieces = [
        (place, (gate_sum, rows_in, 0, qw + kvw, FF, 512)),
        (place, (up_sum, rows_in, 0, qw + kvw + FF, FF, 512)),
        (place, (q_sum, rows_in, 0, 0, qw, 512)),
        (place, (kv_sum, rows_in, 0, qw, kvw, 512)),
    ]
    width = w_out.shape[2]
    out_pieces = [
        (by_y, (down_sum, rows_out, rows_out, 0, width, 512)),
        (place, (proj_sum, rows_out, 0, 0, width, 512)),
    ]
    out_grads, out_steps = weight_steps(
        out_pieces, flat(first_out[0]), flat(second_out[0]), flat(w_out), flat(outer_out), rate_out
    )
    in_grads, in_steps = weight_steps(in_pieces, first_in[0], second_in[0], w_in, outer_in, rate_in)

    gain_full = jnp.stack([jnp.sum(gain_one, axis=0), jnp.sum(gain_two, axis=0)])
    gain_share = lax.psum_scatter(gain_full, "fsdp", scatter_dimension=1, tiled=True)
    first_gains_new, second_gains_new, delta = adam_step(gain_share, first_gains[0], second_gains[0], gains, rate_gains)
    sum_gains = lax.psum(delta, "rep")
    diff_gains, outer_gains_new, new_gains = outer_step(sum_gains, outer_gains, gains, rep)

    out_shape = lambda a: a.reshape(2, rows_out, width)
    diff_in, outer_in_new, new_in, copy_in = in_steps
    diff_out, outer_out_new, new_out, copy_out = (out_shape(a) for a in out_steps)
    grad_in, first_in_new, second_in_new = in_grads
    grad_out, first_out_new, second_out_new = (out_shape(a) for a in out_grads)
    return (
        activations[None],
        input_grad[None],
        grad_in[None],
        grad_out[None],
        gain_share[None],
        first_in_new[None],
        first_out_new[None],
        first_gains_new[None],
        second_in_new[None],
        second_out_new[None],
        second_gains_new[None],
        diff_in,
        diff_out,
        diff_gains,
        outer_in_new,
        outer_out_new,
        outer_gains_new,
        new_in,
        new_out,
        new_gains,
        copy_in,
        copy_out,
        new_gains.astype(bf16),
    )


def solution(mesh):
    rows = P(("rep", "fsdp"), None, None)
    pair = P(("rep", "fsdp"), None)
    w_in, w_out, gains = P("fsdp", None), P(None, "fsdp", None), P(None, "fsdp")
    m_in, m_out, m_gains = P("rep", "fsdp", None), P("rep", None, "fsdp", None), P("rep", None, "fsdp")
    weights, moments = (w_in, w_out, gains), (m_in, m_out, m_gains)
    return jax.shard_map(
        body,
        mesh=mesh,
        in_specs=(rows, rows, pair, pair, P(), *weights, *moments, *moments, *weights),
        out_specs=(rows, rows, *moments, *moments, *moments, *weights, *weights, *weights, *weights),
        check_vma=False,
    )
```

```python
import functools
import jax
import jax.numpy as jnp
from jax import lax
from jax.experimental import pallas as pl
from jax.experimental.pallas import tpu as pltpu
from jax.sharding import PartitionSpec as P

H = 16
HD = 64
KVH = 4
FF = 1024
LEN = 1024
NCORP = 8
f32 = jnp.float32
bf16 = jnp.bfloat16
norm_eps = 1e-06
BQ = 256
NT = (((1,), (1,)), ((), ()))
TN = (((0,), (0,)), ((), ()))


def mm(a, b, dims=(((1,), (0,)), ((), ()))):
    return lax.dot_general(a, b, dims, preferred_element_type=f32)


def params(**kw):
    return pltpu.CompilerParams(vmem_limit_bytes=60 << 20, **kw)


def one(shape, index):
    return pl.BlockSpec(shape, index, pipeline_mode=pl.Buffered(1))


def qkv_kernel(x_ref, g_ref, w_ref, first_ref, packed_ref):
    x = x_ref[...].astype(f32)
    r = lax.rsqrt(jnp.mean(x * x, axis=-1, keepdims=True) + norm_eps)
    first = (x * r * g_ref[0:1, :]).astype(bf16)
    first_ref[...] = first
    packed_ref[...] = mm(first, w_ref[...]).astype(bf16)


def qkv(x, gains, w):
    rows, width = x.shape
    cols = w.shape[1]
    return pl.pallas_call(
        qkv_kernel,
        grid=(rows // BQ,),
        in_specs=[
            pl.BlockSpec((BQ, width), lambda i: (i, 0)),
            one(gains.shape, lambda i: (0, 0)),
            one((width, cols), lambda i: (0, 0)),
        ],
        out_specs=[
            pl.BlockSpec((BQ, width), lambda i: (i, 0)),
            pl.BlockSpec((BQ, cols), lambda i: (i, 0)),
        ],
        out_shape=[
            jax.ShapeDtypeStruct((rows, width), bf16),
            jax.ShapeDtypeStruct((rows, cols), bf16),
        ],
        compiler_params=params(),
        cost_estimate=pl.CostEstimate(
            flops=2 * rows * width * cols, bytes_accessed=rows * width * 4 + width * cols * 2, transcendentals=0
        ),
        name="norm_qkv",
    )(x, gains, w)


def doc_start(lengths_ref, position):
    end = jnp.int32(0)
    start = jnp.zeros_like(position)
    for j in range(lengths_ref.shape[0]):
        end = end + lengths_ref[j]
        start = jnp.where(position >= end, end, start)
    return start


def key_blocks(lengths_ref, i):
    first_row = i * BQ
    return i + 1 - doc_start(lengths_ref, first_row) // BQ


def max_blocks():
    return LEN // (2 * BQ) + 1


def attn_kernel(len_ref, q_ref, k_ref, v_ref, o_ref, lse_ref):
    i = pl.program_id(0)
    count = key_blocks(len_ref, i)
    row = i * BQ + lax.broadcasted_iota(jnp.int32, (BQ, 1), 0)
    start = doc_start(len_ref, row)
    lane = lax.broadcasted_iota(jnp.int32, (BQ, 128), 1)
    for nb in range(1, max_blocks() + 1):

        @pl.when(count == nb)
        def _():
            span = nb * BQ
            base = pl.multiple_of((i - (nb - 1)) * BQ, BQ)
            col = base + lax.broadcasted_iota(jnp.int32, (BQ, span), 1)
            bias = jnp.where((col >= start) & (col <= row), 0.0, -1e30)
            k2 = k_ref[pl.ds(base, span), :]
            v2 = v_ref[pl.ds(base, span), :]
            tile = jnp.zeros((BQ, 128), f32)
            outs = []
            for kv in range(2):
                k = k2[:, kv * HD : (kv + 1) * HD]
                v = v2[:, kv * HD : (kv + 1) * HD]
                for g in range(H // KVH):
                    h = kv * (H // KVH) + g
                    q = q_ref[:, h * HD : (h + 1) * HD] * jnp.asarray(HD**-0.5, bf16)
                    s = mm(q, k, NT) + bias
                    m = jnp.max(s, axis=-1, keepdims=True)
                    e = jnp.exp(s - m)
                    total = jnp.sum(e, axis=-1, keepdims=True)
                    o = mm(e.astype(bf16), v) * (1.0 / total)
                    outs.append(o.astype(bf16))
                    tile = jnp.where(lane == h, m + jnp.log(total), tile)
            o_ref[...] = jnp.concatenate(outs, axis=1)
            lse_ref[...] = tile.T[0:8, :]


def attention(lengths, packed):
    qw = H // 2 * HD
    kcol = H * HD // 128
    vcol = kcol + KVH * HD // 128
    return pl.pallas_call(
        attn_kernel,
        grid_spec=pltpu.PrefetchScalarGridSpec(
            num_scalar_prefetch=1,
            grid=(LEN // BQ, 2),
            in_specs=[
                pl.BlockSpec((BQ, qw), lambda i, p, s: (i, p)),
                pl.BlockSpec((LEN, 128), lambda i, p, s: (0, kcol + p)),
                pl.BlockSpec((LEN, 128), lambda i, p, s: (0, vcol + p)),
            ],
            out_specs=[
                pl.BlockSpec((BQ, qw), lambda i, p, s: (i, p)),
                pl.BlockSpec((8, BQ), lambda i, p, s: (p, i)),
            ],
        ),
        out_shape=[
            jax.ShapeDtypeStruct((LEN, H * HD), bf16),
            jax.ShapeDtypeStruct((H, LEN), f32),
        ],
        compiler_params=params(),
        cost_estimate=pl.CostEstimate(flops=4 * H * LEN * LEN * HD * 4, bytes_accessed=1 << 24, transcendentals=0),
        name="attention",
    )(lengths, packed, packed, packed)


def attention_back_step(len_ref, i, q_ref, k_ref, v_ref, d_ref, o_ref, lse_ref, dq_ref, dk_acc, dv_acc, count=None):
    if count is None:
        count = jnp.minimum(i + 1, max_blocks())
    row = i * BQ + lax.broadcasted_iota(jnp.int32, (1, BQ), 1)
    start = doc_start(len_ref, row)
    lane = lax.broadcasted_iota(jnp.int32, (BQ, 128), 1)
    group = H // KVH
    scale = jnp.asarray(HD**-0.5, bf16)
    tile = jnp.zeros((BQ, 128), f32)
    for h in range(2 * group):
        cols = slice(h * HD, (h + 1) * HD)
        dot = jnp.sum(d_ref[:, cols].astype(f32) * o_ref[:, cols].astype(f32), axis=-1, keepdims=True)
        tile = jnp.where(lane == h, dot, tile)
    inner = tile.T
    for nb in range(1, max_blocks() + 1):

        @pl.when(count == nb)
        def _():
            span = nb * BQ
            base = pl.multiple_of((i - (nb - 1)) * BQ, BQ)
            key = base + lax.broadcasted_iota(jnp.int32, (span, BQ), 0)
            bias = jnp.where((key >= start) & (key <= row), 0.0, -1e30)
            k2 = k_ref[pl.ds(base, span), :]
            v2 = v_ref[pl.ds(base, span), :]
            dks, dvs = [], []
            for kv in range(2):
                k = k2[:, kv * HD : (kv + 1) * HD]
                v = v2[:, kv * HD : (kv + 1) * HD]
                dk = dv = None
                dqs = []
                for g in range(group):
                    h = kv * group + g
                    cols = slice(h * HD, (h + 1) * HD)
                    q = q_ref[:, cols] * scale
                    d = d_ref[:, cols]
                    s = mm(k, q, NT) + bias
                    p = jnp.exp(s - lse_ref[h : h + 1, :])
                    dp = mm(v, d, NT)
                    ds = (p * (dp - inner[h : h + 1, :])).astype(bf16)
                    dv_h = mm(p.astype(bf16), d)
                    dk_h = mm(ds, q)
                    dv = dv_h if dv is None else dv + dv_h
                    dk = dk_h if dk is None else dk + dk_h
                    dqs.append(mm(k, ds, TN))
                dq = jnp.concatenate(dqs, axis=0) * (HD**-0.5)
                dq_ref[:, kv * group * HD : (kv + 1) * group * HD] = dq.T.astype(bf16)
                dks.append(dk)
                dvs.append(dv)
            dk_acc[pl.ds(base, span), :] += jnp.concatenate(dks, axis=1)
            dv_acc[pl.ds(base, span), :] += jnp.concatenate(dvs, axis=1)


def attn_back_kernel(len_ref, q_ref, k_ref, v_ref, d_ref, o_ref, lse_ref, dq_ref, dk_ref, dv_ref, dk_acc, dv_acc):
    i = pl.program_id(1)

    @pl.when(i == 0)
    def _():
        dk_acc[...] = jnp.zeros_like(dk_acc)
        dv_acc[...] = jnp.zeros_like(dv_acc)

    attention_back_step(
        len_ref, i, q_ref, k_ref, v_ref, d_ref, o_ref, lse_ref, dq_ref, dk_acc, dv_acc, key_blocks(len_ref, i)
    )

    @pl.when(i == pl.num_programs(1) - 1)
    def _():
        dk_ref[...] = dk_acc[...].astype(bf16)
        dv_ref[...] = dv_acc[...].astype(bf16)


def attention_back(lengths, packed, d_mixed, mixed, lse):
    qw = H // 2 * HD
    kcol = H * HD // 128
    vcol = kcol + KVH * HD // 128
    return pl.pallas_call(
        attn_back_kernel,
        grid_spec=pltpu.PrefetchScalarGridSpec(
            num_scalar_prefetch=1,
            grid=(2, LEN // BQ),
            in_specs=[
                pl.BlockSpec((BQ, qw), lambda p, i, s: (i, p)),
                pl.BlockSpec((LEN, 128), lambda p, i, s: (0, kcol + p)),
                pl.BlockSpec((LEN, 128), lambda p, i, s: (0, vcol + p)),
                pl.BlockSpec((BQ, qw), lambda p, i, s: (i, p)),
                pl.BlockSpec((BQ, qw), lambda p, i, s: (i, p)),
                pl.BlockSpec((8, BQ), lambda p, i, s: (p, i)),
            ],
            out_specs=[
                pl.BlockSpec((BQ, qw), lambda p, i, s: (i, p)),
                pl.BlockSpec((LEN, 128), lambda p, i, s: (0, p)),
                pl.BlockSpec((LEN, 128), lambda p, i, s: (0, p)),
            ],
            scratch_shapes=[pltpu.VMEM((LEN, 128), f32), pltpu.VMEM((LEN, 128), f32)],
        ),
        out_shape=[
            jax.ShapeDtypeStruct((LEN, H * HD), bf16),
            jax.ShapeDtypeStruct((LEN, KVH * HD), bf16),
            jax.ShapeDtypeStruct((LEN, KVH * HD), bf16),
        ],
        compiler_params=params(),
        cost_estimate=pl.CostEstimate(flops=10 * H * LEN * LEN * HD * 4, bytes_accessed=1 << 24, transcendentals=0),
        name="attention_back",
    )(lengths, packed, packed, packed, d_mixed, mixed, lse)


def token_weight(table_ref, ids):
    weight = jnp.zeros(ids.shape, f32)
    for j in range(table_ref.shape[0]):
        weight = jnp.where(ids == j, table_ref[j].astype(f32) * 0.25, weight)
    return weight


def ffn_kernel(table_ref, x_ref, mixed_ref, t_ref, ids_ref, g_ref, proj_ref, wf_ref, down_ref,
               middle_ref, second_ref, hidden_ref, dboth_ref, dy_ref, c_ref):
    middle = x_ref[...].astype(f32) + mm(mixed_ref[...], proj_ref[...])
    middle_ref[...] = middle
    r = lax.rsqrt(jnp.mean(middle * middle, axis=-1, keepdims=True) + norm_eps)
    second = (middle * r * g_ref[1:2, :]).astype(bf16)
    second_ref[...] = second
    c = token_weight(table_ref, ids_ref[...])
    c_ref[...] = jnp.broadcast_to(c, c_ref.shape)
    dy = (c * t_ref[...].astype(f32)).astype(bf16)
    dy_ref[...] = dy
    step = 512
    for c in range(0, FF, step):
        gate = mm(second, wf_ref[:, c : c + step])
        up = mm(second, wf_ref[:, FF + c : FF + c + step])
        dh = mm(dy, down_ref[c : c + step, :], NT)
        sig = jax.nn.sigmoid(gate)
        silu = gate * sig
        hidden_ref[:, c : c + step] = (silu * up).astype(bf16)
        dboth_ref[:, c : c + step] = (dh * up * sig * (1.0 + gate * (1.0 - sig))).astype(bf16)
        dboth_ref[:, FF + c : FF + c + step] = (dh * silu).astype(bf16)


def ffn(table, x, mixed, target, ids, gains, proj, wf, down):
    width = x.shape[1]
    rowb = lambda n: pl.BlockSpec((BQ, n), lambda i, s: (i, 0))
    whole = lambda a: one(a.shape, lambda i, s: (0, 0))
    return pl.pallas_call(
        ffn_kernel,
        grid_spec=pltpu.PrefetchScalarGridSpec(
            num_scalar_prefetch=1,
            grid=(LEN // BQ,),
            in_specs=[rowb(width), rowb(H * HD), rowb(width), rowb(1), whole(gains), whole(proj), whole(wf), whole(down)],
            out_specs=[rowb(width), rowb(width), rowb(FF), rowb(2 * FF), rowb(width), rowb(128)],
        ),
        out_shape=[
            jax.ShapeDtypeStruct((LEN, width), f32),
            jax.ShapeDtypeStruct((LEN, width), bf16),
            jax.ShapeDtypeStruct((LEN, FF), bf16),
            jax.ShapeDtypeStruct((LEN, 2 * FF), bf16),
            jax.ShapeDtypeStruct((LEN, width), bf16),
            jax.ShapeDtypeStruct((LEN, 128), f32),
        ],
        compiler_params=params(),
        cost_estimate=pl.CostEstimate(flops=2 * LEN * width * FF * 4, bytes_accessed=40 << 20, transcendentals=0),
        name="ffn",
    )(table, x, mixed, target, ids, gains, proj, wf, down)


def mid_kernel(table_ref, middle_ref, hidden_ref, dboth_ref, t_ref, ids_ref, g_ref, proj_ref, wf_ref, down_ref,
               act_ref, dmid_ref, dlow_ref, dmix_ref, gain_ref):
    middle = middle_ref[...]
    act_ref[...] = (middle + mm(hidden_ref[...], down_ref[...])).astype(bf16)
    r = lax.rsqrt(jnp.mean(middle * middle, axis=-1, keepdims=True) + norm_eps)
    n2 = middle * r
    ds2 = mm(dboth_ref[...], wf_ref[...], NT)
    prod = ds2 * n2
    part = jnp.sum(prod.reshape(BQ // 8, 8, prod.shape[1]), axis=0)

    @pl.when(pl.program_id(0) == 0)
    def _():
        gain_ref[...] = jnp.zeros_like(gain_ref)

    gain_ref[...] += part
    g = g_ref[1:2, :]
    e2 = ds2 * g
    dy = token_weight(table_ref, ids_ref[...]) * t_ref[...].astype(f32)
    dmid = dy + r * (e2 - n2 * jnp.mean(prod * g, axis=-1, keepdims=True))
    dmid_ref[...] = dmid
    low = dmid.astype(bf16)
    dlow_ref[...] = low
    dmix_ref[...] = mm(low, proj_ref[...], NT).astype(bf16)


def mid(table, middle, hidden, dboth, target, ids, gains, proj, wf, down):
    width = middle.shape[1]
    rowb = lambda n: pl.BlockSpec((BQ, n), lambda i, s: (i, 0))
    whole = lambda a: one(a.shape, lambda i, s: (0, 0))
    return pl.pallas_call(
        mid_kernel,
        grid_spec=pltpu.PrefetchScalarGridSpec(
            num_scalar_prefetch=1,
            grid=(LEN // BQ,),
            in_specs=[rowb(width), rowb(FF), rowb(2 * FF), rowb(width), rowb(1), whole(gains), whole(proj), whole(wf), whole(down)],
            out_specs=[rowb(width), rowb(width), rowb(width), rowb(H * HD), pl.BlockSpec((8, width), lambda i, s: (0, 0))],
        ),
        out_shape=[
            jax.ShapeDtypeStruct((LEN, width), bf16),
            jax.ShapeDtypeStruct((LEN, width), f32),
            jax.ShapeDtypeStruct((LEN, width), bf16),
            jax.ShapeDtypeStruct((LEN, H * HD), bf16),
            jax.ShapeDtypeStruct((8, width), f32),
        ],
        compiler_params=params(),
        cost_estimate=pl.CostEstimate(flops=2 * LEN * width * FF * 4, bytes_accessed=40 << 20, transcendentals=0),
        name="mid",
    )(table, middle, hidden, dboth, target, ids, gains, proj, wf, down)


def input_kernel(x_ref, dmid_ref, dq_ref, dk_ref, dv_ref, g_ref, w_ref, out_ref, gain_ref):
    x = x_ref[...].astype(f32)
    r = lax.rsqrt(jnp.mean(x * x, axis=-1, keepdims=True) + norm_eps)
    n1 = x * r
    q, k = H * HD, H * HD + KVH * HD
    ds1 = mm(dq_ref[...], w_ref[:, :q], NT) + mm(dk_ref[...], w_ref[:, q:k], NT) + mm(dv_ref[...], w_ref[:, k:], NT)
    prod = ds1 * n1
    part = jnp.sum(prod.reshape(BQ // 8, 8, prod.shape[1]), axis=0)

    @pl.when(pl.program_id(0) == 0)
    def _():
        gain_ref[...] = jnp.zeros_like(gain_ref)

    gain_ref[...] += part
    g = g_ref[0:1, :]
    out = dmid_ref[...] + r * (ds1 * g - n1 * jnp.mean(prod * g, axis=-1, keepdims=True))
    out_ref[...] = out.astype(bf16)


def input_back(x, dmid, dq, dk, dv, gains, w):
    width = x.shape[1]
    rowb = lambda n: pl.BlockSpec((BQ, n), lambda i: (i, 0))
    whole = lambda a: one(a.shape, lambda i: (0, 0))
    return pl.pallas_call(
        input_kernel,
        grid=(LEN // BQ,),
        in_specs=[rowb(width), rowb(width), rowb(H * HD), rowb(KVH * HD), rowb(KVH * HD), whole(gains), whole(w)],
        out_specs=[rowb(width), pl.BlockSpec((8, width), lambda i: (0, 0))],
        out_shape=[jax.ShapeDtypeStruct((LEN, width), bf16), jax.ShapeDtypeStruct((8, width), f32)],
        compiler_params=params(),
        cost_estimate=pl.CostEstimate(flops=2 * LEN * width * 1536, bytes_accessed=24 << 20, transcendentals=0),
        name="input_back",
    )(x, dmid, dq, dk, dv, gains, w)


def grad_kernel(pick_ref, a_ref, *refs):
    out_ref = refs[-1]
    b_refs = refs[:-1]
    add_ref = None
    if len(b_refs) > 1 and len(b_refs[-1].shape) == 3:
        add_ref, b_refs = b_refs[-1], b_refs[:-1]
    col = 0
    a = a_ref[...]
    for b_ref in b_refs:
        n = b_ref.shape[1]
        g = mm(a, b_ref[...], TN)
        if add_ref is not None:
            g = g + add_ref[0, :, col : col + n].astype(f32)
        out_ref[0, :, col : col + n] = g.astype(bf16)
        col += n


def grad_rows(pick, a, bs, rows, add=None, name="grad"):
    cols = sum(width for _, _, width in bs)
    count = pick.shape[0]
    specs = [pl.BlockSpec((LEN, rows), lambda j, p: (0, p[j]))]
    specs += [one((LEN, width), functools.partial(lambda at, j, p: (0, at), at)) for _, at, width in bs]
    ops = [a, *(b for b, _, _ in bs)]
    if add is not None:
        specs.append(pl.BlockSpec((1, rows, cols), lambda j, p: (j, 0, 0)))
        ops.append(add)
    return pl.pallas_call(
        grad_kernel,
        grid_spec=pltpu.PrefetchScalarGridSpec(
            num_scalar_prefetch=1,
            grid=(count,),
            in_specs=specs,
            out_specs=pl.BlockSpec((1, rows, cols), lambda j, p: (j, 0, 0)),
        ),
        out_shape=jax.ShapeDtypeStruct((count, rows, cols), bf16),
        compiler_params=params(),
        cost_estimate=pl.CostEstimate(flops=2 * LEN * rows * count * cols, bytes_accessed=12 << 20, transcendentals=0),
        name=name,
    )(pick, *ops)


def flip_pairs(n):
    return [(i, i ^ 1) for i in range(n)]


def add_low(a, b):
    return (a.astype(f32) + b.astype(f32)).astype(a.dtype)


beta_first = 0.9
beta_second = 0.95
adam_eps = 1e-08
decay_rate = 0.1
outer_decay = 0.5
outer_rate = 0.7
STEP = 10


def adam_step(grad, first, second, weight, rate):
    first_new = beta_first * first + (1.0 - beta_first) * grad
    second_new = beta_second * second + (1.0 - beta_second) * grad * grad
    ratio = first_new / (1.0 - beta_first**STEP) / (jnp.sqrt(second_new / (1.0 - beta_second**STEP)) + adam_eps)
    local = weight - rate * (ratio + decay_rate * weight)
    return first_new, second_new, weight - local


def outer_step(delta_sum, momentum, weight, groups):
    average = delta_sum / groups
    momentum_new = outer_decay * momentum + average
    return average, momentum_new, weight - outer_rate * (average + outer_decay * momentum_new)


def adam_kernel(place_ref, own_ref, *refs, terms, rate):
    refs = list(refs)
    slots = refs.pop(0) if terms else None
    first_ref, second_ref, w_ref = refs[:3]
    grad_ref, first_new_ref, second_new_ref, keep_ref, send_ref = refs[-5:]
    grad = own_ref[0].astype(f32)
    if terms:
        grad = grad + slots[0].astype(f32)
        grad = grad + jnp.where(place_ref[3] == 1, slots[1].astype(f32), 0.0)
    first_new, second_new, delta = adam_step(grad, first_ref[...], second_ref[...], w_ref[...], rate)
    grad_ref[...] = grad
    first_new_ref[...] = first_new
    second_new_ref[...] = second_new
    half = delta.shape[0] // 2
    low = delta.astype(bf16)
    core = place_ref[1]

    @pl.when(core == 0)
    def _():
        keep_ref[...] = low[:half]
        send_ref[...] = low[half:]

    @pl.when(core != 0)
    def _():
        keep_ref[...] = low[half:]
        send_ref[...] = low[:half]


def adam_piece(place, own, terms, first, second, w, held, rows, row_at, col_at, cols, tile, rate):
    at = lambda j, p: (row_at // rows, col_at // tile + j)
    piece = pl.BlockSpec((pl.Element(2), pl.Element(rows), pl.Element(tile)), lambda j, p: (2, 0, j * tile))
    half = pl.BlockSpec((rows // 2, tile), lambda j, p: (0, j))
    state = pl.BlockSpec((rows, tile), at)
    full = jax.ShapeDtypeStruct(first.shape, f32)
    low = jax.ShapeDtypeStruct((rows // 2, cols), bf16)
    specs = [pl.BlockSpec((1, rows, tile), lambda j, p: (p[0], 0, j))] + [piece] * len(terms) + [state] * 3
    ops = [own, *terms, first, second, w]
    aliases = {}
    if held is not None:
        aliases = {1 + len(ops) + k: k for k in range(3)}
        ops += list(held)
        specs += [pl.BlockSpec(memory_space=pl.ANY)] * 3
    out = pl.pallas_call(
        functools.partial(adam_kernel, terms=len(terms), rate=rate),
        grid_spec=pltpu.PrefetchScalarGridSpec(
            num_scalar_prefetch=1,
            grid=(cols // tile,),
            in_specs=specs,
            out_specs=[state, state, state, half, half],
        ),
        out_shape=[full, full, full, low, low],
        input_output_aliases=aliases,
        compiler_params=params(),
        cost_estimate=pl.CostEstimate(flops=0, bytes_accessed=rows * cols * 28, transcendentals=0),
        name="adam",
    )(place, *ops)
    return out[:3], out[3], out[4]


def outer_kernel(place_ref, keep_ref, other_ref, outer_ref, w_ref, *refs, groups):
    diff_ref, outer_new_ref, new_ref, copy_ref = refs[-4:]
    core = place_ref[1]
    half = keep_ref.shape[0]

    def write(rows, total_ref):
        average, momentum, weight = outer_step(total_ref[...].astype(f32), outer_ref[rows, :], w_ref[rows, :], groups)
        diff_ref[rows, :] = average
        outer_new_ref[rows, :] = momentum
        new_ref[rows, :] = weight
        copy_ref[rows, :] = weight.astype(bf16)

    @pl.when(core == 0)
    def _():
        write(slice(0, half), keep_ref)
        write(slice(half, 2 * half), other_ref)

    @pl.when(core != 0)
    def _():
        write(slice(0, half), other_ref)
        write(slice(half, 2 * half), keep_ref)


def outer_piece(place, keep, other, outer, w, held, rows, row_at, col_at, cols, tile, groups):
    half = pl.BlockSpec((rows // 2, tile), lambda j, p: (0, j))
    state = pl.BlockSpec((rows, tile), lambda j, p: (row_at // rows, col_at // tile + j))
    full = jax.ShapeDtypeStruct(outer.shape, f32)
    specs = [half, half, state, state]
    ops = [keep, other, outer, w]
    aliases = {}
    if held is not None:
        aliases = {1 + len(ops) + k: k for k in range(4)}
        ops += list(held)
        specs += [pl.BlockSpec(memory_space=pl.ANY)] * 4
    return pl.pallas_call(
        functools.partial(outer_kernel, groups=groups),
        grid_spec=pltpu.PrefetchScalarGridSpec(
            num_scalar_prefetch=1, grid=(cols // tile,), in_specs=specs, out_specs=[state] * 4
        ),
        out_shape=[full, full, full, jax.ShapeDtypeStruct(outer.shape, bf16)],
        input_output_aliases=aliases,
        compiler_params=params(),
        cost_estimate=pl.CostEstimate(flops=0, bytes_accessed=rows * cols * 24, transcendentals=0),
        name="outer",
    )(place, *ops)


def rep_sum(keep, send, rep):
    pair = flip_pairs(rep)
    part = add_low(keep, lax.ppermute(send, "rep", pair))
    for hop in range(1, (rep - 1).bit_length()):
        part = add_low(part, lax.ppermute(part, "rep", [(i, i ^ (1 << hop)) for i in range(rep)]))
    return part, lax.ppermute(part, "rep", pair)


def gather_kernel(*refs, count, line, shares):
    ins, outs = refs[:count], refs[count : 2 * count]
    send, recv, local = refs[2 * count :]
    r, f = lax.axis_index("rep"), lax.axis_index("fsdp")
    x, core, z, y = r // 2, r % 2, f // 2, f % 2
    to_y = (r, f + 1 - 2 * y)
    to_x = (r + 2 - 4 * x, f)
    to_core = (r + 1 - 2 * core, f)
    barrier = pltpu.get_barrier_semaphore()
    greet = lambda to: pl.semaphore_signal(barrier, inc=1, device_id=to, device_id_type=pl.DeviceIdType.MESH)
    for to in (to_y, to_x, to_core):
        greet(to)
    pl.when(z > 0)(lambda: greet((r, f - 2)))
    pl.when(z < line - 1)(lambda: greet((r, f + 2)))
    pl.semaphore_wait(barrier, 3 + jnp.where(z > 0, 1, 0) + jnp.where(z < line - 1, 1, 0))

    def item(side, d):
        return 0 if d == 0 else 2 * d - 1 + (side > 0)

    def exists(side, d):
        return None if d == 0 else (z - d >= 0 if side < 0 else z + d < line)

    def guard(cond, fn):
        if cond is None:
            fn()
        else:
            pl.when(cond)(fn)

    def rows_of(m):
        rows = ins[m].shape[0]
        half = rows // 2
        return half, shares[m]

    def copy(src, dst, stage, m, k, to):
        return pltpu.make_async_remote_copy(
            src_ref=src, dst_ref=dst, send_sem=send.at[stage, m, k], recv_sem=recv.at[stage, m, k],
            device_id=to, device_id_type=pl.DeviceIdType.MESH,
        )

    def portion(m):
        half, bx = rows_of(m)
        return pl.ds(pl.multiple_of(core * half + x * bx, 16), half - bx)

    def line_copy(m, side, d):
        plane = z - (d - 1) if side < 0 else z + (d - 1)
        to = (r, f + 2) if side < 0 else (r, f - 2)
        rows = portion(m)
        dst = outs[m].at[plane * 2 + y, rows, :]
        src = ins[m].at[rows, :] if d == 1 else dst
        return copy(src, dst, 0, m, item(side, d), to)

    def line_arrival(m, side, d):
        plane = z - d if side < 0 else z + d
        dst = outs[m].at[plane * 2 + y, portion(m), :]
        return copy(dst, dst, 0, m, item(side, d), to_y)

    def y_copy(m, side, d):
        plane = z + side * d
        dst = outs[m].at[plane * 2 + y, portion(m), :]
        return copy(ins[m].at[portion(m), :] if d == 0 else dst, dst, 1, m, item(side, d), to_y)

    def x_copy(m, side, d):
        half, bx = rows_of(m)
        rows = pl.ds(pl.multiple_of(core * half + x * (half - bx), 16), bx)
        return both_copy(m, side, d, rows, 2, to_x)

    def core_copy(m, side, d):
        half, _ = rows_of(m)
        rows = pl.ds(pl.multiple_of(core * half, 16), half)
        return both_copy(m, side, d, rows, 3, to_core)

    def both_copy(m, side, d, rows, stage, to):
        if d == 0:
            ref = outs[m].at[pl.ds(z * 2 + 1 - y, 1), rows, :]
        else:
            ref = outs[m].at[pl.ds((z + side * d) * 2, 2), rows, :]
        return copy(ref, ref, stage, m, item(side, d), to)

    sides = lambda d: (1,) if d == 0 else (-1, 1)
    order = []
    for m in range(count):
        blocks = [[(m, s, d) for s in sides(d)] for d in range(line)]
        if m == 0:
            order += blocks[0] + blocks[1]
        else:
            order += blocks[1]
        if m + 1 < count:
            order += [(m + 1, 1, 0)]
        for block in blocks[2:]:
            order += block

    def line_stage(m, side, d):
        if d > 0:
            line_arrival(m, side, d).wait_recv()
        if d == 0:
            pl.when(z < line - 1)(lambda: line_copy(m, -1, 1).start())
            pl.when(z > 0)(lambda: line_copy(m, 1, 1).start())
        elif d < line - 1:
            onward = z < line - 1 if side < 0 else z > 0
            pl.when(onward)(lambda: line_copy(m, side, d + 1).start())
        y_copy(m, side, d).start()

    def y_stage(m, side, d):
        y_copy(m, side, d).wait_recv()
        x_copy(m, side, d).start()

    def x_stage(m, side, d):
        x_copy(m, side, d).wait_recv()
        core_copy(m, side, d).start()

    stages = (line_stage, y_stage, x_stage)
    for m in range(count):
        pltpu.make_async_copy(ins[m], outs[m].at[f], local.at[m]).start()
    for k in range(len(order) + len(stages) - 1):
        for lag, stage in enumerate(stages):
            if 0 <= k - lag < len(order):
                it = order[k - lag]
                guard(exists(*it[1:]), functools.partial(stage, *it))
    for it in order:
        m, side, d = it

        def finish():
            core_copy(m, side, d).wait()
            x_copy(m, side, d).wait_send()
            y_copy(m, side, d).wait_send()

        guard(exists(side, d), finish)
        if d > 0:
            sent = z - (d - 1) >= 0 if side < 0 else z + (d - 1) < line
            onward = z < line - 1 if side < 0 else z > 0
            pl.when(sent & onward)(lambda: line_copy(m, side, d).wait_send())
    for m in range(count):
        pltpu.make_async_copy(ins[m], outs[m].at[f], local.at[m]).wait()


def gather(shards, n, shares):
    count = len(shards)
    items = n - 1
    return pl.pallas_call(
        functools.partial(gather_kernel, count=count, line=n // 2, shares=shares),
        out_shape=[jax.ShapeDtypeStruct((n, *a.shape), a.dtype) for a in shards],
        in_specs=[pl.BlockSpec(memory_space=pl.ANY)] * count,
        out_specs=[pl.BlockSpec(memory_space=pl.ANY)] * count,
        scratch_shapes=[
            pltpu.SemaphoreType.DMA((4, count, items)),
            pltpu.SemaphoreType.DMA((4, count, items)),
            pltpu.SemaphoreType.DMA((count,)),
        ],
        compiler_params=pltpu.CompilerParams(collective_id=0, has_side_effects=True),
        cost_estimate=pl.CostEstimate(flops=0, bytes_accessed=200 << 20, transcendentals=0),
        name="gather",
    )(*shards)


def by_neighbours(n, rep):
    return n == 8 and rep == 4


def all_weights(w_in, w_out, gains, n, rep):
    split = H * HD + 2 * KVH * HD
    low_in, low_out = w_in.astype(bf16), w_out.astype(bf16)
    low_gains = jnp.pad(gains.astype(bf16), ((0, 62), (0, 0)))
    shards = [low_gains, low_in[:, :split], low_out[0], low_in[:, split:], low_out[1]]
    if by_neighbours(n, rep):
        full = gather(shards, n, (16, 48, 16, 48, 32))
    else:
        full = [lax.all_gather(a, "fsdp") for a in shards]
    gain_full = full[0][:, :8].astype(f32).transpose(1, 0, 2).reshape(8, -1)
    return [gain_full] + [a.reshape(-1, a.shape[-1]) for a in full[1:]]


PIECES = ("down", "gate", "up", "proj", "q", "kv")


def back_kernel(*refs, names, line):
    R = dict(zip(names, refs))
    r, f = lax.axis_index("rep"), lax.axis_index("fsdp")
    z, y = f // 2, f % 2
    n = 2 * line
    barrier = pltpu.get_barrier_semaphore()
    for step in range(1, n):
        pl.semaphore_signal(barrier, inc=1, device_id=(r, lax.rem(f + step, n)), device_id_type=pl.DeviceIdType.MESH)
    pl.semaphore_wait(barrier, n - 1)

    loads = ("proj", "wf", "down", "wq")
    load = lambda k: pltpu.make_async_copy(R[loads[k]], R["v_" + loads[k]], R["load_sem"].at[k])
    for k in range(len(loads)):
        load(k).start()

    def remote(src, dst, send, recv, to):
        return pltpu.make_async_remote_copy(
            src_ref=src, dst_ref=dst, send_sem=send, recv_sem=recv, device_id=(r, to), device_id_type=pl.DeviceIdType.MESH
        )

    def run(body, grid, ins, outs):
        pltpu.emit_pipeline(body, grid=grid, in_specs=[s for _, s in ins], out_specs=[s for _, s in outs])(
            *[a for a, _ in ins], *[a for a, _ in outs]
        )

    rows_of = {p: R["own_" + p].shape[1] for p in PIECES}
    cols_of = {p: R["own_" + p].shape[2] for p in PIECES}
    sources = {
        "down": ("hidden", [("dy", 0, R["dy"].shape[1])]),
        "gate": ("second", [("dboth", 0, FF)]),
        "up": ("second", [("dboth", 1, FF)]),
        "proj": ("mixed", [("dlow", 0, R["dlow"].shape[1])]),
        "q": ("first", [("dq", 0, H * HD)]),
        "kv": ("first", [("dk", 0, KVH * HD), ("dv", 0, KVH * HD)]),
    }

    def gradient(p, side, out, add=None):
        a, bs = sources[p]
        rows, cols = rows_of[p], cols_of[p]
        block = pl.BlockSpec((1, rows, cols), lambda j: (j, 0, 0))
        ins = [(R[a], pl.BlockSpec((LEN, rows), lambda j: (0, j * 2 + side)))]
        for b, at, width in bs:
            ins.append((R[b], pl.BlockSpec((LEN, width), functools.partial(lambda at, j: (0, at), at))))
        if add is not None:
            ins.append((add, block))

        def step(*refs):
            out_ref, a_ref, b_refs = refs[-1], refs[0], refs[1 : 1 + len(bs)]
            col = 0
            for b_ref in b_refs:
                width = b_ref.shape[1]
                g = mm(a_ref[...], b_ref[...], TN)
                if add is not None:
                    g = g + refs[-2][0, :, col : col + width].astype(f32)
                out_ref[0, :, col : col + width] = g.astype(bf16)
                col += width

        run(step, (line,), ins, [(out, block)])

    def pair_copy(p):
        k = PIECES.index(p)
        return remote(R["away_" + p], R["came_" + p], R["y_send"].at[k], R["y_recv"].at[k], f + 1 - 2 * y)

    def send_away(p):
        gradient(p, 1 - y, R["away_" + p])
        pair_copy(p).start()

    middle = (z > 0) & (z < line - 1)
    low = z < line // 2
    inner = jnp.where(low, f + 2, f - 2)
    outer = jnp.where(low, f - 2, f + 2)

    def end_copy(p, k):
        i = PIECES.index(p)
        t = jnp.where(low, line - 1 - k, k)
        return remote(R["own_" + p].at[t], R["slot_" + p].at[k], R["z_send"].at[i, k], R["z_recv"].at[i, k], inner)

    def middle_copy(p, k):
        i = PIECES.index(p)
        slot = (4, 3, 2)[k]
        to = outer if k == 2 else inner
        return remote(R["msg_" + p].at[k], R["slot_" + p].at[slot], R["z_send"].at[i, k], R["z_recv"].at[i, slot], to)

    def slot_wait(p, slot):
        i = PIECES.index(p)
        ref = R["slot_" + p].at[slot]
        remote(ref, ref, R["z_send"].at[i, 0], R["z_recv"].at[i, slot], inner).wait_recv()

    def keep(p):
        pair_copy(p).wait_recv()
        gradient(p, y, R["own_" + p], R["came_" + p])

        @pl.when(~middle)
        def _():
            for k in range(3):
                end_copy(p, k).start()

    def serve(p, k):
        @pl.when(middle)
        def _():
            slot = (0, 1, 4)[k]
            slot_wait(p, slot)
            t = (3 * (2 - z), 3 - z, 3 * (z - 1))[k]
            rows, cols = rows_of[p], cols_of[p]
            block = pl.BlockSpec((rows // 2, cols), lambda j: (j, 0))

            def step(a_ref, b_ref, o_ref):
                o_ref[...] = (a_ref[...].astype(f32) + b_ref[...].astype(f32)).astype(bf16)

            run(step, (2,), [(R["own_" + p].at[t], block), (R["slot_" + p].at[slot], block)], [(R["msg_" + p].at[k], block)])
            middle_copy(p, k).start()

    rowb = lambda width: pl.BlockSpec((BQ, width), lambda i: (i, 0))
    width = R["x"].shape[1]
    R["gain_acc"][...] = jnp.zeros_like(R["gain_acc"])
    gain_rows = R["gain"][...]

    def mid_step(middle_ref, hidden_ref, dboth_ref, t_ref, c_ref, act_ref, dmid_ref, dlow_ref, dmix_ref):
        mid_v = middle_ref[...]
        act_ref[...] = (mid_v + mm(hidden_ref[...], R["v_down"][...])).astype(bf16)
        inv = lax.rsqrt(jnp.mean(mid_v * mid_v, axis=-1, keepdims=True) + norm_eps)
        n2 = mid_v * inv
        ds2 = mm(dboth_ref[...], R["v_wf"][...], NT)
        prod = ds2 * n2
        R["gain_acc"][8:16, :] += jnp.sum(prod.reshape(BQ // 8, 8, width), axis=0)
        g = gain_rows[1:2, :]
        dy = c_ref[:, 0:1] * t_ref[...].astype(f32)
        dmid = dy + inv * (ds2 * g - n2 * jnp.mean(prod * g, axis=-1, keepdims=True))
        dmid_ref[...] = dmid
        dlow = dmid.astype(bf16)
        dlow_ref[...] = dlow
        dmix_ref[...] = mm(dlow, R["v_proj"][...], NT).astype(bf16)

    def mid_phase():
        run(
            mid_step,
            (LEN // BQ,),
            [(R["middle"], rowb(width)), (R["hidden"], rowb(FF)), (R["dboth"], rowb(2 * FF)), (R["target"], rowb(width)), (R["c"], rowb(128))],
            [(R["act"], rowb(width)), (R["dmid"], rowb(width)), (R["dlow"], rowb(width)), (R["dmix"], rowb(H * HD))],
        )

    qw = H // 2 * HD
    kcol = H * HD // 128
    vcol = kcol + KVH * HD // 128

    def attention_phase(p):
        qspec = pl.BlockSpec((BQ, qw), lambda i: (i, p))
        whole = lambda at: pl.BlockSpec((LEN, 128), lambda i: (0, at))
        R["dk_acc"][...] = jnp.zeros_like(R["dk_acc"])
        R["dv_acc"][...] = jnp.zeros_like(R["dv_acc"])

        def step(q_ref, k_ref, v_ref, d_ref, o_ref, lse_ref, dq_ref):
            attention_back_step(R["lengths"], pl.program_id(0), q_ref, k_ref, v_ref, d_ref, o_ref, lse_ref, dq_ref, R["dk_acc"], R["dv_acc"])

        pltpu.emit_pipeline(
            step, grid=(LEN // BQ,),
            in_specs=[qspec, whole(kcol + p), whole(vcol + p), qspec, qspec, pl.BlockSpec((8, BQ), lambda i: (p, i))],
            out_specs=[qspec],
        )(R["packed"], R["packed"], R["packed"], R["dmix"], R["mixed"], R["lse"], R["dq"])

        def flush(dk_ref, dv_ref):
            dk_ref[...] = R["dk_acc"][...].astype(bf16)
            dv_ref[...] = R["dv_acc"][...].astype(bf16)

        run(flush, (1,), [], [(R["dk"], pl.BlockSpec((LEN, 128), lambda i: (0, p))), (R["dv"], pl.BlockSpec((LEN, 128), lambda i: (0, p)))])

    def input_step(x_ref, dmid_ref, dq_ref, dk_ref, dv_ref, out_ref):
        x = x_ref[...].astype(f32)
        inv = lax.rsqrt(jnp.mean(x * x, axis=-1, keepdims=True) + norm_eps)
        n1 = x * inv
        q, k = H * HD, H * HD + KVH * HD
        w = R["v_wq"]
        ds1 = mm(dq_ref[...], w[:, :q], NT) + mm(dk_ref[...], w[:, q:k], NT) + mm(dv_ref[...], w[:, k:], NT)
        prod = ds1 * n1
        R["gain_acc"][0:8, :] += jnp.sum(prod.reshape(BQ // 8, 8, width), axis=0)
        g = gain_rows[0:1, :]
        out_ref[...] = (dmid_ref[...] + inv * (ds1 * g - n1 * jnp.mean(prod * g, axis=-1, keepdims=True))).astype(bf16)

    def input_phase():
        run(
            input_step,
            (LEN // BQ,),
            [(R["x"], rowb(width)), (R["dmid"], rowb(width)), (R["dq"], rowb(H * HD)), (R["dk"], rowb(KVH * HD)), (R["dv"], rowb(KVH * HD))],
            [(R["xgrad"], rowb(width))],
        )

    part = width // n

    def gain_copy(step, receive=False):
        peer = lax.rem(f + step, n)
        home = lax.rem(f + n - step, n) if receive else f
        return remote(
            R["gain_acc"].at[:, pl.ds(pl.multiple_of(peer * part, part), part)], R["gain_got"].at[home],
            R["g_send"].at[step - 1], R["g_recv"].at[step - 1], peer,
        )

    own_gain = pltpu.make_async_copy(
        R["gain_acc"].at[:, pl.ds(pl.multiple_of(f * part, part), part)], R["gain_got"].at[f], R["g_send"].at[n - 1]
    )

    for p in ("down", "gate", "up"):
        send_away(p)
    for k in range(3):
        load(k).wait()
    mid_phase()
    send_away("proj")
    keep("down")
    attention_phase(0)
    serve("down", 0)
    attention_phase(1)
    serve("down", 1)
    keep("gate")
    serve("down", 2)
    send_away("q")
    send_away("kv")
    serve("gate", 0)
    load(3).wait()
    input_phase()
    for step in range(1, n):
        gain_copy(step).start()
    own_gain.start()
    serve("gate", 1)
    keep("up")
    serve("gate", 2)
    for k in range(3):
        serve("up", k)
    for p in ("proj", "q", "kv"):
        keep(p)
        for k in range(3):
            serve(p, k)

    for step in range(1, n):
        gain_copy(step, True).wait_recv()
        gain_copy(step).wait_send()
    own_gain.wait()
    for p in PIECES:
        pair_copy(p).wait_send()
        slot_wait(p, 2)

        @pl.when(middle)
        def _():
            slot_wait(p, 3)
            for k in range(3):
                middle_copy(p, k).wait_send()

        @pl.when(~middle)
        def _():
            for k in range(3):
                end_copy(p, k).wait_send()


def backward(lengths, gain, arrays, n, rows_in, rows_out):
    line = n // 2
    width = arrays["x"].shape[1]
    kvw = KVH * HD
    sizes = {
        "down": (rows_out, width), "gate": (rows_in, FF), "up": (rows_in, FF),
        "proj": (rows_out, width), "q": (rows_in, H * HD), "kv": (rows_in, 2 * kvw),
    }
    outs = {
        "act": ((LEN, width), bf16), "dmid": ((LEN, width), f32), "dlow": ((LEN, width), bf16),
        "dmix": ((LEN, H * HD), bf16), "dq": ((LEN, H * HD), bf16), "dk": ((LEN, kvw), bf16), "dv": ((LEN, kvw), bf16),
        "xgrad": ((LEN, width), bf16), "gain_got": ((n, 16, width // n), f32),
    }
    for p, (rows, cols) in sizes.items():
        for kind, count in (("away_", line), ("came_", line), ("own_", line), ("slot_", 5), ("msg_", 3)):
            outs[kind + p] = ((count, rows, cols), bf16)
    dma = pltpu.SemaphoreType.DMA
    pieces = len(PIECES)
    scratch = {
        "v_proj": pltpu.VMEM(arrays["proj"].shape, bf16), "v_wf": pltpu.VMEM(arrays["wf"].shape, bf16),
        "v_down": pltpu.VMEM(arrays["down"].shape, bf16), "v_wq": pltpu.VMEM(arrays["wq"].shape, bf16),
        "gain_acc": pltpu.VMEM((16, width), f32), "dk_acc": pltpu.VMEM((LEN, 128), f32), "dv_acc": pltpu.VMEM((LEN, 128), f32),
        "load_sem": dma((4,)), "y_send": dma((pieces,)), "y_recv": dma((pieces,)),
        "z_send": dma((pieces, 3)), "z_recv": dma((pieces, 5)), "g_send": dma((n,)), "g_recv": dma((n,)),
    }
    names = ["lengths", "gain", *arrays, *outs, *scratch]
    anywhere = pl.BlockSpec(memory_space=pl.ANY)
    got = pl.pallas_call(
        functools.partial(back_kernel, names=names, line=line),
        in_specs=[pl.BlockSpec(memory_space=pltpu.SMEM), pl.BlockSpec(memory_space=pltpu.VMEM)] + [anywhere] * len(arrays),
        out_specs=[anywhere] * len(outs),
        out_shape=[jax.ShapeDtypeStruct(*v) for v in outs.values()],
        scratch_shapes=list(scratch.values()),
        compiler_params=pltpu.CompilerParams(collective_id=1, has_side_effects=True, vmem_limit_bytes=62 << 20),
        cost_estimate=pl.CostEstimate(flops=200 << 30, bytes_accessed=400 << 20, transcendentals=0),
        name="backward",
    )(lengths, gain, *arrays.values())
    return dict(zip(outs, got))


rate_in = 0.02
rate_out = 0.08
rate_gains = 1.2


def body(
    tokens,
    target,
    doc_lengths,
    corpus_ids,
    corpus_weights,
    w_in,
    w_out,
    gains,
    first_in,
    first_out,
    first_gains,
    second_in,
    second_out,
    second_gains,
    outer_in,
    outer_out,
    outer_gains,
):
    n, rep = lax.axis_size("fsdp"), lax.axis_size("rep")
    line = n // 2
    f, r = lax.axis_index("fsdp"), lax.axis_index("rep")
    z, y = f // 2, f % 2
    direct = by_neighbours(n, rep)
    inside = (z > 0) & (z < line - 1)
    place = jnp.stack([z if direct else 0 * z, r % 2, y, inside]).astype(jnp.int32)
    rows_in, rows_out = w_in.shape[0], w_out.shape[1]
    gain_full, wq, proj, wf, down = all_weights(w_in, w_out, gains, n, rep)
    x, tgt, lengths = tokens[0], target[0], doc_lengths[0]
    ids = corpus_ids[0][:, None]

    first_low, packed = qkv(x, gain_full, wq)
    mixed, lse = attention(lengths, packed)
    middle, second_low, hidden, d_both, dy, c = ffn(corpus_weights, x, mixed, tgt, ids, gain_full, proj, wf, down)

    if direct:
        got = backward(
            lengths, gain_full,
            dict(x=x, target=tgt, c=c, middle=middle, hidden=hidden, second=second_low, dboth=d_both, dy=dy, mixed=mixed,
                 packed=packed, lse=lse, first=first_low, proj=proj, wf=wf, down=down, wq=wq),
            n, rows_in, rows_out,
        )
        activations, input_grad = got["act"], got["xgrad"]
        gain_share = jnp.sum(got["gain_got"].reshape(n, 2, 8, -1), axis=(0, 2))
        gate_sum, up_sum, q_sum, kv_sum, down_sum, proj_sum = (
            (got["own_" + p], (got["slot_" + p],)) for p in ("gate", "up", "q", "kv", "down", "proj")
        )
    else:

        def by_library(a, bs, name):
            block = 2 * BQ if a.shape[1] % (2 * BQ) == 0 else BQ
            every_row = jnp.arange(a.shape[1] // block, dtype=jnp.int32)
            total = grad_rows(every_row, a, bs, block, name=name)
            return lax.psum_scatter(total.reshape(a.shape[1], -1), "fsdp", scatter_dimension=0, tiled=True)[None], ()

        gate_sum = by_library(second_low, [(d_both, 0, FF)], "grad_gate")
        down_sum = by_library(hidden, [(dy, 0, dy.shape[1])], "grad_down")
        up_sum = by_library(second_low, [(d_both, 1, FF)], "grad_up")
        activations, d_mid, d_low, d_mix, gain_two = mid(
            corpus_weights, middle, hidden, d_both, tgt, ids, gain_full, proj, wf, down
        )
        proj_sum = by_library(mixed, [(d_low, 0, d_low.shape[1])], "grad_proj")
        dq, dk, dv = attention_back(lengths, packed, d_mix, mixed, lse)
        q_sum = by_library(first_low, [(dq, 0, H * HD)], "grad_q")
        kv_sum = by_library(first_low, [(dk, 0, KVH * HD), (dv, 0, KVH * HD)], "grad_kv")
        input_grad, gain_one = input_back(x, d_mid, dq, dk, dv, gain_full, wq)
        both = jnp.stack([jnp.sum(gain_one, axis=0), jnp.sum(gain_two, axis=0)])
        gain_share = lax.psum_scatter(both, "fsdp", scatter_dimension=1, tiled=True)

    flat = lambda a: a.reshape(-1, a.shape[-1])

    def weight_steps(pieces, first, second, w, outer, rate):
        grads = steps = None
        for spot, ((own, terms), rows, row_at, col_at, cols, tile) in pieces:
            grads, keep, send = adam_piece(
                spot, own, terms, first, second, w, grads, rows, row_at, col_at, cols, tile, rate
            )
            keep, other = rep_sum(keep, send, rep)
            steps = outer_piece(place, keep, other, outer, w, steps, rows, row_at, col_at, cols, tile, rep)
        return grads, steps

    qw, kvw = H * HD, 2 * KVH * HD
    in_pieces = [
        (place, (gate_sum, rows_in, 0, qw + kvw, FF, 512)),
        (place, (up_sum, rows_in, 0, qw + kvw + FF, FF, 512)),
        (place, (q_sum, rows_in, 0, 0, qw, 512)),
        (place, (kv_sum, rows_in, 0, qw, kvw, 512)),
    ]
    width = w_out.shape[2]
    out_pieces = [
        (place, (down_sum, rows_out, rows_out, 0, width, 512)),
        (place, (proj_sum, rows_out, 0, 0, width, 512)),
    ]
    out_grads, out_steps = weight_steps(
        out_pieces, flat(first_out[0]), flat(second_out[0]), flat(w_out), flat(outer_out), rate_out
    )
    in_grads, in_steps = weight_steps(in_pieces, first_in[0], second_in[0], w_in, outer_in, rate_in)

    first_gains_new, second_gains_new, delta = adam_step(gain_share, first_gains[0], second_gains[0], gains, rate_gains)
    sum_gains = lax.psum(delta, "rep")
    diff_gains, outer_gains_new, new_gains = outer_step(sum_gains, outer_gains, gains, rep)

    out_shape = lambda a: a.reshape(2, rows_out, width)
    diff_in, outer_in_new, new_in, copy_in = in_steps
    diff_out, outer_out_new, new_out, copy_out = (out_shape(a) for a in out_steps)
    grad_in, first_in_new, second_in_new = in_grads
    grad_out, first_out_new, second_out_new = (out_shape(a) for a in out_grads)
    return (
        activations[None],
        input_grad[None],
        grad_in[None],
        grad_out[None],
        gain_share[None],
        first_in_new[None],
        first_out_new[None],
        first_gains_new[None],
        second_in_new[None],
        second_out_new[None],
        second_gains_new[None],
        diff_in,
        diff_out,
        diff_gains,
        outer_in_new,
        outer_out_new,
        outer_gains_new,
        new_in,
        new_out,
        new_gains,
        copy_in,
        copy_out,
        new_gains.astype(bf16),
    )


def solution(mesh):
    rows = P(("rep", "fsdp"), None, None)
    pair = P(("rep", "fsdp"), None)
    w_in, w_out, gains = P("fsdp", None), P(None, "fsdp", None), P(None, "fsdp")
    m_in, m_out, m_gains = P("rep", "fsdp", None), P("rep", None, "fsdp", None), P("rep", None, "fsdp")
    weights, moments = (w_in, w_out, gains), (m_in, m_out, m_gains)
    return jax.shard_map(
        body,
        mesh=mesh,
        in_specs=(rows, rows, pair, pair, P(), *weights, *moments, *moments, *weights),
        out_specs=(rows, rows, *moments, *moments, *moments, *weights, *weights, *weights, *weights),
        check_vma=False,
    )
```

```python
import functools
import jax
import jax.numpy as jnp
from jax import lax
from jax.experimental import pallas as pl
from jax.experimental.pallas import tpu as pltpu
from jax.sharding import PartitionSpec as P

H = 16
HD = 64
KVH = 4
FF = 1024
LEN = 1024
NCORP = 8
f32 = jnp.float32
bf16 = jnp.bfloat16
norm_eps = 1e-06
BQ = 256
NT = (((1,), (1,)), ((), ()))
TN = (((0,), (0,)), ((), ()))


def mm(a, b, dims=(((1,), (0,)), ((), ()))):
    return lax.dot_general(a, b, dims, preferred_element_type=f32)


def params(**kw):
    return pltpu.CompilerParams(vmem_limit_bytes=60 << 20, **kw)


def one(shape, index):
    return pl.BlockSpec(shape, index, pipeline_mode=pl.Buffered(1))


def qkv_kernel(x_ref, g_ref, w_ref, first_ref, packed_ref):
    x = x_ref[...].astype(f32)
    r = lax.rsqrt(jnp.mean(x * x, axis=-1, keepdims=True) + norm_eps)
    first = (x * r * g_ref[0:1, :]).astype(bf16)
    first_ref[...] = first
    packed_ref[...] = mm(first, w_ref[...]).astype(bf16)


def qkv(x, gains, w):
    rows, width = x.shape
    cols = w.shape[1]
    return pl.pallas_call(
        qkv_kernel,
        grid=(rows // BQ,),
        in_specs=[
            pl.BlockSpec((BQ, width), lambda i: (i, 0)),
            one(gains.shape, lambda i: (0, 0)),
            one((width, cols), lambda i: (0, 0)),
        ],
        out_specs=[
            pl.BlockSpec((BQ, width), lambda i: (i, 0)),
            pl.BlockSpec((BQ, cols), lambda i: (i, 0)),
        ],
        out_shape=[
            jax.ShapeDtypeStruct((rows, width), bf16),
            jax.ShapeDtypeStruct((rows, cols), bf16),
        ],
        compiler_params=params(),
        cost_estimate=pl.CostEstimate(
            flops=2 * rows * width * cols, bytes_accessed=rows * width * 4 + width * cols * 2, transcendentals=0
        ),
        name="norm_qkv",
    )(x, gains, w)


def doc_start(lengths_ref, position):
    end = jnp.int32(0)
    start = jnp.zeros_like(position)
    for j in range(lengths_ref.shape[0]):
        end = end + lengths_ref[j]
        start = jnp.where(position >= end, end, start)
    return start


def key_blocks(lengths_ref, i):
    first_row = i * BQ
    return i + 1 - doc_start(lengths_ref, first_row) // BQ


def max_blocks():
    return LEN // (2 * BQ) + 1


def attention_step(len_ref, i, count, q_ref, k_ref, v_ref, o_ref, lse_ref):
    row = i * BQ + lax.broadcasted_iota(jnp.int32, (BQ, 1), 0)
    start = doc_start(len_ref, row)
    lane = lax.broadcasted_iota(jnp.int32, (BQ, 128), 1)
    for nb in range(1, max_blocks() + 1):

        @pl.when(count == nb)
        def _():
            span = nb * BQ
            base = pl.multiple_of((i - (nb - 1)) * BQ, BQ)
            col = base + lax.broadcasted_iota(jnp.int32, (BQ, span), 1)
            bias = jnp.where((col >= start) & (col <= row), 0.0, -1e30)
            k2 = k_ref[pl.ds(base, span), :]
            v2 = v_ref[pl.ds(base, span), :]
            tile = jnp.zeros((BQ, 128), f32)
            outs = []
            for kv in range(2):
                k = k2[:, kv * HD : (kv + 1) * HD]
                v = v2[:, kv * HD : (kv + 1) * HD]
                for g in range(H // KVH):
                    h = kv * (H // KVH) + g
                    q = q_ref[:, h * HD : (h + 1) * HD] * jnp.asarray(HD**-0.5, bf16)
                    s = mm(q, k, NT) + bias
                    m = jnp.max(s, axis=-1, keepdims=True)
                    e = jnp.exp(s - m)
                    total = jnp.sum(e, axis=-1, keepdims=True)
                    o = mm(e.astype(bf16), v) * (1.0 / total)
                    outs.append(o.astype(bf16))
                    tile = jnp.where(lane == h, m + jnp.log(total), tile)
            o_ref[...] = jnp.concatenate(outs, axis=1)
            lse_ref[...] = tile.T[0:8, :]


def attn_kernel(len_ref, *refs):
    i = pl.program_id(0)
    attention_step(len_ref, i, key_blocks(len_ref, i), *refs)


def attention(lengths, packed):
    qw = H // 2 * HD
    kcol = H * HD // 128
    vcol = kcol + KVH * HD // 128
    return pl.pallas_call(
        attn_kernel,
        grid_spec=pltpu.PrefetchScalarGridSpec(
            num_scalar_prefetch=1,
            grid=(LEN // BQ, 2),
            in_specs=[
                pl.BlockSpec((BQ, qw), lambda i, p, s: (i, p)),
                pl.BlockSpec((LEN, 128), lambda i, p, s: (0, kcol + p)),
                pl.BlockSpec((LEN, 128), lambda i, p, s: (0, vcol + p)),
            ],
            out_specs=[
                pl.BlockSpec((BQ, qw), lambda i, p, s: (i, p)),
                pl.BlockSpec((8, BQ), lambda i, p, s: (p, i)),
            ],
        ),
        out_shape=[
            jax.ShapeDtypeStruct((LEN, H * HD), bf16),
            jax.ShapeDtypeStruct((H, LEN), f32),
        ],
        compiler_params=params(),
        cost_estimate=pl.CostEstimate(flops=4 * H * LEN * LEN * HD * 4, bytes_accessed=1 << 24, transcendentals=0),
        name="attention",
    )(lengths, packed, packed, packed)


def attention_back_step(len_ref, i, q_ref, k_ref, v_ref, d_ref, o_ref, lse_ref, dq_ref, dk_acc, dv_acc, count=None):
    if count is None:
        count = jnp.minimum(i + 1, max_blocks())
    row = i * BQ + lax.broadcasted_iota(jnp.int32, (1, BQ), 1)
    start = doc_start(len_ref, row)
    lane = lax.broadcasted_iota(jnp.int32, (BQ, 128), 1)
    group = H // KVH
    scale = jnp.asarray(HD**-0.5, bf16)
    tile = jnp.zeros((BQ, 128), f32)
    for h in range(2 * group):
        cols = slice(h * HD, (h + 1) * HD)
        dot = jnp.sum(d_ref[:, cols].astype(f32) * o_ref[:, cols].astype(f32), axis=-1, keepdims=True)
        tile = jnp.where(lane == h, dot, tile)
    inner = tile.T
    for nb in range(1, max_blocks() + 1):

        @pl.when(count == nb)
        def _():
            span = nb * BQ
            base = pl.multiple_of((i - (nb - 1)) * BQ, BQ)
            key = base + lax.broadcasted_iota(jnp.int32, (span, BQ), 0)
            bias = jnp.where((key >= start) & (key <= row), 0.0, -1e30)
            k2 = k_ref[pl.ds(base, span), :]
            v2 = v_ref[pl.ds(base, span), :]
            dks, dvs = [], []
            for kv in range(2):
                k = k2[:, kv * HD : (kv + 1) * HD]
                v = v2[:, kv * HD : (kv + 1) * HD]
                dk = dv = None
                dqs = []
                for g in range(group):
                    h = kv * group + g
                    cols = slice(h * HD, (h + 1) * HD)
                    q = q_ref[:, cols] * scale
                    d = d_ref[:, cols]
                    s = mm(k, q, NT) + bias
                    p = jnp.exp(s - lse_ref[h : h + 1, :])
                    dp = mm(v, d, NT)
                    ds = (p * (dp - inner[h : h + 1, :])).astype(bf16)
                    dv_h = mm(p.astype(bf16), d)
                    dk_h = mm(ds, q)
                    dv = dv_h if dv is None else dv + dv_h
                    dk = dk_h if dk is None else dk + dk_h
                    dqs.append(mm(k, ds, TN))
                dq = jnp.concatenate(dqs, axis=0) * (HD**-0.5)
                dq_ref[:, kv * group * HD : (kv + 1) * group * HD] = dq.T.astype(bf16)
                dks.append(dk)
                dvs.append(dv)
            dk_acc[pl.ds(base, span), :] += jnp.concatenate(dks, axis=1)
            dv_acc[pl.ds(base, span), :] += jnp.concatenate(dvs, axis=1)


def attn_back_kernel(len_ref, q_ref, k_ref, v_ref, d_ref, o_ref, lse_ref, dq_ref, dk_ref, dv_ref, dk_acc, dv_acc):
    i = pl.program_id(1)

    @pl.when(i == 0)
    def _():
        dk_acc[...] = jnp.zeros_like(dk_acc)
        dv_acc[...] = jnp.zeros_like(dv_acc)

    attention_back_step(
        len_ref, i, q_ref, k_ref, v_ref, d_ref, o_ref, lse_ref, dq_ref, dk_acc, dv_acc, key_blocks(len_ref, i)
    )

    @pl.when(i == pl.num_programs(1) - 1)
    def _():
        dk_ref[...] = dk_acc[...].astype(bf16)
        dv_ref[...] = dv_acc[...].astype(bf16)


def attention_back(lengths, packed, d_mixed, mixed, lse):
    qw = H // 2 * HD
    kcol = H * HD // 128
    vcol = kcol + KVH * HD // 128
    return pl.pallas_call(
        attn_back_kernel,
        grid_spec=pltpu.PrefetchScalarGridSpec(
            num_scalar_prefetch=1,
            grid=(2, LEN // BQ),
            in_specs=[
                pl.BlockSpec((BQ, qw), lambda p, i, s: (i, p)),
                pl.BlockSpec((LEN, 128), lambda p, i, s: (0, kcol + p)),
                pl.BlockSpec((LEN, 128), lambda p, i, s: (0, vcol + p)),
                pl.BlockSpec((BQ, qw), lambda p, i, s: (i, p)),
                pl.BlockSpec((BQ, qw), lambda p, i, s: (i, p)),
                pl.BlockSpec((8, BQ), lambda p, i, s: (p, i)),
            ],
            out_specs=[
                pl.BlockSpec((BQ, qw), lambda p, i, s: (i, p)),
                pl.BlockSpec((LEN, 128), lambda p, i, s: (0, p)),
                pl.BlockSpec((LEN, 128), lambda p, i, s: (0, p)),
            ],
            scratch_shapes=[pltpu.VMEM((LEN, 128), f32), pltpu.VMEM((LEN, 128), f32)],
        ),
        out_shape=[
            jax.ShapeDtypeStruct((LEN, H * HD), bf16),
            jax.ShapeDtypeStruct((LEN, KVH * HD), bf16),
            jax.ShapeDtypeStruct((LEN, KVH * HD), bf16),
        ],
        compiler_params=params(),
        cost_estimate=pl.CostEstimate(flops=10 * H * LEN * LEN * HD * 4, bytes_accessed=1 << 24, transcendentals=0),
        name="attention_back",
    )(lengths, packed, packed, packed, d_mixed, mixed, lse)


def token_weight(table_ref, ids):
    weight = jnp.zeros(ids.shape, f32)
    for j in range(table_ref.shape[0]):
        weight = jnp.where(ids == j, table_ref[j].astype(f32) * 0.25, weight)
    return weight


def ffn_kernel(table_ref, x_ref, mixed_ref, t_ref, ids_ref, g_ref, proj_ref, wf_ref, down_ref,
               middle_ref, second_ref, hidden_ref, dboth_ref, dy_ref, c_ref):
    middle = x_ref[...].astype(f32) + mm(mixed_ref[...], proj_ref[...])
    middle_ref[...] = middle
    r = lax.rsqrt(jnp.mean(middle * middle, axis=-1, keepdims=True) + norm_eps)
    second = (middle * r * g_ref[1:2, :]).astype(bf16)
    second_ref[...] = second
    c = token_weight(table_ref, ids_ref[...])
    c_ref[...] = jnp.broadcast_to(c, c_ref.shape)
    dy = (c * t_ref[...].astype(f32)).astype(bf16)
    dy_ref[...] = dy
    step = 512
    for c in range(0, FF, step):
        gate = mm(second, wf_ref[:, c : c + step])
        up = mm(second, wf_ref[:, FF + c : FF + c + step])
        dh = mm(dy, down_ref[c : c + step, :], NT)
        sig = jax.nn.sigmoid(gate)
        silu = gate * sig
        hidden_ref[:, c : c + step] = (silu * up).astype(bf16)
        dboth_ref[:, c : c + step] = (dh * up * sig * (1.0 + gate * (1.0 - sig))).astype(bf16)
        dboth_ref[:, FF + c : FF + c + step] = (dh * silu).astype(bf16)


def ffn(table, x, mixed, target, ids, gains, proj, wf, down):
    width = x.shape[1]
    rowb = lambda n: pl.BlockSpec((BQ, n), lambda i, s: (i, 0))
    whole = lambda a: one(a.shape, lambda i, s: (0, 0))
    return pl.pallas_call(
        ffn_kernel,
        grid_spec=pltpu.PrefetchScalarGridSpec(
            num_scalar_prefetch=1,
            grid=(LEN // BQ,),
            in_specs=[rowb(width), rowb(H * HD), rowb(width), rowb(1), whole(gains), whole(proj), whole(wf), whole(down)],
            out_specs=[rowb(width), rowb(width), rowb(FF), rowb(2 * FF), rowb(width), rowb(128)],
        ),
        out_shape=[
            jax.ShapeDtypeStruct((LEN, width), f32),
            jax.ShapeDtypeStruct((LEN, width), bf16),
            jax.ShapeDtypeStruct((LEN, FF), bf16),
            jax.ShapeDtypeStruct((LEN, 2 * FF), bf16),
            jax.ShapeDtypeStruct((LEN, width), bf16),
            jax.ShapeDtypeStruct((LEN, 128), f32),
        ],
        compiler_params=params(),
        cost_estimate=pl.CostEstimate(flops=2 * LEN * width * FF * 4, bytes_accessed=40 << 20, transcendentals=0),
        name="ffn",
    )(table, x, mixed, target, ids, gains, proj, wf, down)


def mid_kernel(table_ref, middle_ref, hidden_ref, dboth_ref, t_ref, ids_ref, g_ref, proj_ref, wf_ref, down_ref,
               act_ref, dmid_ref, dlow_ref, dmix_ref, gain_ref):
    middle = middle_ref[...]
    act_ref[...] = (middle + mm(hidden_ref[...], down_ref[...])).astype(bf16)
    r = lax.rsqrt(jnp.mean(middle * middle, axis=-1, keepdims=True) + norm_eps)
    n2 = middle * r
    ds2 = mm(dboth_ref[...], wf_ref[...], NT)
    prod = ds2 * n2
    part = jnp.sum(prod.reshape(BQ // 8, 8, prod.shape[1]), axis=0)

    @pl.when(pl.program_id(0) == 0)
    def _():
        gain_ref[...] = jnp.zeros_like(gain_ref)

    gain_ref[...] += part
    g = g_ref[1:2, :]
    e2 = ds2 * g
    dy = token_weight(table_ref, ids_ref[...]) * t_ref[...].astype(f32)
    dmid = dy + r * (e2 - n2 * jnp.mean(prod * g, axis=-1, keepdims=True))
    dmid_ref[...] = dmid
    low = dmid.astype(bf16)
    dlow_ref[...] = low
    dmix_ref[...] = mm(low, proj_ref[...], NT).astype(bf16)


def mid(table, middle, hidden, dboth, target, ids, gains, proj, wf, down):
    width = middle.shape[1]
    rowb = lambda n: pl.BlockSpec((BQ, n), lambda i, s: (i, 0))
    whole = lambda a: one(a.shape, lambda i, s: (0, 0))
    return pl.pallas_call(
        mid_kernel,
        grid_spec=pltpu.PrefetchScalarGridSpec(
            num_scalar_prefetch=1,
            grid=(LEN // BQ,),
            in_specs=[rowb(width), rowb(FF), rowb(2 * FF), rowb(width), rowb(1), whole(gains), whole(proj), whole(wf), whole(down)],
            out_specs=[rowb(width), rowb(width), rowb(width), rowb(H * HD), pl.BlockSpec((8, width), lambda i, s: (0, 0))],
        ),
        out_shape=[
            jax.ShapeDtypeStruct((LEN, width), bf16),
            jax.ShapeDtypeStruct((LEN, width), f32),
            jax.ShapeDtypeStruct((LEN, width), bf16),
            jax.ShapeDtypeStruct((LEN, H * HD), bf16),
            jax.ShapeDtypeStruct((8, width), f32),
        ],
        compiler_params=params(),
        cost_estimate=pl.CostEstimate(flops=2 * LEN * width * FF * 4, bytes_accessed=40 << 20, transcendentals=0),
        name="mid",
    )(table, middle, hidden, dboth, target, ids, gains, proj, wf, down)


def input_kernel(x_ref, dmid_ref, dq_ref, dk_ref, dv_ref, g_ref, w_ref, out_ref, gain_ref):
    x = x_ref[...].astype(f32)
    r = lax.rsqrt(jnp.mean(x * x, axis=-1, keepdims=True) + norm_eps)
    n1 = x * r
    q, k = H * HD, H * HD + KVH * HD
    ds1 = mm(dq_ref[...], w_ref[:, :q], NT) + mm(dk_ref[...], w_ref[:, q:k], NT) + mm(dv_ref[...], w_ref[:, k:], NT)
    prod = ds1 * n1
    part = jnp.sum(prod.reshape(BQ // 8, 8, prod.shape[1]), axis=0)

    @pl.when(pl.program_id(0) == 0)
    def _():
        gain_ref[...] = jnp.zeros_like(gain_ref)

    gain_ref[...] += part
    g = g_ref[0:1, :]
    out = dmid_ref[...] + r * (ds1 * g - n1 * jnp.mean(prod * g, axis=-1, keepdims=True))
    out_ref[...] = out.astype(bf16)


def input_back(x, dmid, dq, dk, dv, gains, w):
    width = x.shape[1]
    rowb = lambda n: pl.BlockSpec((BQ, n), lambda i: (i, 0))
    whole = lambda a: one(a.shape, lambda i: (0, 0))
    return pl.pallas_call(
        input_kernel,
        grid=(LEN // BQ,),
        in_specs=[rowb(width), rowb(width), rowb(H * HD), rowb(KVH * HD), rowb(KVH * HD), whole(gains), whole(w)],
        out_specs=[rowb(width), pl.BlockSpec((8, width), lambda i: (0, 0))],
        out_shape=[jax.ShapeDtypeStruct((LEN, width), bf16), jax.ShapeDtypeStruct((8, width), f32)],
        compiler_params=params(),
        cost_estimate=pl.CostEstimate(flops=2 * LEN * width * 1536, bytes_accessed=24 << 20, transcendentals=0),
        name="input_back",
    )(x, dmid, dq, dk, dv, gains, w)


def grad_kernel(pick_ref, a_ref, *refs):
    out_ref = refs[-1]
    b_refs = refs[:-1]
    add_ref = None
    if len(b_refs) > 1 and len(b_refs[-1].shape) == 3:
        add_ref, b_refs = b_refs[-1], b_refs[:-1]
    col = 0
    a = a_ref[...]
    for b_ref in b_refs:
        n = b_ref.shape[1]
        g = mm(a, b_ref[...], TN)
        if add_ref is not None:
            g = g + add_ref[0, :, col : col + n].astype(f32)
        out_ref[0, :, col : col + n] = g.astype(bf16)
        col += n


def grad_rows(pick, a, bs, rows, add=None, name="grad"):
    cols = sum(width for _, _, width in bs)
    count = pick.shape[0]
    specs = [pl.BlockSpec((LEN, rows), lambda j, p: (0, p[j]))]
    specs += [one((LEN, width), functools.partial(lambda at, j, p: (0, at), at)) for _, at, width in bs]
    ops = [a, *(b for b, _, _ in bs)]
    if add is not None:
        specs.append(pl.BlockSpec((1, rows, cols), lambda j, p: (j, 0, 0)))
        ops.append(add)
    return pl.pallas_call(
        grad_kernel,
        grid_spec=pltpu.PrefetchScalarGridSpec(
            num_scalar_prefetch=1,
            grid=(count,),
            in_specs=specs,
            out_specs=pl.BlockSpec((1, rows, cols), lambda j, p: (j, 0, 0)),
        ),
        out_shape=jax.ShapeDtypeStruct((count, rows, cols), bf16),
        compiler_params=params(),
        cost_estimate=pl.CostEstimate(flops=2 * LEN * rows * count * cols, bytes_accessed=12 << 20, transcendentals=0),
        name=name,
    )(pick, *ops)


def flip_pairs(n):
    return [(i, i ^ 1) for i in range(n)]


def add_low(a, b):
    return (a.astype(f32) + b.astype(f32)).astype(a.dtype)


beta_first = 0.9
beta_second = 0.95
adam_eps = 1e-08
decay_rate = 0.1
outer_decay = 0.5
outer_rate = 0.7
STEP = 10


def adam_step(grad, first, second, weight, rate):
    first_new = beta_first * first + (1.0 - beta_first) * grad
    second_new = beta_second * second + (1.0 - beta_second) * grad * grad
    ratio = first_new / (1.0 - beta_first**STEP) / (jnp.sqrt(second_new / (1.0 - beta_second**STEP)) + adam_eps)
    local = weight - rate * (ratio + decay_rate * weight)
    return first_new, second_new, weight - local


def outer_step(delta_sum, momentum, weight, groups):
    average = delta_sum / groups
    momentum_new = outer_decay * momentum + average
    return average, momentum_new, weight - outer_rate * (average + outer_decay * momentum_new)


def adam_kernel(place_ref, own_ref, *refs, terms, rate):
    refs = list(refs)
    slots = refs.pop(0) if terms else None
    first_ref, second_ref, w_ref = refs[:3]
    grad_ref, first_new_ref, second_new_ref, keep_ref, send_ref = refs[-5:]
    grad = own_ref[0].astype(f32)
    if terms:
        grad = grad + slots[0].astype(f32)
        grad = grad + jnp.where(place_ref[3] == 1, slots[1].astype(f32), 0.0)
    first_new, second_new, delta = adam_step(grad, first_ref[...], second_ref[...], w_ref[...], rate)
    grad_ref[...] = grad
    first_new_ref[...] = first_new
    second_new_ref[...] = second_new
    half = delta.shape[0] // 2
    low = delta.astype(bf16)
    core = place_ref[1]

    @pl.when(core == 0)
    def _():
        keep_ref[...] = low[:half]
        send_ref[...] = low[half:]

    @pl.when(core != 0)
    def _():
        keep_ref[...] = low[half:]
        send_ref[...] = low[:half]


def adam_piece(place, own, terms, first, second, w, held, rows, row_at, col_at, cols, tile, rate):
    at = lambda j, p: (row_at // rows, col_at // tile + j)
    piece = pl.BlockSpec((pl.Element(2), pl.Element(rows), pl.Element(tile)), lambda j, p: (2, 0, j * tile))
    half = pl.BlockSpec((rows // 2, tile), lambda j, p: (0, j))
    state = pl.BlockSpec((rows, tile), at)
    full = jax.ShapeDtypeStruct(first.shape, f32)
    low = jax.ShapeDtypeStruct((rows // 2, cols), bf16)
    specs = [pl.BlockSpec((1, rows, tile), lambda j, p: (p[0], 0, j))] + [piece] * len(terms) + [state] * 3
    ops = [own, *terms, first, second, w]
    aliases = {}
    if held is not None:
        aliases = {1 + len(ops) + k: k for k in range(3)}
        ops += list(held)
        specs += [pl.BlockSpec(memory_space=pl.ANY)] * 3
    out = pl.pallas_call(
        functools.partial(adam_kernel, terms=len(terms), rate=rate),
        grid_spec=pltpu.PrefetchScalarGridSpec(
            num_scalar_prefetch=1,
            grid=(cols // tile,),
            in_specs=specs,
            out_specs=[state, state, state, half, half],
        ),
        out_shape=[full, full, full, low, low],
        input_output_aliases=aliases,
        compiler_params=params(),
        cost_estimate=pl.CostEstimate(flops=0, bytes_accessed=rows * cols * 28, transcendentals=0),
        name="adam",
    )(place, *ops)
    return out[:3], out[3], out[4]


def outer_kernel(place_ref, keep_ref, other_ref, outer_ref, w_ref, *refs, groups):
    diff_ref, outer_new_ref, new_ref, copy_ref = refs[-4:]
    core = place_ref[1]
    half = keep_ref.shape[0]

    def write(rows, total_ref):
        average, momentum, weight = outer_step(total_ref[...].astype(f32), outer_ref[rows, :], w_ref[rows, :], groups)
        diff_ref[rows, :] = average
        outer_new_ref[rows, :] = momentum
        new_ref[rows, :] = weight
        copy_ref[rows, :] = weight.astype(bf16)

    @pl.when(core == 0)
    def _():
        write(slice(0, half), keep_ref)
        write(slice(half, 2 * half), other_ref)

    @pl.when(core != 0)
    def _():
        write(slice(0, half), other_ref)
        write(slice(half, 2 * half), keep_ref)


def outer_piece(place, keep, other, outer, w, held, rows, row_at, col_at, cols, tile, groups):
    half = pl.BlockSpec((rows // 2, tile), lambda j, p: (0, j))
    state = pl.BlockSpec((rows, tile), lambda j, p: (row_at // rows, col_at // tile + j))
    full = jax.ShapeDtypeStruct(outer.shape, f32)
    specs = [half, half, state, state]
    ops = [keep, other, outer, w]
    aliases = {}
    if held is not None:
        aliases = {1 + len(ops) + k: k for k in range(4)}
        ops += list(held)
        specs += [pl.BlockSpec(memory_space=pl.ANY)] * 4
    return pl.pallas_call(
        functools.partial(outer_kernel, groups=groups),
        grid_spec=pltpu.PrefetchScalarGridSpec(
            num_scalar_prefetch=1, grid=(cols // tile,), in_specs=specs, out_specs=[state] * 4
        ),
        out_shape=[full, full, full, jax.ShapeDtypeStruct(outer.shape, bf16)],
        input_output_aliases=aliases,
        compiler_params=params(),
        cost_estimate=pl.CostEstimate(flops=0, bytes_accessed=rows * cols * 24, transcendentals=0),
        name="outer",
    )(place, *ops)


def rep_sum(keep, send, rep):
    pair = flip_pairs(rep)
    part = add_low(keep, lax.ppermute(send, "rep", pair))
    for hop in range(1, (rep - 1).bit_length()):
        part = add_low(part, lax.ppermute(part, "rep", [(i, i ^ (1 << hop)) for i in range(rep)]))
    return part, lax.ppermute(part, "rep", pair)


def by_neighbours(n, rep):
    return n == 8 and rep == 4


def all_weights(w_in, w_out, gains):
    split = H * HD + 2 * KVH * HD
    low_in, low_out = w_in.astype(bf16), w_out.astype(bf16)
    low_gains = jnp.pad(gains.astype(bf16), ((0, 62), (0, 0)))
    shards = [low_gains, low_in[:, :split], low_out[0], low_in[:, split:], low_out[1]]
    full = [lax.all_gather(a, "fsdp") for a in shards]
    gain_full = full[0][:, :8].astype(f32).transpose(1, 0, 2).reshape(8, -1)
    return [gain_full] + [a.reshape(-1, a.shape[-1]) for a in full[1:]]


CHUNKS = ("q", "kv", "proj", "gate", "up", "down")
CHIP_SHARE = {"q": 48, "kv": 48, "proj": 16, "gate": 48, "up": 48, "down": 32}
LAGS = (0, 2, 4, 5)


def forward_kernel(*refs, names, line):
    R = dict(zip(names, refs))
    r, f = lax.axis_index("rep"), lax.axis_index("fsdp")
    x, core, z, y = r // 2, r % 2, f // 2, f % 2
    n = 2 * line
    to_y = (r, f + 1 - 2 * y)
    to_x = (r + 2 - 4 * x, f)
    to_core = (r + 1 - 2 * core, f)
    barrier = pltpu.get_barrier_semaphore()
    peers = [(r, lax.rem(f + step, n)) for step in range(1, n)]
    for to in (*peers, to_x, to_core):
        pl.semaphore_signal(barrier, inc=1, device_id=to, device_id_type=pl.DeviceIdType.MESH)
    pl.semaphore_wait(barrier, n + 1)

    def remote(src, dst, send, recv, to):
        return pltpu.make_async_remote_copy(
            src_ref=src, dst_ref=dst, send_sem=send, recv_sem=recv, device_id=to, device_id_type=pl.DeviceIdType.MESH
        )

    held = {c: R["v_" + c] if "v_" + c in R else R["full_" + c] for c in CHUNKS}
    rows_of = {c: R["low_" + c].shape[0] for c in CHUNKS}
    item = lambda side, d: 0 if d == 0 else 2 * d - 1 + (side > 0)
    exists = lambda side, d: None if d == 0 else (z - d >= 0 if side < 0 else z + d < line)

    def guard(cond, fn):
        if cond is None:
            fn()
        else:
            pl.when(cond)(fn)

    def copy(src, dst, stage, c, side, d, to):
        m, k = CHUNKS.index(c), item(side, d)
        return remote(src, dst, R["f_send"].at[stage, m, k], R["f_recv"].at[stage, m, k], to)

    def portion(c):
        half, share = rows_of[c] // 2, CHIP_SHARE[c]
        return pl.ds(pl.multiple_of(core * half + x * share, 16), half - share)

    def line_copy(c, side, d):
        plane = z + side * (d - 1)
        dst = held[c].at[plane * 2 + y, portion(c), :]
        src = R["low_" + c].at[portion(c), :] if d == 1 else dst
        return copy(src, dst, 0, c, side, d, (r, f - 2 * side))

    def line_arrival(c, side, d):
        dst = held[c].at[(z + side * d) * 2 + y, portion(c), :]
        return copy(dst, dst, 0, c, side, d, to_y)

    def y_copy(c, side, d):
        dst = held[c].at[(z + side * d) * 2 + y, portion(c), :]
        return copy(R["low_" + c].at[portion(c), :] if d == 0 else dst, dst, 1, c, side, d, to_y)

    def both_copy(c, side, d, start, rows, stage, to):
        planes = pl.ds(z * 2 + 1 - y, 1) if d == 0 else pl.ds((z + side * d) * 2, 2)
        ref = held[c].at[planes, pl.ds(pl.multiple_of(start, 16), rows), :]
        return copy(ref, ref, stage, c, side, d, to)

    def x_copy(c, side, d):
        half, share = rows_of[c] // 2, CHIP_SHARE[c]
        return both_copy(c, side, d, core * half + x * (half - share), share, 2, to_x)

    def core_copy(c, side, d):
        half = rows_of[c] // 2
        return both_copy(c, side, d, core * half, half, 3, to_core)

    def onward(side):
        return z < line - 1 if side < 0 else z > 0

    def line_stage(c, side, d):
        if d == 0:
            for way in (-1, 1):
                pl.when(onward(way))(lambda way=way: line_copy(c, way, 1).start())
        else:
            line_arrival(c, side, d).wait_recv()
            if d < line - 1:
                pl.when(onward(side))(lambda: line_copy(c, side, d + 1).start())
        y_copy(c, side, d).start()

    def y_stage(c, side, d):
        y_copy(c, side, d).wait_recv()
        x_copy(c, side, d).start()

    def x_stage(c, side, d):
        x_copy(c, side, d).wait_recv()
        core_copy(c, side, d).start()

    def core_stage(c, side, d):
        core_copy(c, side, d).wait_recv()

    stages = (line_stage, y_stage, x_stage, core_stage)
    sides = lambda d: (1,) if d == 0 else (-1, 1)
    body = [(c, d) for c in CHUNKS for d in range(1, line)]
    own = [(c, 0) for c in CHUNKS]
    order = []
    for at, group in enumerate(body):
        while own and body.index((own[0][0], 1)) - 2 <= at:
            order.append(own.pop(0))
        order.append(group)
    last_tick = {c: order.index((c, line - 1)) + LAGS[-1] for c in CHUNKS}
    ticks = len(order) + LAGS[-1]
    clock = [0]

    def tick(k):
        for lag, stage in zip(LAGS, stages):
            if 0 <= k - lag < len(order):
                c, d = order[k - lag]
                for side in sides(d):
                    guard(exists(side, d), functools.partial(stage, c, side, d))

    def advance(count):
        start = clock[0]
        clock[0] = min(ticks, start + max(count, 0))
        return list(range(start, clock[0]))

    def catch_up(c):
        for k in advance(last_tick[c] + 1 - clock[0]):
            tick(k)

    def spread(steps, per_step):
        plan = [advance(per_step) for _ in range(steps)]

        def serve(at):
            for step, todo in enumerate(plan):
                if todo:

                    @pl.when(at == step)
                    def _():
                        for k in todo:
                            tick(k)

        return serve

    def keep(c):
        return pltpu.make_async_copy(R["v_" + c], R["full_" + c], R["keep_sem"].at[CHUNKS.index(c)])

    def place_own(c):
        return pltpu.make_async_copy(R["low_" + c], held[c].at[f], R["own_sem"].at[CHUNKS.index(c)])

    gain_send = lambda step: remote(R["low_gain"], R["v_gain"].at[f], R["g_send"].at[step - 1], R["g_recv"].at[step - 1], peers[step - 1])
    for step in range(1, n):
        gain_send(step).start()
    own_gain = pltpu.make_async_copy(R["low_gain"], R["v_gain"].at[f], R["g_send"].at[n - 1])
    own_gain.start()
    for k in advance(3):
        tick(k)
    for c in CHUNKS:
        place_own(c).start()

    rowb = lambda width: pl.BlockSpec((BQ, width), lambda i: (i, 0))
    width = R["x"].shape[1]
    steps = LEN // BQ

    def run(body, grid, ins, outs):
        pltpu.emit_pipeline(body, grid=grid, in_specs=[s for _, s in ins], out_specs=[s for _, s in outs])(
            *[R[a] for a, _ in ins], *[R[a] for a, _ in outs]
        )

    def target_step(t_ref, dy_ref, c_ref):
        at = pl.multiple_of(pl.program_id(0) * BQ, BQ)
        c = token_weight(R["table"], R["ids"][pl.ds(at, BQ), :])
        c_ref[...] = jnp.broadcast_to(c, c_ref.shape)
        dy_ref[...] = (c * t_ref[...].astype(f32)).astype(bf16)

    run(target_step, (steps,), [("target", rowb(width))], [("dy", rowb(width)), ("c", rowb(128))])
    own_gain.wait()
    for step in range(1, n):
        gain_send(step).wait()
    gains = jnp.concatenate([R["v_gain"][k] for k in range(n)], axis=1).astype(f32)[0:8]
    R["gain_rows"][...] = gains
    keep_gain = pltpu.make_async_copy(R["gain_rows"], R["gain"], R["g_send"].at[n - 1])
    keep_gain.start()

    def norm_step(x_ref, first_ref):
        v = x_ref[...].astype(f32)
        inv = lax.rsqrt(jnp.mean(v * v, axis=-1, keepdims=True) + norm_eps)
        first_ref[...] = (v * inv * R["gain_rows"][0:1, :]).astype(bf16)

    serve_norm = spread(steps, 1)

    def norm_body(x_ref, first_ref):
        norm_step(x_ref, first_ref)
        serve_norm(pl.program_id(0))

    run(norm_body, (steps,), [("x", rowb(width))], [("first", rowb(width))])
    for c in CHUNKS:
        place_own(c).wait()
    whole = lambda c: held[c][...].reshape(-1, held[c].shape[2])

    catch_up("kv")
    keep("q").start()
    keep("kv").start()
    serve_qkv = spread(steps, 1)

    def qkv_body(first_ref, packed_ref):
        first = first_ref[...]
        split = H * HD
        packed_ref[:, :split] = mm(first, whole("q")).astype(bf16)
        packed_ref[:, split:] = mm(first, whole("kv")).astype(bf16)
        serve_qkv(pl.program_id(0))

    run(qkv_body, (steps,), [("first", rowb(width))], [("packed", rowb(R["packed"].shape[1]))])

    qw = H // 2 * HD
    kcol = H * HD // 128
    vcol = kcol + KVH * HD // 128
    serve_attention = spread(2 * steps, 1)

    def attention_body(q_ref, k_ref, v_ref, o_ref, lse_ref):
        s = pl.program_id(0)
        i = lax.rem(s, steps)
        attention_step(R["lengths"], i, jnp.minimum(i + 1, max_blocks()), q_ref, k_ref, v_ref, o_ref, lse_ref)
        serve_attention(s)

    qspec = pl.BlockSpec((BQ, qw), lambda s: (s % steps, s // steps))
    run(
        attention_body,
        (2 * steps,),
        [
            ("packed", qspec),
            ("packed", pl.BlockSpec((LEN, 128), lambda s: (0, kcol + s // steps))),
            ("packed", pl.BlockSpec((LEN, 128), lambda s: (0, vcol + s // steps))),
        ],
        [("mixed", qspec), ("lse", pl.BlockSpec((8, BQ), lambda s: (s // steps, s % steps)))],
    )

    catch_up("proj")
    keep("proj").start()
    serve_proj = spread(steps, 1)

    def proj_body(x_ref, mixed_ref, middle_ref, second_ref):
        middle = x_ref[...].astype(f32) + mm(mixed_ref[...], whole("proj"))
        middle_ref[...] = middle
        inv = lax.rsqrt(jnp.mean(middle * middle, axis=-1, keepdims=True) + norm_eps)
        second_ref[...] = (middle * inv * R["gain_rows"][1:2, :]).astype(bf16)
        serve_proj(pl.program_id(0))

    run(proj_body, (steps,), [("x", rowb(width)), ("mixed", rowb(H * HD))], [("middle", rowb(width)), ("second", rowb(width))])

    catch_up("gate")
    keep("gate").start()
    serve_gate = spread(steps, 1)

    def gate_body(second_ref, gate_ref):
        gate_ref[...] = mm(second_ref[...], whole("gate"))
        serve_gate(pl.program_id(0))

    run(gate_body, (steps,), [("second", rowb(width))], [("gate", rowb(FF))])

    catch_up("up")
    keep("up").start()
    serve_up = spread(steps, 1)

    def up_body(second_ref, gate_ref, up_ref, hidden_ref):
        up = mm(second_ref[...], whole("up"))
        up_ref[...] = up
        gate = gate_ref[...]
        hidden_ref[...] = (gate * jax.nn.sigmoid(gate) * up).astype(bf16)
        serve_up(pl.program_id(0))

    run(up_body, (steps,), [("second", rowb(width)), ("gate", rowb(FF))], [("up", rowb(FF)), ("hidden", rowb(FF))])
    catch_up("down")

    for c in CHUNKS[:-1]:
        keep(c).wait()
    keep_gain.wait()
    for c in CHUNKS:
        for d in range(line):
            for side in sides(d):

                def finish():
                    core_copy(c, side, d).wait_send()
                    x_copy(c, side, d).wait_send()
                    y_copy(c, side, d).wait_send()

                guard(exists(side, d), finish)
                if d > 0:
                    had = z - (d - 1) >= 0 if side < 0 else z + (d - 1) < line
                    pl.when(had & onward(side))(lambda: line_copy(c, side, d).wait_send())


def forward(lengths, table, ids, arrays, shards, gain_shard, n):
    line = n // 2
    width = arrays["x"].shape[1]
    packed = H * HD + 2 * KVH * HD
    outs = {"full_" + c: ((n, *shards[c].shape), bf16) for c in CHUNKS}
    outs |= {
        "gain": ((8, width), f32), "dy": ((LEN, width), bf16), "c": ((LEN, 128), f32), "first": ((LEN, width), bf16),
        "packed": ((LEN, packed), bf16), "mixed": ((LEN, H * HD), bf16), "lse": ((H, LEN), f32),
        "middle": ((LEN, width), f32), "second": ((LEN, width), bf16), "gate": ((LEN, FF), f32), "up": ((LEN, FF), f32),
        "hidden": ((LEN, FF), bf16),
    }
    dma = pltpu.SemaphoreType.DMA
    count, items = len(CHUNKS), n - 1
    scratch = {"v_" + c: pltpu.VMEM((n, *shards[c].shape), bf16) for c in CHUNKS[:-1]}
    scratch |= {
        "v_gain": pltpu.VMEM((n, *gain_shard.shape), bf16), "gain_rows": pltpu.VMEM((8, width), f32),
        "f_send": dma((4, count, items)), "f_recv": dma((4, count, items)), "keep_sem": dma((count,)),
        "own_sem": dma((count,)), "g_send": dma((n,)), "g_recv": dma((n,)),
    }
    inputs = dict(arrays) | {"low_" + c: shards[c] for c in CHUNKS} | {"low_gain": gain_shard}
    names = ["lengths", "table", "ids", *inputs, *outs, *scratch]
    anywhere = pl.BlockSpec(memory_space=pl.ANY)
    smem = pl.BlockSpec(memory_space=pltpu.SMEM)
    got = pl.pallas_call(
        functools.partial(forward_kernel, names=names, line=line),
        in_specs=[smem, smem, pl.BlockSpec(memory_space=pltpu.VMEM)] + [anywhere] * len(inputs),
        out_specs=[anywhere] * len(outs),
        out_shape=[jax.ShapeDtypeStruct(*v) for v in outs.values()],
        scratch_shapes=list(scratch.values()),
        compiler_params=pltpu.CompilerParams(collective_id=0, has_side_effects=True, vmem_limit_bytes=62 << 20),
        cost_estimate=pl.CostEstimate(flops=60 << 30, bytes_accessed=200 << 20, transcendentals=0),
        name="forward",
    )(lengths, table, ids, *inputs.values())
    return dict(zip(outs, got))


PIECES = ("down", "gate", "up", "proj", "q", "kv")


def back_kernel(*refs, names, line):
    R = dict(zip(names, refs))
    r, f = lax.axis_index("rep"), lax.axis_index("fsdp")
    z, y = f // 2, f % 2
    n = 2 * line
    barrier = pltpu.get_barrier_semaphore()
    for step in range(1, n):
        pl.semaphore_signal(barrier, inc=1, device_id=(r, lax.rem(f + step, n)), device_id_type=pl.DeviceIdType.MESH)
    pl.semaphore_wait(barrier, n - 1)

    loads = ("down", "gate_w", "up_w", "proj", "q_w", "kv_w")
    load = lambda k: pltpu.make_async_copy(R[loads[k]], R["v_" + loads[k]], R["load_sem"].at[k])
    for k in range(len(loads)):
        load(k).start()

    def remote(src, dst, send, recv, to):
        return pltpu.make_async_remote_copy(
            src_ref=src, dst_ref=dst, send_sem=send, recv_sem=recv, device_id=(r, to), device_id_type=pl.DeviceIdType.MESH
        )

    def run(body, grid, ins, outs):
        pltpu.emit_pipeline(body, grid=grid, in_specs=[s for _, s in ins], out_specs=[s for _, s in outs])(
            *[a for a, _ in ins], *[a for a, _ in outs]
        )

    rows_of = {p: R["own_" + p].shape[1] for p in PIECES}
    cols_of = {p: R["own_" + p].shape[2] for p in PIECES}
    sources = {
        "down": ("hidden", [("dy", 0, R["dy"].shape[1])]),
        "gate": ("second", [("dboth", 0, FF)]),
        "up": ("second", [("dboth", 1, FF)]),
        "proj": ("mixed", [("dlow", 0, R["dlow"].shape[1])]),
        "q": ("first", [("dq", 0, H * HD)]),
        "kv": ("first", [("dk", 0, KVH * HD), ("dv", 0, KVH * HD)]),
    }

    def gradient(p, side, out, add=None):
        a, bs = sources[p]
        rows, cols = rows_of[p], cols_of[p]
        block = pl.BlockSpec((1, rows, cols), lambda j: (j, 0, 0))
        ins = [(R[a], pl.BlockSpec((LEN, rows), lambda j: (0, j * 2 + side)))]
        for b, at, width in bs:
            ins.append((R[b], pl.BlockSpec((LEN, width), functools.partial(lambda at, j: (0, at), at))))
        if add is not None:
            ins.append((add, block))

        def step(*refs):
            out_ref, a_ref, b_refs = refs[-1], refs[0], refs[1 : 1 + len(bs)]
            col = 0
            for b_ref in b_refs:
                width = b_ref.shape[1]
                g = mm(a_ref[...], b_ref[...], TN)
                if add is not None:
                    g = g + refs[-2][0, :, col : col + width].astype(f32)
                out_ref[0, :, col : col + width] = g.astype(bf16)
                col += width

        run(step, (line,), ins, [(out, block)])

    def pair_copy(p):
        k = PIECES.index(p)
        return remote(R["away_" + p], R["came_" + p], R["y_send"].at[k], R["y_recv"].at[k], f + 1 - 2 * y)

    def send_away(p):
        gradient(p, 1 - y, R["away_" + p])
        pair_copy(p).start()

    middle = (z > 0) & (z < line - 1)
    low = z < line // 2
    inner = jnp.where(low, f + 2, f - 2)
    outer = jnp.where(low, f - 2, f + 2)

    def end_copy(p, k):
        i = PIECES.index(p)
        t = jnp.where(low, line - 1 - k, k)
        return remote(R["own_" + p].at[t], R["slot_" + p].at[k], R["z_send"].at[i, k], R["z_recv"].at[i, k], inner)

    def middle_copy(p, k):
        i = PIECES.index(p)
        slot = (4, 3, 2)[k]
        to = outer if k == 2 else inner
        return remote(R["msg_" + p].at[k], R["slot_" + p].at[slot], R["z_send"].at[i, k], R["z_recv"].at[i, slot], to)

    def slot_wait(p, slot):
        i = PIECES.index(p)
        ref = R["slot_" + p].at[slot]
        remote(ref, ref, R["z_send"].at[i, 0], R["z_recv"].at[i, slot], inner).wait_recv()

    def keep(p):
        pair_copy(p).wait_recv()
        gradient(p, y, R["own_" + p], R["came_" + p])

        @pl.when(~middle)
        def _():
            for k in range(3):
                end_copy(p, k).start()

    def serve(p, k):
        @pl.when(middle)
        def _():
            slot = (0, 1, 4)[k]
            slot_wait(p, slot)
            t = (3 * (2 - z), 3 - z, 3 * (z - 1))[k]
            rows, cols = rows_of[p], cols_of[p]
            block = pl.BlockSpec((rows // 2, cols), lambda j: (j, 0))

            def step(a_ref, b_ref, o_ref):
                o_ref[...] = (a_ref[...].astype(f32) + b_ref[...].astype(f32)).astype(bf16)

            run(step, (2,), [(R["own_" + p].at[t], block), (R["slot_" + p].at[slot], block)], [(R["msg_" + p].at[k], block)])
            middle_copy(p, k).start()

    rowb = lambda width: pl.BlockSpec((BQ, width), lambda i: (i, 0))
    width = R["x"].shape[1]
    R["gain_acc"][...] = jnp.zeros_like(R["gain_acc"])
    gain_rows = R["gain"][...]

    def mid_step(middle_ref, hidden_ref, dboth_ref, t_ref, c_ref, act_ref, dmid_ref, dlow_ref, dmix_ref):
        mid_v = middle_ref[...]
        act_ref[...] = (mid_v + mm(hidden_ref[...], R["v_down"][...])).astype(bf16)
        inv = lax.rsqrt(jnp.mean(mid_v * mid_v, axis=-1, keepdims=True) + norm_eps)
        n2 = mid_v * inv
        ds2 = mm(dboth_ref[:, :FF], R["v_gate_w"][...], NT) + mm(dboth_ref[:, FF:], R["v_up_w"][...], NT)
        prod = ds2 * n2
        R["gain_acc"][8:16, :] += jnp.sum(prod.reshape(BQ // 8, 8, width), axis=0)
        g = gain_rows[1:2, :]
        dy = c_ref[:, 0:1] * t_ref[...].astype(f32)
        dmid = dy + inv * (ds2 * g - n2 * jnp.mean(prod * g, axis=-1, keepdims=True))
        dmid_ref[...] = dmid
        dlow = dmid.astype(bf16)
        dlow_ref[...] = dlow
        dmix_ref[...] = mm(dlow, R["v_proj"][...], NT).astype(bf16)

    def mid_phase():
        run(
            mid_step,
            (LEN // BQ,),
            [(R["middle"], rowb(width)), (R["hidden"], rowb(FF)), (R["dboth"], rowb(2 * FF)), (R["target"], rowb(width)), (R["c"], rowb(128))],
            [(R["act"], rowb(width)), (R["dmid"], rowb(width)), (R["dlow"], rowb(width)), (R["dmix"], rowb(H * HD))],
        )

    qw = H // 2 * HD
    kcol = H * HD // 128
    vcol = kcol + KVH * HD // 128

    def attention_phase(p):
        qspec = pl.BlockSpec((BQ, qw), lambda i: (i, p))
        whole = lambda at: pl.BlockSpec((LEN, 128), lambda i: (0, at))
        R["dk_acc"][...] = jnp.zeros_like(R["dk_acc"])
        R["dv_acc"][...] = jnp.zeros_like(R["dv_acc"])

        def step(q_ref, k_ref, v_ref, d_ref, o_ref, lse_ref, dq_ref):
            attention_back_step(R["lengths"], pl.program_id(0), q_ref, k_ref, v_ref, d_ref, o_ref, lse_ref, dq_ref, R["dk_acc"], R["dv_acc"])

        pltpu.emit_pipeline(
            step, grid=(LEN // BQ,),
            in_specs=[qspec, whole(kcol + p), whole(vcol + p), qspec, qspec, pl.BlockSpec((8, BQ), lambda i: (p, i))],
            out_specs=[qspec],
        )(R["packed"], R["packed"], R["packed"], R["dmix"], R["mixed"], R["lse"], R["dq"])

        def flush(dk_ref, dv_ref):
            dk_ref[...] = R["dk_acc"][...].astype(bf16)
            dv_ref[...] = R["dv_acc"][...].astype(bf16)

        run(flush, (1,), [], [(R["dk"], pl.BlockSpec((LEN, 128), lambda i: (0, p))), (R["dv"], pl.BlockSpec((LEN, 128), lambda i: (0, p)))])

    def input_step(x_ref, dmid_ref, dq_ref, dk_ref, dv_ref, out_ref):
        x = x_ref[...].astype(f32)
        inv = lax.rsqrt(jnp.mean(x * x, axis=-1, keepdims=True) + norm_eps)
        n1 = x * inv
        kv_w, split = R["v_kv_w"], KVH * HD
        ds1 = mm(dq_ref[...], R["v_q_w"][...], NT) + mm(dk_ref[...], kv_w[:, :split], NT) + mm(dv_ref[...], kv_w[:, split:], NT)
        prod = ds1 * n1
        R["gain_acc"][0:8, :] += jnp.sum(prod.reshape(BQ // 8, 8, width), axis=0)
        g = gain_rows[0:1, :]
        out_ref[...] = (dmid_ref[...] + inv * (ds1 * g - n1 * jnp.mean(prod * g, axis=-1, keepdims=True))).astype(bf16)

    def input_phase():
        run(
            input_step,
            (LEN // BQ,),
            [(R["x"], rowb(width)), (R["dmid"], rowb(width)), (R["dq"], rowb(H * HD)), (R["dk"], rowb(KVH * HD)), (R["dv"], rowb(KVH * HD))],
            [(R["xgrad"], rowb(width))],
        )

    part = width // n

    def gain_copy(step, receive=False):
        peer = lax.rem(f + step, n)
        home = lax.rem(f + n - step, n) if receive else f
        return remote(
            R["gain_acc"].at[:, pl.ds(pl.multiple_of(peer * part, part), part)], R["gain_got"].at[home],
            R["g_send"].at[step - 1], R["g_recv"].at[step - 1], peer,
        )

    own_gain = pltpu.make_async_copy(
        R["gain_acc"].at[:, pl.ds(pl.multiple_of(f * part, part), part)], R["gain_got"].at[f], R["g_send"].at[n - 1]
    )

    def dboth_step(dy_ref, gate_ref, up_ref, dboth_ref):
        dh = mm(dy_ref[...], R["v_down"][...], NT)
        gate = gate_ref[...]
        sig = jax.nn.sigmoid(gate)
        dboth_ref[:, :FF] = (dh * up_ref[...] * sig * (1.0 + gate * (1.0 - sig))).astype(bf16)
        dboth_ref[:, FF:] = (dh * (gate * sig)).astype(bf16)

    send_away("down")
    load(0).wait()
    run(
        dboth_step,
        (LEN // BQ,),
        [(R["dy"], rowb(width)), (R["gate"], rowb(FF)), (R["up"], rowb(FF))],
        [(R["dboth"], rowb(2 * FF))],
    )
    send_away("gate")
    send_away("up")
    for k in range(1, 4):
        load(k).wait()
    mid_phase()
    send_away("proj")
    keep("down")
    attention_phase(0)
    serve("down", 0)
    attention_phase(1)
    serve("down", 1)
    keep("gate")
    serve("down", 2)
    send_away("q")
    send_away("kv")
    serve("gate", 0)
    load(4).wait()
    load(5).wait()
    input_phase()
    for step in range(1, n):
        gain_copy(step).start()
    own_gain.start()
    serve("gate", 1)
    keep("up")
    serve("gate", 2)
    for k in range(3):
        serve("up", k)
    for p in ("proj", "q", "kv"):
        keep(p)
        for k in range(3):
            serve(p, k)

    for step in range(1, n):
        gain_copy(step, True).wait_recv()
        gain_copy(step).wait_send()
    own_gain.wait()
    for p in PIECES:
        pair_copy(p).wait_send()
        slot_wait(p, 2)

        @pl.when(middle)
        def _():
            slot_wait(p, 3)
            for k in range(3):
                middle_copy(p, k).wait_send()

        @pl.when(~middle)
        def _():
            for k in range(3):
                end_copy(p, k).wait_send()


def backward(lengths, gain, arrays, n, rows_in, rows_out):
    line = n // 2
    width = arrays["x"].shape[1]
    kvw = KVH * HD
    sizes = {
        "down": (rows_out, width), "gate": (rows_in, FF), "up": (rows_in, FF),
        "proj": (rows_out, width), "q": (rows_in, H * HD), "kv": (rows_in, 2 * kvw),
    }
    outs = {
        "act": ((LEN, width), bf16), "dboth": ((LEN, 2 * FF), bf16), "dmid": ((LEN, width), f32), "dlow": ((LEN, width), bf16),
        "dmix": ((LEN, H * HD), bf16), "dq": ((LEN, H * HD), bf16), "dk": ((LEN, kvw), bf16), "dv": ((LEN, kvw), bf16),
        "xgrad": ((LEN, width), bf16), "gain_got": ((n, 16, width // n), f32),
    }
    for p, (rows, cols) in sizes.items():
        for kind, count in (("away_", line), ("came_", line), ("own_", line), ("slot_", 5), ("msg_", 3)):
            outs[kind + p] = ((count, rows, cols), bf16)
    dma = pltpu.SemaphoreType.DMA
    pieces = len(PIECES)
    scratch = {
        **{"v_" + k: pltpu.VMEM(arrays[k].shape, bf16) for k in ("down", "gate_w", "up_w", "proj", "q_w", "kv_w")},
        "gain_acc": pltpu.VMEM((16, width), f32), "dk_acc": pltpu.VMEM((LEN, 128), f32), "dv_acc": pltpu.VMEM((LEN, 128), f32),
        "load_sem": dma((6,)), "y_send": dma((pieces,)), "y_recv": dma((pieces,)),
        "z_send": dma((pieces, 3)), "z_recv": dma((pieces, 5)), "g_send": dma((n,)), "g_recv": dma((n,)),
    }
    names = ["lengths", "gain", *arrays, *outs, *scratch]
    anywhere = pl.BlockSpec(memory_space=pl.ANY)
    got = pl.pallas_call(
        functools.partial(back_kernel, names=names, line=line),
        in_specs=[pl.BlockSpec(memory_space=pltpu.SMEM), pl.BlockSpec(memory_space=pltpu.VMEM)] + [anywhere] * len(arrays),
        out_specs=[anywhere] * len(outs),
        out_shape=[jax.ShapeDtypeStruct(*v) for v in outs.values()],
        scratch_shapes=list(scratch.values()),
        compiler_params=pltpu.CompilerParams(collective_id=1, has_side_effects=True, vmem_limit_bytes=62 << 20),
        cost_estimate=pl.CostEstimate(flops=200 << 30, bytes_accessed=400 << 20, transcendentals=0),
        name="backward",
    )(lengths, gain, *arrays.values())
    return dict(zip(outs, got))


rate_in = 0.02
rate_out = 0.08
rate_gains = 1.2


def body(
    tokens,
    target,
    doc_lengths,
    corpus_ids,
    corpus_weights,
    w_in,
    w_out,
    gains,
    first_in,
    first_out,
    first_gains,
    second_in,
    second_out,
    second_gains,
    outer_in,
    outer_out,
    outer_gains,
):
    n, rep = lax.axis_size("fsdp"), lax.axis_size("rep")
    line = n // 2
    f, r = lax.axis_index("fsdp"), lax.axis_index("rep")
    z, y = f // 2, f % 2
    direct = by_neighbours(n, rep)
    inside = (z > 0) & (z < line - 1)
    place = jnp.stack([z if direct else 0 * z, r % 2, y, inside]).astype(jnp.int32)
    rows_in, rows_out = w_in.shape[0], w_out.shape[1]
    x, tgt, lengths = tokens[0], target[0], doc_lengths[0]
    ids = corpus_ids[0][:, None]

    if direct:
        qw, attn = H * HD, H * HD + 2 * KVH * HD
        low_in, low_out = w_in.astype(bf16), w_out.astype(bf16)
        shards = dict(
            q=low_in[:, :qw], kv=low_in[:, qw:attn], gate=low_in[:, attn : attn + FF], up=low_in[:, attn + FF :],
            proj=low_out[0], down=low_out[1],
        )
        low_gain = jnp.pad(gains.astype(bf16), ((0, 14), (0, 0)))
        fwd = forward(lengths, corpus_weights, ids, dict(x=x, target=tgt), shards, low_gain, n)
        weight = lambda c: fwd["full_" + c].reshape(-1, shards[c].shape[1])
        kept = {k: fwd[k] for k in ("c", "middle", "hidden", "second", "gate", "up", "dy", "mixed", "packed", "lse", "first")}
        got = backward(
            lengths, fwd["gain"],
            dict(x=x, target=tgt, proj=weight("proj"), down=weight("down"), q_w=weight("q"), kv_w=weight("kv"),
                 gate_w=weight("gate"), up_w=weight("up"), **kept),
            n, rows_in, rows_out,
        )
        activations, input_grad = got["act"], got["xgrad"]
        gain_share = jnp.sum(got["gain_got"].reshape(n, 2, 8, -1), axis=(0, 2))
        gate_sum, up_sum, q_sum, kv_sum, down_sum, proj_sum = (
            (got["own_" + p], (got["slot_" + p],)) for p in ("gate", "up", "q", "kv", "down", "proj")
        )
    else:
        gain_full, wq, proj, wf, down = all_weights(w_in, w_out, gains)
        first_low, packed = qkv(x, gain_full, wq)
        mixed, lse = attention(lengths, packed)
        middle, second_low, hidden, d_both, dy, _ = ffn(corpus_weights, x, mixed, tgt, ids, gain_full, proj, wf, down)

        def by_library(a, bs, name):
            block = 2 * BQ if a.shape[1] % (2 * BQ) == 0 else BQ
            every_row = jnp.arange(a.shape[1] // block, dtype=jnp.int32)
            total = grad_rows(every_row, a, bs, block, name=name)
            return lax.psum_scatter(total.reshape(a.shape[1], -1), "fsdp", scatter_dimension=0, tiled=True)[None], ()

        gate_sum = by_library(second_low, [(d_both, 0, FF)], "grad_gate")
        down_sum = by_library(hidden, [(dy, 0, dy.shape[1])], "grad_down")
        up_sum = by_library(second_low, [(d_both, 1, FF)], "grad_up")
        activations, d_mid, d_low, d_mix, gain_two = mid(
            corpus_weights, middle, hidden, d_both, tgt, ids, gain_full, proj, wf, down
        )
        proj_sum = by_library(mixed, [(d_low, 0, d_low.shape[1])], "grad_proj")
        dq, dk, dv = attention_back(lengths, packed, d_mix, mixed, lse)
        q_sum = by_library(first_low, [(dq, 0, H * HD)], "grad_q")
        kv_sum = by_library(first_low, [(dk, 0, KVH * HD), (dv, 0, KVH * HD)], "grad_kv")
        input_grad, gain_one = input_back(x, d_mid, dq, dk, dv, gain_full, wq)
        both = jnp.stack([jnp.sum(gain_one, axis=0), jnp.sum(gain_two, axis=0)])
        gain_share = lax.psum_scatter(both, "fsdp", scatter_dimension=1, tiled=True)

    flat = lambda a: a.reshape(-1, a.shape[-1])

    def weight_steps(pieces, first, second, w, outer, rate):
        grads = steps = None
        for spot, ((own, terms), rows, row_at, col_at, cols, tile) in pieces:
            grads, keep, send = adam_piece(
                spot, own, terms, first, second, w, grads, rows, row_at, col_at, cols, tile, rate
            )
            keep, other = rep_sum(keep, send, rep)
            steps = outer_piece(place, keep, other, outer, w, steps, rows, row_at, col_at, cols, tile, rep)
        return grads, steps

    qw, kvw = H * HD, 2 * KVH * HD
    in_pieces = [
        (place, (gate_sum, rows_in, 0, qw + kvw, FF, 512)),
        (place, (up_sum, rows_in, 0, qw + kvw + FF, FF, 512)),
        (place, (q_sum, rows_in, 0, 0, qw, 512)),
        (place, (kv_sum, rows_in, 0, qw, kvw, 512)),
    ]
    width = w_out.shape[2]
    out_pieces = [
        (place, (down_sum, rows_out, rows_out, 0, width, 512)),
        (place, (proj_sum, rows_out, 0, 0, width, 512)),
    ]
    out_grads, out_steps = weight_steps(
        out_pieces, flat(first_out[0]), flat(second_out[0]), flat(w_out), flat(outer_out), rate_out
    )
    in_grads, in_steps = weight_steps(in_pieces, first_in[0], second_in[0], w_in, outer_in, rate_in)

    first_gains_new, second_gains_new, delta = adam_step(gain_share, first_gains[0], second_gains[0], gains, rate_gains)
    sum_gains = lax.psum(delta, "rep")
    diff_gains, outer_gains_new, new_gains = outer_step(sum_gains, outer_gains, gains, rep)

    out_shape = lambda a: a.reshape(2, rows_out, width)
    diff_in, outer_in_new, new_in, copy_in = in_steps
    diff_out, outer_out_new, new_out, copy_out = (out_shape(a) for a in out_steps)
    grad_in, first_in_new, second_in_new = in_grads
    grad_out, first_out_new, second_out_new = (out_shape(a) for a in out_grads)
    return (
        activations[None],
        input_grad[None],
        grad_in[None],
        grad_out[None],
        gain_share[None],
        first_in_new[None],
        first_out_new[None],
        first_gains_new[None],
        second_in_new[None],
        second_out_new[None],
        second_gains_new[None],
        diff_in,
        diff_out,
        diff_gains,
        outer_in_new,
        outer_out_new,
        outer_gains_new,
        new_in,
        new_out,
        new_gains,
        copy_in,
        copy_out,
        new_gains.astype(bf16),
    )


def solution(mesh):
    rows = P(("rep", "fsdp"), None, None)
    pair = P(("rep", "fsdp"), None)
    w_in, w_out, gains = P("fsdp", None), P(None, "fsdp", None), P(None, "fsdp")
    m_in, m_out, m_gains = P("rep", "fsdp", None), P("rep", None, "fsdp", None), P("rep", None, "fsdp")
    weights, moments = (w_in, w_out, gains), (m_in, m_out, m_gains)
    return jax.shard_map(
        body,
        mesh=mesh,
        in_specs=(rows, rows, pair, pair, P(), *weights, *moments, *moments, *weights),
        out_specs=(rows, rows, *moments, *moments, *moments, *weights, *weights, *weights, *weights),
        check_vma=False,
    )
```

```python
import functools
import jax
import jax.numpy as jnp
from jax import lax
from jax.experimental import pallas as pl
from jax.experimental.pallas import tpu as pltpu
from jax.sharding import PartitionSpec as P

H = 16
HD = 64
KVH = 4
FF = 1024
LEN = 1024
NCORP = 8
f32 = jnp.float32
bf16 = jnp.bfloat16
norm_eps = 1e-06
BQ = 256
NT = (((1,), (1,)), ((), ()))
TN = (((0,), (0,)), ((), ()))


def mm(a, b, dims=(((1,), (0,)), ((), ()))):
    return lax.dot_general(a, b, dims, preferred_element_type=f32)


def params(**kw):
    return pltpu.CompilerParams(vmem_limit_bytes=60 << 20, **kw)


def one(shape, index):
    return pl.BlockSpec(shape, index, pipeline_mode=pl.Buffered(1))


def qkv_kernel(x_ref, g_ref, w_ref, first_ref, packed_ref):
    x = x_ref[...].astype(f32)
    r = lax.rsqrt(jnp.mean(x * x, axis=-1, keepdims=True) + norm_eps)
    first = (x * r * g_ref[0:1, :]).astype(bf16)
    first_ref[...] = first
    packed_ref[...] = mm(first, w_ref[...]).astype(bf16)


def qkv(x, gains, w):
    rows, width = x.shape
    cols = w.shape[1]
    return pl.pallas_call(
        qkv_kernel,
        grid=(rows // BQ,),
        in_specs=[
            pl.BlockSpec((BQ, width), lambda i: (i, 0)),
            one(gains.shape, lambda i: (0, 0)),
            one((width, cols), lambda i: (0, 0)),
        ],
        out_specs=[
            pl.BlockSpec((BQ, width), lambda i: (i, 0)),
            pl.BlockSpec((BQ, cols), lambda i: (i, 0)),
        ],
        out_shape=[
            jax.ShapeDtypeStruct((rows, width), bf16),
            jax.ShapeDtypeStruct((rows, cols), bf16),
        ],
        compiler_params=params(),
        cost_estimate=pl.CostEstimate(
            flops=2 * rows * width * cols, bytes_accessed=rows * width * 4 + width * cols * 2, transcendentals=0
        ),
        name="norm_qkv",
    )(x, gains, w)


def doc_start(lengths_ref, position):
    end = jnp.int32(0)
    start = jnp.zeros_like(position)
    for j in range(lengths_ref.shape[0]):
        end = end + lengths_ref[j]
        start = jnp.where(position >= end, end, start)
    return start


def key_blocks(lengths_ref, i):
    first_row = i * BQ
    return i + 1 - doc_start(lengths_ref, first_row) // BQ


def max_blocks():
    return LEN // (2 * BQ) + 1


def attention_step(len_ref, i, count, q_ref, k_ref, v_ref, o_ref, lse_ref):
    row = i * BQ + lax.broadcasted_iota(jnp.int32, (BQ, 1), 0)
    start = doc_start(len_ref, row)
    lane = lax.broadcasted_iota(jnp.int32, (BQ, 128), 1)
    for nb in range(1, max_blocks() + 1):

        @pl.when(count == nb)
        def _():
            span = nb * BQ
            base = pl.multiple_of((i - (nb - 1)) * BQ, BQ)
            col = base + lax.broadcasted_iota(jnp.int32, (BQ, span), 1)
            bias = jnp.where((col >= start) & (col <= row), 0.0, -1e30)
            k2 = k_ref[pl.ds(base, span), :]
            v2 = v_ref[pl.ds(base, span), :]
            tile = jnp.zeros((BQ, 128), f32)
            outs = []
            for kv in range(2):
                k = k2[:, kv * HD : (kv + 1) * HD]
                v = v2[:, kv * HD : (kv + 1) * HD]
                for g in range(H // KVH):
                    h = kv * (H // KVH) + g
                    q = q_ref[:, h * HD : (h + 1) * HD] * jnp.asarray(HD**-0.5, bf16)
                    s = mm(q, k, NT) + bias
                    m = jnp.max(s, axis=-1, keepdims=True)
                    e = jnp.exp(s - m)
                    total = jnp.sum(e, axis=-1, keepdims=True)
                    o = mm(e.astype(bf16), v) * (1.0 / total)
                    outs.append(o.astype(bf16))
                    tile = jnp.where(lane == h, m + jnp.log(total), tile)
            o_ref[...] = jnp.concatenate(outs, axis=1)
            lse_ref[...] = tile.T[0:8, :]


def attn_kernel(len_ref, *refs):
    i = pl.program_id(0)
    attention_step(len_ref, i, key_blocks(len_ref, i), *refs)


def attention(lengths, packed):
    qw = H // 2 * HD
    kcol = H * HD // 128
    vcol = kcol + KVH * HD // 128
    return pl.pallas_call(
        attn_kernel,
        grid_spec=pltpu.PrefetchScalarGridSpec(
            num_scalar_prefetch=1,
            grid=(LEN // BQ, 2),
            in_specs=[
                pl.BlockSpec((BQ, qw), lambda i, p, s: (i, p)),
                pl.BlockSpec((LEN, 128), lambda i, p, s: (0, kcol + p)),
                pl.BlockSpec((LEN, 128), lambda i, p, s: (0, vcol + p)),
            ],
            out_specs=[
                pl.BlockSpec((BQ, qw), lambda i, p, s: (i, p)),
                pl.BlockSpec((8, BQ), lambda i, p, s: (p, i)),
            ],
        ),
        out_shape=[
            jax.ShapeDtypeStruct((LEN, H * HD), bf16),
            jax.ShapeDtypeStruct((H, LEN), f32),
        ],
        compiler_params=params(),
        cost_estimate=pl.CostEstimate(flops=4 * H * LEN * LEN * HD * 4, bytes_accessed=1 << 24, transcendentals=0),
        name="attention",
    )(lengths, packed, packed, packed)


def attention_back_step(len_ref, i, q_ref, k_ref, v_ref, d_ref, o_ref, lse_ref, dq_ref, dk_acc, dv_acc, count=None):
    if count is None:
        count = jnp.minimum(i + 1, max_blocks())
    row = i * BQ + lax.broadcasted_iota(jnp.int32, (1, BQ), 1)
    start = doc_start(len_ref, row)
    lane = lax.broadcasted_iota(jnp.int32, (BQ, 128), 1)
    group = H // KVH
    scale = jnp.asarray(HD**-0.5, bf16)
    tile = jnp.zeros((BQ, 128), f32)
    for h in range(2 * group):
        cols = slice(h * HD, (h + 1) * HD)
        dot = jnp.sum(d_ref[:, cols].astype(f32) * o_ref[:, cols].astype(f32), axis=-1, keepdims=True)
        tile = jnp.where(lane == h, dot, tile)
    inner = tile.T
    for nb in range(1, max_blocks() + 1):

        @pl.when(count == nb)
        def _():
            span = nb * BQ
            base = pl.multiple_of((i - (nb - 1)) * BQ, BQ)
            key = base + lax.broadcasted_iota(jnp.int32, (span, BQ), 0)
            bias = jnp.where((key >= start) & (key <= row), 0.0, -1e30)
            k2 = k_ref[pl.ds(base, span), :]
            v2 = v_ref[pl.ds(base, span), :]
            dks, dvs = [], []
            for kv in range(2):
                k = k2[:, kv * HD : (kv + 1) * HD]
                v = v2[:, kv * HD : (kv + 1) * HD]
                dk = dv = None
                dqs = []
                for g in range(group):
                    h = kv * group + g
                    cols = slice(h * HD, (h + 1) * HD)
                    q = q_ref[:, cols] * scale
                    d = d_ref[:, cols]
                    s = mm(k, q, NT) + bias
                    p = jnp.exp(s - lse_ref[h : h + 1, :])
                    dp = mm(v, d, NT)
                    ds = (p * (dp - inner[h : h + 1, :])).astype(bf16)
                    dv_h = mm(p.astype(bf16), d)
                    dk_h = mm(ds, q)
                    dv = dv_h if dv is None else dv + dv_h
                    dk = dk_h if dk is None else dk + dk_h
                    dqs.append(mm(k, ds, TN))
                dq = jnp.concatenate(dqs, axis=0) * (HD**-0.5)
                dq_ref[:, kv * group * HD : (kv + 1) * group * HD] = dq.T.astype(bf16)
                dks.append(dk)
                dvs.append(dv)
            dk_acc[pl.ds(base, span), :] += jnp.concatenate(dks, axis=1)
            dv_acc[pl.ds(base, span), :] += jnp.concatenate(dvs, axis=1)


def attn_back_kernel(len_ref, q_ref, k_ref, v_ref, d_ref, o_ref, lse_ref, dq_ref, dk_ref, dv_ref, dk_acc, dv_acc):
    i = pl.program_id(1)

    @pl.when(i == 0)
    def _():
        dk_acc[...] = jnp.zeros_like(dk_acc)
        dv_acc[...] = jnp.zeros_like(dv_acc)

    attention_back_step(
        len_ref, i, q_ref, k_ref, v_ref, d_ref, o_ref, lse_ref, dq_ref, dk_acc, dv_acc, key_blocks(len_ref, i)
    )

    @pl.when(i == pl.num_programs(1) - 1)
    def _():
        dk_ref[...] = dk_acc[...].astype(bf16)
        dv_ref[...] = dv_acc[...].astype(bf16)


def attention_back(lengths, packed, d_mixed, mixed, lse):
    qw = H // 2 * HD
    kcol = H * HD // 128
    vcol = kcol + KVH * HD // 128
    return pl.pallas_call(
        attn_back_kernel,
        grid_spec=pltpu.PrefetchScalarGridSpec(
            num_scalar_prefetch=1,
            grid=(2, LEN // BQ),
            in_specs=[
                pl.BlockSpec((BQ, qw), lambda p, i, s: (i, p)),
                pl.BlockSpec((LEN, 128), lambda p, i, s: (0, kcol + p)),
                pl.BlockSpec((LEN, 128), lambda p, i, s: (0, vcol + p)),
                pl.BlockSpec((BQ, qw), lambda p, i, s: (i, p)),
                pl.BlockSpec((BQ, qw), lambda p, i, s: (i, p)),
                pl.BlockSpec((8, BQ), lambda p, i, s: (p, i)),
            ],
            out_specs=[
                pl.BlockSpec((BQ, qw), lambda p, i, s: (i, p)),
                pl.BlockSpec((LEN, 128), lambda p, i, s: (0, p)),
                pl.BlockSpec((LEN, 128), lambda p, i, s: (0, p)),
            ],
            scratch_shapes=[pltpu.VMEM((LEN, 128), f32), pltpu.VMEM((LEN, 128), f32)],
        ),
        out_shape=[
            jax.ShapeDtypeStruct((LEN, H * HD), bf16),
            jax.ShapeDtypeStruct((LEN, KVH * HD), bf16),
            jax.ShapeDtypeStruct((LEN, KVH * HD), bf16),
        ],
        compiler_params=params(),
        cost_estimate=pl.CostEstimate(flops=10 * H * LEN * LEN * HD * 4, bytes_accessed=1 << 24, transcendentals=0),
        name="attention_back",
    )(lengths, packed, packed, packed, d_mixed, mixed, lse)


def token_weight(table_ref, ids):
    weight = jnp.zeros(ids.shape, f32)
    for j in range(table_ref.shape[0]):
        weight = jnp.where(ids == j, table_ref[j].astype(f32) * 0.25, weight)
    return weight


def ffn_kernel(table_ref, x_ref, mixed_ref, t_ref, ids_ref, g_ref, proj_ref, wf_ref, down_ref,
               middle_ref, second_ref, hidden_ref, dboth_ref, dy_ref, c_ref):
    middle = x_ref[...].astype(f32) + mm(mixed_ref[...], proj_ref[...])
    middle_ref[...] = middle
    r = lax.rsqrt(jnp.mean(middle * middle, axis=-1, keepdims=True) + norm_eps)
    second = (middle * r * g_ref[1:2, :]).astype(bf16)
    second_ref[...] = second
    c = token_weight(table_ref, ids_ref[...])
    c_ref[...] = jnp.broadcast_to(c, c_ref.shape)
    dy = (c * t_ref[...].astype(f32)).astype(bf16)
    dy_ref[...] = dy
    step = 512
    for c in range(0, FF, step):
        gate = mm(second, wf_ref[:, c : c + step])
        up = mm(second, wf_ref[:, FF + c : FF + c + step])
        dh = mm(dy, down_ref[c : c + step, :], NT)
        sig = jax.nn.sigmoid(gate)
        silu = gate * sig
        hidden_ref[:, c : c + step] = (silu * up).astype(bf16)
        dboth_ref[:, c : c + step] = (dh * up * sig * (1.0 + gate * (1.0 - sig))).astype(bf16)
        dboth_ref[:, FF + c : FF + c + step] = (dh * silu).astype(bf16)


def ffn(table, x, mixed, target, ids, gains, proj, wf, down):
    width = x.shape[1]
    rowb = lambda n: pl.BlockSpec((BQ, n), lambda i, s: (i, 0))
    whole = lambda a: one(a.shape, lambda i, s: (0, 0))
    return pl.pallas_call(
        ffn_kernel,
        grid_spec=pltpu.PrefetchScalarGridSpec(
            num_scalar_prefetch=1,
            grid=(LEN // BQ,),
            in_specs=[rowb(width), rowb(H * HD), rowb(width), rowb(1), whole(gains), whole(proj), whole(wf), whole(down)],
            out_specs=[rowb(width), rowb(width), rowb(FF), rowb(2 * FF), rowb(width), rowb(128)],
        ),
        out_shape=[
            jax.ShapeDtypeStruct((LEN, width), f32),
            jax.ShapeDtypeStruct((LEN, width), bf16),
            jax.ShapeDtypeStruct((LEN, FF), bf16),
            jax.ShapeDtypeStruct((LEN, 2 * FF), bf16),
            jax.ShapeDtypeStruct((LEN, width), bf16),
            jax.ShapeDtypeStruct((LEN, 128), f32),
        ],
        compiler_params=params(),
        cost_estimate=pl.CostEstimate(flops=2 * LEN * width * FF * 4, bytes_accessed=40 << 20, transcendentals=0),
        name="ffn",
    )(table, x, mixed, target, ids, gains, proj, wf, down)


def mid_kernel(table_ref, middle_ref, hidden_ref, dboth_ref, t_ref, ids_ref, g_ref, proj_ref, wf_ref, down_ref,
               act_ref, dmid_ref, dlow_ref, dmix_ref, gain_ref):
    middle = middle_ref[...]
    act_ref[...] = (middle + mm(hidden_ref[...], down_ref[...])).astype(bf16)
    r = lax.rsqrt(jnp.mean(middle * middle, axis=-1, keepdims=True) + norm_eps)
    n2 = middle * r
    ds2 = mm(dboth_ref[...], wf_ref[...], NT)
    prod = ds2 * n2
    part = jnp.sum(prod.reshape(BQ // 8, 8, prod.shape[1]), axis=0)

    @pl.when(pl.program_id(0) == 0)
    def _():
        gain_ref[...] = jnp.zeros_like(gain_ref)

    gain_ref[...] += part
    g = g_ref[1:2, :]
    e2 = ds2 * g
    dy = token_weight(table_ref, ids_ref[...]) * t_ref[...].astype(f32)
    dmid = dy + r * (e2 - n2 * jnp.mean(prod * g, axis=-1, keepdims=True))
    dmid_ref[...] = dmid
    low = dmid.astype(bf16)
    dlow_ref[...] = low
    dmix_ref[...] = mm(low, proj_ref[...], NT).astype(bf16)


def mid(table, middle, hidden, dboth, target, ids, gains, proj, wf, down):
    width = middle.shape[1]
    rowb = lambda n: pl.BlockSpec((BQ, n), lambda i, s: (i, 0))
    whole = lambda a: one(a.shape, lambda i, s: (0, 0))
    return pl.pallas_call(
        mid_kernel,
        grid_spec=pltpu.PrefetchScalarGridSpec(
            num_scalar_prefetch=1,
            grid=(LEN // BQ,),
            in_specs=[rowb(width), rowb(FF), rowb(2 * FF), rowb(width), rowb(1), whole(gains), whole(proj), whole(wf), whole(down)],
            out_specs=[rowb(width), rowb(width), rowb(width), rowb(H * HD), pl.BlockSpec((8, width), lambda i, s: (0, 0))],
        ),
        out_shape=[
            jax.ShapeDtypeStruct((LEN, width), bf16),
            jax.ShapeDtypeStruct((LEN, width), f32),
            jax.ShapeDtypeStruct((LEN, width), bf16),
            jax.ShapeDtypeStruct((LEN, H * HD), bf16),
            jax.ShapeDtypeStruct((8, width), f32),
        ],
        compiler_params=params(),
        cost_estimate=pl.CostEstimate(flops=2 * LEN * width * FF * 4, bytes_accessed=40 << 20, transcendentals=0),
        name="mid",
    )(table, middle, hidden, dboth, target, ids, gains, proj, wf, down)


def input_kernel(x_ref, dmid_ref, dq_ref, dk_ref, dv_ref, g_ref, w_ref, out_ref, gain_ref):
    x = x_ref[...].astype(f32)
    r = lax.rsqrt(jnp.mean(x * x, axis=-1, keepdims=True) + norm_eps)
    n1 = x * r
    q, k = H * HD, H * HD + KVH * HD
    ds1 = mm(dq_ref[...], w_ref[:, :q], NT) + mm(dk_ref[...], w_ref[:, q:k], NT) + mm(dv_ref[...], w_ref[:, k:], NT)
    prod = ds1 * n1
    part = jnp.sum(prod.reshape(BQ // 8, 8, prod.shape[1]), axis=0)

    @pl.when(pl.program_id(0) == 0)
    def _():
        gain_ref[...] = jnp.zeros_like(gain_ref)

    gain_ref[...] += part
    g = g_ref[0:1, :]
    out = dmid_ref[...] + r * (ds1 * g - n1 * jnp.mean(prod * g, axis=-1, keepdims=True))
    out_ref[...] = out.astype(bf16)


def input_back(x, dmid, dq, dk, dv, gains, w):
    width = x.shape[1]
    rowb = lambda n: pl.BlockSpec((BQ, n), lambda i: (i, 0))
    whole = lambda a: one(a.shape, lambda i: (0, 0))
    return pl.pallas_call(
        input_kernel,
        grid=(LEN // BQ,),
        in_specs=[rowb(width), rowb(width), rowb(H * HD), rowb(KVH * HD), rowb(KVH * HD), whole(gains), whole(w)],
        out_specs=[rowb(width), pl.BlockSpec((8, width), lambda i: (0, 0))],
        out_shape=[jax.ShapeDtypeStruct((LEN, width), bf16), jax.ShapeDtypeStruct((8, width), f32)],
        compiler_params=params(),
        cost_estimate=pl.CostEstimate(flops=2 * LEN * width * 1536, bytes_accessed=24 << 20, transcendentals=0),
        name="input_back",
    )(x, dmid, dq, dk, dv, gains, w)


def grad_kernel(pick_ref, a_ref, *refs):
    out_ref = refs[-1]
    b_refs = refs[:-1]
    add_ref = None
    if len(b_refs) > 1 and len(b_refs[-1].shape) == 3:
        add_ref, b_refs = b_refs[-1], b_refs[:-1]
    col = 0
    a = a_ref[...]
    for b_ref in b_refs:
        n = b_ref.shape[1]
        g = mm(a, b_ref[...], TN)
        if add_ref is not None:
            g = g + add_ref[0, :, col : col + n].astype(f32)
        out_ref[0, :, col : col + n] = g.astype(bf16)
        col += n


def grad_rows(pick, a, bs, rows, add=None, name="grad"):
    cols = sum(width for _, _, width in bs)
    count = pick.shape[0]
    specs = [pl.BlockSpec((LEN, rows), lambda j, p: (0, p[j]))]
    specs += [one((LEN, width), functools.partial(lambda at, j, p: (0, at), at)) for _, at, width in bs]
    ops = [a, *(b for b, _, _ in bs)]
    if add is not None:
        specs.append(pl.BlockSpec((1, rows, cols), lambda j, p: (j, 0, 0)))
        ops.append(add)
    return pl.pallas_call(
        grad_kernel,
        grid_spec=pltpu.PrefetchScalarGridSpec(
            num_scalar_prefetch=1,
            grid=(count,),
            in_specs=specs,
            out_specs=pl.BlockSpec((1, rows, cols), lambda j, p: (j, 0, 0)),
        ),
        out_shape=jax.ShapeDtypeStruct((count, rows, cols), bf16),
        compiler_params=params(),
        cost_estimate=pl.CostEstimate(flops=2 * LEN * rows * count * cols, bytes_accessed=12 << 20, transcendentals=0),
        name=name,
    )(pick, *ops)


beta_first = 0.9
beta_second = 0.95
adam_eps = 1e-08
decay_rate = 0.1
outer_decay = 0.5
outer_rate = 0.7
STEP = 10


def adam_step(grad, first, second, weight, rate):
    first_new = beta_first * first + (1.0 - beta_first) * grad
    second_new = beta_second * second + (1.0 - beta_second) * grad * grad
    ratio = first_new / (1.0 - beta_first**STEP) / (jnp.sqrt(second_new / (1.0 - beta_second**STEP)) + adam_eps)
    local = weight - rate * (ratio + decay_rate * weight)
    return first_new, second_new, weight - local


def outer_step(delta_sum, momentum, weight, groups):
    average = delta_sum / groups
    momentum_new = outer_decay * momentum + average
    return average, momentum_new, weight - outer_rate * (average + outer_decay * momentum_new)


def adam_kernel(place_ref, own_ref, *refs, slots, deltas, rate, groups):
    refs = list(refs)
    grad = own_ref[0].astype(f32)
    if slots:
        b, c, d = (refs.pop(0)[0].astype(f32) for _ in range(3))
        grad = grad + b + c + jnp.where(place_ref[1] == 1, d, 0.0)
    first_ref, second_ref, w_ref = refs[:3]
    first_new, second_new, delta = adam_step(grad, first_ref[...], second_ref[...], w_ref[...], rate)
    outs = refs[-7:] if deltas else refs[-4:]
    outs[0][...] = grad
    outs[1][...] = first_new
    outs[2][...] = second_new
    if not deltas:
        outs[3][...] = delta.astype(bf16)
        return
    outer_ref, delta_ref = refs[3:5]
    d = [delta_ref[k].astype(f32) for k in range(delta_ref.shape[0])]
    write_outer((d[0] + d[1]) + (d[2] + d[3]), outer_ref, w_ref, outs[3:], groups)


def write_outer(total, outer_ref, w_ref, outs, groups):
    average, momentum, weight = outer_step(total, outer_ref[...], w_ref[...], groups)
    outs[0][...] = average
    outs[1][...] = momentum
    outs[2][...] = weight
    outs[3][...] = weight.astype(bf16)


TILE = 256


def adam_tiles(place, own, slots, first, second, w, outer, deltas, held, own_at, tiles, rate, groups):
    rows = w.shape[0]
    start, count, hole, skip = tiles
    at = lambda j: start + j + jnp.where(j >= hole, skip, 0)
    state = pl.BlockSpec((rows, TILE), lambda j, p: (0, at(j)))
    plane = lambda pick: pl.BlockSpec((1, rows, TILE), lambda j, p: (pick(p), 0, at(j) - own_at))
    full = jax.ShapeDtypeStruct(w.shape, f32)
    ops, specs = [own], [plane(lambda p: p[0])]
    if slots is not None:
        ops += [slots] * 3
        specs += [plane(lambda p: 1), plane(lambda p: 2), plane(lambda p: 2 + p[1])]
    ops += [first, second, w]
    specs += [state] * 3
    out_shape, out_specs = [full] * 3, [state] * 3
    if deltas is not None:
        ops += [outer, deltas]
        specs += [state, pl.BlockSpec((deltas.shape[0], rows, TILE), lambda j, p: (0, 0, at(j)))]
        out_shape += [full] * 3 + [jax.ShapeDtypeStruct(w.shape, bf16)]
        out_specs += [state] * 4
    else:
        out_shape.append(jax.ShapeDtypeStruct((rows, count * TILE), bf16))
        out_specs.append(pl.BlockSpec((rows, TILE), lambda j, p: (0, j)))
    aliases = {}
    if held is not None:
        aliases = {1 + len(ops) + k: k for k in range(3)}
        ops += list(held)
        specs += [pl.BlockSpec(memory_space=pl.ANY)] * 3
    return pl.pallas_call(
        functools.partial(adam_kernel, slots=slots is not None, deltas=deltas is not None, rate=rate, groups=groups),
        grid_spec=pltpu.PrefetchScalarGridSpec(num_scalar_prefetch=1, grid=(count,), in_specs=specs, out_specs=out_specs),
        out_shape=out_shape,
        input_output_aliases=aliases,
        compiler_params=params(),
        cost_estimate=pl.CostEstimate(flops=0, bytes_accessed=rows * count * TILE * 48, transcendentals=0),
        name="adam",
    )(place, *ops)


def outer_kernel(*refs, terms, groups):
    d = [ref[...].astype(f32) for ref in refs[:terms]]
    total = (d[0] + d[1]) + (d[2] + d[3]) if terms == 4 else sum(d[1:], d[0])
    write_outer(total, refs[terms], refs[terms + 1], refs[-4:], groups)


def outer_tiles(deltas, outer, w, held, start, groups):
    rows, cols = deltas[0].shape
    state = pl.BlockSpec((rows, TILE), lambda j: (0, start + j))
    full = jax.ShapeDtypeStruct(w.shape, f32)
    ops = [*deltas, outer, w]
    specs = [pl.BlockSpec((rows, TILE), lambda j: (0, j))] * len(deltas) + [state] * 2
    aliases = {}
    if held is not None:
        aliases = {len(ops) + k: k for k in range(4)}
        ops += list(held)
        specs += [pl.BlockSpec(memory_space=pl.ANY)] * 4
    return pl.pallas_call(
        functools.partial(outer_kernel, terms=len(deltas), groups=groups),
        grid=(cols // TILE,),
        in_specs=specs,
        out_specs=[state] * 4,
        out_shape=[full, full, full, jax.ShapeDtypeStruct(w.shape, bf16)],
        input_output_aliases=aliases,
        compiler_params=params(),
        cost_estimate=pl.CostEstimate(flops=0, bytes_accessed=rows * cols * 24, transcendentals=0),
        name="outer",
    )(*ops)


def groups_terms(delta, rep):
    to = lambda a, k: lax.ppermute(a, "rep", [(i, i ^ k) for i in range(rep)])
    if rep != 4:
        return [delta] + [to(delta, k) for k in range(1, rep)]
    near, far = to(delta, 1), to(delta, 2)
    return [delta, near, far, to(far, 1)]


def by_neighbours(n, rep):
    return n == 8 and rep == 4


def all_weights(w_in, w_out, gains):
    split = H * HD + 2 * KVH * HD
    low_in, low_out = w_in.astype(bf16), w_out.astype(bf16)
    low_gains = jnp.pad(gains.astype(bf16), ((0, 62), (0, 0)))
    shards = [low_gains, low_in[:, :split], low_out[0], low_in[:, split:], low_out[1]]
    full = [lax.all_gather(a, "fsdp") for a in shards]
    gain_full = full[0][:, :8].astype(f32).transpose(1, 0, 2).reshape(8, -1)
    return [gain_full] + [a.reshape(-1, a.shape[-1]) for a in full[1:]]


CHUNKS = ("q", "kv", "proj", "gate", "up", "down")
CHIP_SHARE = {"q": 48, "kv": 48, "proj": 16, "gate": 48, "up": 48, "down": 32}
LAGS = (0, 2, 4, 5)


def forward_kernel(*refs, names, line):
    R = dict(zip(names, refs))
    r, f = lax.axis_index("rep"), lax.axis_index("fsdp")
    x, core, z, y = r // 2, r % 2, f // 2, f % 2
    n = 2 * line
    to_y = (r, f + 1 - 2 * y)
    to_x = (r + 2 - 4 * x, f)
    to_core = (r + 1 - 2 * core, f)
    barrier = pltpu.get_barrier_semaphore()
    peers = [(r, lax.rem(f + step, n)) for step in range(1, n)]
    for to in (*peers, to_x, to_core):
        pl.semaphore_signal(barrier, inc=1, device_id=to, device_id_type=pl.DeviceIdType.MESH)
    pl.semaphore_wait(barrier, n + 1)

    def remote(src, dst, send, recv, to):
        return pltpu.make_async_remote_copy(
            src_ref=src, dst_ref=dst, send_sem=send, recv_sem=recv, device_id=to, device_id_type=pl.DeviceIdType.MESH
        )

    held = {c: R["v_" + c] if "v_" + c in R else R["full_" + c] for c in CHUNKS}
    rows_of = {c: R["low_" + c].shape[0] for c in CHUNKS}
    item = lambda side, d: 0 if d == 0 else 2 * d - 1 + (side > 0)
    exists = lambda side, d: None if d == 0 else (z - d >= 0 if side < 0 else z + d < line)

    def guard(cond, fn):
        if cond is None:
            fn()
        else:
            pl.when(cond)(fn)

    def copy(src, dst, stage, c, side, d, to):
        m, k = CHUNKS.index(c), item(side, d)
        return remote(src, dst, R["f_send"].at[stage, m, k], R["f_recv"].at[stage, m, k], to)

    def portion(c):
        half, share = rows_of[c] // 2, CHIP_SHARE[c]
        return pl.ds(pl.multiple_of(core * half + x * share, 16), half - share)

    def line_copy(c, side, d):
        plane = z + side * (d - 1)
        dst = held[c].at[plane * 2 + y, portion(c), :]
        src = R["low_" + c].at[portion(c), :] if d == 1 else dst
        return copy(src, dst, 0, c, side, d, (r, f - 2 * side))

    def line_arrival(c, side, d):
        dst = held[c].at[(z + side * d) * 2 + y, portion(c), :]
        return copy(dst, dst, 0, c, side, d, to_y)

    def y_copy(c, side, d):
        dst = held[c].at[(z + side * d) * 2 + y, portion(c), :]
        return copy(R["low_" + c].at[portion(c), :] if d == 0 else dst, dst, 1, c, side, d, to_y)

    def both_copy(c, side, d, start, rows, stage, to):
        planes = pl.ds(z * 2 + 1 - y, 1) if d == 0 else pl.ds((z + side * d) * 2, 2)
        ref = held[c].at[planes, pl.ds(pl.multiple_of(start, 16), rows), :]
        return copy(ref, ref, stage, c, side, d, to)

    def x_copy(c, side, d):
        half, share = rows_of[c] // 2, CHIP_SHARE[c]
        return both_copy(c, side, d, core * half + x * (half - share), share, 2, to_x)

    def core_copy(c, side, d):
        half = rows_of[c] // 2
        return both_copy(c, side, d, core * half, half, 3, to_core)

    def onward(side):
        return z < line - 1 if side < 0 else z > 0

    def line_stage(c, side, d):
        if d == 0:
            for way in (-1, 1):
                pl.when(onward(way))(lambda way=way: line_copy(c, way, 1).start())
        else:
            line_arrival(c, side, d).wait_recv()
            if d < line - 1:
                pl.when(onward(side))(lambda: line_copy(c, side, d + 1).start())
        y_copy(c, side, d).start()

    def y_stage(c, side, d):
        y_copy(c, side, d).wait_recv()
        x_copy(c, side, d).start()

    def x_stage(c, side, d):
        x_copy(c, side, d).wait_recv()
        core_copy(c, side, d).start()

    def core_stage(c, side, d):
        core_copy(c, side, d).wait_recv()

    stages = (line_stage, y_stage, x_stage, core_stage)
    sides = lambda d: (1,) if d == 0 else (-1, 1)
    body = [(c, d) for c in CHUNKS for d in range(1, line)]
    own = [(c, 0) for c in CHUNKS]
    order = []
    for at, group in enumerate(body):
        while own and body.index((own[0][0], 1)) - 2 <= at:
            order.append(own.pop(0))
        order.append(group)
    last_tick = {c: order.index((c, line - 1)) + LAGS[-1] for c in CHUNKS}
    ticks = len(order) + LAGS[-1]
    clock = [0]

    def tick(k):
        for lag, stage in zip(LAGS, stages):
            if 0 <= k - lag < len(order):
                c, d = order[k - lag]
                for side in sides(d):
                    guard(exists(side, d), functools.partial(stage, c, side, d))

    def advance(count):
        start = clock[0]
        clock[0] = min(ticks, start + max(count, 0))
        return list(range(start, clock[0]))

    def catch_up(c):
        for k in advance(last_tick[c] + 1 - clock[0]):
            tick(k)

    def spread(steps, per_step):
        plan = [advance(per_step) for _ in range(steps)]

        def serve(at):
            for step, todo in enumerate(plan):
                if todo:

                    @pl.when(at == step)
                    def _():
                        for k in todo:
                            tick(k)

        return serve

    def keep(c):
        return pltpu.make_async_copy(R["v_" + c], R["full_" + c], R["keep_sem"].at[CHUNKS.index(c)])

    def place_own(c):
        return pltpu.make_async_copy(R["low_" + c], held[c].at[f], R["own_sem"].at[CHUNKS.index(c)])

    gain_send = lambda step: remote(R["low_gain"], R["v_gain"].at[f], R["g_send"].at[step - 1], R["g_recv"].at[step - 1], peers[step - 1])
    for step in range(1, n):
        gain_send(step).start()
    own_gain = pltpu.make_async_copy(R["low_gain"], R["v_gain"].at[f], R["g_send"].at[n - 1])
    own_gain.start()
    for k in advance(3):
        tick(k)
    for c in CHUNKS:
        place_own(c).start()

    rowb = lambda width: pl.BlockSpec((BQ, width), lambda i: (i, 0))
    width = R["x"].shape[1]
    steps = LEN // BQ

    def run(body, grid, ins, outs):
        pltpu.emit_pipeline(body, grid=grid, in_specs=[s for _, s in ins], out_specs=[s for _, s in outs])(
            *[R[a] for a, _ in ins], *[R[a] for a, _ in outs]
        )

    def target_step(t_ref, dy_ref, c_ref):
        at = pl.multiple_of(pl.program_id(0) * BQ, BQ)
        c = token_weight(R["table"], R["ids"][pl.ds(at, BQ), :])
        c_ref[...] = jnp.broadcast_to(c, c_ref.shape)
        dy_ref[...] = (c * t_ref[...].astype(f32)).astype(bf16)

    run(target_step, (steps,), [("target", rowb(width))], [("dy", rowb(width)), ("c", rowb(128))])
    own_gain.wait()
    for step in range(1, n):
        gain_send(step).wait()
    gains = jnp.concatenate([R["v_gain"][k] for k in range(n)], axis=1).astype(f32)[0:8]
    R["gain_rows"][...] = gains
    keep_gain = pltpu.make_async_copy(R["gain_rows"], R["gain"], R["g_send"].at[n - 1])
    keep_gain.start()

    def norm_step(x_ref, first_ref):
        v = x_ref[...].astype(f32)
        inv = lax.rsqrt(jnp.mean(v * v, axis=-1, keepdims=True) + norm_eps)
        first_ref[...] = (v * inv * R["gain_rows"][0:1, :]).astype(bf16)

    serve_norm = spread(steps, 1)

    def norm_body(x_ref, first_ref):
        norm_step(x_ref, first_ref)
        serve_norm(pl.program_id(0))

    run(norm_body, (steps,), [("x", rowb(width))], [("first", rowb(width))])
    for c in CHUNKS:
        place_own(c).wait()
    whole = lambda c: held[c][...].reshape(-1, held[c].shape[2])

    catch_up("kv")
    keep("q").start()
    keep("kv").start()
    serve_qkv = spread(steps, 1)

    def qkv_body(first_ref, packed_ref):
        first = first_ref[...]
        split = H * HD
        packed_ref[:, :split] = mm(first, whole("q")).astype(bf16)
        packed_ref[:, split:] = mm(first, whole("kv")).astype(bf16)
        serve_qkv(pl.program_id(0))

    run(qkv_body, (steps,), [("first", rowb(width))], [("packed", rowb(R["packed"].shape[1]))])

    qw = H // 2 * HD
    kcol = H * HD // 128
    vcol = kcol + KVH * HD // 128
    serve_attention = spread(2 * steps, 1)

    def attention_body(q_ref, k_ref, v_ref, o_ref, lse_ref):
        s = pl.program_id(0)
        i = lax.rem(s, steps)
        attention_step(R["lengths"], i, jnp.minimum(i + 1, max_blocks()), q_ref, k_ref, v_ref, o_ref, lse_ref)
        serve_attention(s)

    qspec = pl.BlockSpec((BQ, qw), lambda s: (s % steps, s // steps))
    run(
        attention_body,
        (2 * steps,),
        [
            ("packed", qspec),
            ("packed", pl.BlockSpec((LEN, 128), lambda s: (0, kcol + s // steps))),
            ("packed", pl.BlockSpec((LEN, 128), lambda s: (0, vcol + s // steps))),
        ],
        [("mixed", qspec), ("lse", pl.BlockSpec((8, BQ), lambda s: (s // steps, s % steps)))],
    )

    catch_up("proj")
    keep("proj").start()
    serve_proj = spread(steps, 1)

    def proj_body(x_ref, mixed_ref, middle_ref, second_ref):
        middle = x_ref[...].astype(f32) + mm(mixed_ref[...], whole("proj"))
        middle_ref[...] = middle
        inv = lax.rsqrt(jnp.mean(middle * middle, axis=-1, keepdims=True) + norm_eps)
        second_ref[...] = (middle * inv * R["gain_rows"][1:2, :]).astype(bf16)
        serve_proj(pl.program_id(0))

    run(proj_body, (steps,), [("x", rowb(width)), ("mixed", rowb(H * HD))], [("middle", rowb(width)), ("second", rowb(width))])

    catch_up("gate")
    keep("gate").start()
    serve_gate = spread(steps, 1)

    def gate_body(second_ref, gate_ref):
        gate_ref[...] = mm(second_ref[...], whole("gate"))
        serve_gate(pl.program_id(0))

    run(gate_body, (steps,), [("second", rowb(width))], [("gate", rowb(FF))])

    catch_up("up")
    keep("up").start()
    serve_up = spread(steps, 1)

    def up_body(second_ref, gate_ref, up_ref, hidden_ref):
        up = mm(second_ref[...], whole("up"))
        up_ref[...] = up
        gate = gate_ref[...]
        hidden_ref[...] = (gate * jax.nn.sigmoid(gate) * up).astype(bf16)
        serve_up(pl.program_id(0))

    run(up_body, (steps,), [("second", rowb(width)), ("gate", rowb(FF))], [("up", rowb(FF)), ("hidden", rowb(FF))])
    catch_up("down")

    for c in CHUNKS[:-1]:
        keep(c).wait()
    keep_gain.wait()
    for c in CHUNKS:
        for d in range(line):
            for side in sides(d):

                def finish():
                    core_copy(c, side, d).wait_send()
                    x_copy(c, side, d).wait_send()
                    y_copy(c, side, d).wait_send()

                guard(exists(side, d), finish)
                if d > 0:
                    had = z - (d - 1) >= 0 if side < 0 else z + (d - 1) < line
                    pl.when(had & onward(side))(lambda: line_copy(c, side, d).wait_send())


def forward(lengths, table, ids, arrays, shards, gain_shard, n):
    line = n // 2
    width = arrays["x"].shape[1]
    packed = H * HD + 2 * KVH * HD
    outs = {"full_" + c: ((n, *shards[c].shape), bf16) for c in CHUNKS}
    outs |= {
        "gain": ((8, width), f32), "dy": ((LEN, width), bf16), "c": ((LEN, 128), f32), "first": ((LEN, width), bf16),
        "packed": ((LEN, packed), bf16), "mixed": ((LEN, H * HD), bf16), "lse": ((H, LEN), f32),
        "middle": ((LEN, width), f32), "second": ((LEN, width), bf16), "gate": ((LEN, FF), f32), "up": ((LEN, FF), f32),
        "hidden": ((LEN, FF), bf16),
    }
    dma = pltpu.SemaphoreType.DMA
    count, items = len(CHUNKS), n - 1
    scratch = {"v_" + c: pltpu.VMEM((n, *shards[c].shape), bf16) for c in CHUNKS[:-1]}
    scratch |= {
        "v_gain": pltpu.VMEM((n, *gain_shard.shape), bf16), "gain_rows": pltpu.VMEM((8, width), f32),
        "f_send": dma((4, count, items)), "f_recv": dma((4, count, items)), "keep_sem": dma((count,)),
        "own_sem": dma((count,)), "g_send": dma((n,)), "g_recv": dma((n,)),
    }
    inputs = dict(arrays) | {"low_" + c: shards[c] for c in CHUNKS} | {"low_gain": gain_shard}
    names = ["lengths", "table", "ids", *inputs, *outs, *scratch]
    anywhere = pl.BlockSpec(memory_space=pl.ANY)
    smem = pl.BlockSpec(memory_space=pltpu.SMEM)
    got = pl.pallas_call(
        functools.partial(forward_kernel, names=names, line=line),
        in_specs=[smem, smem, pl.BlockSpec(memory_space=pltpu.VMEM)] + [anywhere] * len(inputs),
        out_specs=[anywhere] * len(outs),
        out_shape=[jax.ShapeDtypeStruct(*v) for v in outs.values()],
        scratch_shapes=list(scratch.values()),
        compiler_params=pltpu.CompilerParams(collective_id=0, has_side_effects=True, vmem_limit_bytes=62 << 20),
        cost_estimate=pl.CostEstimate(flops=60 << 30, bytes_accessed=200 << 20, transcendentals=0),
        name="forward",
    )(lengths, table, ids, *inputs.values())
    return dict(zip(outs, got))


HALF = 1024
PIECES = {
    "down_y": ("y", "out", 1, HALF, HALF, "hidden", [("dy", 1, HALF)]),
    "down_z": ("z", "out", 1, 0, HALF, "hidden", [("dy", 0, HALF)]),
    "gate": ("y", "in", 0, H * HD + 2 * KVH * HD, FF, "second", [("dboth", 0, FF)]),
    "up": ("y", "in", 0, H * HD + 2 * KVH * HD + FF, FF, "second", [("dboth", 1, FF)]),
    "proj_z": ("z", "out", 0, 0, HALF, "mixed", [("dlow", 0, HALF)]),
    "proj_y": ("y", "out", 0, HALF, HALF, "mixed", [("dlow", 1, HALF)]),
    "q": ("y", "in", 0, 0, H * HD, "first", [("dq", 0, H * HD)]),
    "kv": ("y", "in", 0, H * HD, 2 * KVH * HD, "first", [("dk", 0, KVH * HD), ("dv", 0, KVH * HD)]),
}
REGIONS = {
    "down": ("out", ("down_z", "down_y"), 1, 0, 2 * HALF),
    "ffn": ("in", ("gate", "up"), 0, H * HD + 2 * KVH * HD, 2 * FF),
    "proj": ("out", ("proj_z", "proj_y"), 0, 0, 2 * HALF),
}


def back_kernel(*refs, names, line, rep, rates):
    R = dict(zip(names, refs))
    r, f = lax.axis_index("rep"), lax.axis_index("fsdp")
    z, y = f // 2, f % 2
    n = 2 * line
    other = lambda k: (r + (1 - 2 * (r % 2)) * (k % 2) + 2 * (1 - 2 * (r // 2)) * (k // 2), f)
    barrier = pltpu.get_barrier_semaphore()
    for step in range(1, n):
        pl.semaphore_signal(barrier, inc=1, device_id=(r, lax.rem(f + step, n)), device_id_type=pl.DeviceIdType.MESH)
    for k in range(1, rep):
        pl.semaphore_signal(barrier, inc=1, device_id=other(k), device_id_type=pl.DeviceIdType.MESH)
    pl.semaphore_wait(barrier, n - 1 + rep - 1)

    loads = ("down", "gate_w", "up_w", "proj", "q_w", "kv_w")
    load = lambda k: pltpu.make_async_copy(R[loads[k]], R["v_" + loads[k]], R["load_sem"].at[k])
    for k in range(len(loads)):
        load(k).start()

    def remote(src, dst, send, recv, to):
        return pltpu.make_async_remote_copy(
            src_ref=src, dst_ref=dst, send_sem=send, recv_sem=recv, device_id=(r, to), device_id_type=pl.DeviceIdType.MESH
        )

    def run(body, grid, ins, outs):
        pltpu.emit_pipeline(body, grid=grid, in_specs=[s for _, s in ins], out_specs=[s for _, s in outs])(
            *[a for a, _ in ins], *[a for a, _ in outs]
        )

    order = list(PIECES)
    middle = (z > 0) & (z < line - 1)
    low = z < line // 2
    inner = jnp.where(low, f + 2, f - 2)
    outer = jnp.where(low, f - 2, f + 2)
    to_y = f + 1 - 2 * y
    third = jnp.where(middle, 3, 2)
    far = jnp.where(low, z + 2, z - 2) * 2 + y

    def shard_rows(p):
        rows = R["own_" + PIECES[p][1]].shape[1]
        return rows // 2 if PIECES[p][1] == "out" else rows

    def span(rows, row, col, cols):
        return pl.ds(row * rows, rows), pl.ds(col, cols)

    def area(p):
        _, _, row, col, cols, _, _ = PIECES[p]
        return span(shard_rows(p), row, col, cols)

    def own(p, t):
        return R["own_" + p].at[t] if PIECES[p][0] == "z" else R["own_" + PIECES[p][1]].at[(t, *area(p))]

    def slot(p, k):
        return R["slot_" + p].at[k] if PIECES[p][0] == "z" else R["slot_" + PIECES[p][1]].at[(k, *area(p))]

    def gradient(p, side, out, add=None):
        mode, _, _, _, cols, a, bs = PIECES[p]
        rows = shard_rows(p)
        pick = lambda j: (0, j * 2 + side)
        if mode == "z":
            rows, pick = 2 * rows, lambda j: (0, j)
        block = pl.BlockSpec((1, rows, cols), lambda j: (j, 0, 0))
        ins = [(R[a], pl.BlockSpec((LEN, rows), pick))]
        for b, at, width in bs:
            ins.append((R[b], pl.BlockSpec((LEN, width), functools.partial(lambda at, j: (0, at), at))))
        if add is not None:
            ins.append((add, block))

        def step(*refs):
            out_ref, a_ref, b_refs = refs[-1], refs[0], refs[1 : 1 + len(bs)]
            col = 0
            for b_ref in b_refs:
                width = b_ref.shape[1]
                g = mm(a_ref[...], b_ref[...], TN)
                if add is not None:
                    g = g + refs[-2][0, :, col : col + width].astype(f32)
                out_ref[0, :, col : col + width] = g.astype(bf16)
                col += width

        run(step, (line,), ins, [(out, block)])

    def pair_copy(p):
        k = order.index(p)
        if PIECES[p][0] == "z":
            dst = R["slot_" + PIECES[p][1]].at[(1, *area(p))]
        else:
            dst = R["came_" + p]
        return remote(R["away_" + p], dst, R["y_send"].at[k], R["y_recv"].at[k], to_y)

    def line_copy(p, k, src, slot_at, to):
        i = order.index(p)
        return remote(src, slot(p, slot_at), R["z_send"].at[i, k], R["z_recv"].at[i, slot_at], to)

    def end_copies(p):
        t = lambda k: jnp.where(low, line - 1 - k, k)
        to = (inner, far, inner)
        return [functools.partial(line_copy, p, k, own(p, t(k)), (0, 1, 3)[k], to[k]) for k in range(3)]

    def middle_copies(p):
        return [
            functools.partial(line_copy, p, 0, R["msg_" + p], 1, far),
            functools.partial(line_copy, p, 1, own(p, 3 - z), 2, inner),
            functools.partial(line_copy, p, 2, own(p, 3 * (z - 1)), 2, outer),
        ]

    def slot_wait(p, at):
        i = order.index(p)
        remote(slot(p, at), slot(p, at), R["z_send"].at[i, 0], R["z_recv"].at[i, at], inner).wait_recv()

    def line_start(p):
        @pl.when(~middle)
        def _():
            for copy in end_copies(p):
                copy().start()

        @pl.when(middle)
        def _():
            for copy in middle_copies(p)[1:]:
                copy().start()

    def send_away(p):
        gradient(p, 1 - y, R["away_" + p])
        pair_copy(p).start()

    def keep(p):
        pair_copy(p).wait_recv()
        gradient(p, y, R["own_" + PIECES[p][1]].at[(pl.ds(0, line), *area(p))], R["came_" + p])
        line_start(p)

    def send_line(p):
        gradient(p, None, R["own_" + p])
        line_start(p)

    def serve(p):
        @pl.when(middle)
        def _():
            slot_wait(p, 0)
            rows, cols = R["msg_" + p].shape
            block = pl.BlockSpec((rows // 2, cols), lambda j: (j, 0))

            def step(a_ref, b_ref, o_ref):
                o_ref[...] = (a_ref[...].astype(f32) + b_ref[...].astype(f32)).astype(bf16)

            run(step, (2,), [(own(p, 3 * (2 - z)), block), (slot(p, 0), block)], [(R["msg_" + p], block)])
            middle_copies(p)[0]().start()

    def line_end(p):
        slot_wait(p, 1)
        slot_wait(p, 2)
        pl.when(middle)(lambda: slot_wait(p, 3))

    def total(refs):
        a, b, c, d = (ref[...].astype(f32) for ref in refs)
        return a + b + c + jnp.where(middle, d, 0.0)

    def close(p):
        line_end(p)
        rows, cols = shard_rows(p), PIECES[p][4]

        def send_step(*refs):
            refs[-1][...] = total(refs[:4]).astype(bf16)

        def stay_step(*refs):
            refs[4][...] = total(refs[:4]).astype(bf16)
            for ref in refs[5:]:
                ref[...] = jnp.zeros_like(ref)

        piece = pl.BlockSpec((rows // 2, cols), lambda j: (j, 0))
        terms = (own(p, z), slot(p, 1), slot(p, 2), slot(p, third))
        ins = lambda side: [(ref, pl.BlockSpec((rows // 2, cols), lambda j: (side * 2 + j, 0))) for ref in terms]
        run(send_step, (2,), ins(1 - y), [(R["away_" + p], piece)])
        pair_copy(p).start()
        kind = PIECES[p][1]
        outs = [R["own_" + kind].at[(z, *area(p))]] + [R["slot_" + kind].at[(k, *area(p))] for k in (2, 3)]
        run(stay_step, (2,), ins(y), [(ref, piece) for ref in outs])

    def delta_copy(name, k):
        kind, pieces, row, col, cols = REGIONS[name]
        i = list(REGIONS).index(name)
        spot = lambda at: R["delta_" + kind].at[(at, *span(shard_rows(pieces[0]), row, col, cols))]
        return pltpu.make_async_remote_copy(
            src_ref=spot(2 if k == 3 else 0), dst_ref=spot(k), send_sem=R["d_send"].at[i, k - 1], recv_sem=R["d_recv"].at[i, k - 1],
            device_id=other(1 if k == 3 else k), device_id_type=pl.DeviceIdType.MESH,
        )

    def delta(name):
        kind, pieces, row, col, cols = REGIONS[name]
        for p in pieces:
            if PIECES[p][0] == "z":
                pair_copy(p).wait_recv()
            else:
                line_end(p)
        rows = shard_rows(pieces[0])
        where = span(rows, row, col, cols)
        block = pl.BlockSpec((rows, 256), lambda j: (0, j))
        terms = [R["own_" + kind].at[(z, *where)]] + [R["slot_" + kind].at[(k, *where)] for k in (1, 2, third)]
        state = [R[k + "_" + kind].at[where] for k in ("first", "second", "w")]

        def step(*refs):
            first_ref, second_ref, w_ref, o_ref = refs[4:]
            o_ref[...] = adam_step(total(refs[:4]), first_ref[...], second_ref[...], w_ref[...], rates[kind])[2].astype(bf16)

        run(step, (cols // 256,), [(ref, block) for ref in terms + state], [(R["delta_" + kind].at[(0, *where)], block)])
        for k in (1, 2):
            delta_copy(name, k).start()

    def relay(name):
        delta_copy(name, 2).wait_recv()
        delta_copy(name, 3).start()

    rowb = lambda width: pl.BlockSpec((BQ, width), lambda i: (i, 0))
    width = R["x"].shape[1]
    R["gain_acc"][...] = jnp.zeros_like(R["gain_acc"])
    gain_rows = R["gain"][...]

    def mid_step(middle_ref, hidden_ref, dboth_ref, t_ref, c_ref, act_ref, dmid_ref, dlow_ref, dmix_ref):
        mid_v = middle_ref[...]
        act_ref[...] = (mid_v + mm(hidden_ref[...], R["v_down"][...])).astype(bf16)
        inv = lax.rsqrt(jnp.mean(mid_v * mid_v, axis=-1, keepdims=True) + norm_eps)
        n2 = mid_v * inv
        ds2 = mm(dboth_ref[:, :FF], R["v_gate_w"][...], NT) + mm(dboth_ref[:, FF:], R["v_up_w"][...], NT)
        prod = ds2 * n2
        R["gain_acc"][8:16, :] += jnp.sum(prod.reshape(BQ // 8, 8, width), axis=0)
        g = gain_rows[1:2, :]
        dy = c_ref[:, 0:1] * t_ref[...].astype(f32)
        dmid = dy + inv * (ds2 * g - n2 * jnp.mean(prod * g, axis=-1, keepdims=True))
        dmid_ref[...] = dmid
        dlow = dmid.astype(bf16)
        dlow_ref[...] = dlow
        dmix_ref[...] = mm(dlow, R["v_proj"][...], NT).astype(bf16)

    def mid_phase(part):
        count = LEN // BQ // 2
        late = lambda width: pl.BlockSpec((BQ, width), lambda i: (i + part * count, 0))
        run(
            mid_step,
            (count,),
            [(R["middle"], late(width)), (R["hidden"], late(FF)), (R["dboth"], late(2 * FF)), (R["target"], late(width)), (R["c"], late(128))],
            [(R["act"], late(width)), (R["dmid"], late(width)), (R["dlow"], late(width)), (R["dmix"], late(H * HD))],
        )

    qw = H // 2 * HD
    kcol = H * HD // 128
    vcol = kcol + KVH * HD // 128

    def attention_phase(p):
        qspec = pl.BlockSpec((BQ, qw), lambda i: (i, p))
        whole = lambda at: pl.BlockSpec((LEN, 128), lambda i: (0, at))
        R["dk_acc"][...] = jnp.zeros_like(R["dk_acc"])
        R["dv_acc"][...] = jnp.zeros_like(R["dv_acc"])

        def step(q_ref, k_ref, v_ref, d_ref, o_ref, lse_ref, dq_ref):
            attention_back_step(R["lengths"], pl.program_id(0), q_ref, k_ref, v_ref, d_ref, o_ref, lse_ref, dq_ref, R["dk_acc"], R["dv_acc"])

        pltpu.emit_pipeline(
            step, grid=(LEN // BQ,),
            in_specs=[qspec, whole(kcol + p), whole(vcol + p), qspec, qspec, pl.BlockSpec((8, BQ), lambda i: (p, i))],
            out_specs=[qspec],
        )(R["packed"], R["packed"], R["packed"], R["dmix"], R["mixed"], R["lse"], R["dq"])

        def flush(dk_ref, dv_ref):
            dk_ref[...] = R["dk_acc"][...].astype(bf16)
            dv_ref[...] = R["dv_acc"][...].astype(bf16)

        run(flush, (1,), [], [(R["dk"], pl.BlockSpec((LEN, 128), lambda i: (0, p))), (R["dv"], pl.BlockSpec((LEN, 128), lambda i: (0, p)))])

    def input_step(x_ref, dmid_ref, dq_ref, dk_ref, dv_ref, out_ref):
        x = x_ref[...].astype(f32)
        inv = lax.rsqrt(jnp.mean(x * x, axis=-1, keepdims=True) + norm_eps)
        n1 = x * inv
        kv_w, split = R["v_kv_w"], KVH * HD
        ds1 = mm(dq_ref[...], R["v_q_w"][...], NT) + mm(dk_ref[...], kv_w[:, :split], NT) + mm(dv_ref[...], kv_w[:, split:], NT)
        prod = ds1 * n1
        R["gain_acc"][0:8, :] += jnp.sum(prod.reshape(BQ // 8, 8, width), axis=0)
        g = gain_rows[0:1, :]
        out_ref[...] = (dmid_ref[...] + inv * (ds1 * g - n1 * jnp.mean(prod * g, axis=-1, keepdims=True))).astype(bf16)

    def input_phase():
        run(
            input_step,
            (LEN // BQ,),
            [(R["x"], rowb(width)), (R["dmid"], rowb(width)), (R["dq"], rowb(H * HD)), (R["dk"], rowb(KVH * HD)), (R["dv"], rowb(KVH * HD))],
            [(R["xgrad"], rowb(width))],
        )

    part = width // n

    def gain_copy(step, receive=False):
        peer = lax.rem(f + step, n)
        home = lax.rem(f + n - step, n) if receive else f
        return remote(
            R["gain_acc"].at[:, pl.ds(pl.multiple_of(peer * part, part), part)], R["gain_got"].at[home],
            R["g_send"].at[step - 1], R["g_recv"].at[step - 1], peer,
        )

    own_gain = pltpu.make_async_copy(
        R["gain_acc"].at[:, pl.ds(pl.multiple_of(f * part, part), part)], R["gain_got"].at[f], R["g_send"].at[n - 1]
    )

    def dboth_step(dy_ref, gate_ref, up_ref, dboth_ref):
        dh = mm(dy_ref[...], R["v_down"][...], NT)
        gate = gate_ref[...]
        sig = jax.nn.sigmoid(gate)
        dboth_ref[:, :FF] = (dh * up_ref[...] * sig * (1.0 + gate * (1.0 - sig))).astype(bf16)
        dboth_ref[:, FF:] = (dh * (gate * sig)).astype(bf16)

    send_away("down_y")
    send_line("down_z")
    load(0).wait()
    run(
        dboth_step,
        (LEN // BQ,),
        [(R["dy"], rowb(width)), (R["gate"], rowb(FF)), (R["up"], rowb(FF))],
        [(R["dboth"], rowb(2 * FF))],
    )
    send_away("gate")
    for k in range(1, 4):
        load(k).wait()
    mid_phase(0)
    keep("down_y")
    serve("down_z")
    mid_phase(1)
    send_line("proj_z")
    serve("down_y")
    send_away("up")
    serve("proj_z")
    send_away("proj_y")
    attention_phase(0)
    keep("gate")
    serve("gate")
    attention_phase(1)
    send_away("q")
    keep("up")
    close("down_z")
    serve("up")
    load(4).wait()
    load(5).wait()
    input_phase()
    for step in range(1, n):
        gain_copy(step).start()
    own_gain.start()
    keep("proj_y")
    send_away("kv")
    delta("ffn")
    serve("proj_y")
    keep("q")
    delta("down")
    close("proj_z")
    serve("q")
    delta("proj")
    relay("ffn")
    relay("down")
    keep("kv")
    serve("kv")
    relay("proj")

    for step in range(1, n):
        gain_copy(step, True).wait_recv()
        gain_copy(step).wait_send()
    own_gain.wait()
    for name in REGIONS:
        for k in (1, 3):
            delta_copy(name, k).wait()
        delta_copy(name, 2).wait_send()
    line_end("q")
    line_end("kv")
    for p in order:
        pair_copy(p).wait_send()

        @pl.when(middle)
        def _():
            for copy in middle_copies(p):
                copy().wait_send()

        @pl.when(~middle)
        def _():
            for copy in end_copies(p):
                copy().wait_send()


def backward(lengths, gain, arrays, n, rep, rates):
    line = n // 2
    width = arrays["x"].shape[1]
    kvw = KVH * HD
    outs = {
        "act": ((LEN, width), bf16), "dboth": ((LEN, 2 * FF), bf16), "dmid": ((LEN, width), f32), "dlow": ((LEN, width), bf16),
        "dmix": ((LEN, H * HD), bf16), "dq": ((LEN, H * HD), bf16), "dk": ((LEN, kvw), bf16), "dv": ((LEN, kvw), bf16),
        "xgrad": ((LEN, width), bf16), "gain_got": ((n, 16, width // n), f32),
    }
    for kind in ("in", "out"):
        for name, count in (("own_", line), ("slot_", 4), ("delta_", rep)):
            outs[name + kind] = ((count, *arrays["w_" + kind].shape), bf16)
    for p, (mode, kind, _, _, cols, _, _) in PIECES.items():
        rows = arrays["w_" + kind].shape[0] // (2 if kind == "out" else 1)
        if mode == "y":
            counts = (("away_", (line, rows)), ("came_", (line, rows)), ("msg_", (rows,)))
        else:
            counts = (("away_", (rows,)), ("own_", (line, 2 * rows)), ("slot_", (4, 2 * rows)), ("msg_", (2 * rows,)))
        for name, lead in counts:
            outs[name + p] = ((*lead, cols), bf16)
    dma = pltpu.SemaphoreType.DMA
    pieces = len(PIECES)
    scratch = {
        **{"v_" + k: pltpu.VMEM(arrays[k].shape, bf16) for k in ("down", "gate_w", "up_w", "proj", "q_w", "kv_w")},
        "gain_acc": pltpu.VMEM((16, width), f32), "dk_acc": pltpu.VMEM((LEN, 128), f32), "dv_acc": pltpu.VMEM((LEN, 128), f32),
        "load_sem": dma((6,)), "y_send": dma((pieces,)), "y_recv": dma((pieces,)),
        "z_send": dma((pieces, 3)), "z_recv": dma((pieces, 4)),
        "d_send": dma((len(REGIONS), rep - 1)), "d_recv": dma((len(REGIONS), rep - 1)), "g_send": dma((n,)), "g_recv": dma((n,)),
    }
    names = ["lengths", "gain", *arrays, *outs, *scratch]
    anywhere = pl.BlockSpec(memory_space=pl.ANY)
    got = pl.pallas_call(
        functools.partial(back_kernel, names=names, line=line, rep=rep, rates=rates),
        in_specs=[pl.BlockSpec(memory_space=pltpu.SMEM), pl.BlockSpec(memory_space=pltpu.VMEM)] + [anywhere] * len(arrays),
        out_specs=[anywhere] * len(outs),
        out_shape=[jax.ShapeDtypeStruct(*v) for v in outs.values()],
        scratch_shapes=list(scratch.values()),
        compiler_params=pltpu.CompilerParams(collective_id=1, has_side_effects=True, vmem_limit_bytes=62 << 20),
        cost_estimate=pl.CostEstimate(flops=200 << 30, bytes_accessed=400 << 20, transcendentals=0),
        name="backward",
    )(lengths, gain, *arrays.values())
    return dict(zip(outs, got))


rate_in = 0.02
rate_out = 0.08
rate_gains = 1.2


def body(
    tokens,
    target,
    doc_lengths,
    corpus_ids,
    corpus_weights,
    w_in,
    w_out,
    gains,
    first_in,
    first_out,
    first_gains,
    second_in,
    second_out,
    second_gains,
    outer_in,
    outer_out,
    outer_gains,
):
    n, rep = lax.axis_size("fsdp"), lax.axis_size("rep")
    line = n // 2
    f, r = lax.axis_index("fsdp"), lax.axis_index("rep")
    z, y = f // 2, f % 2
    direct = by_neighbours(n, rep)
    inside = (z > 0) & (z < line - 1)
    place = jnp.stack([z, inside]).astype(jnp.int32)
    width = w_out.shape[2]
    flat = lambda a: a.reshape(-1, a.shape[-1])
    state_in = first_in[0], second_in[0], w_in
    state_out = flat(first_out[0]), flat(second_out[0]), flat(w_out)
    moved_out = flat(outer_out)
    rates = {"in": rate_in, "out": rate_out}
    rows_in, rows_out = w_in.shape[0], w_out.shape[1]
    x, tgt, lengths = tokens[0], target[0], doc_lengths[0]
    ids = corpus_ids[0][:, None]

    if direct:
        qw, attn = H * HD, H * HD + 2 * KVH * HD
        low_in, low_out = w_in.astype(bf16), w_out.astype(bf16)
        shards = dict(
            q=low_in[:, :qw], kv=low_in[:, qw:attn], gate=low_in[:, attn : attn + FF], up=low_in[:, attn + FF :],
            proj=low_out[0], down=low_out[1],
        )
        low_gain = jnp.pad(gains.astype(bf16), ((0, 14), (0, 0)))
        fwd = forward(lengths, corpus_weights, ids, dict(x=x, target=tgt), shards, low_gain, n)
        weight = lambda c: fwd["full_" + c].reshape(-1, shards[c].shape[1])
        kept = {k: fwd[k] for k in ("c", "middle", "hidden", "second", "gate", "up", "dy", "mixed", "packed", "lse", "first")}
        got = backward(
            lengths, fwd["gain"],
            dict(x=x, target=tgt, proj=weight("proj"), down=weight("down"), q_w=weight("q"), kv_w=weight("kv"),
                 gate_w=weight("gate"), up_w=weight("up"), first_in=state_in[0], second_in=state_in[1], w_in=w_in,
                 first_out=state_out[0], second_out=state_out[1], w_out=state_out[2], **kept),
            n, rep, rates,
        )
        activations, input_grad = got["act"], got["xgrad"]
        gain_share = jnp.sum(got["gain_got"].reshape(n, 2, 8, -1), axis=(0, 2))
        late = (H * HD + 2 * KVH * HD) // TILE
        *held, late_delta = adam_tiles(
            place, got["own_in"], got["slot_in"], *state_in, None, None, None, 0, (0, late, late, 0), rate_in, rep
        )
        late_terms = groups_terms(late_delta, rep)
        rest = w_in.shape[1] // TILE - late
        in_got = adam_tiles(
            place, got["own_in"], got["slot_in"], *state_in, outer_in, got["delta_in"], held,
            0, (late, rest, rest, 0), rate_in, rep,
        )
        out_count = width // TILE
        out_got = adam_tiles(
            place, got["own_out"], got["slot_out"], *state_out, moved_out, got["delta_out"], None,
            0, (0, out_count, out_count, 0), rate_out, rep,
        )
        in_grads, in_steps = in_got[:3], outer_tiles(late_terms, outer_in, w_in, in_got[3:], 0, rep)
        out_grads, out_steps = out_got[:3], out_got[3:]
    else:
        gain_full, wq, proj, wf, down = all_weights(w_in, w_out, gains)
        first_low, packed = qkv(x, gain_full, wq)
        mixed, lse = attention(lengths, packed)
        middle, second_low, hidden, d_both, dy, _ = ffn(corpus_weights, x, mixed, tgt, ids, gain_full, proj, wf, down)

        def by_library(a, bs, name):
            block = 2 * BQ if a.shape[1] % (2 * BQ) == 0 else BQ
            every_row = jnp.arange(a.shape[1] // block, dtype=jnp.int32)
            total = grad_rows(every_row, a, bs, block, name=name)
            return lax.psum_scatter(total.reshape(a.shape[1], -1), "fsdp", scatter_dimension=0, tiled=True)[None]

        activations, d_mid, d_low, d_mix, gain_two = mid(
            corpus_weights, middle, hidden, d_both, tgt, ids, gain_full, proj, wf, down
        )
        dq, dk, dv = attention_back(lengths, packed, d_mix, mixed, lse)
        input_grad, gain_one = input_back(x, d_mid, dq, dk, dv, gain_full, wq)
        both = jnp.stack([jnp.sum(gain_one, axis=0), jnp.sum(gain_two, axis=0)])
        gain_share = lax.psum_scatter(both, "fsdp", scatter_dimension=1, tiled=True)
        own_in = jnp.concatenate(
            [
                by_library(first_low, [(dq, 0, H * HD), (dk, 0, KVH * HD), (dv, 0, KVH * HD)], "grad_attn"),
                by_library(second_low, [(d_both, 0, 2 * FF)], "grad_ffn"),
            ],
            axis=2,
        )
        own_out = jnp.concatenate(
            [by_library(mixed, [(d_low, 0, width)], "grad_proj"), by_library(hidden, [(dy, 0, width)], "grad_down")], axis=1
        )

        def all_tiles(own, state, outer, rate):
            count = own.shape[2] // TILE
            *grads, delta = adam_tiles(0 * place, own, None, *state, None, None, None, 0, (0, count, count, 0), rate, rep)
            return grads, outer_tiles(groups_terms(delta, rep), outer, state[2], None, 0, rep)

        in_grads, in_steps = all_tiles(own_in, state_in, outer_in, rate_in)
        out_grads, out_steps = all_tiles(own_out, state_out, moved_out, rate_out)

    first_gains_new, second_gains_new, delta = adam_step(gain_share, first_gains[0], second_gains[0], gains, rate_gains)
    terms = groups_terms(delta, rep)
    sum_gains = (terms[0] + terms[1]) + (terms[2] + terms[3]) if rep == 4 else sum(terms[1:], terms[0])
    diff_gains, outer_gains_new, new_gains = outer_step(sum_gains, outer_gains, gains, rep)

    out_shape = lambda a: a.reshape(2, rows_out, width)
    diff_in, outer_in_new, new_in, copy_in = in_steps
    diff_out, outer_out_new, new_out, copy_out = (out_shape(a) for a in out_steps)
    grad_in, first_in_new, second_in_new = in_grads
    grad_out, first_out_new, second_out_new = (out_shape(a) for a in out_grads)
    return (
        activations[None],
        input_grad[None],
        grad_in[None],
        grad_out[None],
        gain_share[None],
        first_in_new[None],
        first_out_new[None],
        first_gains_new[None],
        second_in_new[None],
        second_out_new[None],
        second_gains_new[None],
        diff_in,
        diff_out,
        diff_gains,
        outer_in_new,
        outer_out_new,
        outer_gains_new,
        new_in,
        new_out,
        new_gains,
        copy_in,
        copy_out,
        new_gains.astype(bf16),
    )


def solution(mesh):
    rows = P(("rep", "fsdp"), None, None)
    pair = P(("rep", "fsdp"), None)
    w_in, w_out, gains = P("fsdp", None), P(None, "fsdp", None), P(None, "fsdp")
    m_in, m_out, m_gains = P("rep", "fsdp", None), P("rep", None, "fsdp", None), P("rep", None, "fsdp")
    weights, moments = (w_in, w_out, gains), (m_in, m_out, m_gains)
    return jax.shard_map(
        body,
        mesh=mesh,
        in_specs=(rows, rows, pair, pair, P(), *weights, *moments, *moments, *weights),
        out_specs=(rows, rows, *moments, *moments, *moments, *weights, *weights, *weights, *weights),
        check_vma=False,
    )
```

```python
import functools
import jax
import jax.numpy as jnp
from jax import lax
from jax.experimental import pallas as pl
from jax.experimental.pallas import tpu as pltpu
from jax.sharding import PartitionSpec as P

H = 16
HD = 64
KVH = 4
FF = 1024
LEN = 1024
NCORP = 8
f32 = jnp.float32
bf16 = jnp.bfloat16
norm_eps = 1e-06
BQ = 256
NT = (((1,), (1,)), ((), ()))
TN = (((0,), (0,)), ((), ()))


def mm(a, b, dims=(((1,), (0,)), ((), ()))):
    return lax.dot_general(a, b, dims, preferred_element_type=f32)


def params(**kw):
    return pltpu.CompilerParams(vmem_limit_bytes=60 << 20, **kw)


def one(shape, index):
    return pl.BlockSpec(shape, index, pipeline_mode=pl.Buffered(1))


def qkv_kernel(x_ref, g_ref, w_ref, first_ref, packed_ref):
    x = x_ref[...].astype(f32)
    r = lax.rsqrt(jnp.mean(x * x, axis=-1, keepdims=True) + norm_eps)
    first = (x * r * g_ref[0:1, :]).astype(bf16)
    first_ref[...] = first
    packed_ref[...] = mm(first, w_ref[...]).astype(bf16)


def qkv(x, gains, w):
    rows, width = x.shape
    cols = w.shape[1]
    return pl.pallas_call(
        qkv_kernel,
        grid=(rows // BQ,),
        in_specs=[
            pl.BlockSpec((BQ, width), lambda i: (i, 0)),
            one(gains.shape, lambda i: (0, 0)),
            one((width, cols), lambda i: (0, 0)),
        ],
        out_specs=[
            pl.BlockSpec((BQ, width), lambda i: (i, 0)),
            pl.BlockSpec((BQ, cols), lambda i: (i, 0)),
        ],
        out_shape=[
            jax.ShapeDtypeStruct((rows, width), bf16),
            jax.ShapeDtypeStruct((rows, cols), bf16),
        ],
        compiler_params=params(),
        cost_estimate=pl.CostEstimate(
            flops=2 * rows * width * cols, bytes_accessed=rows * width * 4 + width * cols * 2, transcendentals=0
        ),
        name="norm_qkv",
    )(x, gains, w)


def doc_start(lengths_ref, position):
    end = jnp.int32(0)
    start = jnp.zeros_like(position)
    for j in range(lengths_ref.shape[0]):
        end = end + lengths_ref[j]
        start = jnp.where(position >= end, end, start)
    return start


def key_blocks(lengths_ref, i):
    first_row = i * BQ
    return i + 1 - doc_start(lengths_ref, first_row) // BQ


def max_blocks():
    return LEN // (2 * BQ) + 1


def attention_step(len_ref, i, count, q_ref, k_ref, v_ref, o_ref, lse_ref):
    row = i * BQ + lax.broadcasted_iota(jnp.int32, (BQ, 1), 0)
    start = doc_start(len_ref, row)
    lane = lax.broadcasted_iota(jnp.int32, (BQ, 128), 1)
    for nb in range(1, max_blocks() + 1):

        @pl.when(count == nb)
        def _():
            span = nb * BQ
            base = pl.multiple_of((i - (nb - 1)) * BQ, BQ)
            col = base + lax.broadcasted_iota(jnp.int32, (BQ, span), 1)
            bias = jnp.where((col >= start) & (col <= row), 0.0, -1e30)
            k2 = k_ref[pl.ds(base, span), :]
            v2 = v_ref[pl.ds(base, span), :]
            tile = jnp.zeros((BQ, 128), f32)
            outs = []
            for kv in range(2):
                k = k2[:, kv * HD : (kv + 1) * HD]
                v = v2[:, kv * HD : (kv + 1) * HD]
                for g in range(H // KVH):
                    h = kv * (H // KVH) + g
                    q = q_ref[:, h * HD : (h + 1) * HD] * jnp.asarray(HD**-0.5, bf16)
                    s = mm(q, k, NT) + bias
                    m = jnp.max(s, axis=-1, keepdims=True)
                    e = jnp.exp(s - m)
                    total = jnp.sum(e, axis=-1, keepdims=True)
                    o = mm(e.astype(bf16), v) * (1.0 / total)
                    outs.append(o.astype(bf16))
                    tile = jnp.where(lane == h, m + jnp.log(total), tile)
            o_ref[...] = jnp.concatenate(outs, axis=1)
            lse_ref[...] = tile.T[0:8, :]


def attn_kernel(len_ref, *refs):
    i = pl.program_id(0)
    attention_step(len_ref, i, key_blocks(len_ref, i), *refs)


def attention(lengths, packed):
    qw = H // 2 * HD
    kcol = H * HD // 128
    vcol = kcol + KVH * HD // 128
    return pl.pallas_call(
        attn_kernel,
        grid_spec=pltpu.PrefetchScalarGridSpec(
            num_scalar_prefetch=1,
            grid=(LEN // BQ, 2),
            in_specs=[
                pl.BlockSpec((BQ, qw), lambda i, p, s: (i, p)),
                pl.BlockSpec((LEN, 128), lambda i, p, s: (0, kcol + p)),
                pl.BlockSpec((LEN, 128), lambda i, p, s: (0, vcol + p)),
            ],
            out_specs=[
                pl.BlockSpec((BQ, qw), lambda i, p, s: (i, p)),
                pl.BlockSpec((8, BQ), lambda i, p, s: (p, i)),
            ],
        ),
        out_shape=[
            jax.ShapeDtypeStruct((LEN, H * HD), bf16),
            jax.ShapeDtypeStruct((H, LEN), f32),
        ],
        compiler_params=params(),
        cost_estimate=pl.CostEstimate(flops=4 * H * LEN * LEN * HD * 4, bytes_accessed=1 << 24, transcendentals=0),
        name="attention",
    )(lengths, packed, packed, packed)


def attention_back_step(len_ref, i, q_ref, k_ref, v_ref, d_ref, o_ref, lse_ref, dq_ref, dk_acc, dv_acc, count=None):
    if count is None:
        count = jnp.minimum(i + 1, max_blocks())
    row = i * BQ + lax.broadcasted_iota(jnp.int32, (1, BQ), 1)
    start = doc_start(len_ref, row)
    lane = lax.broadcasted_iota(jnp.int32, (BQ, 128), 1)
    group = H // KVH
    scale = jnp.asarray(HD**-0.5, bf16)
    tile = jnp.zeros((BQ, 128), f32)
    for h in range(2 * group):
        cols = slice(h * HD, (h + 1) * HD)
        dot = jnp.sum(d_ref[:, cols].astype(f32) * o_ref[:, cols].astype(f32), axis=-1, keepdims=True)
        tile = jnp.where(lane == h, dot, tile)
    inner = tile.T
    for nb in range(1, max_blocks() + 1):

        @pl.when(count == nb)
        def _():
            span = nb * BQ
            base = pl.multiple_of((i - (nb - 1)) * BQ, BQ)
            key = base + lax.broadcasted_iota(jnp.int32, (span, BQ), 0)
            bias = jnp.where((key >= start) & (key <= row), 0.0, -1e30)
            k2 = k_ref[pl.ds(base, span), :]
            v2 = v_ref[pl.ds(base, span), :]
            dks, dvs = [], []
            for kv in range(2):
                k = k2[:, kv * HD : (kv + 1) * HD]
                v = v2[:, kv * HD : (kv + 1) * HD]
                dk = dv = None
                dqs = []
                for g in range(group):
                    h = kv * group + g
                    cols = slice(h * HD, (h + 1) * HD)
                    q = q_ref[:, cols] * scale
                    d = d_ref[:, cols]
                    s = mm(k, q, NT) + bias
                    p = jnp.exp(s - lse_ref[h : h + 1, :])
                    dp = mm(v, d, NT)
                    ds = (p * (dp - inner[h : h + 1, :])).astype(bf16)
                    dv_h = mm(p.astype(bf16), d)
                    dk_h = mm(ds, q)
                    dv = dv_h if dv is None else dv + dv_h
                    dk = dk_h if dk is None else dk + dk_h
                    dqs.append(mm(k, ds, TN))
                dq = jnp.concatenate(dqs, axis=0) * (HD**-0.5)
                dq_ref[:, kv * group * HD : (kv + 1) * group * HD] = dq.T.astype(bf16)
                dks.append(dk)
                dvs.append(dv)
            dk_acc[pl.ds(base, span), :] += jnp.concatenate(dks, axis=1)
            dv_acc[pl.ds(base, span), :] += jnp.concatenate(dvs, axis=1)


def attn_back_kernel(len_ref, q_ref, k_ref, v_ref, d_ref, o_ref, lse_ref, dq_ref, dk_ref, dv_ref, dk_acc, dv_acc):
    i = pl.program_id(1)

    @pl.when(i == 0)
    def _():
        dk_acc[...] = jnp.zeros_like(dk_acc)
        dv_acc[...] = jnp.zeros_like(dv_acc)

    attention_back_step(
        len_ref, i, q_ref, k_ref, v_ref, d_ref, o_ref, lse_ref, dq_ref, dk_acc, dv_acc, key_blocks(len_ref, i)
    )

    @pl.when(i == pl.num_programs(1) - 1)
    def _():
        dk_ref[...] = dk_acc[...].astype(bf16)
        dv_ref[...] = dv_acc[...].astype(bf16)


def attention_back(lengths, packed, d_mixed, mixed, lse):
    qw = H // 2 * HD
    kcol = H * HD // 128
    vcol = kcol + KVH * HD // 128
    return pl.pallas_call(
        attn_back_kernel,
        grid_spec=pltpu.PrefetchScalarGridSpec(
            num_scalar_prefetch=1,
            grid=(2, LEN // BQ),
            in_specs=[
                pl.BlockSpec((BQ, qw), lambda p, i, s: (i, p)),
                pl.BlockSpec((LEN, 128), lambda p, i, s: (0, kcol + p)),
                pl.BlockSpec((LEN, 128), lambda p, i, s: (0, vcol + p)),
                pl.BlockSpec((BQ, qw), lambda p, i, s: (i, p)),
                pl.BlockSpec((BQ, qw), lambda p, i, s: (i, p)),
                pl.BlockSpec((8, BQ), lambda p, i, s: (p, i)),
            ],
            out_specs=[
                pl.BlockSpec((BQ, qw), lambda p, i, s: (i, p)),
                pl.BlockSpec((LEN, 128), lambda p, i, s: (0, p)),
                pl.BlockSpec((LEN, 128), lambda p, i, s: (0, p)),
            ],
            scratch_shapes=[pltpu.VMEM((LEN, 128), f32), pltpu.VMEM((LEN, 128), f32)],
        ),
        out_shape=[
            jax.ShapeDtypeStruct((LEN, H * HD), bf16),
            jax.ShapeDtypeStruct((LEN, KVH * HD), bf16),
            jax.ShapeDtypeStruct((LEN, KVH * HD), bf16),
        ],
        compiler_params=params(),
        cost_estimate=pl.CostEstimate(flops=10 * H * LEN * LEN * HD * 4, bytes_accessed=1 << 24, transcendentals=0),
        name="attention_back",
    )(lengths, packed, packed, packed, d_mixed, mixed, lse)


def token_weight(table_ref, ids):
    weight = jnp.zeros(ids.shape, f32)
    for j in range(table_ref.shape[0]):
        weight = jnp.where(ids == j, table_ref[j].astype(f32) * 0.25, weight)
    return weight


def ffn_kernel(table_ref, x_ref, mixed_ref, t_ref, ids_ref, g_ref, proj_ref, wf_ref, down_ref,
               middle_ref, second_ref, hidden_ref, dboth_ref, dy_ref, c_ref):
    middle = x_ref[...].astype(f32) + mm(mixed_ref[...], proj_ref[...])
    middle_ref[...] = middle
    r = lax.rsqrt(jnp.mean(middle * middle, axis=-1, keepdims=True) + norm_eps)
    second = (middle * r * g_ref[1:2, :]).astype(bf16)
    second_ref[...] = second
    c = token_weight(table_ref, ids_ref[...])
    c_ref[...] = jnp.broadcast_to(c, c_ref.shape)
    dy = (c * t_ref[...].astype(f32)).astype(bf16)
    dy_ref[...] = dy
    step = 512
    for c in range(0, FF, step):
        gate = mm(second, wf_ref[:, c : c + step])
        up = mm(second, wf_ref[:, FF + c : FF + c + step])
        dh = mm(dy, down_ref[c : c + step, :], NT)
        sig = jax.nn.sigmoid(gate)
        silu = gate * sig
        hidden_ref[:, c : c + step] = (silu * up).astype(bf16)
        dboth_ref[:, c : c + step] = (dh * up * sig * (1.0 + gate * (1.0 - sig))).astype(bf16)
        dboth_ref[:, FF + c : FF + c + step] = (dh * silu).astype(bf16)


def ffn(table, x, mixed, target, ids, gains, proj, wf, down):
    width = x.shape[1]
    rowb = lambda n: pl.BlockSpec((BQ, n), lambda i, s: (i, 0))
    whole = lambda a: one(a.shape, lambda i, s: (0, 0))
    return pl.pallas_call(
        ffn_kernel,
        grid_spec=pltpu.PrefetchScalarGridSpec(
            num_scalar_prefetch=1,
            grid=(LEN // BQ,),
            in_specs=[rowb(width), rowb(H * HD), rowb(width), rowb(1), whole(gains), whole(proj), whole(wf), whole(down)],
            out_specs=[rowb(width), rowb(width), rowb(FF), rowb(2 * FF), rowb(width), rowb(128)],
        ),
        out_shape=[
            jax.ShapeDtypeStruct((LEN, width), f32),
            jax.ShapeDtypeStruct((LEN, width), bf16),
            jax.ShapeDtypeStruct((LEN, FF), bf16),
            jax.ShapeDtypeStruct((LEN, 2 * FF), bf16),
            jax.ShapeDtypeStruct((LEN, width), bf16),
            jax.ShapeDtypeStruct((LEN, 128), f32),
        ],
        compiler_params=params(),
        cost_estimate=pl.CostEstimate(flops=2 * LEN * width * FF * 4, bytes_accessed=40 << 20, transcendentals=0),
        name="ffn",
    )(table, x, mixed, target, ids, gains, proj, wf, down)


def mid_kernel(table_ref, middle_ref, hidden_ref, dboth_ref, t_ref, ids_ref, g_ref, proj_ref, wf_ref, down_ref,
               act_ref, dmid_ref, dlow_ref, dmix_ref, gain_ref):
    middle = middle_ref[...]
    act_ref[...] = (middle + mm(hidden_ref[...], down_ref[...])).astype(bf16)
    r = lax.rsqrt(jnp.mean(middle * middle, axis=-1, keepdims=True) + norm_eps)
    n2 = middle * r
    ds2 = mm(dboth_ref[...], wf_ref[...], NT)
    prod = ds2 * n2
    part = jnp.sum(prod.reshape(BQ // 8, 8, prod.shape[1]), axis=0)

    @pl.when(pl.program_id(0) == 0)
    def _():
        gain_ref[...] = jnp.zeros_like(gain_ref)

    gain_ref[...] += part
    g = g_ref[1:2, :]
    e2 = ds2 * g
    dy = token_weight(table_ref, ids_ref[...]) * t_ref[...].astype(f32)
    dmid = dy + r * (e2 - n2 * jnp.mean(prod * g, axis=-1, keepdims=True))
    dmid_ref[...] = dmid
    low = dmid.astype(bf16)
    dlow_ref[...] = low
    dmix_ref[...] = mm(low, proj_ref[...], NT).astype(bf16)


def mid(table, middle, hidden, dboth, target, ids, gains, proj, wf, down):
    width = middle.shape[1]
    rowb = lambda n: pl.BlockSpec((BQ, n), lambda i, s: (i, 0))
    whole = lambda a: one(a.shape, lambda i, s: (0, 0))
    return pl.pallas_call(
        mid_kernel,
        grid_spec=pltpu.PrefetchScalarGridSpec(
            num_scalar_prefetch=1,
            grid=(LEN // BQ,),
            in_specs=[rowb(width), rowb(FF), rowb(2 * FF), rowb(width), rowb(1), whole(gains), whole(proj), whole(wf), whole(down)],
            out_specs=[rowb(width), rowb(width), rowb(width), rowb(H * HD), pl.BlockSpec((8, width), lambda i, s: (0, 0))],
        ),
        out_shape=[
            jax.ShapeDtypeStruct((LEN, width), bf16),
            jax.ShapeDtypeStruct((LEN, width), f32),
            jax.ShapeDtypeStruct((LEN, width), bf16),
            jax.ShapeDtypeStruct((LEN, H * HD), bf16),
            jax.ShapeDtypeStruct((8, width), f32),
        ],
        compiler_params=params(),
        cost_estimate=pl.CostEstimate(flops=2 * LEN * width * FF * 4, bytes_accessed=40 << 20, transcendentals=0),
        name="mid",
    )(table, middle, hidden, dboth, target, ids, gains, proj, wf, down)


def input_kernel(x_ref, dmid_ref, dq_ref, dk_ref, dv_ref, g_ref, w_ref, out_ref, gain_ref):
    x = x_ref[...].astype(f32)
    r = lax.rsqrt(jnp.mean(x * x, axis=-1, keepdims=True) + norm_eps)
    n1 = x * r
    q, k = H * HD, H * HD + KVH * HD
    ds1 = mm(dq_ref[...], w_ref[:, :q], NT) + mm(dk_ref[...], w_ref[:, q:k], NT) + mm(dv_ref[...], w_ref[:, k:], NT)
    prod = ds1 * n1
    part = jnp.sum(prod.reshape(BQ // 8, 8, prod.shape[1]), axis=0)

    @pl.when(pl.program_id(0) == 0)
    def _():
        gain_ref[...] = jnp.zeros_like(gain_ref)

    gain_ref[...] += part
    g = g_ref[0:1, :]
    out = dmid_ref[...] + r * (ds1 * g - n1 * jnp.mean(prod * g, axis=-1, keepdims=True))
    out_ref[...] = out.astype(bf16)


def input_back(x, dmid, dq, dk, dv, gains, w):
    width = x.shape[1]
    rowb = lambda n: pl.BlockSpec((BQ, n), lambda i: (i, 0))
    whole = lambda a: one(a.shape, lambda i: (0, 0))
    return pl.pallas_call(
        input_kernel,
        grid=(LEN // BQ,),
        in_specs=[rowb(width), rowb(width), rowb(H * HD), rowb(KVH * HD), rowb(KVH * HD), whole(gains), whole(w)],
        out_specs=[rowb(width), pl.BlockSpec((8, width), lambda i: (0, 0))],
        out_shape=[jax.ShapeDtypeStruct((LEN, width), bf16), jax.ShapeDtypeStruct((8, width), f32)],
        compiler_params=params(),
        cost_estimate=pl.CostEstimate(flops=2 * LEN * width * 1536, bytes_accessed=24 << 20, transcendentals=0),
        name="input_back",
    )(x, dmid, dq, dk, dv, gains, w)


def grad_kernel(pick_ref, a_ref, *refs):
    out_ref = refs[-1]
    b_refs = refs[:-1]
    add_ref = None
    if len(b_refs) > 1 and len(b_refs[-1].shape) == 3:
        add_ref, b_refs = b_refs[-1], b_refs[:-1]
    col = 0
    a = a_ref[...]
    for b_ref in b_refs:
        n = b_ref.shape[1]
        g = mm(a, b_ref[...], TN)
        if add_ref is not None:
            g = g + add_ref[0, :, col : col + n].astype(f32)
        out_ref[0, :, col : col + n] = g.astype(bf16)
        col += n


def grad_rows(pick, a, bs, rows, add=None, name="grad"):
    cols = sum(width for _, _, width in bs)
    count = pick.shape[0]
    specs = [pl.BlockSpec((LEN, rows), lambda j, p: (0, p[j]))]
    specs += [one((LEN, width), functools.partial(lambda at, j, p: (0, at), at)) for _, at, width in bs]
    ops = [a, *(b for b, _, _ in bs)]
    if add is not None:
        specs.append(pl.BlockSpec((1, rows, cols), lambda j, p: (j, 0, 0)))
        ops.append(add)
    return pl.pallas_call(
        grad_kernel,
        grid_spec=pltpu.PrefetchScalarGridSpec(
            num_scalar_prefetch=1,
            grid=(count,),
            in_specs=specs,
            out_specs=pl.BlockSpec((1, rows, cols), lambda j, p: (j, 0, 0)),
        ),
        out_shape=jax.ShapeDtypeStruct((count, rows, cols), bf16),
        compiler_params=params(),
        cost_estimate=pl.CostEstimate(flops=2 * LEN * rows * count * cols, bytes_accessed=12 << 20, transcendentals=0),
        name=name,
    )(pick, *ops)


beta_first = 0.9
beta_second = 0.95
adam_eps = 1e-08
decay_rate = 0.1
outer_decay = 0.5
outer_rate = 0.7
STEP = 10


def adam_step(grad, first, second, weight, rate):
    first_new = beta_first * first + (1.0 - beta_first) * grad
    second_new = beta_second * second + (1.0 - beta_second) * grad * grad
    ratio = first_new / (1.0 - beta_first**STEP) / (jnp.sqrt(second_new / (1.0 - beta_second**STEP)) + adam_eps)
    local = weight - rate * (ratio + decay_rate * weight)
    return first_new, second_new, weight - local


def outer_step(delta_sum, momentum, weight, groups):
    average = delta_sum / groups
    momentum_new = outer_decay * momentum + average
    return average, momentum_new, weight - outer_rate * (average + outer_decay * momentum_new)


def adam_kernel(place_ref, own_ref, *refs, slots, deltas, rate, groups):
    refs = list(refs)
    grad = own_ref[0].astype(f32)
    if slots:
        b, c, d = (refs.pop(0)[0].astype(f32) for _ in range(3))
        grad = grad + b + c + jnp.where(place_ref[1] == 1, d, 0.0)
    first_ref, second_ref, w_ref = refs[:3]
    first_new, second_new, delta = adam_step(grad, first_ref[...], second_ref[...], w_ref[...], rate)
    outs = refs[-7:] if deltas else refs[-4:]
    outs[0][...] = grad
    outs[1][...] = first_new
    outs[2][...] = second_new
    if not deltas:
        outs[3][...] = delta.astype(bf16)
        return
    outer_ref, delta_ref = refs[3:5]
    d = [delta_ref[k].astype(f32) for k in range(delta_ref.shape[0])]
    write_outer((d[0] + d[1]) + (d[2] + d[3]), outer_ref, w_ref, outs[3:], groups)


def write_outer(total, outer_ref, w_ref, outs, groups):
    average, momentum, weight = outer_step(total, outer_ref[...], w_ref[...], groups)
    outs[0][...] = average
    outs[1][...] = momentum
    outs[2][...] = weight
    outs[3][...] = weight.astype(bf16)


TILE = 256


def adam_tiles(place, own, slots, first, second, w, outer, deltas, held, own_at, tiles, rate, groups):
    rows = w.shape[0]
    start, count, hole, skip = tiles
    at = lambda j: start + j + jnp.where(j >= hole, skip, 0)
    state = pl.BlockSpec((rows, TILE), lambda j, p: (0, at(j)))
    plane = lambda pick: pl.BlockSpec((1, rows, TILE), lambda j, p: (pick(p), 0, at(j) - own_at))
    full = jax.ShapeDtypeStruct(w.shape, f32)
    ops, specs = [own], [plane(lambda p: p[0])]
    if slots is not None:
        ops += [slots] * 3
        specs += [plane(lambda p: 1), plane(lambda p: 2), plane(lambda p: 2 + p[1])]
    ops += [first, second, w]
    specs += [state] * 3
    out_shape, out_specs = [full] * 3, [state] * 3
    if deltas is not None:
        ops += [outer, deltas]
        specs += [state, pl.BlockSpec((deltas.shape[0], rows, TILE), lambda j, p: (0, 0, at(j)))]
        out_shape += [full] * 3 + [jax.ShapeDtypeStruct(w.shape, bf16)]
        out_specs += [state] * 4
    else:
        out_shape.append(jax.ShapeDtypeStruct((rows, count * TILE), bf16))
        out_specs.append(pl.BlockSpec((rows, TILE), lambda j, p: (0, j)))
    aliases = {}
    if held is not None:
        aliases = {1 + len(ops) + k: k for k in range(3)}
        ops += list(held)
        specs += [pl.BlockSpec(memory_space=pl.ANY)] * 3
    return pl.pallas_call(
        functools.partial(adam_kernel, slots=slots is not None, deltas=deltas is not None, rate=rate, groups=groups),
        grid_spec=pltpu.PrefetchScalarGridSpec(num_scalar_prefetch=1, grid=(count,), in_specs=specs, out_specs=out_specs),
        out_shape=out_shape,
        input_output_aliases=aliases,
        compiler_params=params(),
        cost_estimate=pl.CostEstimate(flops=0, bytes_accessed=rows * count * TILE * 48, transcendentals=0),
        name="adam",
    )(place, *ops)


def outer_kernel(*refs, terms, groups):
    d = [ref[...].astype(f32) for ref in refs[:terms]]
    total = (d[0] + d[1]) + (d[2] + d[3]) if terms == 4 else sum(d[1:], d[0])
    write_outer(total, refs[terms], refs[terms + 1], refs[-4:], groups)


def outer_tiles(deltas, outer, w, held, start, groups):
    rows, cols = deltas[0].shape
    state = pl.BlockSpec((rows, TILE), lambda j: (0, start + j))
    full = jax.ShapeDtypeStruct(w.shape, f32)
    ops = [*deltas, outer, w]
    specs = [pl.BlockSpec((rows, TILE), lambda j: (0, j))] * len(deltas) + [state] * 2
    aliases = {}
    if held is not None:
        aliases = {len(ops) + k: k for k in range(4)}
        ops += list(held)
        specs += [pl.BlockSpec(memory_space=pl.ANY)] * 4
    return pl.pallas_call(
        functools.partial(outer_kernel, terms=len(deltas), groups=groups),
        grid=(cols // TILE,),
        in_specs=specs,
        out_specs=[state] * 4,
        out_shape=[full, full, full, jax.ShapeDtypeStruct(w.shape, bf16)],
        input_output_aliases=aliases,
        compiler_params=params(),
        cost_estimate=pl.CostEstimate(flops=0, bytes_accessed=rows * cols * 24, transcendentals=0),
        name="outer",
    )(*ops)


def groups_terms(delta, rep):
    to = lambda a, k: lax.ppermute(a, "rep", [(i, i ^ k) for i in range(rep)])
    if rep != 4:
        return [delta] + [to(delta, k) for k in range(1, rep)]
    near, far = to(delta, 1), to(delta, 2)
    return [delta, near, far, to(far, 1)]


def by_neighbours(n, rep):
    return n == 8 and rep == 4


def all_weights(w_in, w_out, gains):
    split = H * HD + 2 * KVH * HD
    low_in, low_out = w_in.astype(bf16), w_out.astype(bf16)
    low_gains = jnp.pad(gains.astype(bf16), ((0, 62), (0, 0)))
    shards = [low_gains, low_in[:, :split], low_out[0], low_in[:, split:], low_out[1]]
    full = [lax.all_gather(a, "fsdp") for a in shards]
    gain_full = full[0][:, :8].astype(f32).transpose(1, 0, 2).reshape(8, -1)
    return [gain_full] + [a.reshape(-1, a.shape[-1]) for a in full[1:]]


CHUNKS = ("q", "kv", "proj", "gate", "up", "down")
IN_COLUMNS = {"q": (0, H * HD), "kv": (H * HD, 2 * KVH * HD), "gate": (H * HD + 2 * KVH * HD, FF), "up": (H * HD + 2 * KVH * HD + FF, FF)}
CHIP_SHARE = {"q": 48, "kv": 48, "proj": 32, "gate": 48, "up": 48, "down": 16}
PLAN = {
    "begin": (
        (("z", "q", 0), ("z", "kv", 0), ("z", "q", 1), ("y", "q", 0), ("z", "kv", 1), ("y", "kv", 0), ("z", "proj", 0), ("y", "q", 1), ("z", "kv", 2), ("z", "q", 2),),
    ),
    "dy": (
        (("y", "kv", 2), ("z", "q", 3), ("x", "kv", 0), ("z", "kv", 3), ("z", "proj", 1), ("x", "q", 1), ("z", "gate", 0), ("y", "q", 2), ("y", "q", 3), ("y", "kv", 1),),
    ),
    "norm": (
        (("y", "kv", 3), ("x", "q", 0), ("z", "proj", 2), ("x", "kv", 2),),
        (("x", "q", 2), ("z", "gate", 1),),
        (("x", "q", 3), ("c", "q", 1),),
        (("c", "q", 2), ("x", "kv", 1), ("z", "proj", 3), ("y", "proj", 0), ("z", "up", 0), ("x", "kv", 3), ("y", "gate", 0), ("z", "down", 0), ("c", "kv", 2), ("c", "kv", 0), ("z", "gate", 2), ("y", "proj", 2), ("c", "q", 0), ("c", "q", 3), ("y", "proj", 1), ("c", "kv", 1), ("c", "kv", 3),),
    ),
    "qkv": (
        (),
        (),
        (("y", "up", 0),),
        (("y", "gate", 1), ("x", "proj", 2), ("z", "up", 1), ("z", "gate", 3), ("y", "proj", 3),),
    ),
    "attn": (
        (("z", "down", 1),),
        (("z", "up", 2),),
        (("y", "up", 1), ("x", "up", 0),),
        (("z", "down", 2), ("x", "proj", 0), ("x", "proj", 3), ("c", "up", 0), ("y", "gate", 2), ("y", "down", 0),),
        (("x", "gate", 1),),
        (("c", "proj", 0), ("z", "up", 3), ("y", "up", 2), ("c", "gate", 1), ("x", "proj", 1), ("c", "proj", 3),),
        (),
        (("y", "gate", 3), ("x", "up", 1), ("x", "down", 0), ("y", "up", 3), ("z", "down", 3), ("c", "proj", 1), ("c", "proj", 2), ("y", "down", 2),),
    ),
    "proj": (
        (("x", "gate", 2),),
        (("x", "gate", 3), ("y", "down", 3), ("y", "down", 1),),
        (("c", "gate", 2), ("c", "down", 0), ("x", "gate", 0), ("c", "up", 1),),
        (("x", "up", 2), ("x", "down", 2), ("c", "gate", 0), ("c", "gate", 3),),
    ),
    "gate": (
        (),
        (("x", "up", 3), ("x", "down", 1), ("c", "up", 2),),
        (("x", "down", 3),),
        (("c", "up", 3),),
    ),
    "up": (
        (("c", "down", 1),),
        (),
        (),
        (("c", "down", 2), ("c", "down", 3),),
    ),
}


def forward_kernel(*refs, names, line):
    R = dict(zip(names, refs))
    r, f = lax.axis_index("rep"), lax.axis_index("fsdp")
    x, core, z, y = r // 2, r % 2, f // 2, f % 2
    n = 2 * line
    to_y = (r, f + 1 - 2 * y)
    to_x = (r + 2 - 4 * x, f)
    to_core = (r + 1 - 2 * core, f)
    barrier = pltpu.get_barrier_semaphore()
    peers = [(r, lax.rem(f + step, n)) for step in range(1, n)]
    for to in (*peers, to_x, to_core):
        pl.semaphore_signal(barrier, inc=1, device_id=to, device_id_type=pl.DeviceIdType.MESH)
    pl.semaphore_wait(barrier, n + 1)

    def remote(src, dst, send, recv, to):
        return pltpu.make_async_remote_copy(
            src_ref=src, dst_ref=dst, send_sem=send, recv_sem=recv, device_id=to, device_id_type=pl.DeviceIdType.MESH
        )

    held = {c: R["v_" + c] if "v_" + c in R else R["full_" + c] for c in CHUNKS}
    low = {c: R["low_in"].at[:, pl.ds(at, cols)] for c, (at, cols) in IN_COLUMNS.items()}
    low |= {"proj": R["low_out"].at[0], "down": R["low_out"].at[1]}
    rows_of = {c: R["low_out"].shape[1] if c in ("proj", "down") else R["low_in"].shape[0] for c in CHUNKS}
    item = lambda side, d: 0 if d == 0 else 2 * d - 1 + (side > 0)
    exists = lambda side, d: None if d == 0 else (z - d >= 0 if side < 0 else z + d < line)

    def guard(cond, fn):
        if cond is None:
            fn()
        else:
            pl.when(cond)(fn)

    def copy(src, dst, stage, c, side, d, to):
        m, k = CHUNKS.index(c), item(side, d)
        return remote(src, dst, R["f_send"].at[stage, m, k], R["f_recv"].at[stage, m, k], to)

    def portion(c):
        half, share = rows_of[c] // 2, CHIP_SHARE[c]
        return pl.ds(pl.multiple_of(core * half + x * share, 16), half - share)

    def line_copy(c, side, d):
        plane = z + side * (d - 1)
        dst = held[c].at[plane * 2 + y, portion(c), :]
        src = low[c].at[portion(c), :] if d == 1 else dst
        return copy(src, dst, 0, c, side, d, (r, f - 2 * side))

    def line_arrival(c, side, d):
        dst = held[c].at[(z + side * d) * 2 + y, portion(c), :]
        return copy(dst, dst, 0, c, side, d, to_y)

    def y_copy(c, side, d):
        dst = held[c].at[(z + side * d) * 2 + y, portion(c), :]
        return copy(low[c].at[portion(c), :] if d == 0 else dst, dst, 1, c, side, d, to_y)

    def both_copy(c, side, d, start, rows, stage, to):
        planes = pl.ds(z * 2 + 1 - y, 1) if d == 0 else pl.ds((z + side * d) * 2, 2)
        ref = held[c].at[planes, pl.ds(pl.multiple_of(start, 16), rows), :]
        return copy(ref, ref, stage, c, side, d, to)

    def x_copy(c, side, d):
        half, share = rows_of[c] // 2, CHIP_SHARE[c]
        return both_copy(c, side, d, core * half + x * (half - share), share, 2, to_x)

    def core_copy(c, side, d):
        half = rows_of[c] // 2
        return both_copy(c, side, d, core * half, half, 3, to_core)

    def onward(side):
        return z < line - 1 if side < 0 else z > 0

    def line_stage(c, side, d):
        if d == 0:
            for way in (-1, 1):
                pl.when(onward(way))(lambda way=way: line_copy(c, way, 1).start())
        else:
            line_arrival(c, side, d).wait_recv()
            if d < line - 1:
                pl.when(onward(side))(lambda: line_copy(c, side, d + 1).start())
        y_copy(c, side, d).start()

    def y_stage(c, side, d):
        y_copy(c, side, d).wait_recv()
        x_copy(c, side, d).start()

    def x_stage(c, side, d):
        x_copy(c, side, d).wait_recv()
        core_copy(c, side, d).start()

    def core_stage(c, side, d):
        core_copy(c, side, d).wait_recv()

    stages = {"z": line_stage, "y": y_stage, "x": x_stage, "c": core_stage}
    sides = lambda d: (1,) if d == 0 else (-1, 1)

    def act(todo):
        for hop, c, d in todo:
            for side in sides(d):
                guard(exists(side, d), functools.partial(stages[hop], c, side, d))

    def serve(phase, at):
        for step, todo in enumerate(PLAN[phase]):
            if todo:

                @pl.when(at == step)
                def _():
                    act(todo)

    def keep(c):
        return pltpu.make_async_copy(R["v_" + c], R["full_" + c], R["keep_sem"].at[CHUNKS.index(c)])

    def place_own(c):
        return pltpu.make_async_copy(low[c], held[c].at[f], R["own_sem"].at[CHUNKS.index(c)])

    gain_send = lambda step: remote(R["low_gain"], R["v_gain"].at[f], R["g_send"].at[step - 1], R["g_recv"].at[step - 1], peers[step - 1])
    for step in range(1, n):
        gain_send(step).start()
    own_gain = pltpu.make_async_copy(R["low_gain"], R["v_gain"].at[f], R["g_send"].at[n - 1])
    own_gain.start()
    act(PLAN["begin"][0])
    for c in CHUNKS:
        place_own(c).start()

    rowb = lambda width: pl.BlockSpec((BQ, width), lambda i: (i, 0))
    width = R["x"].shape[1]
    steps = LEN // BQ

    def run(body, grid, ins, outs):
        pltpu.emit_pipeline(body, grid=grid, in_specs=[s for _, s in ins], out_specs=[s for _, s in outs])(
            *[R[a] for a, _ in ins], *[R[a] for a, _ in outs]
        )

    def target_step(t_ref, dy_ref, c_ref):
        at = pl.multiple_of(pl.program_id(0) * BQ, BQ)
        c = token_weight(R["table"], R["ids"][pl.ds(at, BQ), :])
        c_ref[...] = jnp.broadcast_to(c, c_ref.shape)
        dy_ref[...] = (c * t_ref[...].astype(f32)).astype(bf16)

    run(target_step, (steps,), [("target", rowb(width))], [("dy", rowb(width)), ("c", rowb(128))])
    act(PLAN["dy"][0])
    own_gain.wait()
    for step in range(1, n):
        gain_send(step).wait()
    gains = jnp.concatenate([R["v_gain"][k] for k in range(n)], axis=1).astype(f32)[0:8]
    R["gain_rows"][...] = gains
    keep_gain = pltpu.make_async_copy(R["gain_rows"], R["gain"], R["g_send"].at[n - 1])
    keep_gain.start()

    def norm_step(x_ref, first_ref):
        v = x_ref[...].astype(f32)
        inv = lax.rsqrt(jnp.mean(v * v, axis=-1, keepdims=True) + norm_eps)
        first_ref[...] = (v * inv * R["gain_rows"][0:1, :]).astype(bf16)

    def norm_body(x_ref, first_ref):
        norm_step(x_ref, first_ref)
        serve("norm", pl.program_id(0))

    run(norm_body, (steps,), [("x", rowb(width))], [("first", rowb(width))])
    for c in CHUNKS:
        place_own(c).wait()
    whole = lambda c: held[c][...].reshape(-1, held[c].shape[2])

    keep("q").start()
    keep("kv").start()

    def qkv_body(first_ref, packed_ref):
        first = first_ref[...]
        split = H * HD
        packed_ref[:, :split] = mm(first, whole("q")).astype(bf16)
        packed_ref[:, split:] = mm(first, whole("kv")).astype(bf16)
        serve("qkv", pl.program_id(0))

    run(qkv_body, (steps,), [("first", rowb(width))], [("packed", rowb(R["packed"].shape[1]))])

    qw = H // 2 * HD
    kcol = H * HD // 128
    vcol = kcol + KVH * HD // 128

    def attention_body(q_ref, k_ref, v_ref, o_ref, lse_ref):
        s = pl.program_id(0)
        i = lax.rem(s, steps)
        attention_step(R["lengths"], i, jnp.minimum(i + 1, max_blocks()), q_ref, k_ref, v_ref, o_ref, lse_ref)
        serve("attn", s)

    qspec = pl.BlockSpec((BQ, qw), lambda s: (s % steps, s // steps))
    run(
        attention_body,
        (2 * steps,),
        [
            ("packed", qspec),
            ("packed", pl.BlockSpec((LEN, 128), lambda s: (0, kcol + s // steps))),
            ("packed", pl.BlockSpec((LEN, 128), lambda s: (0, vcol + s // steps))),
        ],
        [("mixed", qspec), ("lse", pl.BlockSpec((8, BQ), lambda s: (s // steps, s % steps)))],
    )

    keep("proj").start()

    def proj_body(x_ref, mixed_ref, middle_ref, second_ref):
        middle = x_ref[...].astype(f32) + mm(mixed_ref[...], whole("proj"))
        middle_ref[...] = middle
        inv = lax.rsqrt(jnp.mean(middle * middle, axis=-1, keepdims=True) + norm_eps)
        second_ref[...] = (middle * inv * R["gain_rows"][1:2, :]).astype(bf16)
        serve("proj", pl.program_id(0))

    run(proj_body, (steps,), [("x", rowb(width)), ("mixed", rowb(H * HD))], [("middle", rowb(width)), ("second", rowb(width))])

    keep("gate").start()

    def gate_body(second_ref, gate_ref):
        gate_ref[...] = mm(second_ref[...], whole("gate"))
        serve("gate", pl.program_id(0))

    run(gate_body, (steps,), [("second", rowb(width))], [("gate", rowb(FF))])

    keep("up").start()

    def up_body(second_ref, gate_ref, up_ref, hidden_ref):
        up = mm(second_ref[...], whole("up"))
        up_ref[...] = up
        gate = gate_ref[...]
        hidden_ref[...] = (gate * jax.nn.sigmoid(gate) * up).astype(bf16)
        serve("up", pl.program_id(0))

    run(up_body, (steps,), [("second", rowb(width)), ("gate", rowb(FF))], [("up", rowb(FF)), ("hidden", rowb(FF))])

    for c in CHUNKS[:-1]:
        keep(c).wait()
    keep_gain.wait()
    for c in CHUNKS:
        for d in range(line):
            for side in sides(d):

                def finish():
                    core_copy(c, side, d).wait_send()
                    x_copy(c, side, d).wait_send()
                    y_copy(c, side, d).wait_send()

                guard(exists(side, d), finish)
                if d > 0:
                    had = z - (d - 1) >= 0 if side < 0 else z + (d - 1) < line
                    pl.when(had & onward(side))(lambda: line_copy(c, side, d).wait_send())


def forward(lengths, table, ids, arrays, low_in, low_out, gain_shard, n):
    line = n // 2
    width = arrays["x"].shape[1]
    packed = H * HD + 2 * KVH * HD
    shape = {c: (low_in.shape[0], cols) for c, (_, cols) in IN_COLUMNS.items()} | dict.fromkeys(("proj", "down"), low_out.shape[1:])
    outs = {"full_" + c: ((n, *shape[c]), bf16) for c in CHUNKS}
    outs |= {
        "gain": ((8, width), f32), "dy": ((LEN, width), bf16), "c": ((LEN, 128), f32), "first": ((LEN, width), bf16),
        "packed": ((LEN, packed), bf16), "mixed": ((LEN, H * HD), bf16), "lse": ((H, LEN), f32),
        "middle": ((LEN, width), f32), "second": ((LEN, width), bf16), "gate": ((LEN, FF), f32), "up": ((LEN, FF), f32),
        "hidden": ((LEN, FF), bf16),
    }
    dma = pltpu.SemaphoreType.DMA
    count, items = len(CHUNKS), n - 1
    scratch = {"v_" + c: pltpu.VMEM((n, *shape[c]), bf16) for c in CHUNKS[:-1]}
    scratch |= {
        "v_gain": pltpu.VMEM((n, *gain_shard.shape), bf16), "gain_rows": pltpu.VMEM((8, width), f32),
        "f_send": dma((4, count, items)), "f_recv": dma((4, count, items)), "keep_sem": dma((count,)),
        "own_sem": dma((count,)), "g_send": dma((n,)), "g_recv": dma((n,)),
    }
    inputs = dict(arrays) | {"low_in": low_in, "low_out": low_out, "low_gain": gain_shard}
    names = ["lengths", "table", "ids", *inputs, *outs, *scratch]
    anywhere = pl.BlockSpec(memory_space=pl.ANY)
    smem = pl.BlockSpec(memory_space=pltpu.SMEM)
    got = pl.pallas_call(
        functools.partial(forward_kernel, names=names, line=line),
        in_specs=[smem, smem, pl.BlockSpec(memory_space=pltpu.VMEM)] + [anywhere] * len(inputs),
        out_specs=[anywhere] * len(outs),
        out_shape=[jax.ShapeDtypeStruct(*v) for v in outs.values()],
        scratch_shapes=list(scratch.values()),
        compiler_params=pltpu.CompilerParams(collective_id=0, has_side_effects=True, vmem_limit_bytes=62 << 20),
        cost_estimate=pl.CostEstimate(flops=60 << 30, bytes_accessed=200 << 20, transcendentals=0),
        name="forward",
    )(lengths, table, ids, *inputs.values())
    return dict(zip(outs, got))


HALF = 1024
PIECES = {
    "down_y": ("y", "out", 1, HALF, HALF, "hidden", [("dy", 1, HALF)]),
    "down_z": ("z", "out", 1, 0, HALF, "hidden", [("dy", 0, HALF)]),
    "gate": ("y", "in", 0, H * HD + 2 * KVH * HD, FF, "second", [("dboth", 0, FF)]),
    "up": ("y", "in", 0, H * HD + 2 * KVH * HD + FF, FF, "second", [("dboth", 1, FF)]),
    "proj_z": ("z", "out", 0, 0, HALF, "mixed", [("dlow", 0, HALF)]),
    "proj_y": ("y", "out", 0, HALF, HALF, "mixed", [("dlow", 1, HALF)]),
    "q": ("y", "in", 0, 0, H * HD, "first", [("dq", 0, H * HD)]),
    "kv": ("y", "in", 0, H * HD, 2 * KVH * HD, "first", [("dk", 0, KVH * HD), ("dv", 0, KVH * HD)]),
}
REGIONS = {
    "down": ("out", ("down_z", "down_y"), 1, 0, 2 * HALF),
    "ffn": ("in", ("gate", "up"), 0, H * HD + 2 * KVH * HD, 2 * FF),
    "proj": ("out", ("proj_z", "proj_y"), 0, 0, 2 * HALF),
}


def back_kernel(*refs, names, line, rep, rates):
    R = dict(zip(names, refs))
    r, f = lax.axis_index("rep"), lax.axis_index("fsdp")
    z, y = f // 2, f % 2
    n = 2 * line
    other = lambda k: (r + (1 - 2 * (r % 2)) * (k % 2) + 2 * (1 - 2 * (r // 2)) * (k // 2), f)
    barrier = pltpu.get_barrier_semaphore()
    for step in range(1, n):
        pl.semaphore_signal(barrier, inc=1, device_id=(r, lax.rem(f + step, n)), device_id_type=pl.DeviceIdType.MESH)
    for k in range(1, rep):
        pl.semaphore_signal(barrier, inc=1, device_id=other(k), device_id_type=pl.DeviceIdType.MESH)
    pl.semaphore_wait(barrier, n - 1 + rep - 1)

    loads = ("down", "gate_w", "up_w", "proj", "q_w", "kv_w")
    load = lambda k: pltpu.make_async_copy(R[loads[k]], R["v_" + loads[k]], R["load_sem"].at[k])
    for k in range(len(loads)):
        load(k).start()

    def remote(src, dst, send, recv, to):
        return pltpu.make_async_remote_copy(
            src_ref=src, dst_ref=dst, send_sem=send, recv_sem=recv, device_id=(r, to), device_id_type=pl.DeviceIdType.MESH
        )

    def run(body, grid, ins, outs):
        pltpu.emit_pipeline(body, grid=grid, in_specs=[s for _, s in ins], out_specs=[s for _, s in outs])(
            *[a for a, _ in ins], *[a for a, _ in outs]
        )

    order = list(PIECES)
    middle = (z > 0) & (z < line - 1)
    low = z < line // 2
    inner = jnp.where(low, f + 2, f - 2)
    outer = jnp.where(low, f - 2, f + 2)
    to_y = f + 1 - 2 * y
    third = jnp.where(middle, 3, 2)
    far = jnp.where(low, z + 2, z - 2) * 2 + y

    def shard_rows(p):
        rows = R["own_" + PIECES[p][1]].shape[1]
        return rows // 2 if PIECES[p][1] == "out" else rows

    def span(rows, row, col, cols):
        return pl.ds(row * rows, rows), pl.ds(col, cols)

    def area(p):
        _, _, row, col, cols, _, _ = PIECES[p]
        return span(shard_rows(p), row, col, cols)

    def own(p, t):
        return R["own_" + p].at[t] if PIECES[p][0] == "z" else R["own_" + PIECES[p][1]].at[(t, *area(p))]

    def slot(p, k):
        return R["slot_" + p].at[k] if PIECES[p][0] == "z" else R["slot_" + PIECES[p][1]].at[(k, *area(p))]

    def gradient(p, side, out, add=None):
        mode, _, _, _, cols, a, bs = PIECES[p]
        rows = shard_rows(p)
        pick = lambda j: (0, j * 2 + side)
        if mode == "z":
            rows, pick = 2 * rows, lambda j: (0, j)
        block = pl.BlockSpec((1, rows, cols), lambda j: (j, 0, 0))
        ins = [(R[a], pl.BlockSpec((LEN, rows), pick))]
        for b, at, width in bs:
            ins.append((R[b], pl.BlockSpec((LEN, width), functools.partial(lambda at, j: (0, at), at))))
        if add is not None:
            ins.append((add, block))

        def step(*refs):
            out_ref, a_ref, b_refs = refs[-1], refs[0], refs[1 : 1 + len(bs)]
            col = 0
            for b_ref in b_refs:
                width = b_ref.shape[1]
                g = mm(a_ref[...], b_ref[...], TN)
                if add is not None:
                    g = g + refs[-2][0, :, col : col + width].astype(f32)
                out_ref[0, :, col : col + width] = g.astype(bf16)
                col += width

        run(step, (line,), ins, [(out, block)])

    def pair_copy(p):
        k = order.index(p)
        if PIECES[p][0] == "z":
            dst = R["slot_" + PIECES[p][1]].at[(1, *area(p))]
        else:
            dst = R["came_" + p]
        return remote(R["away_" + p], dst, R["y_send"].at[k], R["y_recv"].at[k], to_y)

    def line_copy(p, k, src, slot_at, to):
        i = order.index(p)
        return remote(src, slot(p, slot_at), R["z_send"].at[i, k], R["z_recv"].at[i, slot_at], to)

    def end_copies(p):
        t = lambda k: jnp.where(low, line - 1 - k, k)
        to = (inner, far, inner)
        return [functools.partial(line_copy, p, k, own(p, t(k)), (0, 1, 3)[k], to[k]) for k in range(3)]

    def middle_copies(p):
        return [
            functools.partial(line_copy, p, 0, R["msg_" + p], 1, far),
            functools.partial(line_copy, p, 1, own(p, 3 - z), 2, inner),
            functools.partial(line_copy, p, 2, own(p, 3 * (z - 1)), 2, outer),
        ]

    def slot_wait(p, at):
        i = order.index(p)
        remote(slot(p, at), slot(p, at), R["z_send"].at[i, 0], R["z_recv"].at[i, at], inner).wait_recv()

    def line_start(p):
        @pl.when(~middle)
        def _():
            for copy in end_copies(p):
                copy().start()

        @pl.when(middle)
        def _():
            for copy in middle_copies(p)[1:]:
                copy().start()

    def send_away(p):
        gradient(p, 1 - y, R["away_" + p])
        pair_copy(p).start()

    def keep(p):
        pair_copy(p).wait_recv()
        gradient(p, y, R["own_" + PIECES[p][1]].at[(pl.ds(0, line), *area(p))], R["came_" + p])
        line_start(p)

    def send_line(p):
        gradient(p, None, R["own_" + p])
        line_start(p)

    def serve(p):
        @pl.when(middle)
        def _():
            slot_wait(p, 0)
            rows, cols = R["msg_" + p].shape
            block = pl.BlockSpec((rows // 2, cols), lambda j: (j, 0))

            def step(a_ref, b_ref, o_ref):
                o_ref[...] = (a_ref[...].astype(f32) + b_ref[...].astype(f32)).astype(bf16)

            run(step, (2,), [(own(p, 3 * (2 - z)), block), (slot(p, 0), block)], [(R["msg_" + p], block)])
            middle_copies(p)[0]().start()

    def line_end(p):
        slot_wait(p, 1)
        slot_wait(p, 2)
        pl.when(middle)(lambda: slot_wait(p, 3))

    def total(refs):
        a, b, c, d = (ref[...].astype(f32) for ref in refs)
        return a + b + c + jnp.where(middle, d, 0.0)

    def close(p):
        line_end(p)
        rows, cols = shard_rows(p), PIECES[p][4]

        def send_step(*refs):
            refs[-1][...] = total(refs[:4]).astype(bf16)

        def stay_step(*refs):
            refs[4][...] = total(refs[:4]).astype(bf16)
            for ref in refs[5:]:
                ref[...] = jnp.zeros_like(ref)

        piece = pl.BlockSpec((rows // 2, cols), lambda j: (j, 0))
        terms = (own(p, z), slot(p, 1), slot(p, 2), slot(p, third))
        ins = lambda side: [(ref, pl.BlockSpec((rows // 2, cols), lambda j: (side * 2 + j, 0))) for ref in terms]
        run(send_step, (2,), ins(1 - y), [(R["away_" + p], piece)])
        pair_copy(p).start()
        kind = PIECES[p][1]
        outs = [R["own_" + kind].at[(z, *area(p))]] + [R["slot_" + kind].at[(k, *area(p))] for k in (2, 3)]
        run(stay_step, (2,), ins(y), [(ref, piece) for ref in outs])

    def delta_copy(name, k):
        kind, pieces, row, col, cols = REGIONS[name]
        i = list(REGIONS).index(name)
        spot = lambda at: R["delta_" + kind].at[(at, *span(shard_rows(pieces[0]), row, col, cols))]
        return pltpu.make_async_remote_copy(
            src_ref=spot(2 if k == 3 else 0), dst_ref=spot(k), send_sem=R["d_send"].at[i, k - 1], recv_sem=R["d_recv"].at[i, k - 1],
            device_id=other(1 if k == 3 else k), device_id_type=pl.DeviceIdType.MESH,
        )

    def delta(name):
        kind, pieces, row, col, cols = REGIONS[name]
        for p in pieces:
            if PIECES[p][0] == "z":
                pair_copy(p).wait_recv()
            else:
                line_end(p)
        rows = shard_rows(pieces[0])
        where = span(rows, row, col, cols)
        block = pl.BlockSpec((rows, 256), lambda j: (0, j))
        terms = [R["own_" + kind].at[(z, *where)]] + [R["slot_" + kind].at[(k, *where)] for k in (1, 2, third)]
        state = [R[k + "_" + kind].at[where] for k in ("first", "second", "w")]

        def step(*refs):
            first_ref, second_ref, w_ref, o_ref = refs[4:]
            o_ref[...] = adam_step(total(refs[:4]), first_ref[...], second_ref[...], w_ref[...], rates[kind])[2].astype(bf16)

        run(step, (cols // 256,), [(ref, block) for ref in terms + state], [(R["delta_" + kind].at[(0, *where)], block)])
        for k in (1, 2):
            delta_copy(name, k).start()

    def relay(name):
        delta_copy(name, 2).wait_recv()
        delta_copy(name, 3).start()

    rowb = lambda width: pl.BlockSpec((BQ, width), lambda i: (i, 0))
    width = R["x"].shape[1]
    R["gain_acc"][...] = jnp.zeros_like(R["gain_acc"])
    gain_rows = R["gain"][...]

    def mid_step(middle_ref, hidden_ref, dboth_ref, t_ref, c_ref, act_ref, dmid_ref, dlow_ref, dmix_ref):
        mid_v = middle_ref[...]
        act_ref[...] = (mid_v + mm(hidden_ref[...], R["v_down"][...])).astype(bf16)
        inv = lax.rsqrt(jnp.mean(mid_v * mid_v, axis=-1, keepdims=True) + norm_eps)
        n2 = mid_v * inv
        ds2 = mm(dboth_ref[:, :FF], R["v_gate_w"][...], NT) + mm(dboth_ref[:, FF:], R["v_up_w"][...], NT)
        prod = ds2 * n2
        R["gain_acc"][8:16, :] += jnp.sum(prod.reshape(BQ // 8, 8, width), axis=0)
        g = gain_rows[1:2, :]
        dy = c_ref[:, 0:1] * t_ref[...].astype(f32)
        dmid = dy + inv * (ds2 * g - n2 * jnp.mean(prod * g, axis=-1, keepdims=True))
        dmid_ref[...] = dmid
        dlow = dmid.astype(bf16)
        dlow_ref[...] = dlow
        dmix_ref[...] = mm(dlow, R["v_proj"][...], NT).astype(bf16)

    def mid_phase(part):
        count = LEN // BQ // 2
        late = lambda width: pl.BlockSpec((BQ, width), lambda i: (i + part * count, 0))
        run(
            mid_step,
            (count,),
            [(R["middle"], late(width)), (R["hidden"], late(FF)), (R["dboth"], late(2 * FF)), (R["target"], late(width)), (R["c"], late(128))],
            [(R["act"], late(width)), (R["dmid"], late(width)), (R["dlow"], late(width)), (R["dmix"], late(H * HD))],
        )

    qw = H // 2 * HD
    kcol = H * HD // 128
    vcol = kcol + KVH * HD // 128

    def attention_phase(p):
        qspec = pl.BlockSpec((BQ, qw), lambda i: (i, p))
        whole = lambda at: pl.BlockSpec((LEN, 128), lambda i: (0, at))
        R["dk_acc"][...] = jnp.zeros_like(R["dk_acc"])
        R["dv_acc"][...] = jnp.zeros_like(R["dv_acc"])

        def step(q_ref, k_ref, v_ref, d_ref, o_ref, lse_ref, dq_ref):
            attention_back_step(R["lengths"], pl.program_id(0), q_ref, k_ref, v_ref, d_ref, o_ref, lse_ref, dq_ref, R["dk_acc"], R["dv_acc"])

        pltpu.emit_pipeline(
            step, grid=(LEN // BQ,),
            in_specs=[qspec, whole(kcol + p), whole(vcol + p), qspec, qspec, pl.BlockSpec((8, BQ), lambda i: (p, i))],
            out_specs=[qspec],
        )(R["packed"], R["packed"], R["packed"], R["dmix"], R["mixed"], R["lse"], R["dq"])

        def flush(dk_ref, dv_ref):
            dk_ref[...] = R["dk_acc"][...].astype(bf16)
            dv_ref[...] = R["dv_acc"][...].astype(bf16)

        run(flush, (1,), [], [(R["dk"], pl.BlockSpec((LEN, 128), lambda i: (0, p))), (R["dv"], pl.BlockSpec((LEN, 128), lambda i: (0, p)))])

    def input_step(x_ref, dmid_ref, dq_ref, dk_ref, dv_ref, out_ref):
        x = x_ref[...].astype(f32)
        inv = lax.rsqrt(jnp.mean(x * x, axis=-1, keepdims=True) + norm_eps)
        n1 = x * inv
        kv_w, split = R["v_kv_w"], KVH * HD
        ds1 = mm(dq_ref[...], R["v_q_w"][...], NT) + mm(dk_ref[...], kv_w[:, :split], NT) + mm(dv_ref[...], kv_w[:, split:], NT)
        prod = ds1 * n1
        R["gain_acc"][0:8, :] += jnp.sum(prod.reshape(BQ // 8, 8, width), axis=0)
        g = gain_rows[0:1, :]
        out_ref[...] = (dmid_ref[...] + inv * (ds1 * g - n1 * jnp.mean(prod * g, axis=-1, keepdims=True))).astype(bf16)

    def input_phase():
        run(
            input_step,
            (LEN // BQ,),
            [(R["x"], rowb(width)), (R["dmid"], rowb(width)), (R["dq"], rowb(H * HD)), (R["dk"], rowb(KVH * HD)), (R["dv"], rowb(KVH * HD))],
            [(R["xgrad"], rowb(width))],
        )

    part = width // n

    def gain_copy(step, receive=False):
        peer = lax.rem(f + step, n)
        home = lax.rem(f + n - step, n) if receive else f
        return remote(
            R["gain_acc"].at[:, pl.ds(pl.multiple_of(peer * part, part), part)], R["gain_got"].at[home],
            R["g_send"].at[step - 1], R["g_recv"].at[step - 1], peer,
        )

    own_gain = pltpu.make_async_copy(
        R["gain_acc"].at[:, pl.ds(pl.multiple_of(f * part, part), part)], R["gain_got"].at[f], R["g_send"].at[n - 1]
    )

    def dboth_step(dy_ref, gate_ref, up_ref, dboth_ref):
        dh = mm(dy_ref[...], R["v_down"][...], NT)
        gate = gate_ref[...]
        sig = jax.nn.sigmoid(gate)
        dboth_ref[:, :FF] = (dh * up_ref[...] * sig * (1.0 + gate * (1.0 - sig))).astype(bf16)
        dboth_ref[:, FF:] = (dh * (gate * sig)).astype(bf16)

    send_away("down_y")
    send_line("down_z")
    load(0).wait()
    run(
        dboth_step,
        (LEN // BQ,),
        [(R["dy"], rowb(width)), (R["gate"], rowb(FF)), (R["up"], rowb(FF))],
        [(R["dboth"], rowb(2 * FF))],
    )
    send_away("gate")
    for k in range(1, 4):
        load(k).wait()
    mid_phase(0)
    keep("down_y")
    serve("down_z")
    mid_phase(1)
    send_line("proj_z")
    serve("down_y")
    send_away("up")
    serve("proj_z")
    send_away("proj_y")
    attention_phase(0)
    keep("gate")
    serve("gate")
    attention_phase(1)
    send_away("q")
    keep("up")
    close("down_z")
    serve("up")
    load(4).wait()
    load(5).wait()
    input_phase()
    for step in range(1, n):
        gain_copy(step).start()
    own_gain.start()
    keep("proj_y")
    send_away("kv")
    delta("ffn")
    serve("proj_y")
    keep("q")
    delta("down")
    close("proj_z")
    serve("q")
    delta("proj")
    relay("ffn")
    relay("down")
    keep("kv")
    serve("kv")
    relay("proj")

    for step in range(1, n):
        gain_copy(step, True).wait_recv()
        gain_copy(step).wait_send()
    own_gain.wait()
    for name in REGIONS:
        for k in (1, 3):
            delta_copy(name, k).wait()
        delta_copy(name, 2).wait_send()
    line_end("q")
    line_end("kv")
    for p in order:
        pair_copy(p).wait_send()

        @pl.when(middle)
        def _():
            for copy in middle_copies(p):
                copy().wait_send()

        @pl.when(~middle)
        def _():
            for copy in end_copies(p):
                copy().wait_send()


def backward(lengths, gain, arrays, n, rep, rates):
    line = n // 2
    width = arrays["x"].shape[1]
    kvw = KVH * HD
    outs = {
        "act": ((LEN, width), bf16), "dboth": ((LEN, 2 * FF), bf16), "dmid": ((LEN, width), f32), "dlow": ((LEN, width), bf16),
        "dmix": ((LEN, H * HD), bf16), "dq": ((LEN, H * HD), bf16), "dk": ((LEN, kvw), bf16), "dv": ((LEN, kvw), bf16),
        "xgrad": ((LEN, width), bf16), "gain_got": ((n, 16, width // n), f32),
    }
    for kind in ("in", "out"):
        for name, count in (("own_", line), ("slot_", 4), ("delta_", rep)):
            outs[name + kind] = ((count, *arrays["w_" + kind].shape), bf16)
    for p, (mode, kind, _, _, cols, _, _) in PIECES.items():
        rows = arrays["w_" + kind].shape[0] // (2 if kind == "out" else 1)
        if mode == "y":
            counts = (("away_", (line, rows)), ("came_", (line, rows)), ("msg_", (rows,)))
        else:
            counts = (("away_", (rows,)), ("own_", (line, 2 * rows)), ("slot_", (4, 2 * rows)), ("msg_", (2 * rows,)))
        for name, lead in counts:
            outs[name + p] = ((*lead, cols), bf16)
    dma = pltpu.SemaphoreType.DMA
    pieces = len(PIECES)
    scratch = {
        **{"v_" + k: pltpu.VMEM(arrays[k].shape, bf16) for k in ("down", "gate_w", "up_w", "proj", "q_w", "kv_w")},
        "gain_acc": pltpu.VMEM((16, width), f32), "dk_acc": pltpu.VMEM((LEN, 128), f32), "dv_acc": pltpu.VMEM((LEN, 128), f32),
        "load_sem": dma((6,)), "y_send": dma((pieces,)), "y_recv": dma((pieces,)),
        "z_send": dma((pieces, 3)), "z_recv": dma((pieces, 4)),
        "d_send": dma((len(REGIONS), rep - 1)), "d_recv": dma((len(REGIONS), rep - 1)), "g_send": dma((n,)), "g_recv": dma((n,)),
    }
    names = ["lengths", "gain", *arrays, *outs, *scratch]
    anywhere = pl.BlockSpec(memory_space=pl.ANY)
    got = pl.pallas_call(
        functools.partial(back_kernel, names=names, line=line, rep=rep, rates=rates),
        in_specs=[pl.BlockSpec(memory_space=pltpu.SMEM), pl.BlockSpec(memory_space=pltpu.VMEM)] + [anywhere] * len(arrays),
        out_specs=[anywhere] * len(outs),
        out_shape=[jax.ShapeDtypeStruct(*v) for v in outs.values()],
        scratch_shapes=list(scratch.values()),
        compiler_params=pltpu.CompilerParams(collective_id=1, has_side_effects=True, vmem_limit_bytes=62 << 20),
        cost_estimate=pl.CostEstimate(flops=200 << 30, bytes_accessed=400 << 20, transcendentals=0),
        name="backward",
    )(lengths, gain, *arrays.values())
    return dict(zip(outs, got))


rate_in = 0.02
rate_out = 0.08
rate_gains = 1.2


def body(
    tokens,
    target,
    doc_lengths,
    corpus_ids,
    corpus_weights,
    w_in,
    w_out,
    gains,
    first_in,
    first_out,
    first_gains,
    second_in,
    second_out,
    second_gains,
    outer_in,
    outer_out,
    outer_gains,
):
    n, rep = lax.axis_size("fsdp"), lax.axis_size("rep")
    line = n // 2
    f, r = lax.axis_index("fsdp"), lax.axis_index("rep")
    z, y = f // 2, f % 2
    direct = by_neighbours(n, rep)
    inside = (z > 0) & (z < line - 1)
    place = jnp.stack([z, inside]).astype(jnp.int32)
    width = w_out.shape[2]
    flat = lambda a: a.reshape(-1, a.shape[-1])
    state_in = first_in[0], second_in[0], w_in
    state_out = flat(first_out[0]), flat(second_out[0]), flat(w_out)
    moved_out = flat(outer_out)
    rates = {"in": rate_in, "out": rate_out}
    rows_in, rows_out = w_in.shape[0], w_out.shape[1]
    x, tgt, lengths = tokens[0], target[0], doc_lengths[0]
    ids = corpus_ids[0][:, None]

    if direct:
        low_gain = jnp.pad(gains.astype(bf16), ((0, 14), (0, 0)))
        fwd = forward(lengths, corpus_weights, ids, dict(x=x, target=tgt), w_in.astype(bf16), w_out.astype(bf16), low_gain, n)
        weight = lambda c: flat(fwd["full_" + c])
        kept = {k: fwd[k] for k in ("c", "middle", "hidden", "second", "gate", "up", "dy", "mixed", "packed", "lse", "first")}
        got = backward(
            lengths, fwd["gain"],
            dict(x=x, target=tgt, proj=weight("proj"), down=weight("down"), q_w=weight("q"), kv_w=weight("kv"),
                 gate_w=weight("gate"), up_w=weight("up"), first_in=state_in[0], second_in=state_in[1], w_in=w_in,
                 first_out=state_out[0], second_out=state_out[1], w_out=state_out[2], **kept),
            n, rep, rates,
        )
        activations, input_grad = got["act"], got["xgrad"]
        gain_share = jnp.sum(got["gain_got"].reshape(n, 2, 8, -1), axis=(0, 2))
        late = (H * HD + 2 * KVH * HD) // TILE
        *held, late_delta = adam_tiles(
            place, got["own_in"], got["slot_in"], *state_in, None, None, None, 0, (0, late, late, 0), rate_in, rep
        )
        late_terms = groups_terms(late_delta, rep)
        rest = w_in.shape[1] // TILE - late
        in_got = adam_tiles(
            place, got["own_in"], got["slot_in"], *state_in, outer_in, got["delta_in"], held,
            0, (late, rest, rest, 0), rate_in, rep,
        )
        out_count = width // TILE
        out_got = adam_tiles(
            place, got["own_out"], got["slot_out"], *state_out, moved_out, got["delta_out"], None,
            0, (0, out_count, out_count, 0), rate_out, rep,
        )
        in_grads, in_steps = in_got[:3], outer_tiles(late_terms, outer_in, w_in, in_got[3:], 0, rep)
        out_grads, out_steps = out_got[:3], out_got[3:]
    else:
        gain_full, wq, proj, wf, down = all_weights(w_in, w_out, gains)
        first_low, packed = qkv(x, gain_full, wq)
        mixed, lse = attention(lengths, packed)
        middle, second_low, hidden, d_both, dy, _ = ffn(corpus_weights, x, mixed, tgt, ids, gain_full, proj, wf, down)

        def by_library(a, bs, name):
            block = 2 * BQ if a.shape[1] % (2 * BQ) == 0 else BQ
            every_row = jnp.arange(a.shape[1] // block, dtype=jnp.int32)
            total = grad_rows(every_row, a, bs, block, name=name)
            return lax.psum_scatter(total.reshape(a.shape[1], -1), "fsdp", scatter_dimension=0, tiled=True)[None]

        activations, d_mid, d_low, d_mix, gain_two = mid(
            corpus_weights, middle, hidden, d_both, tgt, ids, gain_full, proj, wf, down
        )
        dq, dk, dv = attention_back(lengths, packed, d_mix, mixed, lse)
        input_grad, gain_one = input_back(x, d_mid, dq, dk, dv, gain_full, wq)
        both = jnp.stack([jnp.sum(gain_one, axis=0), jnp.sum(gain_two, axis=0)])
        gain_share = lax.psum_scatter(both, "fsdp", scatter_dimension=1, tiled=True)
        own_in = jnp.concatenate(
            [
                by_library(first_low, [(dq, 0, H * HD), (dk, 0, KVH * HD), (dv, 0, KVH * HD)], "grad_attn"),
                by_library(second_low, [(d_both, 0, 2 * FF)], "grad_ffn"),
            ],
            axis=2,
        )
        own_out = jnp.concatenate(
            [by_library(mixed, [(d_low, 0, width)], "grad_proj"), by_library(hidden, [(dy, 0, width)], "grad_down")], axis=1
        )

        def all_tiles(own, state, outer, rate):
            count = own.shape[2] // TILE
            *grads, delta = adam_tiles(0 * place, own, None, *state, None, None, None, 0, (0, count, count, 0), rate, rep)
            return grads, outer_tiles(groups_terms(delta, rep), outer, state[2], None, 0, rep)

        in_grads, in_steps = all_tiles(own_in, state_in, outer_in, rate_in)
        out_grads, out_steps = all_tiles(own_out, state_out, moved_out, rate_out)

    first_gains_new, second_gains_new, delta = adam_step(gain_share, first_gains[0], second_gains[0], gains, rate_gains)
    terms = groups_terms(delta, rep)
    sum_gains = (terms[0] + terms[1]) + (terms[2] + terms[3]) if rep == 4 else sum(terms[1:], terms[0])
    diff_gains, outer_gains_new, new_gains = outer_step(sum_gains, outer_gains, gains, rep)

    out_shape = lambda a: a.reshape(2, rows_out, width)
    diff_in, outer_in_new, new_in, copy_in = in_steps
    diff_out, outer_out_new, new_out, copy_out = (out_shape(a) for a in out_steps)
    grad_in, first_in_new, second_in_new = in_grads
    grad_out, first_out_new, second_out_new = (out_shape(a) for a in out_grads)
    return (
        activations[None],
        input_grad[None],
        grad_in[None],
        grad_out[None],
        gain_share[None],
        first_in_new[None],
        first_out_new[None],
        first_gains_new[None],
        second_in_new[None],
        second_out_new[None],
        second_gains_new[None],
        diff_in,
        diff_out,
        diff_gains,
        outer_in_new,
        outer_out_new,
        outer_gains_new,
        new_in,
        new_out,
        new_gains,
        copy_in,
        copy_out,
        new_gains.astype(bf16),
    )


def solution(mesh):
    rows = P(("rep", "fsdp"), None, None)
    pair = P(("rep", "fsdp"), None)
    w_in, w_out, gains = P("fsdp", None), P(None, "fsdp", None), P(None, "fsdp")
    m_in, m_out, m_gains = P("rep", "fsdp", None), P("rep", None, "fsdp", None), P("rep", None, "fsdp")
    weights, moments = (w_in, w_out, gains), (m_in, m_out, m_gains)
    return jax.shard_map(
        body,
        mesh=mesh,
        in_specs=(rows, rows, pair, pair, P(), *weights, *moments, *moments, *weights),
        out_specs=(rows, rows, *moments, *moments, *moments, *weights, *weights, *weights, *weights),
        check_vma=False,
    )
```

```python
import functools
import jax
import jax.numpy as jnp
from jax import lax
from jax.experimental import pallas as pl
from jax.experimental.pallas import tpu as pltpu
from jax.sharding import PartitionSpec as P

H = 16
HD = 64
KVH = 4
FF = 1024
LEN = 1024
NCORP = 8
f32 = jnp.float32
bf16 = jnp.bfloat16
norm_eps = 1e-06
BQ = 256
NT = (((1,), (1,)), ((), ()))
TN = (((0,), (0,)), ((), ()))


def mm(a, b, dims=(((1,), (0,)), ((), ()))):
    return lax.dot_general(a, b, dims, preferred_element_type=f32)


def params(**kw):
    return pltpu.CompilerParams(vmem_limit_bytes=60 << 20, **kw)


def one(shape, index):
    return pl.BlockSpec(shape, index, pipeline_mode=pl.Buffered(1))


def qkv_kernel(x_ref, g_ref, w_ref, first_ref, packed_ref):
    x = x_ref[...].astype(f32)
    r = lax.rsqrt(jnp.mean(x * x, axis=-1, keepdims=True) + norm_eps)
    first = (x * r * g_ref[0:1, :]).astype(bf16)
    first_ref[...] = first
    packed_ref[...] = mm(first, w_ref[...]).astype(bf16)


def qkv(x, gains, w):
    rows, width = x.shape
    cols = w.shape[1]
    return pl.pallas_call(
        qkv_kernel,
        grid=(rows // BQ,),
        in_specs=[
            pl.BlockSpec((BQ, width), lambda i: (i, 0)),
            one(gains.shape, lambda i: (0, 0)),
            one((width, cols), lambda i: (0, 0)),
        ],
        out_specs=[
            pl.BlockSpec((BQ, width), lambda i: (i, 0)),
            pl.BlockSpec((BQ, cols), lambda i: (i, 0)),
        ],
        out_shape=[
            jax.ShapeDtypeStruct((rows, width), bf16),
            jax.ShapeDtypeStruct((rows, cols), bf16),
        ],
        compiler_params=params(),
        cost_estimate=pl.CostEstimate(
            flops=2 * rows * width * cols, bytes_accessed=rows * width * 4 + width * cols * 2, transcendentals=0
        ),
        name="norm_qkv",
    )(x, gains, w)


def doc_start(lengths_ref, position):
    end = jnp.int32(0)
    start = jnp.zeros_like(position)
    for j in range(lengths_ref.shape[0]):
        end = end + lengths_ref[j]
        start = jnp.where(position >= end, end, start)
    return start


def key_blocks(lengths_ref, i):
    first_row = i * BQ
    return i + 1 - doc_start(lengths_ref, first_row) // BQ


def max_blocks():
    return LEN // (2 * BQ) + 1


def attention_step(len_ref, i, count, q_ref, k_ref, v_ref, o_ref, lse_ref):
    row = i * BQ + lax.broadcasted_iota(jnp.int32, (BQ, 1), 0)
    start = doc_start(len_ref, row)
    lane = lax.broadcasted_iota(jnp.int32, (BQ, 128), 1)
    for nb in range(1, max_blocks() + 1):

        @pl.when(count == nb)
        def _():
            span = nb * BQ
            base = pl.multiple_of((i - (nb - 1)) * BQ, BQ)
            col = base + lax.broadcasted_iota(jnp.int32, (BQ, span), 1)
            bias = jnp.where((col >= start) & (col <= row), 0.0, -1e30)
            k2 = k_ref[pl.ds(base, span), :]
            v2 = v_ref[pl.ds(base, span), :]
            tile = jnp.zeros((BQ, 128), f32)
            outs = []
            for kv in range(2):
                k = k2[:, kv * HD : (kv + 1) * HD]
                v = v2[:, kv * HD : (kv + 1) * HD]
                for g in range(H // KVH):
                    h = kv * (H // KVH) + g
                    q = q_ref[:, h * HD : (h + 1) * HD] * jnp.asarray(HD**-0.5, bf16)
                    s = mm(q, k, NT) + bias
                    m = jnp.max(s, axis=-1, keepdims=True)
                    e = jnp.exp(s - m)
                    total = jnp.sum(e, axis=-1, keepdims=True)
                    o = mm(e.astype(bf16), v) * (1.0 / total)
                    outs.append(o.astype(bf16))
                    tile = jnp.where(lane == h, m + jnp.log(total), tile)
            o_ref[...] = jnp.concatenate(outs, axis=1)
            lse_ref[...] = tile.T[0:8, :]


def attn_kernel(len_ref, *refs):
    i = pl.program_id(0)
    attention_step(len_ref, i, key_blocks(len_ref, i), *refs)


def attention(lengths, packed):
    qw = H // 2 * HD
    kcol = H * HD // 128
    vcol = kcol + KVH * HD // 128
    return pl.pallas_call(
        attn_kernel,
        grid_spec=pltpu.PrefetchScalarGridSpec(
            num_scalar_prefetch=1,
            grid=(LEN // BQ, 2),
            in_specs=[
                pl.BlockSpec((BQ, qw), lambda i, p, s: (i, p)),
                pl.BlockSpec((LEN, 128), lambda i, p, s: (0, kcol + p)),
                pl.BlockSpec((LEN, 128), lambda i, p, s: (0, vcol + p)),
            ],
            out_specs=[
                pl.BlockSpec((BQ, qw), lambda i, p, s: (i, p)),
                pl.BlockSpec((8, BQ), lambda i, p, s: (p, i)),
            ],
        ),
        out_shape=[
            jax.ShapeDtypeStruct((LEN, H * HD), bf16),
            jax.ShapeDtypeStruct((H, LEN), f32),
        ],
        compiler_params=params(),
        cost_estimate=pl.CostEstimate(flops=4 * H * LEN * LEN * HD * 4, bytes_accessed=1 << 24, transcendentals=0),
        name="attention",
    )(lengths, packed, packed, packed)


def attention_back_step(len_ref, i, q_ref, k_ref, v_ref, d_ref, o_ref, lse_ref, dq_ref, dk_acc, dv_acc, count=None):
    if count is None:
        count = jnp.minimum(i + 1, max_blocks())
    row = i * BQ + lax.broadcasted_iota(jnp.int32, (1, BQ), 1)
    start = doc_start(len_ref, row)
    lane = lax.broadcasted_iota(jnp.int32, (BQ, 128), 1)
    group = H // KVH
    scale = jnp.asarray(HD**-0.5, bf16)
    tile = jnp.zeros((BQ, 128), f32)
    for h in range(2 * group):
        cols = slice(h * HD, (h + 1) * HD)
        dot = jnp.sum(d_ref[:, cols].astype(f32) * o_ref[:, cols].astype(f32), axis=-1, keepdims=True)
        tile = jnp.where(lane == h, dot, tile)
    inner = tile.T
    for nb in range(1, max_blocks() + 1):

        @pl.when(count == nb)
        def _():
            span = nb * BQ
            base = pl.multiple_of((i - (nb - 1)) * BQ, BQ)
            key = base + lax.broadcasted_iota(jnp.int32, (span, BQ), 0)
            bias = jnp.where((key >= start) & (key <= row), 0.0, -1e30)
            k2 = k_ref[pl.ds(base, span), :]
            v2 = v_ref[pl.ds(base, span), :]
            dks, dvs = [], []
            for kv in range(2):
                k = k2[:, kv * HD : (kv + 1) * HD]
                v = v2[:, kv * HD : (kv + 1) * HD]
                dk = dv = None
                dqs = []
                for g in range(group):
                    h = kv * group + g
                    cols = slice(h * HD, (h + 1) * HD)
                    q = q_ref[:, cols] * scale
                    d = d_ref[:, cols]
                    s = mm(k, q, NT) + bias
                    p = jnp.exp(s - lse_ref[h : h + 1, :])
                    dp = mm(v, d, NT)
                    ds = (p * (dp - inner[h : h + 1, :])).astype(bf16)
                    dv_h = mm(p.astype(bf16), d)
                    dk_h = mm(ds, q)
                    dv = dv_h if dv is None else dv + dv_h
                    dk = dk_h if dk is None else dk + dk_h
                    dqs.append(mm(k, ds, TN))
                dq = jnp.concatenate(dqs, axis=0) * (HD**-0.5)
                dq_ref[:, kv * group * HD : (kv + 1) * group * HD] = dq.T.astype(bf16)
                dks.append(dk)
                dvs.append(dv)
            dk_acc[pl.ds(base, span), :] += jnp.concatenate(dks, axis=1)
            dv_acc[pl.ds(base, span), :] += jnp.concatenate(dvs, axis=1)


def attn_back_kernel(len_ref, q_ref, k_ref, v_ref, d_ref, o_ref, lse_ref, dq_ref, dk_ref, dv_ref, dk_acc, dv_acc):
    i = pl.program_id(1)

    @pl.when(i == 0)
    def _():
        dk_acc[...] = jnp.zeros_like(dk_acc)
        dv_acc[...] = jnp.zeros_like(dv_acc)

    attention_back_step(
        len_ref, i, q_ref, k_ref, v_ref, d_ref, o_ref, lse_ref, dq_ref, dk_acc, dv_acc, key_blocks(len_ref, i)
    )

    @pl.when(i == pl.num_programs(1) - 1)
    def _():
        dk_ref[...] = dk_acc[...].astype(bf16)
        dv_ref[...] = dv_acc[...].astype(bf16)


def attention_back(lengths, packed, d_mixed, mixed, lse):
    qw = H // 2 * HD
    kcol = H * HD // 128
    vcol = kcol + KVH * HD // 128
    return pl.pallas_call(
        attn_back_kernel,
        grid_spec=pltpu.PrefetchScalarGridSpec(
            num_scalar_prefetch=1,
            grid=(2, LEN // BQ),
            in_specs=[
                pl.BlockSpec((BQ, qw), lambda p, i, s: (i, p)),
                pl.BlockSpec((LEN, 128), lambda p, i, s: (0, kcol + p)),
                pl.BlockSpec((LEN, 128), lambda p, i, s: (0, vcol + p)),
                pl.BlockSpec((BQ, qw), lambda p, i, s: (i, p)),
                pl.BlockSpec((BQ, qw), lambda p, i, s: (i, p)),
                pl.BlockSpec((8, BQ), lambda p, i, s: (p, i)),
            ],
            out_specs=[
                pl.BlockSpec((BQ, qw), lambda p, i, s: (i, p)),
                pl.BlockSpec((LEN, 128), lambda p, i, s: (0, p)),
                pl.BlockSpec((LEN, 128), lambda p, i, s: (0, p)),
            ],
            scratch_shapes=[pltpu.VMEM((LEN, 128), f32), pltpu.VMEM((LEN, 128), f32)],
        ),
        out_shape=[
            jax.ShapeDtypeStruct((LEN, H * HD), bf16),
            jax.ShapeDtypeStruct((LEN, KVH * HD), bf16),
            jax.ShapeDtypeStruct((LEN, KVH * HD), bf16),
        ],
        compiler_params=params(),
        cost_estimate=pl.CostEstimate(flops=10 * H * LEN * LEN * HD * 4, bytes_accessed=1 << 24, transcendentals=0),
        name="attention_back",
    )(lengths, packed, packed, packed, d_mixed, mixed, lse)


def token_weight(table_ref, ids):
    weight = jnp.zeros(ids.shape, f32)
    for j in range(table_ref.shape[0]):
        weight = jnp.where(ids == j, table_ref[j].astype(f32) * 0.25, weight)
    return weight


def ffn_kernel(table_ref, x_ref, mixed_ref, t_ref, ids_ref, g_ref, proj_ref, wf_ref, down_ref,
               middle_ref, second_ref, hidden_ref, dboth_ref, dy_ref, c_ref):
    middle = x_ref[...].astype(f32) + mm(mixed_ref[...], proj_ref[...])
    middle_ref[...] = middle
    r = lax.rsqrt(jnp.mean(middle * middle, axis=-1, keepdims=True) + norm_eps)
    second = (middle * r * g_ref[1:2, :]).astype(bf16)
    second_ref[...] = second
    c = token_weight(table_ref, ids_ref[...])
    c_ref[...] = jnp.broadcast_to(c, c_ref.shape)
    dy = (c * t_ref[...].astype(f32)).astype(bf16)
    dy_ref[...] = dy
    step = 512
    for c in range(0, FF, step):
        gate = mm(second, wf_ref[:, c : c + step])
        up = mm(second, wf_ref[:, FF + c : FF + c + step])
        dh = mm(dy, down_ref[c : c + step, :], NT)
        sig = jax.nn.sigmoid(gate)
        silu = gate * sig
        hidden_ref[:, c : c + step] = (silu * up).astype(bf16)
        dboth_ref[:, c : c + step] = (dh * up * sig * (1.0 + gate * (1.0 - sig))).astype(bf16)
        dboth_ref[:, FF + c : FF + c + step] = (dh * silu).astype(bf16)


def ffn(table, x, mixed, target, ids, gains, proj, wf, down):
    width = x.shape[1]
    rowb = lambda n: pl.BlockSpec((BQ, n), lambda i, s: (i, 0))
    whole = lambda a: one(a.shape, lambda i, s: (0, 0))
    return pl.pallas_call(
        ffn_kernel,
        grid_spec=pltpu.PrefetchScalarGridSpec(
            num_scalar_prefetch=1,
            grid=(LEN // BQ,),
            in_specs=[rowb(width), rowb(H * HD), rowb(width), rowb(1), whole(gains), whole(proj), whole(wf), whole(down)],
            out_specs=[rowb(width), rowb(width), rowb(FF), rowb(2 * FF), rowb(width), rowb(128)],
        ),
        out_shape=[
            jax.ShapeDtypeStruct((LEN, width), f32),
            jax.ShapeDtypeStruct((LEN, width), bf16),
            jax.ShapeDtypeStruct((LEN, FF), bf16),
            jax.ShapeDtypeStruct((LEN, 2 * FF), bf16),
            jax.ShapeDtypeStruct((LEN, width), bf16),
            jax.ShapeDtypeStruct((LEN, 128), f32),
        ],
        compiler_params=params(),
        cost_estimate=pl.CostEstimate(flops=2 * LEN * width * FF * 4, bytes_accessed=40 << 20, transcendentals=0),
        name="ffn",
    )(table, x, mixed, target, ids, gains, proj, wf, down)


def mid_kernel(table_ref, middle_ref, hidden_ref, dboth_ref, t_ref, ids_ref, g_ref, proj_ref, wf_ref, down_ref,
               act_ref, dmid_ref, dlow_ref, dmix_ref, gain_ref):
    middle = middle_ref[...]
    act_ref[...] = (middle + mm(hidden_ref[...], down_ref[...])).astype(bf16)
    r = lax.rsqrt(jnp.mean(middle * middle, axis=-1, keepdims=True) + norm_eps)
    n2 = middle * r
    ds2 = mm(dboth_ref[...], wf_ref[...], NT)
    prod = ds2 * n2
    part = jnp.sum(prod.reshape(BQ // 8, 8, prod.shape[1]), axis=0)

    @pl.when(pl.program_id(0) == 0)
    def _():
        gain_ref[...] = jnp.zeros_like(gain_ref)

    gain_ref[...] += part
    g = g_ref[1:2, :]
    e2 = ds2 * g
    dy = token_weight(table_ref, ids_ref[...]) * t_ref[...].astype(f32)
    dmid = dy + r * (e2 - n2 * jnp.mean(prod * g, axis=-1, keepdims=True))
    dmid_ref[...] = dmid
    low = dmid.astype(bf16)
    dlow_ref[...] = low
    dmix_ref[...] = mm(low, proj_ref[...], NT).astype(bf16)


def mid(table, middle, hidden, dboth, target, ids, gains, proj, wf, down):
    width = middle.shape[1]
    rowb = lambda n: pl.BlockSpec((BQ, n), lambda i, s: (i, 0))
    whole = lambda a: one(a.shape, lambda i, s: (0, 0))
    return pl.pallas_call(
        mid_kernel,
        grid_spec=pltpu.PrefetchScalarGridSpec(
            num_scalar_prefetch=1,
            grid=(LEN // BQ,),
            in_specs=[rowb(width), rowb(FF), rowb(2 * FF), rowb(width), rowb(1), whole(gains), whole(proj), whole(wf), whole(down)],
            out_specs=[rowb(width), rowb(width), rowb(width), rowb(H * HD), pl.BlockSpec((8, width), lambda i, s: (0, 0))],
        ),
        out_shape=[
            jax.ShapeDtypeStruct((LEN, width), bf16),
            jax.ShapeDtypeStruct((LEN, width), f32),
            jax.ShapeDtypeStruct((LEN, width), bf16),
            jax.ShapeDtypeStruct((LEN, H * HD), bf16),
            jax.ShapeDtypeStruct((8, width), f32),
        ],
        compiler_params=params(),
        cost_estimate=pl.CostEstimate(flops=2 * LEN * width * FF * 4, bytes_accessed=40 << 20, transcendentals=0),
        name="mid",
    )(table, middle, hidden, dboth, target, ids, gains, proj, wf, down)


def input_kernel(x_ref, dmid_ref, dq_ref, dk_ref, dv_ref, g_ref, w_ref, out_ref, gain_ref):
    x = x_ref[...].astype(f32)
    r = lax.rsqrt(jnp.mean(x * x, axis=-1, keepdims=True) + norm_eps)
    n1 = x * r
    q, k = H * HD, H * HD + KVH * HD
    ds1 = mm(dq_ref[...], w_ref[:, :q], NT) + mm(dk_ref[...], w_ref[:, q:k], NT) + mm(dv_ref[...], w_ref[:, k:], NT)
    prod = ds1 * n1
    part = jnp.sum(prod.reshape(BQ // 8, 8, prod.shape[1]), axis=0)

    @pl.when(pl.program_id(0) == 0)
    def _():
        gain_ref[...] = jnp.zeros_like(gain_ref)

    gain_ref[...] += part
    g = g_ref[0:1, :]
    out = dmid_ref[...] + r * (ds1 * g - n1 * jnp.mean(prod * g, axis=-1, keepdims=True))
    out_ref[...] = out.astype(bf16)


def input_back(x, dmid, dq, dk, dv, gains, w):
    width = x.shape[1]
    rowb = lambda n: pl.BlockSpec((BQ, n), lambda i: (i, 0))
    whole = lambda a: one(a.shape, lambda i: (0, 0))
    return pl.pallas_call(
        input_kernel,
        grid=(LEN // BQ,),
        in_specs=[rowb(width), rowb(width), rowb(H * HD), rowb(KVH * HD), rowb(KVH * HD), whole(gains), whole(w)],
        out_specs=[rowb(width), pl.BlockSpec((8, width), lambda i: (0, 0))],
        out_shape=[jax.ShapeDtypeStruct((LEN, width), bf16), jax.ShapeDtypeStruct((8, width), f32)],
        compiler_params=params(),
        cost_estimate=pl.CostEstimate(flops=2 * LEN * width * 1536, bytes_accessed=24 << 20, transcendentals=0),
        name="input_back",
    )(x, dmid, dq, dk, dv, gains, w)


def grad_kernel(pick_ref, a_ref, *refs):
    out_ref = refs[-1]
    b_refs = refs[:-1]
    add_ref = None
    if len(b_refs) > 1 and len(b_refs[-1].shape) == 3:
        add_ref, b_refs = b_refs[-1], b_refs[:-1]
    col = 0
    a = a_ref[...]
    for b_ref in b_refs:
        n = b_ref.shape[1]
        g = mm(a, b_ref[...], TN)
        if add_ref is not None:
            g = g + add_ref[0, :, col : col + n].astype(f32)
        out_ref[0, :, col : col + n] = g.astype(bf16)
        col += n


def grad_rows(pick, a, bs, rows, add=None, name="grad"):
    cols = sum(width for _, _, width in bs)
    count = pick.shape[0]
    specs = [pl.BlockSpec((LEN, rows), lambda j, p: (0, p[j]))]
    specs += [one((LEN, width), functools.partial(lambda at, j, p: (0, at), at)) for _, at, width in bs]
    ops = [a, *(b for b, _, _ in bs)]
    if add is not None:
        specs.append(pl.BlockSpec((1, rows, cols), lambda j, p: (j, 0, 0)))
        ops.append(add)
    return pl.pallas_call(
        grad_kernel,
        grid_spec=pltpu.PrefetchScalarGridSpec(
            num_scalar_prefetch=1,
            grid=(count,),
            in_specs=specs,
            out_specs=pl.BlockSpec((1, rows, cols), lambda j, p: (j, 0, 0)),
        ),
        out_shape=jax.ShapeDtypeStruct((count, rows, cols), bf16),
        compiler_params=params(),
        cost_estimate=pl.CostEstimate(flops=2 * LEN * rows * count * cols, bytes_accessed=12 << 20, transcendentals=0),
        name=name,
    )(pick, *ops)


beta_first = 0.9
beta_second = 0.95
adam_eps = 1e-08
decay_rate = 0.1
outer_decay = 0.5
outer_rate = 0.7
STEP = 10


def adam_step(grad, first, second, weight, rate):
    first_new = beta_first * first + (1.0 - beta_first) * grad
    second_new = beta_second * second + (1.0 - beta_second) * grad * grad
    ratio = first_new / (1.0 - beta_first**STEP) / (jnp.sqrt(second_new / (1.0 - beta_second**STEP)) + adam_eps)
    local = weight - rate * (ratio + decay_rate * weight)
    return first_new, second_new, weight - local


def outer_step(delta_sum, momentum, weight, groups):
    average = delta_sum / groups
    momentum_new = outer_decay * momentum + average
    return average, momentum_new, weight - outer_rate * (average + outer_decay * momentum_new)


def adam_kernel(place_ref, own_ref, *refs, slots, deltas, rate, groups):
    refs = list(refs)
    grad = own_ref[0].astype(f32)
    if slots:
        b, c, d = (refs.pop(0)[0].astype(f32) for _ in range(3))
        grad = grad + b + c + jnp.where(place_ref[1] == 1, d, 0.0)
    first_ref, second_ref, w_ref = refs[:3]
    first_new, second_new, delta = adam_step(grad, first_ref[...], second_ref[...], w_ref[...], rate)
    outs = refs[-7:] if deltas else refs[-4:]
    outs[0][...] = grad
    outs[1][...] = first_new
    outs[2][...] = second_new
    if not deltas:
        outs[3][...] = delta.astype(bf16)
        return
    outer_ref, delta_ref = refs[3:5]
    d = [delta_ref[k].astype(f32) for k in range(delta_ref.shape[0])]
    write_outer((d[0] + d[1]) + (d[2] + d[3]), outer_ref, w_ref, outs[3:], groups)


def write_outer(total, outer_ref, w_ref, outs, groups):
    average, momentum, weight = outer_step(total, outer_ref[...], w_ref[...], groups)
    outs[0][...] = average
    outs[1][...] = momentum
    outs[2][...] = weight
    outs[3][...] = weight.astype(bf16)


TILE = 256


def adam_tiles(place, own, slots, first, second, w, outer, deltas, held, own_at, tiles, rate, groups):
    rows = w.shape[0]
    start, count, hole, skip = tiles
    at = lambda j: start + j + jnp.where(j >= hole, skip, 0)
    state = pl.BlockSpec((rows, TILE), lambda j, p: (0, at(j)))
    plane = lambda pick: pl.BlockSpec((1, rows, TILE), lambda j, p: (pick(p), 0, at(j) - own_at))
    full = jax.ShapeDtypeStruct(w.shape, f32)
    ops, specs = [own], [plane(lambda p: p[0])]
    if slots is not None:
        ops += [slots] * 3
        specs += [plane(lambda p: 1), plane(lambda p: 2), plane(lambda p: 2 + p[1])]
    ops += [first, second, w]
    specs += [state] * 3
    out_shape, out_specs = [full] * 3, [state] * 3
    if deltas is not None:
        ops += [outer, deltas]
        specs += [state, pl.BlockSpec((deltas.shape[0], rows, TILE), lambda j, p: (0, 0, at(j)))]
        out_shape += [full] * 3 + [jax.ShapeDtypeStruct(w.shape, bf16)]
        out_specs += [state] * 4
    else:
        out_shape.append(jax.ShapeDtypeStruct((rows, count * TILE), bf16))
        out_specs.append(pl.BlockSpec((rows, TILE), lambda j, p: (0, j)))
    aliases = {}
    if held is not None:
        aliases = {1 + len(ops) + k: k for k in range(3)}
        ops += list(held)
        specs += [pl.BlockSpec(memory_space=pl.ANY)] * 3
    return pl.pallas_call(
        functools.partial(adam_kernel, slots=slots is not None, deltas=deltas is not None, rate=rate, groups=groups),
        grid_spec=pltpu.PrefetchScalarGridSpec(num_scalar_prefetch=1, grid=(count,), in_specs=specs, out_specs=out_specs),
        out_shape=out_shape,
        input_output_aliases=aliases,
        compiler_params=params(),
        cost_estimate=pl.CostEstimate(flops=0, bytes_accessed=rows * count * TILE * 48, transcendentals=0),
        name="adam",
    )(place, *ops)


def outer_kernel(*refs, terms, groups):
    d = [ref[...].astype(f32) for ref in refs[:terms]]
    total = (d[0] + d[1]) + (d[2] + d[3]) if terms == 4 else sum(d[1:], d[0])
    write_outer(total, refs[terms], refs[terms + 1], refs[-4:], groups)


def outer_tiles(deltas, outer, w, held, start, groups):
    rows, cols = deltas[0].shape
    state = pl.BlockSpec((rows, TILE), lambda j: (0, start + j))
    full = jax.ShapeDtypeStruct(w.shape, f32)
    ops = [*deltas, outer, w]
    specs = [pl.BlockSpec((rows, TILE), lambda j: (0, j))] * len(deltas) + [state] * 2
    aliases = {}
    if held is not None:
        aliases = {len(ops) + k: k for k in range(4)}
        ops += list(held)
        specs += [pl.BlockSpec(memory_space=pl.ANY)] * 4
    return pl.pallas_call(
        functools.partial(outer_kernel, terms=len(deltas), groups=groups),
        grid=(cols // TILE,),
        in_specs=specs,
        out_specs=[state] * 4,
        out_shape=[full, full, full, jax.ShapeDtypeStruct(w.shape, bf16)],
        input_output_aliases=aliases,
        compiler_params=params(),
        cost_estimate=pl.CostEstimate(flops=0, bytes_accessed=rows * cols * 24, transcendentals=0),
        name="outer",
    )(*ops)


def to_group(a, k, rep):
    return lax.ppermute(a, "rep", [(i, i ^ k) for i in range(rep)])


def groups_terms(delta, rep):
    if rep != 4:
        return [delta] + [to_group(delta, k, rep) for k in range(1, rep)]
    near, far = to_group(delta, 1, rep), to_group(delta, 2, rep)
    return [delta, near, far, to_group(far, 1, rep)]


def by_neighbours(n, rep):
    return n == 8 and rep == 4


def all_weights(w_in, w_out, gains):
    split = H * HD + 2 * KVH * HD
    low_in, low_out = w_in.astype(bf16), w_out.astype(bf16)
    low_gains = jnp.pad(gains.astype(bf16), ((0, 62), (0, 0)))
    shards = [low_gains, low_in[:, :split], low_out[0], low_in[:, split:], low_out[1]]
    full = [lax.all_gather(a, "fsdp") for a in shards]
    gain_full = full[0][:, :8].astype(f32).transpose(1, 0, 2).reshape(8, -1)
    return [gain_full] + [a.reshape(-1, a.shape[-1]) for a in full[1:]]


CHUNKS = ("q", "kv", "proj", "gate", "up", "down")
IN_COLUMNS = {"q": (0, H * HD), "kv": (H * HD, 2 * KVH * HD), "gate": (H * HD + 2 * KVH * HD, FF), "up": (H * HD + 2 * KVH * HD + FF, FF)}
CHIP_SHARE = {"q": 48, "kv": 48, "proj": 32, "gate": 48, "up": 48, "down": 16}
PLAN = {
    "begin": (
        (("z", "q", 0), ("z", "kv", 0), ("z", "q", 1), ("y", "q", 0), ("z", "kv", 1), ("y", "kv", 0), ("z", "proj", 0), ("y", "q", 1), ("z", "kv", 2), ("z", "q", 2),),
    ),
    "dy": (
        (("y", "kv", 2), ("z", "q", 3), ("x", "kv", 0), ("z", "kv", 3), ("z", "proj", 1), ("x", "q", 1), ("z", "gate", 0), ("y", "q", 2), ("y", "q", 3), ("y", "kv", 1),),
    ),
    "norm": (
        (("y", "kv", 3), ("x", "q", 0), ("z", "proj", 2), ("x", "kv", 2),),
        (("x", "q", 2), ("z", "gate", 1),),
        (("x", "q", 3), ("c", "q", 1),),
        (("c", "q", 2), ("x", "kv", 1), ("z", "proj", 3), ("y", "proj", 0), ("z", "up", 0), ("x", "kv", 3), ("y", "gate", 0), ("z", "down", 0), ("c", "kv", 2), ("c", "kv", 0), ("z", "gate", 2), ("y", "proj", 2), ("c", "q", 0), ("c", "q", 3), ("y", "proj", 1), ("c", "kv", 1), ("c", "kv", 3),),
    ),
    "qkv": (
        (),
        (),
        (("y", "up", 0),),
        (("y", "gate", 1), ("x", "proj", 2), ("z", "up", 1), ("z", "gate", 3), ("y", "proj", 3),),
    ),
    "attn": (
        (("z", "down", 1),),
        (("z", "up", 2),),
        (("y", "up", 1), ("x", "up", 0),),
        (("z", "down", 2), ("x", "proj", 0), ("x", "proj", 3), ("c", "up", 0), ("y", "gate", 2), ("y", "down", 0),),
        (("x", "gate", 1),),
        (("c", "proj", 0), ("z", "up", 3), ("y", "up", 2), ("c", "gate", 1), ("x", "proj", 1), ("c", "proj", 3),),
        (),
        (("y", "gate", 3), ("x", "up", 1), ("x", "down", 0), ("y", "up", 3), ("z", "down", 3), ("c", "proj", 1), ("c", "proj", 2), ("y", "down", 2),),
    ),
    "proj": (
        (("x", "gate", 2),),
        (("x", "gate", 3), ("y", "down", 3), ("y", "down", 1),),
        (("c", "gate", 2), ("c", "down", 0), ("x", "gate", 0), ("c", "up", 1),),
        (("x", "up", 2), ("x", "down", 2), ("c", "gate", 0), ("c", "gate", 3),),
    ),
    "gate": (
        (),
        (("x", "up", 3), ("x", "down", 1), ("c", "up", 2),),
        (("x", "down", 3),),
        (("c", "up", 3),),
    ),
    "up": (
        (("c", "down", 1),),
        (),
        (),
        (("c", "down", 2), ("c", "down", 3),),
    ),
}


def forward_kernel(*refs, names, line):
    R = dict(zip(names, refs))
    r, f = lax.axis_index("rep"), lax.axis_index("fsdp")
    x, core, z, y = r // 2, r % 2, f // 2, f % 2
    n = 2 * line
    to_y = (r, f + 1 - 2 * y)
    to_x = (r + 2 - 4 * x, f)
    to_core = (r + 1 - 2 * core, f)
    barrier = pltpu.get_barrier_semaphore()
    peers = [(r, lax.rem(f + step, n)) for step in range(1, n)]
    for to in (*peers, to_x, to_core):
        pl.semaphore_signal(barrier, inc=1, device_id=to, device_id_type=pl.DeviceIdType.MESH)
    pl.semaphore_wait(barrier, n + 1)

    def remote(src, dst, send, recv, to):
        return pltpu.make_async_remote_copy(
            src_ref=src, dst_ref=dst, send_sem=send, recv_sem=recv, device_id=to, device_id_type=pl.DeviceIdType.MESH
        )

    held = {c: R["v_" + c] if "v_" + c in R else R["full_" + c] for c in CHUNKS}
    low = {c: R["low_in"].at[:, pl.ds(at, cols)] for c, (at, cols) in IN_COLUMNS.items()}
    low |= {"proj": R["low_out"].at[0], "down": R["low_out"].at[1]}
    rows_of = {c: R["low_out"].shape[1] if c in ("proj", "down") else R["low_in"].shape[0] for c in CHUNKS}
    item = lambda side, d: 0 if d == 0 else 2 * d - 1 + (side > 0)
    exists = lambda side, d: None if d == 0 else (z - d >= 0 if side < 0 else z + d < line)

    def guard(cond, fn):
        if cond is None:
            fn()
        else:
            pl.when(cond)(fn)

    def copy(src, dst, stage, c, side, d, to):
        m, k = CHUNKS.index(c), item(side, d)
        return remote(src, dst, R["f_send"].at[stage, m, k], R["f_recv"].at[stage, m, k], to)

    def portion(c):
        half, share = rows_of[c] // 2, CHIP_SHARE[c]
        return pl.ds(pl.multiple_of(core * half + x * share, 16), half - share)

    def line_copy(c, side, d):
        plane = z + side * (d - 1)
        dst = held[c].at[plane * 2 + y, portion(c), :]
        src = low[c].at[portion(c), :] if d == 1 else dst
        return copy(src, dst, 0, c, side, d, (r, f - 2 * side))

    def line_arrival(c, side, d):
        dst = held[c].at[(z + side * d) * 2 + y, portion(c), :]
        return copy(dst, dst, 0, c, side, d, to_y)

    def y_copy(c, side, d):
        dst = held[c].at[(z + side * d) * 2 + y, portion(c), :]
        return copy(low[c].at[portion(c), :] if d == 0 else dst, dst, 1, c, side, d, to_y)

    def both_copy(c, side, d, start, rows, stage, to):
        planes = pl.ds(z * 2 + 1 - y, 1) if d == 0 else pl.ds((z + side * d) * 2, 2)
        ref = held[c].at[planes, pl.ds(pl.multiple_of(start, 16), rows), :]
        return copy(ref, ref, stage, c, side, d, to)

    def x_copy(c, side, d):
        half, share = rows_of[c] // 2, CHIP_SHARE[c]
        return both_copy(c, side, d, core * half + x * (half - share), share, 2, to_x)

    def core_copy(c, side, d):
        half = rows_of[c] // 2
        return both_copy(c, side, d, core * half, half, 3, to_core)

    def onward(side):
        return z < line - 1 if side < 0 else z > 0

    def line_stage(c, side, d):
        if d == 0:
            for way in (-1, 1):
                pl.when(onward(way))(lambda way=way: line_copy(c, way, 1).start())
        else:
            line_arrival(c, side, d).wait_recv()
            if d < line - 1:
                pl.when(onward(side))(lambda: line_copy(c, side, d + 1).start())
        y_copy(c, side, d).start()

    def y_stage(c, side, d):
        y_copy(c, side, d).wait_recv()
        x_copy(c, side, d).start()

    def x_stage(c, side, d):
        x_copy(c, side, d).wait_recv()
        core_copy(c, side, d).start()

    def core_stage(c, side, d):
        core_copy(c, side, d).wait_recv()

    stages = {"z": line_stage, "y": y_stage, "x": x_stage, "c": core_stage}
    sides = lambda d: (1,) if d == 0 else (-1, 1)

    def act(todo):
        for hop, c, d in todo:
            for side in sides(d):
                guard(exists(side, d), functools.partial(stages[hop], c, side, d))

    def serve(phase, at):
        for step, todo in enumerate(PLAN[phase]):
            if todo:

                @pl.when(at == step)
                def _():
                    act(todo)

    def keep(c):
        return pltpu.make_async_copy(R["v_" + c], R["full_" + c], R["keep_sem"].at[CHUNKS.index(c)])

    def place_own(c):
        return pltpu.make_async_copy(low[c], held[c].at[f], R["own_sem"].at[CHUNKS.index(c)])

    gain_send = lambda step: remote(R["low_gain"], R["v_gain"].at[f], R["g_send"].at[step - 1], R["g_recv"].at[step - 1], peers[step - 1])
    for step in range(1, n):
        gain_send(step).start()
    own_gain = pltpu.make_async_copy(R["low_gain"], R["v_gain"].at[f], R["g_send"].at[n - 1])
    own_gain.start()
    act(PLAN["begin"][0])
    for c in CHUNKS:
        place_own(c).start()

    rowb = lambda width: pl.BlockSpec((BQ, width), lambda i: (i, 0))
    width = R["x"].shape[1]
    steps = LEN // BQ

    def run(body, grid, ins, outs):
        pltpu.emit_pipeline(body, grid=grid, in_specs=[s for _, s in ins], out_specs=[s for _, s in outs])(
            *[R[a] for a, _ in ins], *[R[a] for a, _ in outs]
        )

    def target_step(t_ref, dy_ref, c_ref):
        at = pl.multiple_of(pl.program_id(0) * BQ, BQ)
        c = token_weight(R["table"], R["ids"][pl.ds(at, BQ), :])
        c_ref[...] = jnp.broadcast_to(c, c_ref.shape)
        dy_ref[...] = (c * t_ref[...].astype(f32)).astype(bf16)

    run(target_step, (steps,), [("target", rowb(width))], [("dy", rowb(width)), ("c", rowb(128))])
    act(PLAN["dy"][0])
    own_gain.wait()
    for step in range(1, n):
        gain_send(step).wait()
    gains = jnp.concatenate([R["v_gain"][k] for k in range(n)], axis=1).astype(f32)[0:8]
    R["gain_rows"][...] = gains
    keep_gain = pltpu.make_async_copy(R["gain_rows"], R["gain"], R["g_send"].at[n - 1])
    keep_gain.start()

    def norm_step(x_ref, first_ref):
        v = x_ref[...].astype(f32)
        inv = lax.rsqrt(jnp.mean(v * v, axis=-1, keepdims=True) + norm_eps)
        first_ref[...] = (v * inv * R["gain_rows"][0:1, :]).astype(bf16)

    def norm_body(x_ref, first_ref):
        norm_step(x_ref, first_ref)
        serve("norm", pl.program_id(0))

    run(norm_body, (steps,), [("x", rowb(width))], [("first", rowb(width))])
    for c in CHUNKS:
        place_own(c).wait()
    whole = lambda c: held[c][...].reshape(-1, held[c].shape[2])

    keep("q").start()
    keep("kv").start()

    def qkv_body(first_ref, packed_ref):
        first = first_ref[...]
        split = H * HD
        packed_ref[:, :split] = mm(first, whole("q")).astype(bf16)
        packed_ref[:, split:] = mm(first, whole("kv")).astype(bf16)
        serve("qkv", pl.program_id(0))

    run(qkv_body, (steps,), [("first", rowb(width))], [("packed", rowb(R["packed"].shape[1]))])

    qw = H // 2 * HD
    kcol = H * HD // 128
    vcol = kcol + KVH * HD // 128

    def attention_body(q_ref, k_ref, v_ref, o_ref, lse_ref):
        s = pl.program_id(0)
        i = lax.rem(s, steps)
        attention_step(R["lengths"], i, jnp.minimum(i + 1, max_blocks()), q_ref, k_ref, v_ref, o_ref, lse_ref)
        serve("attn", s)

    qspec = pl.BlockSpec((BQ, qw), lambda s: (s % steps, s // steps))
    run(
        attention_body,
        (2 * steps,),
        [
            ("packed", qspec),
            ("packed", pl.BlockSpec((LEN, 128), lambda s: (0, kcol + s // steps))),
            ("packed", pl.BlockSpec((LEN, 128), lambda s: (0, vcol + s // steps))),
        ],
        [("mixed", qspec), ("lse", pl.BlockSpec((8, BQ), lambda s: (s // steps, s % steps)))],
    )

    keep("proj").start()

    def proj_body(x_ref, mixed_ref, middle_ref, second_ref):
        middle = x_ref[...].astype(f32) + mm(mixed_ref[...], whole("proj"))
        middle_ref[...] = middle
        inv = lax.rsqrt(jnp.mean(middle * middle, axis=-1, keepdims=True) + norm_eps)
        second_ref[...] = (middle * inv * R["gain_rows"][1:2, :]).astype(bf16)
        serve("proj", pl.program_id(0))

    run(proj_body, (steps,), [("x", rowb(width)), ("mixed", rowb(H * HD))], [("middle", rowb(width)), ("second", rowb(width))])

    keep("gate").start()

    def gate_body(second_ref, gate_ref):
        gate_ref[...] = mm(second_ref[...], whole("gate"))
        serve("gate", pl.program_id(0))

    run(gate_body, (steps,), [("second", rowb(width))], [("gate", rowb(FF))])

    keep("up").start()

    def up_body(second_ref, gate_ref, up_ref, hidden_ref):
        up = mm(second_ref[...], whole("up"))
        up_ref[...] = up
        gate = gate_ref[...]
        hidden_ref[...] = (gate * jax.nn.sigmoid(gate) * up).astype(bf16)
        serve("up", pl.program_id(0))

    run(up_body, (steps,), [("second", rowb(width)), ("gate", rowb(FF))], [("up", rowb(FF)), ("hidden", rowb(FF))])

    for c in CHUNKS[:-1]:
        keep(c).wait()
    keep_gain.wait()
    for c in CHUNKS:
        for d in range(line):
            for side in sides(d):

                def finish():
                    core_copy(c, side, d).wait_send()
                    x_copy(c, side, d).wait_send()
                    y_copy(c, side, d).wait_send()

                guard(exists(side, d), finish)
                if d > 0:
                    had = z - (d - 1) >= 0 if side < 0 else z + (d - 1) < line
                    pl.when(had & onward(side))(lambda: line_copy(c, side, d).wait_send())


def forward(lengths, table, ids, arrays, low_in, low_out, gain_shard, n):
    line = n // 2
    width = arrays["x"].shape[1]
    packed = H * HD + 2 * KVH * HD
    shape = {c: (low_in.shape[0], cols) for c, (_, cols) in IN_COLUMNS.items()} | dict.fromkeys(("proj", "down"), low_out.shape[1:])
    outs = {"full_" + c: ((n, *shape[c]), bf16) for c in CHUNKS}
    outs |= {
        "gain": ((8, width), f32), "dy": ((LEN, width), bf16), "c": ((LEN, 128), f32), "first": ((LEN, width), bf16),
        "packed": ((LEN, packed), bf16), "mixed": ((LEN, H * HD), bf16), "lse": ((H, LEN), f32),
        "middle": ((LEN, width), f32), "second": ((LEN, width), bf16), "gate": ((LEN, FF), f32), "up": ((LEN, FF), f32),
        "hidden": ((LEN, FF), bf16),
    }
    dma = pltpu.SemaphoreType.DMA
    count, items = len(CHUNKS), n - 1
    scratch = {"v_" + c: pltpu.VMEM((n, *shape[c]), bf16) for c in CHUNKS[:-1]}
    scratch |= {
        "v_gain": pltpu.VMEM((n, *gain_shard.shape), bf16), "gain_rows": pltpu.VMEM((8, width), f32),
        "f_send": dma((4, count, items)), "f_recv": dma((4, count, items)), "keep_sem": dma((count,)),
        "own_sem": dma((count,)), "g_send": dma((n,)), "g_recv": dma((n,)),
    }
    inputs = dict(arrays) | {"low_in": low_in, "low_out": low_out, "low_gain": gain_shard}
    names = ["lengths", "table", "ids", *inputs, *outs, *scratch]
    anywhere = pl.BlockSpec(memory_space=pl.ANY)
    smem = pl.BlockSpec(memory_space=pltpu.SMEM)
    got = pl.pallas_call(
        functools.partial(forward_kernel, names=names, line=line),
        in_specs=[smem, smem, pl.BlockSpec(memory_space=pltpu.VMEM)] + [anywhere] * len(inputs),
        out_specs=[anywhere] * len(outs),
        out_shape=[jax.ShapeDtypeStruct(*v) for v in outs.values()],
        scratch_shapes=list(scratch.values()),
        compiler_params=pltpu.CompilerParams(collective_id=0, has_side_effects=True, vmem_limit_bytes=62 << 20),
        cost_estimate=pl.CostEstimate(flops=60 << 30, bytes_accessed=200 << 20, transcendentals=0),
        name="forward",
    )(lengths, table, ids, *inputs.values())
    return dict(zip(outs, got))


HALF = 1024
PIECES = {
    "down_y": ("y", "out", 1, HALF, HALF, "hidden", [("dy", 1, HALF)]),
    "down_z": ("z", "out", 1, 0, HALF, "hidden", [("dy", 0, HALF)]),
    "gate": ("y", "in", 0, H * HD + 2 * KVH * HD, FF, "second", [("dboth", 0, FF)]),
    "up": ("y", "in", 0, H * HD + 2 * KVH * HD + FF, FF, "second", [("dboth", 1, FF)]),
    "proj_z": ("z", "out", 0, 0, HALF, "mixed", [("dlow", 0, HALF)]),
    "proj_y": ("y", "out", 0, HALF, HALF, "mixed", [("dlow", 1, HALF)]),
    "q": ("y", "in", 0, 0, H * HD, "first", [("dq", 0, H * HD)]),
    "kv": ("y", "in", 0, H * HD, 2 * KVH * HD, "first", [("dk", 0, KVH * HD), ("dv", 0, KVH * HD)]),
}
REGIONS = {
    "down": ("out", ("down_z", "down_y"), 1, 0, 2 * HALF),
    "ffn": ("in", ("gate", "up"), 0, H * HD + 2 * KVH * HD, 2 * FF),
    "proj": ("out", ("proj_z", "proj_y"), 0, 0, 2 * HALF),
}


def back_kernel(*refs, names, line, rep, rates):
    R = dict(zip(names, refs))
    r, f = lax.axis_index("rep"), lax.axis_index("fsdp")
    z, y = f // 2, f % 2
    n = 2 * line
    other = lambda k: (r + (1 - 2 * (r % 2)) * (k % 2) + 2 * (1 - 2 * (r // 2)) * (k // 2), f)
    barrier = pltpu.get_barrier_semaphore()
    for step in range(1, n):
        pl.semaphore_signal(barrier, inc=1, device_id=(r, lax.rem(f + step, n)), device_id_type=pl.DeviceIdType.MESH)
    for k in range(1, rep):
        pl.semaphore_signal(barrier, inc=1, device_id=other(k), device_id_type=pl.DeviceIdType.MESH)
    pl.semaphore_wait(barrier, n - 1 + rep - 1)

    loads = ("down", "gate_w", "up_w", "proj", "q_w", "kv_w")
    load = lambda k: pltpu.make_async_copy(R[loads[k]], R["v_" + loads[k]], R["load_sem"].at[k])
    for k in range(len(loads)):
        load(k).start()

    def remote(src, dst, send, recv, to):
        return pltpu.make_async_remote_copy(
            src_ref=src, dst_ref=dst, send_sem=send, recv_sem=recv, device_id=(r, to), device_id_type=pl.DeviceIdType.MESH
        )

    def run(body, grid, ins, outs):
        pltpu.emit_pipeline(body, grid=grid, in_specs=[s for _, s in ins], out_specs=[s for _, s in outs])(
            *[a for a, _ in ins], *[a for a, _ in outs]
        )

    order = list(PIECES)
    middle = (z > 0) & (z < line - 1)
    low = z < line // 2
    inner = jnp.where(low, f + 2, f - 2)
    outer = jnp.where(low, f - 2, f + 2)
    to_y = f + 1 - 2 * y
    third = jnp.where(middle, 3, 2)
    far = jnp.where(low, z + 2, z - 2) * 2 + y

    def shard_rows(p):
        rows = R["own_" + PIECES[p][1]].shape[1]
        return rows // 2 if PIECES[p][1] == "out" else rows

    def span(rows, row, col, cols):
        return pl.ds(row * rows, rows), pl.ds(col, cols)

    def area(p):
        _, _, row, col, cols, _, _ = PIECES[p]
        return span(shard_rows(p), row, col, cols)

    def own(p, t):
        return R["own_" + p].at[t] if PIECES[p][0] == "z" else R["own_" + PIECES[p][1]].at[(t, *area(p))]

    def slot(p, k):
        return R["slot_" + p].at[k] if PIECES[p][0] == "z" else R["slot_" + PIECES[p][1]].at[(k, *area(p))]

    def gradient(p, side, out, add=None):
        mode, _, _, _, cols, a, bs = PIECES[p]
        rows = shard_rows(p)
        pick = lambda j: (0, j * 2 + side)
        if mode == "z":
            rows, pick = 2 * rows, lambda j: (0, j)
        block = pl.BlockSpec((1, rows, cols), lambda j: (j, 0, 0))
        ins = [(R[a], pl.BlockSpec((LEN, rows), pick))]
        for b, at, width in bs:
            ins.append((R[b], pl.BlockSpec((LEN, width), functools.partial(lambda at, j: (0, at), at))))
        if add is not None:
            ins.append((add, block))

        def step(*refs):
            out_ref, a_ref, b_refs = refs[-1], refs[0], refs[1 : 1 + len(bs)]
            col = 0
            for b_ref in b_refs:
                width = b_ref.shape[1]
                g = mm(a_ref[...], b_ref[...], TN)
                if add is not None:
                    g = g + refs[-2][0, :, col : col + width].astype(f32)
                out_ref[0, :, col : col + width] = g.astype(bf16)
                col += width

        run(step, (line,), ins, [(out, block)])

    def pair_copy(p):
        k = order.index(p)
        if PIECES[p][0] == "z":
            dst = R["slot_" + PIECES[p][1]].at[(1, *area(p))]
        else:
            dst = R["came_" + p]
        return remote(R["away_" + p], dst, R["y_send"].at[k], R["y_recv"].at[k], to_y)

    def line_copy(p, k, src, slot_at, to):
        i = order.index(p)
        return remote(src, slot(p, slot_at), R["z_send"].at[i, k], R["z_recv"].at[i, slot_at], to)

    def end_copies(p):
        t = lambda k: jnp.where(low, line - 1 - k, k)
        to = (inner, far, inner)
        return [functools.partial(line_copy, p, k, own(p, t(k)), (0, 1, 3)[k], to[k]) for k in range(3)]

    def middle_copies(p):
        return [
            functools.partial(line_copy, p, 0, R["msg_" + p], 1, far),
            functools.partial(line_copy, p, 1, own(p, 3 - z), 2, inner),
            functools.partial(line_copy, p, 2, own(p, 3 * (z - 1)), 2, outer),
        ]

    def slot_wait(p, at):
        i = order.index(p)
        remote(slot(p, at), slot(p, at), R["z_send"].at[i, 0], R["z_recv"].at[i, at], inner).wait_recv()

    def line_start(p):
        @pl.when(~middle)
        def _():
            for copy in end_copies(p):
                copy().start()

        @pl.when(middle)
        def _():
            for copy in middle_copies(p)[1:]:
                copy().start()

    def send_away(p):
        gradient(p, 1 - y, R["away_" + p])
        pair_copy(p).start()

    def keep(p):
        pair_copy(p).wait_recv()
        gradient(p, y, R["own_" + PIECES[p][1]].at[(pl.ds(0, line), *area(p))], R["came_" + p])
        line_start(p)

    def send_line(p):
        gradient(p, None, R["own_" + p])
        line_start(p)

    def serve(p):
        @pl.when(middle)
        def _():
            slot_wait(p, 0)
            rows, cols = R["msg_" + p].shape
            block = pl.BlockSpec((rows // 2, cols), lambda j: (j, 0))

            def step(a_ref, b_ref, o_ref):
                o_ref[...] = (a_ref[...].astype(f32) + b_ref[...].astype(f32)).astype(bf16)

            run(step, (2,), [(own(p, 3 * (2 - z)), block), (slot(p, 0), block)], [(R["msg_" + p], block)])
            middle_copies(p)[0]().start()

    def line_end(p):
        slot_wait(p, 1)
        slot_wait(p, 2)
        pl.when(middle)(lambda: slot_wait(p, 3))

    def total(refs):
        a, b, c, d = (ref[...].astype(f32) for ref in refs)
        return a + b + c + jnp.where(middle, d, 0.0)

    def close(p):
        line_end(p)
        rows, cols = shard_rows(p), PIECES[p][4]

        def send_step(*refs):
            refs[-1][...] = total(refs[:4]).astype(bf16)

        def stay_step(*refs):
            refs[4][...] = total(refs[:4]).astype(bf16)
            for ref in refs[5:]:
                ref[...] = jnp.zeros_like(ref)

        piece = pl.BlockSpec((rows // 2, cols), lambda j: (j, 0))
        terms = (own(p, z), slot(p, 1), slot(p, 2), slot(p, third))
        ins = lambda side: [(ref, pl.BlockSpec((rows // 2, cols), lambda j: (side * 2 + j, 0))) for ref in terms]
        run(send_step, (2,), ins(1 - y), [(R["away_" + p], piece)])
        pair_copy(p).start()
        kind = PIECES[p][1]
        outs = [R["own_" + kind].at[(z, *area(p))]] + [R["slot_" + kind].at[(k, *area(p))] for k in (2, 3)]
        run(stay_step, (2,), ins(y), [(ref, piece) for ref in outs])

    def delta_copy(name, k):
        kind, pieces, row, col, cols = REGIONS[name]
        i = list(REGIONS).index(name)
        spot = lambda at: R["delta_" + kind].at[(at, *span(shard_rows(pieces[0]), row, col, cols))]
        return pltpu.make_async_remote_copy(
            src_ref=spot(2 if k == 3 else 0), dst_ref=spot(k), send_sem=R["d_send"].at[i, k - 1], recv_sem=R["d_recv"].at[i, k - 1],
            device_id=other(1 if k == 3 else k), device_id_type=pl.DeviceIdType.MESH,
        )

    def delta(name):
        kind, pieces, row, col, cols = REGIONS[name]
        for p in pieces:
            if PIECES[p][0] == "z":
                pair_copy(p).wait_recv()
            else:
                line_end(p)
        rows = shard_rows(pieces[0])
        where = span(rows, row, col, cols)
        block = pl.BlockSpec((rows, 256), lambda j: (0, j))
        terms = [R["own_" + kind].at[(z, *where)]] + [R["slot_" + kind].at[(k, *where)] for k in (1, 2, third)]
        state = [R[k + "_" + kind].at[where] for k in ("first", "second", "w")]

        def step(*refs):
            first_ref, second_ref, w_ref, o_ref = refs[4:]
            o_ref[...] = adam_step(total(refs[:4]), first_ref[...], second_ref[...], w_ref[...], rates[kind])[2].astype(bf16)

        run(step, (cols // 256,), [(ref, block) for ref in terms + state], [(R["delta_" + kind].at[(0, *where)], block)])
        for k in (1, 2):
            delta_copy(name, k).start()

    def relay(name):
        delta_copy(name, 2).wait_recv()
        delta_copy(name, 3).start()

    rowb = lambda width: pl.BlockSpec((BQ, width), lambda i: (i, 0))
    width = R["x"].shape[1]
    R["gain_acc"][...] = jnp.zeros_like(R["gain_acc"])
    gain_rows = R["gain"][...]

    def mid_step(middle_ref, hidden_ref, dboth_ref, t_ref, c_ref, act_ref, dmid_ref, dlow_ref, dmix_ref):
        mid_v = middle_ref[...]
        act_ref[...] = (mid_v + mm(hidden_ref[...], R["v_down"][...])).astype(bf16)
        inv = lax.rsqrt(jnp.mean(mid_v * mid_v, axis=-1, keepdims=True) + norm_eps)
        n2 = mid_v * inv
        ds2 = mm(dboth_ref[:, :FF], R["v_gate_w"][...], NT) + mm(dboth_ref[:, FF:], R["v_up_w"][...], NT)
        prod = ds2 * n2
        R["gain_acc"][8:16, :] += jnp.sum(prod.reshape(BQ // 8, 8, width), axis=0)
        g = gain_rows[1:2, :]
        dy = c_ref[:, 0:1] * t_ref[...].astype(f32)
        dmid = dy + inv * (ds2 * g - n2 * jnp.mean(prod * g, axis=-1, keepdims=True))
        dmid_ref[...] = dmid
        dlow = dmid.astype(bf16)
        dlow_ref[...] = dlow
        dmix_ref[...] = mm(dlow, R["v_proj"][...], NT).astype(bf16)

    def mid_phase(part):
        count = LEN // BQ // 2
        late = lambda width: pl.BlockSpec((BQ, width), lambda i: (i + part * count, 0))
        run(
            mid_step,
            (count,),
            [(R["middle"], late(width)), (R["hidden"], late(FF)), (R["dboth"], late(2 * FF)), (R["target"], late(width)), (R["c"], late(128))],
            [(R["act"], late(width)), (R["dmid"], late(width)), (R["dlow"], late(width)), (R["dmix"], late(H * HD))],
        )

    qw = H // 2 * HD
    kcol = H * HD // 128
    vcol = kcol + KVH * HD // 128

    def attention_phase(p):
        qspec = pl.BlockSpec((BQ, qw), lambda i: (i, p))
        whole = lambda at: pl.BlockSpec((LEN, 128), lambda i: (0, at))
        R["dk_acc"][...] = jnp.zeros_like(R["dk_acc"])
        R["dv_acc"][...] = jnp.zeros_like(R["dv_acc"])

        def step(q_ref, k_ref, v_ref, d_ref, o_ref, lse_ref, dq_ref):
            attention_back_step(R["lengths"], pl.program_id(0), q_ref, k_ref, v_ref, d_ref, o_ref, lse_ref, dq_ref, R["dk_acc"], R["dv_acc"])

        pltpu.emit_pipeline(
            step, grid=(LEN // BQ,),
            in_specs=[qspec, whole(kcol + p), whole(vcol + p), qspec, qspec, pl.BlockSpec((8, BQ), lambda i: (p, i))],
            out_specs=[qspec],
        )(R["packed"], R["packed"], R["packed"], R["dmix"], R["mixed"], R["lse"], R["dq"])

        def flush(dk_ref, dv_ref):
            dk_ref[...] = R["dk_acc"][...].astype(bf16)
            dv_ref[...] = R["dv_acc"][...].astype(bf16)

        run(flush, (1,), [], [(R["dk"], pl.BlockSpec((LEN, 128), lambda i: (0, p))), (R["dv"], pl.BlockSpec((LEN, 128), lambda i: (0, p)))])

    def input_step(x_ref, dmid_ref, dq_ref, dk_ref, dv_ref, out_ref):
        x = x_ref[...].astype(f32)
        inv = lax.rsqrt(jnp.mean(x * x, axis=-1, keepdims=True) + norm_eps)
        n1 = x * inv
        kv_w, split = R["v_kv_w"], KVH * HD
        ds1 = mm(dq_ref[...], R["v_q_w"][...], NT) + mm(dk_ref[...], kv_w[:, :split], NT) + mm(dv_ref[...], kv_w[:, split:], NT)
        prod = ds1 * n1
        R["gain_acc"][0:8, :] += jnp.sum(prod.reshape(BQ // 8, 8, width), axis=0)
        g = gain_rows[0:1, :]
        out_ref[...] = (dmid_ref[...] + inv * (ds1 * g - n1 * jnp.mean(prod * g, axis=-1, keepdims=True))).astype(bf16)

    def input_phase():
        run(
            input_step,
            (LEN // BQ,),
            [(R["x"], rowb(width)), (R["dmid"], rowb(width)), (R["dq"], rowb(H * HD)), (R["dk"], rowb(KVH * HD)), (R["dv"], rowb(KVH * HD))],
            [(R["xgrad"], rowb(width))],
        )

    part = width // n

    def gain_copy(step, receive=False):
        peer = lax.rem(f + step, n)
        home = lax.rem(f + n - step, n) if receive else f
        return remote(
            R["gain_acc"].at[:, pl.ds(pl.multiple_of(peer * part, part), part)], R["gain_got"].at[home],
            R["g_send"].at[step - 1], R["g_recv"].at[step - 1], peer,
        )

    own_gain = pltpu.make_async_copy(
        R["gain_acc"].at[:, pl.ds(pl.multiple_of(f * part, part), part)], R["gain_got"].at[f], R["g_send"].at[n - 1]
    )

    def dboth_step(dy_ref, gate_ref, up_ref, dboth_ref):
        dh = mm(dy_ref[...], R["v_down"][...], NT)
        gate = gate_ref[...]
        sig = jax.nn.sigmoid(gate)
        dboth_ref[:, :FF] = (dh * up_ref[...] * sig * (1.0 + gate * (1.0 - sig))).astype(bf16)
        dboth_ref[:, FF:] = (dh * (gate * sig)).astype(bf16)

    send_line("down_z")
    send_away("down_y")
    load(0).wait()
    run(
        dboth_step,
        (LEN // BQ,),
        [(R["dy"], rowb(width)), (R["gate"], rowb(FF)), (R["up"], rowb(FF))],
        [(R["dboth"], rowb(2 * FF))],
    )
    serve("down_z")
    send_away("gate")
    for k in range(1, 4):
        load(k).wait()
    mid_phase(0)
    keep("down_y")
    mid_phase(1)
    serve("down_y")
    send_away("up")
    send_line("proj_z")
    serve("proj_z")
    attention_phase(0)
    keep("gate")
    send_away("proj_y")
    serve("gate")
    attention_phase(1)
    send_away("q")
    keep("up")
    serve("up")
    load(4).wait()
    load(5).wait()
    input_phase()
    for step in range(1, n):
        gain_copy(step).start()
    own_gain.start()
    keep("proj_y")
    serve("proj_y")
    close("proj_z")
    delta("ffn")
    keep("q")
    send_away("kv")
    delta("proj")
    close("down_z")
    serve("q")
    keep("kv")
    delta("down")
    relay("proj")
    serve("kv")
    relay("down")
    relay("ffn")

    for step in range(1, n):
        gain_copy(step, True).wait_recv()
        gain_copy(step).wait_send()
    own_gain.wait()
    for name in REGIONS:
        for k in (1, 3):
            delta_copy(name, k).wait()
        delta_copy(name, 2).wait_send()
    line_end("q")
    line_end("kv")
    for p in order:
        pair_copy(p).wait_send()

        @pl.when(middle)
        def _():
            for copy in middle_copies(p):
                copy().wait_send()

        @pl.when(~middle)
        def _():
            for copy in end_copies(p):
                copy().wait_send()


def backward(lengths, gain, arrays, n, rep, rates):
    line = n // 2
    width = arrays["x"].shape[1]
    kvw = KVH * HD
    outs = {
        "act": ((LEN, width), bf16), "dboth": ((LEN, 2 * FF), bf16), "dmid": ((LEN, width), f32), "dlow": ((LEN, width), bf16),
        "dmix": ((LEN, H * HD), bf16), "dq": ((LEN, H * HD), bf16), "dk": ((LEN, kvw), bf16), "dv": ((LEN, kvw), bf16),
        "xgrad": ((LEN, width), bf16), "gain_got": ((n, 16, width // n), f32),
    }
    for kind in ("in", "out"):
        for name, count in (("own_", line), ("slot_", 4), ("delta_", rep)):
            outs[name + kind] = ((count, *arrays["w_" + kind].shape), bf16)
    for p, (mode, kind, _, _, cols, _, _) in PIECES.items():
        rows = arrays["w_" + kind].shape[0] // (2 if kind == "out" else 1)
        if mode == "y":
            counts = (("away_", (line, rows)), ("came_", (line, rows)), ("msg_", (rows,)))
        else:
            counts = (("away_", (rows,)), ("own_", (line, 2 * rows)), ("slot_", (4, 2 * rows)), ("msg_", (2 * rows,)))
        for name, lead in counts:
            outs[name + p] = ((*lead, cols), bf16)
    dma = pltpu.SemaphoreType.DMA
    pieces = len(PIECES)
    scratch = {
        **{"v_" + k: pltpu.VMEM(arrays[k].shape, bf16) for k in ("down", "gate_w", "up_w", "proj", "q_w", "kv_w")},
        "gain_acc": pltpu.VMEM((16, width), f32), "dk_acc": pltpu.VMEM((LEN, 128), f32), "dv_acc": pltpu.VMEM((LEN, 128), f32),
        "load_sem": dma((6,)), "y_send": dma((pieces,)), "y_recv": dma((pieces,)),
        "z_send": dma((pieces, 3)), "z_recv": dma((pieces, 4)),
        "d_send": dma((len(REGIONS), rep - 1)), "d_recv": dma((len(REGIONS), rep - 1)), "g_send": dma((n,)), "g_recv": dma((n,)),
    }
    names = ["lengths", "gain", *arrays, *outs, *scratch]
    anywhere = pl.BlockSpec(memory_space=pl.ANY)
    got = pl.pallas_call(
        functools.partial(back_kernel, names=names, line=line, rep=rep, rates=rates),
        in_specs=[pl.BlockSpec(memory_space=pltpu.SMEM), pl.BlockSpec(memory_space=pltpu.VMEM)] + [anywhere] * len(arrays),
        out_specs=[anywhere] * len(outs),
        out_shape=[jax.ShapeDtypeStruct(*v) for v in outs.values()],
        scratch_shapes=list(scratch.values()),
        compiler_params=pltpu.CompilerParams(collective_id=1, has_side_effects=True, vmem_limit_bytes=62 << 20),
        cost_estimate=pl.CostEstimate(flops=200 << 30, bytes_accessed=400 << 20, transcendentals=0),
        name="backward",
    )(lengths, gain, *arrays.values())
    return dict(zip(outs, got))


rate_in = 0.02
rate_out = 0.08
rate_gains = 1.2


def body(
    tokens,
    target,
    doc_lengths,
    corpus_ids,
    corpus_weights,
    w_in,
    w_out,
    gains,
    first_in,
    first_out,
    first_gains,
    second_in,
    second_out,
    second_gains,
    outer_in,
    outer_out,
    outer_gains,
):
    n, rep = lax.axis_size("fsdp"), lax.axis_size("rep")
    line = n // 2
    f, r = lax.axis_index("fsdp"), lax.axis_index("rep")
    z, y = f // 2, f % 2
    direct = by_neighbours(n, rep)
    inside = (z > 0) & (z < line - 1)
    place = jnp.stack([z, inside]).astype(jnp.int32)
    width = w_out.shape[2]
    flat = lambda a: a.reshape(-1, a.shape[-1])
    state_in = first_in[0], second_in[0], w_in
    state_out = flat(first_out[0]), flat(second_out[0]), flat(w_out)
    moved_out = flat(outer_out)
    rates = {"in": rate_in, "out": rate_out}
    rows_in, rows_out = w_in.shape[0], w_out.shape[1]
    x, tgt, lengths = tokens[0], target[0], doc_lengths[0]
    ids = corpus_ids[0][:, None]

    if direct:
        low_gain = jnp.pad(gains.astype(bf16), ((0, 14), (0, 0)))
        fwd = forward(lengths, corpus_weights, ids, dict(x=x, target=tgt), w_in.astype(bf16), w_out.astype(bf16), low_gain, n)
        weight = lambda c: flat(fwd["full_" + c])
        kept = {k: fwd[k] for k in ("c", "middle", "hidden", "second", "gate", "up", "dy", "mixed", "packed", "lse", "first")}
        got = backward(
            lengths, fwd["gain"],
            dict(x=x, target=tgt, proj=weight("proj"), down=weight("down"), q_w=weight("q"), kv_w=weight("kv"),
                 gate_w=weight("gate"), up_w=weight("up"), first_in=state_in[0], second_in=state_in[1], w_in=w_in,
                 first_out=state_out[0], second_out=state_out[1], w_out=state_out[2], **kept),
            n, rep, rates,
        )
        activations, input_grad = got["act"], got["xgrad"]
        gain_share = jnp.sum(got["gain_got"].reshape(n, 2, 8, -1), axis=(0, 2))
        late = (H * HD + 2 * KVH * HD) // TILE
        *held, late_delta = adam_tiles(
            place, got["own_in"], got["slot_in"], *state_in, None, None, None, 0, (0, late, late, 0), rate_in, rep
        )
        near, far = to_group(late_delta, 1, rep), to_group(late_delta, 2, rep)
        rest = w_in.shape[1] // TILE - late
        in_got = adam_tiles(
            place, got["own_in"], got["slot_in"], *state_in, outer_in, got["delta_in"], held,
            0, (late, rest, rest, 0), rate_in, rep,
        )
        out_count = width // TILE
        out_got = adam_tiles(
            place, got["own_out"], got["slot_out"], *state_out, moved_out, got["delta_out"], None,
            0, (0, out_count, out_count, 0), rate_out, rep,
        )
        out_got, in_got = list(out_got), list(in_got)
        far, out_got[0], in_got[0] = lax.optimization_barrier((far, out_got[0], in_got[0]))
        late_terms = [late_delta, near, far, to_group(far, 1, rep)]
        in_grads, in_steps = in_got[:3], outer_tiles(late_terms, outer_in, w_in, in_got[3:], 0, rep)
        out_grads, out_steps = out_got[:3], out_got[3:]
    else:
        gain_full, wq, proj, wf, down = all_weights(w_in, w_out, gains)
        first_low, packed = qkv(x, gain_full, wq)
        mixed, lse = attention(lengths, packed)
        middle, second_low, hidden, d_both, dy, _ = ffn(corpus_weights, x, mixed, tgt, ids, gain_full, proj, wf, down)

        def by_library(a, bs, name):
            block = 2 * BQ if a.shape[1] % (2 * BQ) == 0 else BQ
            every_row = jnp.arange(a.shape[1] // block, dtype=jnp.int32)
            total = grad_rows(every_row, a, bs, block, name=name)
            return lax.psum_scatter(total.reshape(a.shape[1], -1), "fsdp", scatter_dimension=0, tiled=True)[None]

        activations, d_mid, d_low, d_mix, gain_two = mid(
            corpus_weights, middle, hidden, d_both, tgt, ids, gain_full, proj, wf, down
        )
        dq, dk, dv = attention_back(lengths, packed, d_mix, mixed, lse)
        input_grad, gain_one = input_back(x, d_mid, dq, dk, dv, gain_full, wq)
        both = jnp.stack([jnp.sum(gain_one, axis=0), jnp.sum(gain_two, axis=0)])
        gain_share = lax.psum_scatter(both, "fsdp", scatter_dimension=1, tiled=True)
        own_in = jnp.concatenate(
            [
                by_library(first_low, [(dq, 0, H * HD), (dk, 0, KVH * HD), (dv, 0, KVH * HD)], "grad_attn"),
                by_library(second_low, [(d_both, 0, 2 * FF)], "grad_ffn"),
            ],
            axis=2,
        )
        own_out = jnp.concatenate(
            [by_library(mixed, [(d_low, 0, width)], "grad_proj"), by_library(hidden, [(dy, 0, width)], "grad_down")], axis=1
        )

        def all_tiles(own, state, outer, rate):
            count = own.shape[2] // TILE
            *grads, delta = adam_tiles(0 * place, own, None, *state, None, None, None, 0, (0, count, count, 0), rate, rep)
            return grads, outer_tiles(groups_terms(delta, rep), outer, state[2], None, 0, rep)

        in_grads, in_steps = all_tiles(own_in, state_in, outer_in, rate_in)
        out_grads, out_steps = all_tiles(own_out, state_out, moved_out, rate_out)

    first_gains_new, second_gains_new, delta = adam_step(gain_share, first_gains[0], second_gains[0], gains, rate_gains)
    terms = groups_terms(delta, rep)
    sum_gains = (terms[0] + terms[1]) + (terms[2] + terms[3]) if rep == 4 else sum(terms[1:], terms[0])
    diff_gains, outer_gains_new, new_gains = outer_step(sum_gains, outer_gains, gains, rep)

    out_shape = lambda a: a.reshape(2, rows_out, width)
    diff_in, outer_in_new, new_in, copy_in = in_steps
    diff_out, outer_out_new, new_out, copy_out = (out_shape(a) for a in out_steps)
    grad_in, first_in_new, second_in_new = in_grads
    grad_out, first_out_new, second_out_new = (out_shape(a) for a in out_grads)
    return (
        activations[None],
        input_grad[None],
        grad_in[None],
        grad_out[None],
        gain_share[None],
        first_in_new[None],
        first_out_new[None],
        first_gains_new[None],
        second_in_new[None],
        second_out_new[None],
        second_gains_new[None],
        diff_in,
        diff_out,
        diff_gains,
        outer_in_new,
        outer_out_new,
        outer_gains_new,
        new_in,
        new_out,
        new_gains,
        copy_in,
        copy_out,
        new_gains.astype(bf16),
    )


def solution(mesh):
    rows = P(("rep", "fsdp"), None, None)
    pair = P(("rep", "fsdp"), None)
    w_in, w_out, gains = P("fsdp", None), P(None, "fsdp", None), P(None, "fsdp")
    m_in, m_out, m_gains = P("rep", "fsdp", None), P("rep", None, "fsdp", None), P("rep", None, "fsdp")
    weights, moments = (w_in, w_out, gains), (m_in, m_out, m_gains)
    return jax.shard_map(
        body,
        mesh=mesh,
        in_specs=(rows, rows, pair, pair, P(), *weights, *moments, *moments, *weights),
        out_specs=(rows, rows, *moments, *moments, *moments, *weights, *weights, *weights, *weights),
        check_vma=False,
    )
```

```python
import functools
import jax
import jax.numpy as jnp
from jax import lax
from jax.experimental import pallas as pl
from jax.experimental.pallas import tpu as pltpu
from jax.sharding import PartitionSpec as P

H = 16
HD = 64
KVH = 4
FF = 1024
LEN = 1024
NCORP = 8
f32 = jnp.float32
bf16 = jnp.bfloat16
norm_eps = 1e-06
BQ = 256
NT = (((1,), (1,)), ((), ()))
TN = (((0,), (0,)), ((), ()))


def mm(a, b, dims=(((1,), (0,)), ((), ()))):
    return lax.dot_general(a, b, dims, preferred_element_type=f32)


def params(**kw):
    return pltpu.CompilerParams(vmem_limit_bytes=60 << 20, **kw)


def one(shape, index):
    return pl.BlockSpec(shape, index, pipeline_mode=pl.Buffered(1))


def qkv_kernel(x_ref, g_ref, w_ref, first_ref, packed_ref):
    x = x_ref[...].astype(f32)
    r = lax.rsqrt(jnp.mean(x * x, axis=-1, keepdims=True) + norm_eps)
    first = (x * r * g_ref[0:1, :]).astype(bf16)
    first_ref[...] = first
    packed_ref[...] = mm(first, w_ref[...]).astype(bf16)


def qkv(x, gains, w):
    rows, width = x.shape
    cols = w.shape[1]
    return pl.pallas_call(
        qkv_kernel,
        grid=(rows // BQ,),
        in_specs=[
            pl.BlockSpec((BQ, width), lambda i: (i, 0)),
            one(gains.shape, lambda i: (0, 0)),
            one((width, cols), lambda i: (0, 0)),
        ],
        out_specs=[
            pl.BlockSpec((BQ, width), lambda i: (i, 0)),
            pl.BlockSpec((BQ, cols), lambda i: (i, 0)),
        ],
        out_shape=[
            jax.ShapeDtypeStruct((rows, width), bf16),
            jax.ShapeDtypeStruct((rows, cols), bf16),
        ],
        compiler_params=params(),
        cost_estimate=pl.CostEstimate(
            flops=2 * rows * width * cols, bytes_accessed=rows * width * 4 + width * cols * 2, transcendentals=0
        ),
        name="norm_qkv",
    )(x, gains, w)


def doc_start(lengths_ref, position):
    end = jnp.int32(0)
    start = jnp.zeros_like(position)
    for j in range(lengths_ref.shape[0]):
        end = end + lengths_ref[j]
        start = jnp.where(position >= end, end, start)
    return start


def key_blocks(lengths_ref, i):
    first_row = i * BQ
    return i + 1 - doc_start(lengths_ref, first_row) // BQ


def max_blocks():
    return LEN // (2 * BQ) + 1


def attention_step(len_ref, i, count, q_ref, k_ref, v_ref, o_ref, lse_ref):
    row = i * BQ + lax.broadcasted_iota(jnp.int32, (BQ, 1), 0)
    start = doc_start(len_ref, row)
    lane = lax.broadcasted_iota(jnp.int32, (BQ, 128), 1)
    for nb in range(1, max_blocks() + 1):

        @pl.when(count == nb)
        def _():
            span = nb * BQ
            base = pl.multiple_of((i - (nb - 1)) * BQ, BQ)
            col = base + lax.broadcasted_iota(jnp.int32, (BQ, span), 1)
            bias = jnp.where((col >= start) & (col <= row), 0.0, -1e30)
            k2 = k_ref[pl.ds(base, span), :]
            v2 = v_ref[pl.ds(base, span), :]
            tile = jnp.zeros((BQ, 128), f32)
            outs = []
            for kv in range(2):
                k = k2[:, kv * HD : (kv + 1) * HD]
                v = v2[:, kv * HD : (kv + 1) * HD]
                for g in range(H // KVH):
                    h = kv * (H // KVH) + g
                    q = q_ref[:, h * HD : (h + 1) * HD] * jnp.asarray(HD**-0.5, bf16)
                    s = mm(q, k, NT) + bias
                    m = jnp.max(s, axis=-1, keepdims=True)
                    e = jnp.exp(s - m)
                    total = jnp.sum(e, axis=-1, keepdims=True)
                    o = mm(e.astype(bf16), v) * (1.0 / total)
                    outs.append(o.astype(bf16))
                    tile = jnp.where(lane == h, m + jnp.log(total), tile)
            o_ref[...] = jnp.concatenate(outs, axis=1)
            lse_ref[...] = tile.T[0:8, :]


def attn_kernel(len_ref, *refs):
    i = pl.program_id(0)
    attention_step(len_ref, i, key_blocks(len_ref, i), *refs)


def attention(lengths, packed):
    qw = H // 2 * HD
    kcol = H * HD // 128
    vcol = kcol + KVH * HD // 128
    return pl.pallas_call(
        attn_kernel,
        grid_spec=pltpu.PrefetchScalarGridSpec(
            num_scalar_prefetch=1,
            grid=(LEN // BQ, 2),
            in_specs=[
                pl.BlockSpec((BQ, qw), lambda i, p, s: (i, p)),
                pl.BlockSpec((LEN, 128), lambda i, p, s: (0, kcol + p)),
                pl.BlockSpec((LEN, 128), lambda i, p, s: (0, vcol + p)),
            ],
            out_specs=[
                pl.BlockSpec((BQ, qw), lambda i, p, s: (i, p)),
                pl.BlockSpec((8, BQ), lambda i, p, s: (p, i)),
            ],
        ),
        out_shape=[
            jax.ShapeDtypeStruct((LEN, H * HD), bf16),
            jax.ShapeDtypeStruct((H, LEN), f32),
        ],
        compiler_params=params(),
        cost_estimate=pl.CostEstimate(flops=4 * H * LEN * LEN * HD * 4, bytes_accessed=1 << 24, transcendentals=0),
        name="attention",
    )(lengths, packed, packed, packed)


def attention_back_step(len_ref, i, q_ref, k_ref, v_ref, d_ref, o_ref, lse_ref, dq_ref, dk_acc, dv_acc, count=None):
    if count is None:
        count = jnp.minimum(i + 1, max_blocks())
    row = i * BQ + lax.broadcasted_iota(jnp.int32, (1, BQ), 1)
    start = doc_start(len_ref, row)
    lane = lax.broadcasted_iota(jnp.int32, (BQ, 128), 1)
    group = H // KVH
    scale = jnp.asarray(HD**-0.5, bf16)
    tile = jnp.zeros((BQ, 128), f32)
    for h in range(2 * group):
        cols = slice(h * HD, (h + 1) * HD)
        dot = jnp.sum(d_ref[:, cols].astype(f32) * o_ref[:, cols].astype(f32), axis=-1, keepdims=True)
        tile = jnp.where(lane == h, dot, tile)
    inner = tile.T
    for nb in range(1, max_blocks() + 1):

        @pl.when(count == nb)
        def _():
            span = nb * BQ
            base = pl.multiple_of((i - (nb - 1)) * BQ, BQ)
            key = base + lax.broadcasted_iota(jnp.int32, (span, BQ), 0)
            bias = jnp.where((key >= start) & (key <= row), 0.0, -1e30)
            k2 = k_ref[pl.ds(base, span), :]
            v2 = v_ref[pl.ds(base, span), :]
            dks, dvs = [], []
            for kv in range(2):
                k = k2[:, kv * HD : (kv + 1) * HD]
                v = v2[:, kv * HD : (kv + 1) * HD]
                dk = dv = None
                dqs = []
                for g in range(group):
                    h = kv * group + g
                    cols = slice(h * HD, (h + 1) * HD)
                    q = q_ref[:, cols] * scale
                    d = d_ref[:, cols]
                    s = mm(k, q, NT) + bias
                    p = jnp.exp(s - lse_ref[h : h + 1, :])
                    dp = mm(v, d, NT)
                    ds = (p * (dp - inner[h : h + 1, :])).astype(bf16)
                    dv_h = mm(p.astype(bf16), d)
                    dk_h = mm(ds, q)
                    dv = dv_h if dv is None else dv + dv_h
                    dk = dk_h if dk is None else dk + dk_h
                    dqs.append(mm(k, ds, TN))
                dq = jnp.concatenate(dqs, axis=0) * (HD**-0.5)
                dq_ref[:, kv * group * HD : (kv + 1) * group * HD] = dq.T.astype(bf16)
                dks.append(dk)
                dvs.append(dv)
            dk_acc[pl.ds(base, span), :] += jnp.concatenate(dks, axis=1)
            dv_acc[pl.ds(base, span), :] += jnp.concatenate(dvs, axis=1)


def attn_back_kernel(len_ref, q_ref, k_ref, v_ref, d_ref, o_ref, lse_ref, dq_ref, dk_ref, dv_ref, dk_acc, dv_acc):
    i = pl.program_id(1)

    @pl.when(i == 0)
    def _():
        dk_acc[...] = jnp.zeros_like(dk_acc)
        dv_acc[...] = jnp.zeros_like(dv_acc)

    attention_back_step(
        len_ref, i, q_ref, k_ref, v_ref, d_ref, o_ref, lse_ref, dq_ref, dk_acc, dv_acc, key_blocks(len_ref, i)
    )

    @pl.when(i == pl.num_programs(1) - 1)
    def _():
        dk_ref[...] = dk_acc[...].astype(bf16)
        dv_ref[...] = dv_acc[...].astype(bf16)


def attention_back(lengths, packed, d_mixed, mixed, lse):
    qw = H // 2 * HD
    kcol = H * HD // 128
    vcol = kcol + KVH * HD // 128
    return pl.pallas_call(
        attn_back_kernel,
        grid_spec=pltpu.PrefetchScalarGridSpec(
            num_scalar_prefetch=1,
            grid=(2, LEN // BQ),
            in_specs=[
                pl.BlockSpec((BQ, qw), lambda p, i, s: (i, p)),
                pl.BlockSpec((LEN, 128), lambda p, i, s: (0, kcol + p)),
                pl.BlockSpec((LEN, 128), lambda p, i, s: (0, vcol + p)),
                pl.BlockSpec((BQ, qw), lambda p, i, s: (i, p)),
                pl.BlockSpec((BQ, qw), lambda p, i, s: (i, p)),
                pl.BlockSpec((8, BQ), lambda p, i, s: (p, i)),
            ],
            out_specs=[
                pl.BlockSpec((BQ, qw), lambda p, i, s: (i, p)),
                pl.BlockSpec((LEN, 128), lambda p, i, s: (0, p)),
                pl.BlockSpec((LEN, 128), lambda p, i, s: (0, p)),
            ],
            scratch_shapes=[pltpu.VMEM((LEN, 128), f32), pltpu.VMEM((LEN, 128), f32)],
        ),
        out_shape=[
            jax.ShapeDtypeStruct((LEN, H * HD), bf16),
            jax.ShapeDtypeStruct((LEN, KVH * HD), bf16),
            jax.ShapeDtypeStruct((LEN, KVH * HD), bf16),
        ],
        compiler_params=params(),
        cost_estimate=pl.CostEstimate(flops=10 * H * LEN * LEN * HD * 4, bytes_accessed=1 << 24, transcendentals=0),
        name="attention_back",
    )(lengths, packed, packed, packed, d_mixed, mixed, lse)


def token_weight(table_ref, ids):
    weight = jnp.zeros(ids.shape, f32)
    for j in range(table_ref.shape[0]):
        weight = jnp.where(ids == j, table_ref[j].astype(f32) * 0.25, weight)
    return weight


def ffn_kernel(table_ref, x_ref, mixed_ref, t_ref, ids_ref, g_ref, proj_ref, wf_ref, down_ref,
               middle_ref, second_ref, hidden_ref, dboth_ref, dy_ref, c_ref):
    middle = x_ref[...].astype(f32) + mm(mixed_ref[...], proj_ref[...])
    middle_ref[...] = middle
    r = lax.rsqrt(jnp.mean(middle * middle, axis=-1, keepdims=True) + norm_eps)
    second = (middle * r * g_ref[1:2, :]).astype(bf16)
    second_ref[...] = second
    c = token_weight(table_ref, ids_ref[...])
    c_ref[...] = jnp.broadcast_to(c, c_ref.shape)
    dy = (c * t_ref[...].astype(f32)).astype(bf16)
    dy_ref[...] = dy
    step = 512
    for c in range(0, FF, step):
        gate = mm(second, wf_ref[:, c : c + step])
        up = mm(second, wf_ref[:, FF + c : FF + c + step])
        dh = mm(dy, down_ref[c : c + step, :], NT)
        sig = jax.nn.sigmoid(gate)
        silu = gate * sig
        hidden_ref[:, c : c + step] = (silu * up).astype(bf16)
        dboth_ref[:, c : c + step] = (dh * up * sig * (1.0 + gate * (1.0 - sig))).astype(bf16)
        dboth_ref[:, FF + c : FF + c + step] = (dh * silu).astype(bf16)


def ffn(table, x, mixed, target, ids, gains, proj, wf, down):
    width = x.shape[1]
    rowb = lambda n: pl.BlockSpec((BQ, n), lambda i, s: (i, 0))
    whole = lambda a: one(a.shape, lambda i, s: (0, 0))
    return pl.pallas_call(
        ffn_kernel,
        grid_spec=pltpu.PrefetchScalarGridSpec(
            num_scalar_prefetch=1,
            grid=(LEN // BQ,),
            in_specs=[rowb(width), rowb(H * HD), rowb(width), rowb(1), whole(gains), whole(proj), whole(wf), whole(down)],
            out_specs=[rowb(width), rowb(width), rowb(FF), rowb(2 * FF), rowb(width), rowb(128)],
        ),
        out_shape=[
            jax.ShapeDtypeStruct((LEN, width), f32),
            jax.ShapeDtypeStruct((LEN, width), bf16),
            jax.ShapeDtypeStruct((LEN, FF), bf16),
            jax.ShapeDtypeStruct((LEN, 2 * FF), bf16),
            jax.ShapeDtypeStruct((LEN, width), bf16),
            jax.ShapeDtypeStruct((LEN, 128), f32),
        ],
        compiler_params=params(),
        cost_estimate=pl.CostEstimate(flops=2 * LEN * width * FF * 4, bytes_accessed=40 << 20, transcendentals=0),
        name="ffn",
    )(table, x, mixed, target, ids, gains, proj, wf, down)


def mid_kernel(table_ref, middle_ref, hidden_ref, dboth_ref, t_ref, ids_ref, g_ref, proj_ref, wf_ref, down_ref,
               act_ref, dmid_ref, dlow_ref, dmix_ref, gain_ref):
    middle = middle_ref[...]
    act_ref[...] = (middle + mm(hidden_ref[...], down_ref[...])).astype(bf16)
    r = lax.rsqrt(jnp.mean(middle * middle, axis=-1, keepdims=True) + norm_eps)
    n2 = middle * r
    ds2 = mm(dboth_ref[...], wf_ref[...], NT)
    prod = ds2 * n2
    part = jnp.sum(prod.reshape(BQ // 8, 8, prod.shape[1]), axis=0)

    @pl.when(pl.program_id(0) == 0)
    def _():
        gain_ref[...] = jnp.zeros_like(gain_ref)

    gain_ref[...] += part
    g = g_ref[1:2, :]
    e2 = ds2 * g
    dy = token_weight(table_ref, ids_ref[...]) * t_ref[...].astype(f32)
    dmid = dy + r * (e2 - n2 * jnp.mean(prod * g, axis=-1, keepdims=True))
    dmid_ref[...] = dmid
    low = dmid.astype(bf16)
    dlow_ref[...] = low
    dmix_ref[...] = mm(low, proj_ref[...], NT).astype(bf16)


def mid(table, middle, hidden, dboth, target, ids, gains, proj, wf, down):
    width = middle.shape[1]
    rowb = lambda n: pl.BlockSpec((BQ, n), lambda i, s: (i, 0))
    whole = lambda a: one(a.shape, lambda i, s: (0, 0))
    return pl.pallas_call(
        mid_kernel,
        grid_spec=pltpu.PrefetchScalarGridSpec(
            num_scalar_prefetch=1,
            grid=(LEN // BQ,),
            in_specs=[rowb(width), rowb(FF), rowb(2 * FF), rowb(width), rowb(1), whole(gains), whole(proj), whole(wf), whole(down)],
            out_specs=[rowb(width), rowb(width), rowb(width), rowb(H * HD), pl.BlockSpec((8, width), lambda i, s: (0, 0))],
        ),
        out_shape=[
            jax.ShapeDtypeStruct((LEN, width), bf16),
            jax.ShapeDtypeStruct((LEN, width), f32),
            jax.ShapeDtypeStruct((LEN, width), bf16),
            jax.ShapeDtypeStruct((LEN, H * HD), bf16),
            jax.ShapeDtypeStruct((8, width), f32),
        ],
        compiler_params=params(),
        cost_estimate=pl.CostEstimate(flops=2 * LEN * width * FF * 4, bytes_accessed=40 << 20, transcendentals=0),
        name="mid",
    )(table, middle, hidden, dboth, target, ids, gains, proj, wf, down)


def input_kernel(x_ref, dmid_ref, dq_ref, dk_ref, dv_ref, g_ref, w_ref, out_ref, gain_ref):
    x = x_ref[...].astype(f32)
    r = lax.rsqrt(jnp.mean(x * x, axis=-1, keepdims=True) + norm_eps)
    n1 = x * r
    q, k = H * HD, H * HD + KVH * HD
    ds1 = mm(dq_ref[...], w_ref[:, :q], NT) + mm(dk_ref[...], w_ref[:, q:k], NT) + mm(dv_ref[...], w_ref[:, k:], NT)
    prod = ds1 * n1
    part = jnp.sum(prod.reshape(BQ // 8, 8, prod.shape[1]), axis=0)

    @pl.when(pl.program_id(0) == 0)
    def _():
        gain_ref[...] = jnp.zeros_like(gain_ref)

    gain_ref[...] += part
    g = g_ref[0:1, :]
    out = dmid_ref[...] + r * (ds1 * g - n1 * jnp.mean(prod * g, axis=-1, keepdims=True))
    out_ref[...] = out.astype(bf16)


def input_back(x, dmid, dq, dk, dv, gains, w):
    width = x.shape[1]
    rowb = lambda n: pl.BlockSpec((BQ, n), lambda i: (i, 0))
    whole = lambda a: one(a.shape, lambda i: (0, 0))
    return pl.pallas_call(
        input_kernel,
        grid=(LEN // BQ,),
        in_specs=[rowb(width), rowb(width), rowb(H * HD), rowb(KVH * HD), rowb(KVH * HD), whole(gains), whole(w)],
        out_specs=[rowb(width), pl.BlockSpec((8, width), lambda i: (0, 0))],
        out_shape=[jax.ShapeDtypeStruct((LEN, width), bf16), jax.ShapeDtypeStruct((8, width), f32)],
        compiler_params=params(),
        cost_estimate=pl.CostEstimate(flops=2 * LEN * width * 1536, bytes_accessed=24 << 20, transcendentals=0),
        name="input_back",
    )(x, dmid, dq, dk, dv, gains, w)


def grad_kernel(pick_ref, a_ref, *refs):
    out_ref = refs[-1]
    b_refs = refs[:-1]
    add_ref = None
    if len(b_refs) > 1 and len(b_refs[-1].shape) == 3:
        add_ref, b_refs = b_refs[-1], b_refs[:-1]
    col = 0
    a = a_ref[...]
    for b_ref in b_refs:
        n = b_ref.shape[1]
        g = mm(a, b_ref[...], TN)
        if add_ref is not None:
            g = g + add_ref[0, :, col : col + n].astype(f32)
        out_ref[0, :, col : col + n] = g.astype(bf16)
        col += n


def grad_rows(pick, a, bs, rows, add=None, name="grad"):
    cols = sum(width for _, _, width in bs)
    count = pick.shape[0]
    specs = [pl.BlockSpec((LEN, rows), lambda j, p: (0, p[j]))]
    specs += [one((LEN, width), functools.partial(lambda at, j, p: (0, at), at)) for _, at, width in bs]
    ops = [a, *(b for b, _, _ in bs)]
    if add is not None:
        specs.append(pl.BlockSpec((1, rows, cols), lambda j, p: (j, 0, 0)))
        ops.append(add)
    return pl.pallas_call(
        grad_kernel,
        grid_spec=pltpu.PrefetchScalarGridSpec(
            num_scalar_prefetch=1,
            grid=(count,),
            in_specs=specs,
            out_specs=pl.BlockSpec((1, rows, cols), lambda j, p: (j, 0, 0)),
        ),
        out_shape=jax.ShapeDtypeStruct((count, rows, cols), bf16),
        compiler_params=params(),
        cost_estimate=pl.CostEstimate(flops=2 * LEN * rows * count * cols, bytes_accessed=12 << 20, transcendentals=0),
        name=name,
    )(pick, *ops)


beta_first = 0.9
beta_second = 0.95
adam_eps = 1e-08
decay_rate = 0.1
outer_decay = 0.5
outer_rate = 0.7
STEP = 10


def adam_step(grad, first, second, weight, rate):
    first_new = beta_first * first + (1.0 - beta_first) * grad
    second_new = beta_second * second + (1.0 - beta_second) * grad * grad
    first_unbiased = first_new * (1.0 / (1.0 - beta_first**STEP))
    ratio = first_unbiased / (jnp.sqrt(second_new * (1.0 / (1.0 - beta_second**STEP))) + adam_eps)
    local = weight - rate * (ratio + decay_rate * weight)
    return first_new, second_new, weight - local


def outer_step(delta_sum, momentum, weight, groups):
    average = delta_sum * (1.0 / groups)
    momentum_new = outer_decay * momentum + average
    return average, momentum_new, weight - outer_rate * (average + outer_decay * momentum_new)


def adam_kernel(place_ref, own_ref, *refs, slots, deltas, rate, groups):
    refs = list(refs)
    grad = own_ref[0].astype(f32)
    if slots:
        b, c, d = (refs.pop(0)[0].astype(f32) for _ in range(3))
        grad = grad + b + c + jnp.where(place_ref[1] == 1, d, 0.0)
    first_ref, second_ref, w_ref = refs[:3]
    first_new, second_new, delta = adam_step(grad, first_ref[...], second_ref[...], w_ref[...], rate)
    outs = refs[-7:] if deltas else refs[-4:]
    outs[0][...] = grad
    outs[1][...] = first_new
    outs[2][...] = second_new
    if not deltas:
        outs[3][...] = delta.astype(bf16)
        return
    outer_ref, delta_ref = refs[3:5]
    d = [delta_ref[k].astype(f32) for k in range(delta_ref.shape[0])]
    write_outer((d[0] + d[1]) + (d[2] + d[3]), outer_ref, w_ref, outs[3:], groups)


def write_outer(total, outer_ref, w_ref, outs, groups):
    average, momentum, weight = outer_step(total, outer_ref[...], w_ref[...], groups)
    outs[0][...] = average
    outs[1][...] = momentum
    outs[2][...] = weight
    outs[3][...] = weight.astype(bf16)


TILE = 512
ROW_BLOCKS = 2


def adam_tiles(place, own, slots, first, second, w, outer, deltas, held, own_at, tiles, rate, groups):
    total, rows = w.shape[0], w.shape[0] // ROW_BLOCKS
    start, count, hole, skip = tiles
    at = lambda j: start + j + jnp.where(j >= hole, skip, 0)
    state = pl.BlockSpec((rows, TILE), lambda i, j, p: (i, at(j)))
    plane = lambda pick: pl.BlockSpec((1, rows, TILE), lambda i, j, p: (pick(p), i, at(j) - own_at))
    full = jax.ShapeDtypeStruct(w.shape, f32)
    ops, specs = [own], [plane(lambda p: p[0])]
    if slots is not None:
        ops += [slots] * 3
        specs += [plane(lambda p: 1), plane(lambda p: 2), plane(lambda p: 2 + p[1])]
    ops += [first, second, w]
    specs += [state] * 3
    out_shape, out_specs = [full] * 3, [state] * 3
    if deltas is not None:
        ops += [outer, deltas]
        specs += [state, pl.BlockSpec((deltas.shape[0], rows, TILE), lambda i, j, p: (0, i, at(j)))]
        out_shape += [full] * 3 + [jax.ShapeDtypeStruct(w.shape, bf16)]
        out_specs += [state] * 4
    else:
        out_shape.append(jax.ShapeDtypeStruct((total, count * TILE), bf16))
        out_specs.append(pl.BlockSpec((rows, TILE), lambda i, j, p: (i, j)))
    aliases = {}
    if held is not None:
        aliases = {1 + len(ops) + k: k for k in range(3)}
        ops += list(held)
        specs += [pl.BlockSpec(memory_space=pl.ANY)] * 3
    return pl.pallas_call(
        functools.partial(adam_kernel, slots=slots is not None, deltas=deltas is not None, rate=rate, groups=groups),
        grid_spec=pltpu.PrefetchScalarGridSpec(
            num_scalar_prefetch=1, grid=(ROW_BLOCKS, count), in_specs=specs, out_specs=out_specs
        ),
        out_shape=out_shape,
        input_output_aliases=aliases,
        compiler_params=params(),
        cost_estimate=pl.CostEstimate(flops=0, bytes_accessed=total * count * TILE * 48, transcendentals=0),
        name="adam",
    )(place, *ops)


def outer_kernel(*refs, terms, groups):
    d = [ref[...].astype(f32) for ref in refs[:terms]]
    total = (d[0] + d[1]) + (d[2] + d[3]) if terms == 4 else sum(d[1:], d[0])
    write_outer(total, refs[terms], refs[terms + 1], refs[-4:], groups)


def outer_tiles(deltas, outer, w, held, start, groups):
    total, cols = deltas[0].shape
    rows = total // ROW_BLOCKS
    state = pl.BlockSpec((rows, TILE), lambda i, j: (i, start + j))
    full = jax.ShapeDtypeStruct(w.shape, f32)
    ops = [*deltas, outer, w]
    specs = [pl.BlockSpec((rows, TILE), lambda i, j: (i, j))] * len(deltas) + [state] * 2
    aliases = {}
    if held is not None:
        aliases = {len(ops) + k: k for k in range(4)}
        ops += list(held)
        specs += [pl.BlockSpec(memory_space=pl.ANY)] * 4
    return pl.pallas_call(
        functools.partial(outer_kernel, terms=len(deltas), groups=groups),
        grid=(ROW_BLOCKS, cols // TILE),
        in_specs=specs,
        out_specs=[state] * 4,
        out_shape=[full, full, full, jax.ShapeDtypeStruct(w.shape, bf16)],
        input_output_aliases=aliases,
        compiler_params=params(),
        cost_estimate=pl.CostEstimate(flops=0, bytes_accessed=total * cols * 24, transcendentals=0),
        name="outer",
    )(*ops)


def to_group(a, k, rep):
    return lax.ppermute(a, "rep", [(i, i ^ k) for i in range(rep)])


def groups_terms(delta, rep):
    if rep != 4:
        return [delta] + [to_group(delta, k, rep) for k in range(1, rep)]
    near, far = to_group(delta, 1, rep), to_group(delta, 2, rep)
    return [delta, near, far, to_group(far, 1, rep)]


def by_neighbours(n, rep):
    return n == 8 and rep == 4


def all_weights(w_in, w_out, gains):
    split = H * HD + 2 * KVH * HD
    low_in, low_out = w_in.astype(bf16), w_out.astype(bf16)
    low_gains = jnp.pad(gains.astype(bf16), ((0, 62), (0, 0)))
    shards = [low_gains, low_in[:, :split], low_out[0], low_in[:, split:], low_out[1]]
    full = [lax.all_gather(a, "fsdp") for a in shards]
    gain_full = full[0][:, :8].astype(f32).transpose(1, 0, 2).reshape(8, -1)
    return [gain_full] + [a.reshape(-1, a.shape[-1]) for a in full[1:]]


CHUNKS = ("q", "kv", "proj", "gate", "up", "down")
IN_COLUMNS = {"q": (0, H * HD), "kv": (H * HD, 2 * KVH * HD), "gate": (H * HD + 2 * KVH * HD, FF), "up": (H * HD + 2 * KVH * HD + FF, FF)}
CHIP_SHARE = {"q": 48, "kv": 48, "proj": 32, "gate": 48, "up": 48, "down": 16}
PLAN = {
    "begin": (
        (("z", "q", 0), ("z", "kv", 0), ("z", "q", 1), ("y", "q", 0), ("z", "kv", 1), ("y", "kv", 0), ("z", "proj", 0), ("y", "q", 1), ("z", "kv", 2), ("z", "q", 2),),
    ),
    "dy": (
        (("y", "kv", 2), ("z", "q", 3), ("x", "kv", 0), ("z", "kv", 3), ("z", "proj", 1), ("x", "q", 1), ("z", "gate", 0), ("y", "q", 2), ("y", "q", 3), ("y", "kv", 1),),
    ),
    "norm": (
        (("y", "kv", 3), ("x", "q", 0), ("z", "proj", 2), ("x", "kv", 2),),
        (("x", "q", 2), ("z", "gate", 1),),
        (("x", "q", 3), ("c", "q", 1),),
        (("c", "q", 2), ("x", "kv", 1), ("z", "proj", 3), ("y", "proj", 0), ("z", "up", 0), ("x", "kv", 3), ("y", "gate", 0), ("z", "down", 0), ("c", "kv", 2), ("c", "kv", 0), ("z", "gate", 2), ("y", "proj", 2), ("c", "q", 0), ("c", "q", 3), ("y", "proj", 1), ("c", "kv", 1), ("c", "kv", 3),),
    ),
    "qkv": (
        (),
        (),
        (("y", "up", 0),),
        (("y", "gate", 1), ("x", "proj", 2), ("z", "up", 1), ("z", "gate", 3), ("y", "proj", 3),),
    ),
    "attn": (
        (("z", "down", 1),),
        (("z", "up", 2),),
        (("y", "up", 1), ("x", "up", 0),),
        (("z", "down", 2), ("x", "proj", 0), ("x", "proj", 3), ("c", "up", 0), ("y", "gate", 2), ("y", "down", 0),),
        (("x", "gate", 1),),
        (("c", "proj", 0), ("z", "up", 3), ("y", "up", 2), ("c", "gate", 1), ("x", "proj", 1), ("c", "proj", 3),),
        (),
        (("y", "gate", 3), ("x", "up", 1), ("x", "down", 0), ("y", "up", 3), ("z", "down", 3), ("c", "proj", 1), ("c", "proj", 2), ("y", "down", 2),),
    ),
    "proj": (
        (("x", "gate", 2),),
        (("x", "gate", 3), ("y", "down", 3), ("y", "down", 1),),
        (("c", "gate", 2), ("c", "down", 0), ("x", "gate", 0), ("c", "up", 1),),
        (("x", "up", 2), ("x", "down", 2), ("c", "gate", 0), ("c", "gate", 3),),
    ),
    "gate": (
        (),
        (("x", "up", 3), ("x", "down", 1), ("c", "up", 2),),
        (("x", "down", 3),),
        (("c", "up", 3),),
    ),
    "up": (
        (("c", "down", 1),),
        (),
        (),
        (("c", "down", 2), ("c", "down", 3),),
    ),
}


def forward_kernel(*refs, names, line):
    R = dict(zip(names, refs))
    r, f = lax.axis_index("rep"), lax.axis_index("fsdp")
    x, core, z, y = r // 2, r % 2, f // 2, f % 2
    n = 2 * line
    to_y = (r, f + 1 - 2 * y)
    to_x = (r + 2 - 4 * x, f)
    to_core = (r + 1 - 2 * core, f)
    barrier = pltpu.get_barrier_semaphore()
    peers = [(r, lax.rem(f + step, n)) for step in range(1, n)]
    for to in (*peers, to_x, to_core):
        pl.semaphore_signal(barrier, inc=1, device_id=to, device_id_type=pl.DeviceIdType.MESH)
    pl.semaphore_wait(barrier, n + 1)

    def remote(src, dst, send, recv, to):
        return pltpu.make_async_remote_copy(
            src_ref=src, dst_ref=dst, send_sem=send, recv_sem=recv, device_id=to, device_id_type=pl.DeviceIdType.MESH
        )

    held = {c: R["v_" + c] if "v_" + c in R else R["full_" + c] for c in CHUNKS}
    low = {c: R["low_in"].at[:, pl.ds(at, cols)] for c, (at, cols) in IN_COLUMNS.items()}
    low |= {"proj": R["low_out"].at[0], "down": R["low_out"].at[1]}
    rows_of = {c: R["low_out"].shape[1] if c in ("proj", "down") else R["low_in"].shape[0] for c in CHUNKS}
    item = lambda side, d: 0 if d == 0 else 2 * d - 1 + (side > 0)
    exists = lambda side, d: None if d == 0 else (z - d >= 0 if side < 0 else z + d < line)

    def guard(cond, fn):
        if cond is None:
            fn()
        else:
            pl.when(cond)(fn)

    def copy(src, dst, stage, c, side, d, to):
        m, k = CHUNKS.index(c), item(side, d)
        return remote(src, dst, R["f_send"].at[stage, m, k], R["f_recv"].at[stage, m, k], to)

    def portion(c):
        half, share = rows_of[c] // 2, CHIP_SHARE[c]
        return pl.ds(pl.multiple_of(core * half + x * share, 16), half - share)

    def line_copy(c, side, d):
        plane = z + side * (d - 1)
        dst = held[c].at[plane * 2 + y, portion(c), :]
        src = low[c].at[portion(c), :] if d == 1 else dst
        return copy(src, dst, 0, c, side, d, (r, f - 2 * side))

    def line_arrival(c, side, d):
        dst = held[c].at[(z + side * d) * 2 + y, portion(c), :]
        return copy(dst, dst, 0, c, side, d, to_y)

    def y_copy(c, side, d):
        dst = held[c].at[(z + side * d) * 2 + y, portion(c), :]
        return copy(low[c].at[portion(c), :] if d == 0 else dst, dst, 1, c, side, d, to_y)

    def both_copy(c, side, d, start, rows, stage, to):
        planes = pl.ds(z * 2 + 1 - y, 1) if d == 0 else pl.ds((z + side * d) * 2, 2)
        ref = held[c].at[planes, pl.ds(pl.multiple_of(start, 16), rows), :]
        return copy(ref, ref, stage, c, side, d, to)

    def x_copy(c, side, d):
        half, share = rows_of[c] // 2, CHIP_SHARE[c]
        return both_copy(c, side, d, core * half + x * (half - share), share, 2, to_x)

    def core_copy(c, side, d):
        half = rows_of[c] // 2
        return both_copy(c, side, d, core * half, half, 3, to_core)

    def onward(side):
        return z < line - 1 if side < 0 else z > 0

    def line_stage(c, side, d):
        if d == 0:
            for way in (-1, 1):
                pl.when(onward(way))(lambda way=way: line_copy(c, way, 1).start())
        else:
            line_arrival(c, side, d).wait_recv()
            if d < line - 1:
                pl.when(onward(side))(lambda: line_copy(c, side, d + 1).start())
        y_copy(c, side, d).start()

    def y_stage(c, side, d):
        y_copy(c, side, d).wait_recv()
        x_copy(c, side, d).start()

    def x_stage(c, side, d):
        x_copy(c, side, d).wait_recv()
        core_copy(c, side, d).start()

    def core_stage(c, side, d):
        core_copy(c, side, d).wait_recv()

    stages = {"z": line_stage, "y": y_stage, "x": x_stage, "c": core_stage}
    sides = lambda d: (1,) if d == 0 else (-1, 1)

    def act(todo):
        for hop, c, d in todo:
            for side in sides(d):
                guard(exists(side, d), functools.partial(stages[hop], c, side, d))

    def serve(phase, at):
        for step, todo in enumerate(PLAN[phase]):
            if todo:

                @pl.when(at == step)
                def _():
                    act(todo)

    def keep(c):
        return pltpu.make_async_copy(R["v_" + c], R["full_" + c], R["keep_sem"].at[CHUNKS.index(c)])

    def place_own(c):
        return pltpu.make_async_copy(low[c], held[c].at[f], R["own_sem"].at[CHUNKS.index(c)])

    gain_send = lambda step: remote(R["low_gain"], R["v_gain"].at[f], R["g_send"].at[step - 1], R["g_recv"].at[step - 1], peers[step - 1])
    for step in range(1, n):
        gain_send(step).start()
    own_gain = pltpu.make_async_copy(R["low_gain"], R["v_gain"].at[f], R["g_send"].at[n - 1])
    own_gain.start()
    act(PLAN["begin"][0])
    for c in CHUNKS:
        place_own(c).start()

    rowb = lambda width: pl.BlockSpec((BQ, width), lambda i: (i, 0))
    width = R["x"].shape[1]
    steps = LEN // BQ

    def run(body, grid, ins, outs):
        pltpu.emit_pipeline(body, grid=grid, in_specs=[s for _, s in ins], out_specs=[s for _, s in outs])(
            *[R[a] for a, _ in ins], *[R[a] for a, _ in outs]
        )

    def target_step(t_ref, dy_ref, c_ref):
        at = pl.multiple_of(pl.program_id(0) * BQ, BQ)
        c = token_weight(R["table"], R["ids"][pl.ds(at, BQ), :])
        c_ref[...] = jnp.broadcast_to(c, c_ref.shape)
        dy_ref[...] = (c * t_ref[...].astype(f32)).astype(bf16)

    run(target_step, (steps,), [("target", rowb(width))], [("dy", rowb(width)), ("c", rowb(128))])
    act(PLAN["dy"][0])
    own_gain.wait()
    for step in range(1, n):
        gain_send(step).wait()
    gains = jnp.concatenate([R["v_gain"][k] for k in range(n)], axis=1).astype(f32)[0:8]
    R["gain_rows"][...] = gains
    keep_gain = pltpu.make_async_copy(R["gain_rows"], R["gain"], R["g_send"].at[n - 1])
    keep_gain.start()

    def norm_step(x_ref, first_ref):
        v = x_ref[...].astype(f32)
        inv = lax.rsqrt(jnp.mean(v * v, axis=-1, keepdims=True) + norm_eps)
        first_ref[...] = (v * inv * R["gain_rows"][0:1, :]).astype(bf16)

    def norm_body(x_ref, first_ref):
        norm_step(x_ref, first_ref)
        serve("norm", pl.program_id(0))

    run(norm_body, (steps,), [("x", rowb(width))], [("first", rowb(width))])
    for c in CHUNKS:
        place_own(c).wait()
    whole = lambda c: held[c][...].reshape(-1, held[c].shape[2])

    keep("q").start()
    keep("kv").start()

    def qkv_body(first_ref, packed_ref):
        first = first_ref[...]
        split = H * HD
        packed_ref[:, :split] = mm(first, whole("q")).astype(bf16)
        packed_ref[:, split:] = mm(first, whole("kv")).astype(bf16)
        serve("qkv", pl.program_id(0))

    run(qkv_body, (steps,), [("first", rowb(width))], [("packed", rowb(R["packed"].shape[1]))])

    qw = H // 2 * HD
    kcol = H * HD // 128
    vcol = kcol + KVH * HD // 128

    def attention_body(q_ref, k_ref, v_ref, o_ref, lse_ref):
        s = pl.program_id(0)
        i = lax.rem(s, steps)
        attention_step(R["lengths"], i, jnp.minimum(i + 1, max_blocks()), q_ref, k_ref, v_ref, o_ref, lse_ref)
        serve("attn", s)

    qspec = pl.BlockSpec((BQ, qw), lambda s: (s % steps, s // steps))
    run(
        attention_body,
        (2 * steps,),
        [
            ("packed", qspec),
            ("packed", pl.BlockSpec((LEN, 128), lambda s: (0, kcol + s // steps))),
            ("packed", pl.BlockSpec((LEN, 128), lambda s: (0, vcol + s // steps))),
        ],
        [("mixed", qspec), ("lse", pl.BlockSpec((8, BQ), lambda s: (s // steps, s % steps)))],
    )

    keep("proj").start()

    def proj_body(x_ref, mixed_ref, middle_ref, second_ref):
        middle = x_ref[...].astype(f32) + mm(mixed_ref[...], whole("proj"))
        middle_ref[...] = middle
        inv = lax.rsqrt(jnp.mean(middle * middle, axis=-1, keepdims=True) + norm_eps)
        second_ref[...] = (middle * inv * R["gain_rows"][1:2, :]).astype(bf16)
        serve("proj", pl.program_id(0))

    run(proj_body, (steps,), [("x", rowb(width)), ("mixed", rowb(H * HD))], [("middle", rowb(width)), ("second", rowb(width))])

    keep("gate").start()

    def gate_body(second_ref, gate_ref):
        gate_ref[...] = mm(second_ref[...], whole("gate"))
        serve("gate", pl.program_id(0))

    run(gate_body, (steps,), [("second", rowb(width))], [("gate", rowb(FF))])

    keep("up").start()

    def up_body(second_ref, gate_ref, up_ref, hidden_ref):
        up = mm(second_ref[...], whole("up"))
        up_ref[...] = up
        gate = gate_ref[...]
        hidden_ref[...] = (gate * jax.nn.sigmoid(gate) * up).astype(bf16)
        serve("up", pl.program_id(0))

    run(up_body, (steps,), [("second", rowb(width)), ("gate", rowb(FF))], [("up", rowb(FF)), ("hidden", rowb(FF))])

    for c in CHUNKS[:-1]:
        keep(c).wait()
    keep_gain.wait()
    for c in CHUNKS:
        for d in range(line):
            for side in sides(d):

                def finish():
                    core_copy(c, side, d).wait_send()
                    x_copy(c, side, d).wait_send()
                    y_copy(c, side, d).wait_send()

                guard(exists(side, d), finish)
                if d > 0:
                    had = z - (d - 1) >= 0 if side < 0 else z + (d - 1) < line
                    pl.when(had & onward(side))(lambda: line_copy(c, side, d).wait_send())


def forward(lengths, table, ids, arrays, low_in, low_out, gain_shard, n):
    line = n // 2
    width = arrays["x"].shape[1]
    packed = H * HD + 2 * KVH * HD
    shape = {c: (low_in.shape[0], cols) for c, (_, cols) in IN_COLUMNS.items()} | dict.fromkeys(("proj", "down"), low_out.shape[1:])
    outs = {"full_" + c: ((n, *shape[c]), bf16) for c in CHUNKS}
    outs |= {
        "gain": ((8, width), f32), "dy": ((LEN, width), bf16), "c": ((LEN, 128), f32), "first": ((LEN, width), bf16),
        "packed": ((LEN, packed), bf16), "mixed": ((LEN, H * HD), bf16), "lse": ((H, LEN), f32),
        "middle": ((LEN, width), f32), "second": ((LEN, width), bf16), "gate": ((LEN, FF), f32), "up": ((LEN, FF), f32),
        "hidden": ((LEN, FF), bf16),
    }
    dma = pltpu.SemaphoreType.DMA
    count, items = len(CHUNKS), n - 1
    scratch = {"v_" + c: pltpu.VMEM((n, *shape[c]), bf16) for c in CHUNKS[:-1]}
    scratch |= {
        "v_gain": pltpu.VMEM((n, *gain_shard.shape), bf16), "gain_rows": pltpu.VMEM((8, width), f32),
        "f_send": dma((4, count, items)), "f_recv": dma((4, count, items)), "keep_sem": dma((count,)),
        "own_sem": dma((count,)), "g_send": dma((n,)), "g_recv": dma((n,)),
    }
    inputs = dict(arrays) | {"low_in": low_in, "low_out": low_out, "low_gain": gain_shard}
    names = ["lengths", "table", "ids", *inputs, *outs, *scratch]
    anywhere = pl.BlockSpec(memory_space=pl.ANY)
    smem = pl.BlockSpec(memory_space=pltpu.SMEM)
    got = pl.pallas_call(
        functools.partial(forward_kernel, names=names, line=line),
        in_specs=[smem, smem, pl.BlockSpec(memory_space=pltpu.VMEM)] + [anywhere] * len(inputs),
        out_specs=[anywhere] * len(outs),
        out_shape=[jax.ShapeDtypeStruct(*v) for v in outs.values()],
        scratch_shapes=list(scratch.values()),
        compiler_params=pltpu.CompilerParams(collective_id=0, has_side_effects=True, vmem_limit_bytes=62 << 20),
        cost_estimate=pl.CostEstimate(flops=60 << 30, bytes_accessed=200 << 20, transcendentals=0),
        name="forward",
    )(lengths, table, ids, *inputs.values())
    return dict(zip(outs, got))


HALF = 1024
PIECES = {
    "down_y": ("y", "out", 1, HALF, HALF, "hidden", [("dy", 1, HALF)]),
    "down_z": ("z", "out", 1, 0, HALF, "hidden", [("dy", 0, HALF)]),
    "gate": ("y", "in", 0, H * HD + 2 * KVH * HD, FF, "second", [("dboth", 0, FF)]),
    "up": ("y", "in", 0, H * HD + 2 * KVH * HD + FF, FF, "second", [("dboth", 1, FF)]),
    "proj_z": ("z", "out", 0, 0, HALF, "mixed", [("dlow", 0, HALF)]),
    "proj_y": ("y", "out", 0, HALF, HALF, "mixed", [("dlow", 1, HALF)]),
    "q": ("y", "in", 0, 0, H * HD, "first", [("dq", 0, H * HD)]),
    "kv": ("y", "in", 0, H * HD, 2 * KVH * HD, "first", [("dk", 0, KVH * HD), ("dv", 0, KVH * HD)]),
}
REGIONS = {
    "down": ("out", ("down_z", "down_y"), 1, 0, 2 * HALF),
    "ffn": ("in", ("gate", "up"), 0, H * HD + 2 * KVH * HD, 2 * FF),
    "proj": ("out", ("proj_z", "proj_y"), 0, 0, 2 * HALF),
}


def back_kernel(*refs, names, line, rep, rates):
    R = dict(zip(names, refs))
    r, f = lax.axis_index("rep"), lax.axis_index("fsdp")
    z, y = f // 2, f % 2
    n = 2 * line
    other = lambda k: (r + (1 - 2 * (r % 2)) * (k % 2) + 2 * (1 - 2 * (r // 2)) * (k // 2), f)
    barrier = pltpu.get_barrier_semaphore()
    for step in range(1, n):
        pl.semaphore_signal(barrier, inc=1, device_id=(r, lax.rem(f + step, n)), device_id_type=pl.DeviceIdType.MESH)
    for k in range(1, rep):
        pl.semaphore_signal(barrier, inc=1, device_id=other(k), device_id_type=pl.DeviceIdType.MESH)
    pl.semaphore_wait(barrier, n - 1 + rep - 1)

    loads = ("down", "gate_w", "up_w", "proj", "q_w", "kv_w")
    load = lambda k: pltpu.make_async_copy(R[loads[k]], R["v_" + loads[k]], R["load_sem"].at[k])
    for k in range(len(loads)):
        load(k).start()

    def remote(src, dst, send, recv, to):
        return pltpu.make_async_remote_copy(
            src_ref=src, dst_ref=dst, send_sem=send, recv_sem=recv, device_id=(r, to), device_id_type=pl.DeviceIdType.MESH
        )

    def run(body, grid, ins, outs):
        pltpu.emit_pipeline(body, grid=grid, in_specs=[s for _, s in ins], out_specs=[s for _, s in outs])(
            *[a for a, _ in ins], *[a for a, _ in outs]
        )

    order = list(PIECES)
    middle = (z > 0) & (z < line - 1)
    low = z < line // 2
    inner = jnp.where(low, f + 2, f - 2)
    outer = jnp.where(low, f - 2, f + 2)
    to_y = f + 1 - 2 * y
    third = jnp.where(middle, 3, 2)
    far = jnp.where(low, z + 2, z - 2) * 2 + y

    def shard_rows(p):
        rows = R["own_" + PIECES[p][1]].shape[1]
        return rows // 2 if PIECES[p][1] == "out" else rows

    def span(rows, row, col, cols):
        return pl.ds(row * rows, rows), pl.ds(col, cols)

    def area(p):
        _, _, row, col, cols, _, _ = PIECES[p]
        return span(shard_rows(p), row, col, cols)

    def own(p, t):
        return R["own_" + p].at[t] if PIECES[p][0] == "z" else R["own_" + PIECES[p][1]].at[(t, *area(p))]

    def slot(p, k):
        return R["slot_" + p].at[k] if PIECES[p][0] == "z" else R["slot_" + PIECES[p][1]].at[(k, *area(p))]

    def gradient(p, side, out, add=None):
        mode, _, _, _, cols, a, bs = PIECES[p]
        rows = shard_rows(p)
        pick = lambda j: (0, j * 2 + side)
        if mode == "z":
            rows, pick = 2 * rows, lambda j: (0, j)
        block = pl.BlockSpec((1, rows, cols), lambda j: (j, 0, 0))
        ins = [(R[a], pl.BlockSpec((LEN, rows), pick))]
        for b, at, width in bs:
            ins.append((R[b], pl.BlockSpec((LEN, width), functools.partial(lambda at, j: (0, at), at))))
        if add is not None:
            ins.append((add, block))

        def step(*refs):
            out_ref, a_ref, b_refs = refs[-1], refs[0], refs[1 : 1 + len(bs)]
            col = 0
            for b_ref in b_refs:
                width = b_ref.shape[1]
                g = mm(a_ref[...], b_ref[...], TN)
                if add is not None:
                    g = g + refs[-2][0, :, col : col + width].astype(f32)
                out_ref[0, :, col : col + width] = g.astype(bf16)
                col += width

        run(step, (line,), ins, [(out, block)])

    def pair_copy(p):
        k = order.index(p)
        if PIECES[p][0] == "z":
            dst = R["slot_" + PIECES[p][1]].at[(1, *area(p))]
        else:
            dst = R["came_" + p]
        return remote(R["away_" + p], dst, R["y_send"].at[k], R["y_recv"].at[k], to_y)

    def line_copy(p, k, src, slot_at, to):
        i = order.index(p)
        return remote(src, slot(p, slot_at), R["z_send"].at[i, k], R["z_recv"].at[i, slot_at], to)

    def end_copies(p):
        t = lambda k: jnp.where(low, line - 1 - k, k)
        to = (inner, far, inner)
        return [functools.partial(line_copy, p, k, own(p, t(k)), (0, 1, 3)[k], to[k]) for k in range(3)]

    def middle_copies(p):
        return [
            functools.partial(line_copy, p, 0, R["msg_" + p], 1, far),
            functools.partial(line_copy, p, 1, own(p, 3 - z), 2, inner),
            functools.partial(line_copy, p, 2, own(p, 3 * (z - 1)), 2, outer),
        ]

    def slot_wait(p, at):
        i = order.index(p)
        remote(slot(p, at), slot(p, at), R["z_send"].at[i, 0], R["z_recv"].at[i, at], inner).wait_recv()

    def line_start(p):
        @pl.when(~middle)
        def _():
            for copy in end_copies(p):
                copy().start()

        @pl.when(middle)
        def _():
            for copy in middle_copies(p)[1:]:
                copy().start()

    def send_away(p):
        gradient(p, 1 - y, R["away_" + p])
        pair_copy(p).start()

    def keep(p):
        pair_copy(p).wait_recv()
        gradient(p, y, R["own_" + PIECES[p][1]].at[(pl.ds(0, line), *area(p))], R["came_" + p])
        line_start(p)

    def send_line(p):
        gradient(p, None, R["own_" + p])
        line_start(p)

    def serve(p):
        @pl.when(middle)
        def _():
            slot_wait(p, 0)
            rows, cols = R["msg_" + p].shape
            block = pl.BlockSpec((rows // 2, cols), lambda j: (j, 0))

            def step(a_ref, b_ref, o_ref):
                o_ref[...] = (a_ref[...].astype(f32) + b_ref[...].astype(f32)).astype(bf16)

            run(step, (2,), [(own(p, 3 * (2 - z)), block), (slot(p, 0), block)], [(R["msg_" + p], block)])
            middle_copies(p)[0]().start()

    def line_end(p):
        slot_wait(p, 1)
        slot_wait(p, 2)
        pl.when(middle)(lambda: slot_wait(p, 3))

    def total(refs):
        a, b, c, d = (ref[...].astype(f32) for ref in refs)
        return a + b + c + jnp.where(middle, d, 0.0)

    def close(p):
        line_end(p)
        rows, cols = shard_rows(p), PIECES[p][4]

        def send_step(*refs):
            refs[-1][...] = total(refs[:4]).astype(bf16)

        def stay_step(*refs):
            refs[4][...] = total(refs[:4]).astype(bf16)
            for ref in refs[5:]:
                ref[...] = jnp.zeros_like(ref)

        piece = pl.BlockSpec((rows // 2, cols), lambda j: (j, 0))
        terms = (own(p, z), slot(p, 1), slot(p, 2), slot(p, third))
        ins = lambda side: [(ref, pl.BlockSpec((rows // 2, cols), lambda j: (side * 2 + j, 0))) for ref in terms]
        run(send_step, (2,), ins(1 - y), [(R["away_" + p], piece)])
        pair_copy(p).start()
        kind = PIECES[p][1]
        outs = [R["own_" + kind].at[(z, *area(p))]] + [R["slot_" + kind].at[(k, *area(p))] for k in (2, 3)]
        run(stay_step, (2,), ins(y), [(ref, piece) for ref in outs])

    def delta_copy(name, k):
        kind, pieces, row, col, cols = REGIONS[name]
        i = list(REGIONS).index(name)
        spot = lambda at: R["delta_" + kind].at[(at, *span(shard_rows(pieces[0]), row, col, cols))]
        return pltpu.make_async_remote_copy(
            src_ref=spot(2 if k == 3 else 0), dst_ref=spot(k), send_sem=R["d_send"].at[i, k - 1], recv_sem=R["d_recv"].at[i, k - 1],
            device_id=other(1 if k == 3 else k), device_id_type=pl.DeviceIdType.MESH,
        )

    def delta(name):
        kind, pieces, row, col, cols = REGIONS[name]
        for p in pieces:
            if PIECES[p][0] == "z":
                pair_copy(p).wait_recv()
            else:
                line_end(p)
        rows = shard_rows(pieces[0])
        where = span(rows, row, col, cols)
        block = pl.BlockSpec((rows, 256), lambda j: (0, j))
        terms = [R["own_" + kind].at[(z, *where)]] + [R["slot_" + kind].at[(k, *where)] for k in (1, 2, third)]
        state = [R[k + "_" + kind].at[where] for k in ("first", "second", "w")]

        def step(*refs):
            first_ref, second_ref, w_ref, o_ref = refs[4:]
            o_ref[...] = adam_step(total(refs[:4]), first_ref[...], second_ref[...], w_ref[...], rates[kind])[2].astype(bf16)

        run(step, (cols // 256,), [(ref, block) for ref in terms + state], [(R["delta_" + kind].at[(0, *where)], block)])
        for k in (1, 2):
            delta_copy(name, k).start()

    def relay(name):
        delta_copy(name, 2).wait_recv()
        delta_copy(name, 3).start()

    rowb = lambda width: pl.BlockSpec((BQ, width), lambda i: (i, 0))
    width = R["x"].shape[1]
    R["gain_acc"][...] = jnp.zeros_like(R["gain_acc"])
    gain_rows = R["gain"][...]

    def mid_step(middle_ref, hidden_ref, dboth_ref, t_ref, c_ref, act_ref, dmid_ref, dlow_ref, dmix_ref):
        mid_v = middle_ref[...]
        act_ref[...] = (mid_v + mm(hidden_ref[...], R["v_down"][...])).astype(bf16)
        inv = lax.rsqrt(jnp.mean(mid_v * mid_v, axis=-1, keepdims=True) + norm_eps)
        n2 = mid_v * inv
        ds2 = mm(dboth_ref[:, :FF], R["v_gate_w"][...], NT) + mm(dboth_ref[:, FF:], R["v_up_w"][...], NT)
        prod = ds2 * n2
        R["gain_acc"][8:16, :] += jnp.sum(prod.reshape(BQ // 8, 8, width), axis=0)
        g = gain_rows[1:2, :]
        dy = c_ref[:, 0:1] * t_ref[...].astype(f32)
        dmid = dy + inv * (ds2 * g - n2 * jnp.mean(prod * g, axis=-1, keepdims=True))
        dmid_ref[...] = dmid
        dlow = dmid.astype(bf16)
        dlow_ref[...] = dlow
        dmix_ref[...] = mm(dlow, R["v_proj"][...], NT).astype(bf16)

    def mid_phase(part):
        count = LEN // BQ // 2
        late = lambda width: pl.BlockSpec((BQ, width), lambda i: (i + part * count, 0))
        run(
            mid_step,
            (count,),
            [(R["middle"], late(width)), (R["hidden"], late(FF)), (R["dboth"], late(2 * FF)), (R["target"], late(width)), (R["c"], late(128))],
            [(R["act"], late(width)), (R["dmid"], late(width)), (R["dlow"], late(width)), (R["dmix"], late(H * HD))],
        )

    qw = H // 2 * HD
    kcol = H * HD // 128
    vcol = kcol + KVH * HD // 128

    def attention_phase(p):
        qspec = pl.BlockSpec((BQ, qw), lambda i: (i, p))
        whole = lambda at: pl.BlockSpec((LEN, 128), lambda i: (0, at))
        R["dk_acc"][...] = jnp.zeros_like(R["dk_acc"])
        R["dv_acc"][...] = jnp.zeros_like(R["dv_acc"])

        def step(q_ref, k_ref, v_ref, d_ref, o_ref, lse_ref, dq_ref):
            attention_back_step(R["lengths"], pl.program_id(0), q_ref, k_ref, v_ref, d_ref, o_ref, lse_ref, dq_ref, R["dk_acc"], R["dv_acc"])

        pltpu.emit_pipeline(
            step, grid=(LEN // BQ,),
            in_specs=[qspec, whole(kcol + p), whole(vcol + p), qspec, qspec, pl.BlockSpec((8, BQ), lambda i: (p, i))],
            out_specs=[qspec],
        )(R["packed"], R["packed"], R["packed"], R["dmix"], R["mixed"], R["lse"], R["dq"])

        def flush(dk_ref, dv_ref):
            dk_ref[...] = R["dk_acc"][...].astype(bf16)
            dv_ref[...] = R["dv_acc"][...].astype(bf16)

        run(flush, (1,), [], [(R["dk"], pl.BlockSpec((LEN, 128), lambda i: (0, p))), (R["dv"], pl.BlockSpec((LEN, 128), lambda i: (0, p)))])

    def input_step(x_ref, dmid_ref, dq_ref, dk_ref, dv_ref, out_ref):
        x = x_ref[...].astype(f32)
        inv = lax.rsqrt(jnp.mean(x * x, axis=-1, keepdims=True) + norm_eps)
        n1 = x * inv
        kv_w, split = R["v_kv_w"], KVH * HD
        ds1 = mm(dq_ref[...], R["v_q_w"][...], NT) + mm(dk_ref[...], kv_w[:, :split], NT) + mm(dv_ref[...], kv_w[:, split:], NT)
        prod = ds1 * n1
        R["gain_acc"][0:8, :] += jnp.sum(prod.reshape(BQ // 8, 8, width), axis=0)
        g = gain_rows[0:1, :]
        out_ref[...] = (dmid_ref[...] + inv * (ds1 * g - n1 * jnp.mean(prod * g, axis=-1, keepdims=True))).astype(bf16)

    def input_phase():
        run(
            input_step,
            (LEN // BQ,),
            [(R["x"], rowb(width)), (R["dmid"], rowb(width)), (R["dq"], rowb(H * HD)), (R["dk"], rowb(KVH * HD)), (R["dv"], rowb(KVH * HD))],
            [(R["xgrad"], rowb(width))],
        )

    part = width // n

    def gain_copy(step, receive=False):
        peer = lax.rem(f + step, n)
        home = lax.rem(f + n - step, n) if receive else f
        return remote(
            R["gain_acc"].at[:, pl.ds(pl.multiple_of(peer * part, part), part)], R["gain_got"].at[home],
            R["g_send"].at[step - 1], R["g_recv"].at[step - 1], peer,
        )

    own_gain = pltpu.make_async_copy(
        R["gain_acc"].at[:, pl.ds(pl.multiple_of(f * part, part), part)], R["gain_got"].at[f], R["g_send"].at[n - 1]
    )

    def dboth_step(dy_ref, gate_ref, up_ref, dboth_ref):
        dh = mm(dy_ref[...], R["v_down"][...], NT)
        gate = gate_ref[...]
        sig = jax.nn.sigmoid(gate)
        dboth_ref[:, :FF] = (dh * up_ref[...] * sig * (1.0 + gate * (1.0 - sig))).astype(bf16)
        dboth_ref[:, FF:] = (dh * (gate * sig)).astype(bf16)

    send_line("down_z")
    send_away("down_y")
    load(0).wait()
    run(
        dboth_step,
        (LEN // BQ,),
        [(R["dy"], rowb(width)), (R["gate"], rowb(FF)), (R["up"], rowb(FF))],
        [(R["dboth"], rowb(2 * FF))],
    )
    serve("down_z")
    send_away("gate")
    for k in range(1, 4):
        load(k).wait()
    mid_phase(0)
    keep("down_y")
    mid_phase(1)
    serve("down_y")
    send_away("up")
    send_line("proj_z")
    serve("proj_z")
    attention_phase(0)
    keep("gate")
    send_away("proj_y")
    serve("gate")
    attention_phase(1)
    send_away("q")
    keep("up")
    serve("up")
    load(4).wait()
    load(5).wait()
    input_phase()
    for step in range(1, n):
        gain_copy(step).start()
    own_gain.start()
    keep("proj_y")
    serve("proj_y")
    close("proj_z")
    delta("ffn")
    keep("q")
    send_away("kv")
    delta("proj")
    close("down_z")
    serve("q")
    keep("kv")
    delta("down")
    relay("proj")
    serve("kv")
    relay("down")
    relay("ffn")

    for step in range(1, n):
        gain_copy(step, True).wait_recv()
        gain_copy(step).wait_send()
    own_gain.wait()
    for name in REGIONS:
        for k in (1, 3):
            delta_copy(name, k).wait()
        delta_copy(name, 2).wait_send()
    line_end("q")
    line_end("kv")
    for p in order:
        pair_copy(p).wait_send()

        @pl.when(middle)
        def _():
            for copy in middle_copies(p):
                copy().wait_send()

        @pl.when(~middle)
        def _():
            for copy in end_copies(p):
                copy().wait_send()


def backward(lengths, gain, arrays, n, rep, rates):
    line = n // 2
    width = arrays["x"].shape[1]
    kvw = KVH * HD
    outs = {
        "act": ((LEN, width), bf16), "dboth": ((LEN, 2 * FF), bf16), "dmid": ((LEN, width), f32), "dlow": ((LEN, width), bf16),
        "dmix": ((LEN, H * HD), bf16), "dq": ((LEN, H * HD), bf16), "dk": ((LEN, kvw), bf16), "dv": ((LEN, kvw), bf16),
        "xgrad": ((LEN, width), bf16), "gain_got": ((n, 16, width // n), f32),
    }
    for kind in ("in", "out"):
        for name, count in (("own_", line), ("slot_", 4), ("delta_", rep)):
            outs[name + kind] = ((count, *arrays["w_" + kind].shape), bf16)
    for p, (mode, kind, _, _, cols, _, _) in PIECES.items():
        rows = arrays["w_" + kind].shape[0] // (2 if kind == "out" else 1)
        if mode == "y":
            counts = (("away_", (line, rows)), ("came_", (line, rows)), ("msg_", (rows,)))
        else:
            counts = (("away_", (rows,)), ("own_", (line, 2 * rows)), ("slot_", (4, 2 * rows)), ("msg_", (2 * rows,)))
        for name, lead in counts:
            outs[name + p] = ((*lead, cols), bf16)
    dma = pltpu.SemaphoreType.DMA
    pieces = len(PIECES)
    scratch = {
        **{"v_" + k: pltpu.VMEM(arrays[k].shape, bf16) for k in ("down", "gate_w", "up_w", "proj", "q_w", "kv_w")},
        "gain_acc": pltpu.VMEM((16, width), f32), "dk_acc": pltpu.VMEM((LEN, 128), f32), "dv_acc": pltpu.VMEM((LEN, 128), f32),
        "load_sem": dma((6,)), "y_send": dma((pieces,)), "y_recv": dma((pieces,)),
        "z_send": dma((pieces, 3)), "z_recv": dma((pieces, 4)),
        "d_send": dma((len(REGIONS), rep - 1)), "d_recv": dma((len(REGIONS), rep - 1)), "g_send": dma((n,)), "g_recv": dma((n,)),
    }
    names = ["lengths", "gain", *arrays, *outs, *scratch]
    anywhere = pl.BlockSpec(memory_space=pl.ANY)
    got = pl.pallas_call(
        functools.partial(back_kernel, names=names, line=line, rep=rep, rates=rates),
        in_specs=[pl.BlockSpec(memory_space=pltpu.SMEM), pl.BlockSpec(memory_space=pltpu.VMEM)] + [anywhere] * len(arrays),
        out_specs=[anywhere] * len(outs),
        out_shape=[jax.ShapeDtypeStruct(*v) for v in outs.values()],
        scratch_shapes=list(scratch.values()),
        compiler_params=pltpu.CompilerParams(collective_id=1, has_side_effects=True, vmem_limit_bytes=62 << 20),
        cost_estimate=pl.CostEstimate(flops=200 << 30, bytes_accessed=400 << 20, transcendentals=0),
        name="backward",
    )(lengths, gain, *arrays.values())
    return dict(zip(outs, got))


rate_in = 0.02
rate_out = 0.08
rate_gains = 1.2


def body(
    tokens,
    target,
    doc_lengths,
    corpus_ids,
    corpus_weights,
    w_in,
    w_out,
    gains,
    first_in,
    first_out,
    first_gains,
    second_in,
    second_out,
    second_gains,
    outer_in,
    outer_out,
    outer_gains,
):
    n, rep = lax.axis_size("fsdp"), lax.axis_size("rep")
    line = n // 2
    f, r = lax.axis_index("fsdp"), lax.axis_index("rep")
    z, y = f // 2, f % 2
    direct = by_neighbours(n, rep)
    inside = (z > 0) & (z < line - 1)
    place = jnp.stack([z, inside]).astype(jnp.int32)
    width = w_out.shape[2]
    flat = lambda a: a.reshape(-1, a.shape[-1])
    state_in = first_in[0], second_in[0], w_in
    state_out = flat(first_out[0]), flat(second_out[0]), flat(w_out)
    moved_out = flat(outer_out)
    rates = {"in": rate_in, "out": rate_out}
    rows_in, rows_out = w_in.shape[0], w_out.shape[1]
    x, tgt, lengths = tokens[0], target[0], doc_lengths[0]
    ids = corpus_ids[0][:, None]

    if direct:
        low_gain = jnp.pad(gains.astype(bf16), ((0, 14), (0, 0)))
        fwd = forward(lengths, corpus_weights, ids, dict(x=x, target=tgt), w_in.astype(bf16), w_out.astype(bf16), low_gain, n)
        weight = lambda c: flat(fwd["full_" + c])
        kept = {k: fwd[k] for k in ("c", "middle", "hidden", "second", "gate", "up", "dy", "mixed", "packed", "lse", "first")}
        got = backward(
            lengths, fwd["gain"],
            dict(x=x, target=tgt, proj=weight("proj"), down=weight("down"), q_w=weight("q"), kv_w=weight("kv"),
                 gate_w=weight("gate"), up_w=weight("up"), first_in=state_in[0], second_in=state_in[1], w_in=w_in,
                 first_out=state_out[0], second_out=state_out[1], w_out=state_out[2], **kept),
            n, rep, rates,
        )
        activations, input_grad = got["act"], got["xgrad"]
        gain_share = jnp.sum(got["gain_got"].reshape(n, 2, 8, -1), axis=(0, 2))
        late = (H * HD + 2 * KVH * HD) // TILE
        *held, late_delta = adam_tiles(
            place, got["own_in"], got["slot_in"], *state_in, None, None, None, 0, (0, late, late, 0), rate_in, rep
        )
        near, far = to_group(late_delta, 1, rep), to_group(late_delta, 2, rep)
        rest = w_in.shape[1] // TILE - late
        in_got = adam_tiles(
            place, got["own_in"], got["slot_in"], *state_in, outer_in, got["delta_in"], held,
            0, (late, rest, rest, 0), rate_in, rep,
        )
        out_count = width // TILE
        out_got = adam_tiles(
            place, got["own_out"], got["slot_out"], *state_out, moved_out, got["delta_out"], None,
            0, (0, out_count, out_count, 0), rate_out, rep,
        )
        out_got, in_got = list(out_got), list(in_got)
        far, out_got[0], in_got[0] = lax.optimization_barrier((far, out_got[0], in_got[0]))
        late_terms = [late_delta, near, far, to_group(far, 1, rep)]
        in_grads, in_steps = in_got[:3], outer_tiles(late_terms, outer_in, w_in, in_got[3:], 0, rep)
        out_grads, out_steps = out_got[:3], out_got[3:]
    else:
        gain_full, wq, proj, wf, down = all_weights(w_in, w_out, gains)
        first_low, packed = qkv(x, gain_full, wq)
        mixed, lse = attention(lengths, packed)
        middle, second_low, hidden, d_both, dy, _ = ffn(corpus_weights, x, mixed, tgt, ids, gain_full, proj, wf, down)

        def by_library(a, bs, name):
            block = 2 * BQ if a.shape[1] % (2 * BQ) == 0 else BQ
            every_row = jnp.arange(a.shape[1] // block, dtype=jnp.int32)
            total = grad_rows(every_row, a, bs, block, name=name)
            return lax.psum_scatter(total.reshape(a.shape[1], -1), "fsdp", scatter_dimension=0, tiled=True)[None]

        activations, d_mid, d_low, d_mix, gain_two = mid(
            corpus_weights, middle, hidden, d_both, tgt, ids, gain_full, proj, wf, down
        )
        dq, dk, dv = attention_back(lengths, packed, d_mix, mixed, lse)
        input_grad, gain_one = input_back(x, d_mid, dq, dk, dv, gain_full, wq)
        both = jnp.stack([jnp.sum(gain_one, axis=0), jnp.sum(gain_two, axis=0)])
        gain_share = lax.psum_scatter(both, "fsdp", scatter_dimension=1, tiled=True)
        own_in = jnp.concatenate(
            [
                by_library(first_low, [(dq, 0, H * HD), (dk, 0, KVH * HD), (dv, 0, KVH * HD)], "grad_attn"),
                by_library(second_low, [(d_both, 0, 2 * FF)], "grad_ffn"),
            ],
            axis=2,
        )
        own_out = jnp.concatenate(
            [by_library(mixed, [(d_low, 0, width)], "grad_proj"), by_library(hidden, [(dy, 0, width)], "grad_down")], axis=1
        )

        def all_tiles(own, state, outer, rate):
            count = own.shape[2] // TILE
            *grads, delta = adam_tiles(0 * place, own, None, *state, None, None, None, 0, (0, count, count, 0), rate, rep)
            return grads, outer_tiles(groups_terms(delta, rep), outer, state[2], None, 0, rep)

        in_grads, in_steps = all_tiles(own_in, state_in, outer_in, rate_in)
        out_grads, out_steps = all_tiles(own_out, state_out, moved_out, rate_out)

    first_gains_new, second_gains_new, delta = adam_step(gain_share, first_gains[0], second_gains[0], gains, rate_gains)
    terms = groups_terms(delta, rep)
    sum_gains = (terms[0] + terms[1]) + (terms[2] + terms[3]) if rep == 4 else sum(terms[1:], terms[0])
    diff_gains, outer_gains_new, new_gains = outer_step(sum_gains, outer_gains, gains, rep)

    out_shape = lambda a: a.reshape(2, rows_out, width)
    diff_in, outer_in_new, new_in, copy_in = in_steps
    diff_out, outer_out_new, new_out, copy_out = (out_shape(a) for a in out_steps)
    grad_in, first_in_new, second_in_new = in_grads
    grad_out, first_out_new, second_out_new = (out_shape(a) for a in out_grads)
    return (
        activations[None],
        input_grad[None],
        grad_in[None],
        grad_out[None],
        gain_share[None],
        first_in_new[None],
        first_out_new[None],
        first_gains_new[None],
        second_in_new[None],
        second_out_new[None],
        second_gains_new[None],
        diff_in,
        diff_out,
        diff_gains,
        outer_in_new,
        outer_out_new,
        outer_gains_new,
        new_in,
        new_out,
        new_gains,
        copy_in,
        copy_out,
        new_gains.astype(bf16),
    )


def solution(mesh):
    rows = P(("rep", "fsdp"), None, None)
    pair = P(("rep", "fsdp"), None)
    w_in, w_out, gains = P("fsdp", None), P(None, "fsdp", None), P(None, "fsdp")
    m_in, m_out, m_gains = P("rep", "fsdp", None), P("rep", None, "fsdp", None), P("rep", None, "fsdp")
    weights, moments = (w_in, w_out, gains), (m_in, m_out, m_gains)
    return jax.shard_map(
        body,
        mesh=mesh,
        in_specs=(rows, rows, pair, pair, P(), *weights, *moments, *moments, *weights),
        out_specs=(rows, rows, *moments, *moments, *moments, *weights, *weights, *weights, *weights),
        check_vma=False,
    )
```

```python
import functools
import jax
import jax.numpy as jnp
from jax import lax
from jax.experimental import pallas as pl
from jax.experimental.pallas import tpu as pltpu
from jax.sharding import PartitionSpec as P

H = 16
HD = 64
KVH = 4
FF = 1024
LEN = 1024
NCORP = 8
f32 = jnp.float32
bf16 = jnp.bfloat16
norm_eps = 1e-06
BQ = 256
NT = (((1,), (1,)), ((), ()))
TN = (((0,), (0,)), ((), ()))


def mm(a, b, dims=(((1,), (0,)), ((), ()))):
    return lax.dot_general(a, b, dims, preferred_element_type=f32)


def params(**kw):
    return pltpu.CompilerParams(vmem_limit_bytes=60 << 20, **kw)


def one(shape, index):
    return pl.BlockSpec(shape, index, pipeline_mode=pl.Buffered(1))


def qkv_kernel(x_ref, g_ref, w_ref, first_ref, packed_ref):
    x = x_ref[...].astype(f32)
    r = lax.rsqrt(jnp.mean(x * x, axis=-1, keepdims=True) + norm_eps)
    first = (x * r * g_ref[0:1, :]).astype(bf16)
    first_ref[...] = first
    packed_ref[...] = mm(first, w_ref[...]).astype(bf16)


def qkv(x, gains, w):
    rows, width = x.shape
    cols = w.shape[1]
    return pl.pallas_call(
        qkv_kernel,
        grid=(rows // BQ,),
        in_specs=[
            pl.BlockSpec((BQ, width), lambda i: (i, 0)),
            one(gains.shape, lambda i: (0, 0)),
            one((width, cols), lambda i: (0, 0)),
        ],
        out_specs=[
            pl.BlockSpec((BQ, width), lambda i: (i, 0)),
            pl.BlockSpec((BQ, cols), lambda i: (i, 0)),
        ],
        out_shape=[
            jax.ShapeDtypeStruct((rows, width), bf16),
            jax.ShapeDtypeStruct((rows, cols), bf16),
        ],
        compiler_params=params(),
        cost_estimate=pl.CostEstimate(
            flops=2 * rows * width * cols, bytes_accessed=rows * width * 4 + width * cols * 2, transcendentals=0
        ),
        name="norm_qkv",
    )(x, gains, w)


def doc_start(lengths_ref, position):
    end = jnp.int32(0)
    start = jnp.zeros_like(position)
    for j in range(lengths_ref.shape[0]):
        end = end + lengths_ref[j]
        start = jnp.where(position >= end, end, start)
    return start


def key_blocks(lengths_ref, i):
    first_row = i * BQ
    return i + 1 - doc_start(lengths_ref, first_row) // BQ


def max_blocks():
    return LEN // (2 * BQ) + 1


def attention_step(len_ref, i, count, q_ref, k_ref, v_ref, o_ref, lse_ref):
    row = i * BQ + lax.broadcasted_iota(jnp.int32, (BQ, 1), 0)
    start = doc_start(len_ref, row)
    lane = lax.broadcasted_iota(jnp.int32, (BQ, 128), 1)
    for nb in range(1, max_blocks() + 1):

        @pl.when(count == nb)
        def _():
            span = nb * BQ
            base = pl.multiple_of((i - (nb - 1)) * BQ, BQ)
            col = base + lax.broadcasted_iota(jnp.int32, (BQ, span), 1)
            bias = jnp.where((col >= start) & (col <= row), 0.0, -1e30)
            k2 = k_ref[pl.ds(base, span), :]
            v2 = v_ref[pl.ds(base, span), :]
            tile = jnp.zeros((BQ, 128), f32)
            outs = []
            for kv in range(2):
                k = k2[:, kv * HD : (kv + 1) * HD]
                v = v2[:, kv * HD : (kv + 1) * HD]
                for g in range(H // KVH):
                    h = kv * (H // KVH) + g
                    q = q_ref[:, h * HD : (h + 1) * HD] * jnp.asarray(HD**-0.5, bf16)
                    s = mm(q, k, NT) + bias
                    m = jnp.max(s, axis=-1, keepdims=True)
                    e = jnp.exp(s - m)
                    total = jnp.sum(e, axis=-1, keepdims=True)
                    o = mm(e.astype(bf16), v) * (1.0 / total)
                    outs.append(o.astype(bf16))
                    tile = jnp.where(lane == h, m + jnp.log(total), tile)
            o_ref[...] = jnp.concatenate(outs, axis=1)
            lse_ref[...] = tile.T[0:8, :]


def attn_kernel(len_ref, *refs):
    i = pl.program_id(0)
    attention_step(len_ref, i, key_blocks(len_ref, i), *refs)


def attention(lengths, packed):
    qw = H // 2 * HD
    kcol = H * HD // 128
    vcol = kcol + KVH * HD // 128
    return pl.pallas_call(
        attn_kernel,
        grid_spec=pltpu.PrefetchScalarGridSpec(
            num_scalar_prefetch=1,
            grid=(LEN // BQ, 2),
            in_specs=[
                pl.BlockSpec((BQ, qw), lambda i, p, s: (i, p)),
                pl.BlockSpec((LEN, 128), lambda i, p, s: (0, kcol + p)),
                pl.BlockSpec((LEN, 128), lambda i, p, s: (0, vcol + p)),
            ],
            out_specs=[
                pl.BlockSpec((BQ, qw), lambda i, p, s: (i, p)),
                pl.BlockSpec((8, BQ), lambda i, p, s: (p, i)),
            ],
        ),
        out_shape=[
            jax.ShapeDtypeStruct((LEN, H * HD), bf16),
            jax.ShapeDtypeStruct((H, LEN), f32),
        ],
        compiler_params=params(),
        cost_estimate=pl.CostEstimate(flops=4 * H * LEN * LEN * HD * 4, bytes_accessed=1 << 24, transcendentals=0),
        name="attention",
    )(lengths, packed, packed, packed)


def attention_back_step(len_ref, i, q_ref, k_ref, v_ref, d_ref, o_ref, lse_ref, dq_ref, dk_acc, dv_acc, count=None):
    if count is None:
        count = jnp.minimum(i + 1, max_blocks())
    row = i * BQ + lax.broadcasted_iota(jnp.int32, (1, BQ), 1)
    start = doc_start(len_ref, row)
    lane = lax.broadcasted_iota(jnp.int32, (BQ, 128), 1)
    group = H // KVH
    scale = jnp.asarray(HD**-0.5, bf16)
    tile = jnp.zeros((BQ, 128), f32)
    for h in range(2 * group):
        cols = slice(h * HD, (h + 1) * HD)
        dot = jnp.sum(d_ref[:, cols].astype(f32) * o_ref[:, cols].astype(f32), axis=-1, keepdims=True)
        tile = jnp.where(lane == h, dot, tile)
    inner = tile.T
    for nb in range(1, max_blocks() + 1):

        @pl.when(count == nb)
        def _():
            span = nb * BQ
            base = pl.multiple_of((i - (nb - 1)) * BQ, BQ)
            key = base + lax.broadcasted_iota(jnp.int32, (span, BQ), 0)
            bias = jnp.where((key >= start) & (key <= row), 0.0, -1e30)
            k2 = k_ref[pl.ds(base, span), :]
            v2 = v_ref[pl.ds(base, span), :]
            dks, dvs = [], []
            for kv in range(2):
                k = k2[:, kv * HD : (kv + 1) * HD]
                v = v2[:, kv * HD : (kv + 1) * HD]
                dk = dv = None
                dqs = []
                for g in range(group):
                    h = kv * group + g
                    cols = slice(h * HD, (h + 1) * HD)
                    q = q_ref[:, cols] * scale
                    d = d_ref[:, cols]
                    s = mm(k, q, NT) + bias
                    p = jnp.exp(s - lse_ref[h : h + 1, :])
                    dp = mm(v, d, NT)
                    ds = (p * (dp - inner[h : h + 1, :])).astype(bf16)
                    dv_h = mm(p.astype(bf16), d)
                    dk_h = mm(ds, q)
                    dv = dv_h if dv is None else dv + dv_h
                    dk = dk_h if dk is None else dk + dk_h
                    dqs.append(mm(k, ds, TN))
                dq = jnp.concatenate(dqs, axis=0) * (HD**-0.5)
                dq_ref[:, kv * group * HD : (kv + 1) * group * HD] = dq.T.astype(bf16)
                dks.append(dk)
                dvs.append(dv)
            dk_acc[pl.ds(base, span), :] += jnp.concatenate(dks, axis=1)
            dv_acc[pl.ds(base, span), :] += jnp.concatenate(dvs, axis=1)


def attn_back_kernel(len_ref, q_ref, k_ref, v_ref, d_ref, o_ref, lse_ref, dq_ref, dk_ref, dv_ref, dk_acc, dv_acc):
    i = pl.program_id(1)

    @pl.when(i == 0)
    def _():
        dk_acc[...] = jnp.zeros_like(dk_acc)
        dv_acc[...] = jnp.zeros_like(dv_acc)

    attention_back_step(
        len_ref, i, q_ref, k_ref, v_ref, d_ref, o_ref, lse_ref, dq_ref, dk_acc, dv_acc, key_blocks(len_ref, i)
    )

    @pl.when(i == pl.num_programs(1) - 1)
    def _():
        dk_ref[...] = dk_acc[...].astype(bf16)
        dv_ref[...] = dv_acc[...].astype(bf16)


def attention_back(lengths, packed, d_mixed, mixed, lse):
    qw = H // 2 * HD
    kcol = H * HD // 128
    vcol = kcol + KVH * HD // 128
    return pl.pallas_call(
        attn_back_kernel,
        grid_spec=pltpu.PrefetchScalarGridSpec(
            num_scalar_prefetch=1,
            grid=(2, LEN // BQ),
            in_specs=[
                pl.BlockSpec((BQ, qw), lambda p, i, s: (i, p)),
                pl.BlockSpec((LEN, 128), lambda p, i, s: (0, kcol + p)),
                pl.BlockSpec((LEN, 128), lambda p, i, s: (0, vcol + p)),
                pl.BlockSpec((BQ, qw), lambda p, i, s: (i, p)),
                pl.BlockSpec((BQ, qw), lambda p, i, s: (i, p)),
                pl.BlockSpec((8, BQ), lambda p, i, s: (p, i)),
            ],
            out_specs=[
                pl.BlockSpec((BQ, qw), lambda p, i, s: (i, p)),
                pl.BlockSpec((LEN, 128), lambda p, i, s: (0, p)),
                pl.BlockSpec((LEN, 128), lambda p, i, s: (0, p)),
            ],
            scratch_shapes=[pltpu.VMEM((LEN, 128), f32), pltpu.VMEM((LEN, 128), f32)],
        ),
        out_shape=[
            jax.ShapeDtypeStruct((LEN, H * HD), bf16),
            jax.ShapeDtypeStruct((LEN, KVH * HD), bf16),
            jax.ShapeDtypeStruct((LEN, KVH * HD), bf16),
        ],
        compiler_params=params(),
        cost_estimate=pl.CostEstimate(flops=10 * H * LEN * LEN * HD * 4, bytes_accessed=1 << 24, transcendentals=0),
        name="attention_back",
    )(lengths, packed, packed, packed, d_mixed, mixed, lse)


def token_weight(table_ref, ids):
    weight = jnp.zeros(ids.shape, f32)
    for j in range(table_ref.shape[0]):
        weight = jnp.where(ids == j, table_ref[j].astype(f32) * 0.25, weight)
    return weight


def ffn_kernel(table_ref, x_ref, mixed_ref, t_ref, ids_ref, g_ref, proj_ref, wf_ref, down_ref,
               middle_ref, second_ref, hidden_ref, dboth_ref, dy_ref, c_ref):
    middle = x_ref[...].astype(f32) + mm(mixed_ref[...], proj_ref[...])
    middle_ref[...] = middle
    r = lax.rsqrt(jnp.mean(middle * middle, axis=-1, keepdims=True) + norm_eps)
    second = (middle * r * g_ref[1:2, :]).astype(bf16)
    second_ref[...] = second
    c = token_weight(table_ref, ids_ref[...])
    c_ref[...] = jnp.broadcast_to(c, c_ref.shape)
    dy = (c * t_ref[...].astype(f32)).astype(bf16)
    dy_ref[...] = dy
    step = 512
    for c in range(0, FF, step):
        gate = mm(second, wf_ref[:, c : c + step])
        up = mm(second, wf_ref[:, FF + c : FF + c + step])
        dh = mm(dy, down_ref[c : c + step, :], NT)
        sig = jax.nn.sigmoid(gate)
        silu = gate * sig
        hidden_ref[:, c : c + step] = (silu * up).astype(bf16)
        dboth_ref[:, c : c + step] = (dh * up * sig * (1.0 + gate * (1.0 - sig))).astype(bf16)
        dboth_ref[:, FF + c : FF + c + step] = (dh * silu).astype(bf16)


def ffn(table, x, mixed, target, ids, gains, proj, wf, down):
    width = x.shape[1]
    rowb = lambda n: pl.BlockSpec((BQ, n), lambda i, s: (i, 0))
    whole = lambda a: one(a.shape, lambda i, s: (0, 0))
    return pl.pallas_call(
        ffn_kernel,
        grid_spec=pltpu.PrefetchScalarGridSpec(
            num_scalar_prefetch=1,
            grid=(LEN // BQ,),
            in_specs=[rowb(width), rowb(H * HD), rowb(width), rowb(1), whole(gains), whole(proj), whole(wf), whole(down)],
            out_specs=[rowb(width), rowb(width), rowb(FF), rowb(2 * FF), rowb(width), rowb(128)],
        ),
        out_shape=[
            jax.ShapeDtypeStruct((LEN, width), f32),
            jax.ShapeDtypeStruct((LEN, width), bf16),
            jax.ShapeDtypeStruct((LEN, FF), bf16),
            jax.ShapeDtypeStruct((LEN, 2 * FF), bf16),
            jax.ShapeDtypeStruct((LEN, width), bf16),
            jax.ShapeDtypeStruct((LEN, 128), f32),
        ],
        compiler_params=params(),
        cost_estimate=pl.CostEstimate(flops=2 * LEN * width * FF * 4, bytes_accessed=40 << 20, transcendentals=0),
        name="ffn",
    )(table, x, mixed, target, ids, gains, proj, wf, down)


def mid_kernel(table_ref, middle_ref, hidden_ref, dboth_ref, t_ref, ids_ref, g_ref, proj_ref, wf_ref, down_ref,
               act_ref, dmid_ref, dlow_ref, dmix_ref, gain_ref):
    middle = middle_ref[...]
    act_ref[...] = (middle + mm(hidden_ref[...], down_ref[...])).astype(bf16)
    r = lax.rsqrt(jnp.mean(middle * middle, axis=-1, keepdims=True) + norm_eps)
    n2 = middle * r
    ds2 = mm(dboth_ref[...], wf_ref[...], NT)
    prod = ds2 * n2
    part = jnp.sum(prod.reshape(BQ // 8, 8, prod.shape[1]), axis=0)

    @pl.when(pl.program_id(0) == 0)
    def _():
        gain_ref[...] = jnp.zeros_like(gain_ref)

    gain_ref[...] += part
    g = g_ref[1:2, :]
    e2 = ds2 * g
    dy = token_weight(table_ref, ids_ref[...]) * t_ref[...].astype(f32)
    dmid = dy + r * (e2 - n2 * jnp.mean(prod * g, axis=-1, keepdims=True))
    dmid_ref[...] = dmid
    low = dmid.astype(bf16)
    dlow_ref[...] = low
    dmix_ref[...] = mm(low, proj_ref[...], NT).astype(bf16)


def mid(table, middle, hidden, dboth, target, ids, gains, proj, wf, down):
    width = middle.shape[1]
    rowb = lambda n: pl.BlockSpec((BQ, n), lambda i, s: (i, 0))
    whole = lambda a: one(a.shape, lambda i, s: (0, 0))
    return pl.pallas_call(
        mid_kernel,
        grid_spec=pltpu.PrefetchScalarGridSpec(
            num_scalar_prefetch=1,
            grid=(LEN // BQ,),
            in_specs=[rowb(width), rowb(FF), rowb(2 * FF), rowb(width), rowb(1), whole(gains), whole(proj), whole(wf), whole(down)],
            out_specs=[rowb(width), rowb(width), rowb(width), rowb(H * HD), pl.BlockSpec((8, width), lambda i, s: (0, 0))],
        ),
        out_shape=[
            jax.ShapeDtypeStruct((LEN, width), bf16),
            jax.ShapeDtypeStruct((LEN, width), f32),
            jax.ShapeDtypeStruct((LEN, width), bf16),
            jax.ShapeDtypeStruct((LEN, H * HD), bf16),
            jax.ShapeDtypeStruct((8, width), f32),
        ],
        compiler_params=params(),
        cost_estimate=pl.CostEstimate(flops=2 * LEN * width * FF * 4, bytes_accessed=40 << 20, transcendentals=0),
        name="mid",
    )(table, middle, hidden, dboth, target, ids, gains, proj, wf, down)


def input_kernel(x_ref, dmid_ref, dq_ref, dk_ref, dv_ref, g_ref, w_ref, out_ref, gain_ref):
    x = x_ref[...].astype(f32)
    r = lax.rsqrt(jnp.mean(x * x, axis=-1, keepdims=True) + norm_eps)
    n1 = x * r
    q, k = H * HD, H * HD + KVH * HD
    ds1 = mm(dq_ref[...], w_ref[:, :q], NT) + mm(dk_ref[...], w_ref[:, q:k], NT) + mm(dv_ref[...], w_ref[:, k:], NT)
    prod = ds1 * n1
    part = jnp.sum(prod.reshape(BQ // 8, 8, prod.shape[1]), axis=0)

    @pl.when(pl.program_id(0) == 0)
    def _():
        gain_ref[...] = jnp.zeros_like(gain_ref)

    gain_ref[...] += part
    g = g_ref[0:1, :]
    out = dmid_ref[...] + r * (ds1 * g - n1 * jnp.mean(prod * g, axis=-1, keepdims=True))
    out_ref[...] = out.astype(bf16)


def input_back(x, dmid, dq, dk, dv, gains, w):
    width = x.shape[1]
    rowb = lambda n: pl.BlockSpec((BQ, n), lambda i: (i, 0))
    whole = lambda a: one(a.shape, lambda i: (0, 0))
    return pl.pallas_call(
        input_kernel,
        grid=(LEN // BQ,),
        in_specs=[rowb(width), rowb(width), rowb(H * HD), rowb(KVH * HD), rowb(KVH * HD), whole(gains), whole(w)],
        out_specs=[rowb(width), pl.BlockSpec((8, width), lambda i: (0, 0))],
        out_shape=[jax.ShapeDtypeStruct((LEN, width), bf16), jax.ShapeDtypeStruct((8, width), f32)],
        compiler_params=params(),
        cost_estimate=pl.CostEstimate(flops=2 * LEN * width * 1536, bytes_accessed=24 << 20, transcendentals=0),
        name="input_back",
    )(x, dmid, dq, dk, dv, gains, w)


def grad_kernel(pick_ref, a_ref, *refs):
    out_ref = refs[-1]
    b_refs = refs[:-1]
    add_ref = None
    if len(b_refs) > 1 and len(b_refs[-1].shape) == 3:
        add_ref, b_refs = b_refs[-1], b_refs[:-1]
    col = 0
    a = a_ref[...]
    for b_ref in b_refs:
        n = b_ref.shape[1]
        g = mm(a, b_ref[...], TN)
        if add_ref is not None:
            g = g + add_ref[0, :, col : col + n].astype(f32)
        out_ref[0, :, col : col + n] = g.astype(bf16)
        col += n


def grad_rows(pick, a, bs, rows, add=None, name="grad"):
    cols = sum(width for _, _, width in bs)
    count = pick.shape[0]
    specs = [pl.BlockSpec((LEN, rows), lambda j, p: (0, p[j]))]
    specs += [one((LEN, width), functools.partial(lambda at, j, p: (0, at), at)) for _, at, width in bs]
    ops = [a, *(b for b, _, _ in bs)]
    if add is not None:
        specs.append(pl.BlockSpec((1, rows, cols), lambda j, p: (j, 0, 0)))
        ops.append(add)
    return pl.pallas_call(
        grad_kernel,
        grid_spec=pltpu.PrefetchScalarGridSpec(
            num_scalar_prefetch=1,
            grid=(count,),
            in_specs=specs,
            out_specs=pl.BlockSpec((1, rows, cols), lambda j, p: (j, 0, 0)),
        ),
        out_shape=jax.ShapeDtypeStruct((count, rows, cols), bf16),
        compiler_params=params(),
        cost_estimate=pl.CostEstimate(flops=2 * LEN * rows * count * cols, bytes_accessed=12 << 20, transcendentals=0),
        name=name,
    )(pick, *ops)


beta_first = 0.9
beta_second = 0.95
adam_eps = 1e-08
decay_rate = 0.1
outer_decay = 0.5
outer_rate = 0.7
STEP = 10


def adam_step(grad, first, second, weight, rate):
    first_new = beta_first * first + (1.0 - beta_first) * grad
    second_new = beta_second * second + (1.0 - beta_second) * grad * grad
    first_unbiased = first_new * (1.0 / (1.0 - beta_first**STEP))
    ratio = first_unbiased / (jnp.sqrt(second_new * (1.0 / (1.0 - beta_second**STEP))) + adam_eps)
    local = weight - rate * (ratio + decay_rate * weight)
    return first_new, second_new, weight - local


def outer_step(delta_sum, momentum, weight, groups):
    average = delta_sum * (1.0 / groups)
    momentum_new = outer_decay * momentum + average
    return average, momentum_new, weight - outer_rate * (average + outer_decay * momentum_new)


def adam_kernel(place_ref, own_ref, *refs, slots, deltas, carry, rate, groups):
    refs = list(refs)
    if carry:
        carry_out = refs.pop()
    grad = own_ref[0].astype(f32)
    if slots:
        b, c, d = (refs.pop(0)[0].astype(f32) for _ in range(3))
        grad = grad + b + c + jnp.where(place_ref[1] == 1, d, 0.0)
    first_ref, second_ref, w_ref = refs[:3]
    first_new, second_new, delta = adam_step(grad, first_ref[...], second_ref[...], w_ref[...], rate)
    outs = refs[-7:] if deltas else refs[-4:]
    outs[0][...] = grad
    outs[1][...] = first_new
    outs[2][...] = second_new
    if not deltas:
        outs[3][...] = delta.astype(bf16)
        return
    outer_ref, delta_ref = refs[3:5]
    if carry:
        carry_out[...] = refs[5][...]
    d = [delta_ref[k].astype(f32) for k in range(delta_ref.shape[0])]
    write_outer((d[0] + d[1]) + (d[2] + d[3]), outer_ref, w_ref, outs[3:], groups)


def write_outer(total, outer_ref, w_ref, outs, groups):
    average, momentum, weight = outer_step(total, outer_ref[...], w_ref[...], groups)
    outs[0][...] = average
    outs[1][...] = momentum
    outs[2][...] = weight
    outs[3][...] = weight.astype(bf16)


TILE = 512
ROW_BLOCKS = 2


def adam_tiles(place, own, slots, first, second, w, outer, deltas, held, own_at, tiles, rate, groups, carry=None):
    total, rows = w.shape[0], w.shape[0] // ROW_BLOCKS
    start, count, hole, skip = tiles
    at = lambda j: start + j + jnp.where(j >= hole, skip, 0)
    state = pl.BlockSpec((rows, TILE), lambda i, j, p: (i, at(j)))
    plane = lambda pick: pl.BlockSpec((1, rows, TILE), lambda i, j, p: (pick(p), i, at(j) - own_at))
    full = jax.ShapeDtypeStruct(w.shape, f32)
    ops, specs = [own], [plane(lambda p: p[0])]
    if slots is not None:
        ops += [slots] * 3
        specs += [plane(lambda p: 1), plane(lambda p: 2), plane(lambda p: 2 + p[1])]
    ops += [first, second, w]
    specs += [state] * 3
    out_shape, out_specs = [full] * 3, [state] * 3
    if deltas is not None:
        ops += [outer, deltas]
        specs += [state, pl.BlockSpec((deltas.shape[0], rows, TILE), lambda i, j, p: (0, i, at(j)))]
        out_shape += [full] * 3 + [jax.ShapeDtypeStruct(w.shape, bf16)]
        out_specs += [state] * 4
    else:
        out_shape.append(jax.ShapeDtypeStruct((total, count * TILE), bf16))
        out_specs.append(pl.BlockSpec((rows, TILE), lambda i, j, p: (i, j)))
    if carry is not None:
        part = pl.BlockSpec((carry.shape[0] // (ROW_BLOCKS * count), carry.shape[1]), lambda i, j, p: (i * count + j, 0))
        ops.append(carry)
        specs.append(part)
        out_shape.append(jax.ShapeDtypeStruct(carry.shape, carry.dtype))
        out_specs.append(part)
    aliases = {}
    if held is not None:
        aliases = {1 + len(ops) + k: k for k in range(3)}
        ops += list(held)
        specs += [pl.BlockSpec(memory_space=pl.ANY)] * 3
    return pl.pallas_call(
        functools.partial(adam_kernel, slots=slots is not None, deltas=deltas is not None, carry=carry is not None, rate=rate,
            groups=groups,
        ),
        grid_spec=pltpu.PrefetchScalarGridSpec(
            num_scalar_prefetch=1, grid=(ROW_BLOCKS, count), in_specs=specs, out_specs=out_specs
        ),
        out_shape=out_shape,
        input_output_aliases=aliases,
        compiler_params=params(),
        cost_estimate=pl.CostEstimate(flops=0, bytes_accessed=total * count * TILE * 48, transcendentals=0),
        name="adam",
    )(place, *ops)


def outer_kernel(*refs, terms, groups):
    d = [ref[...].astype(f32) for ref in refs[:terms]]
    total = (d[0] + d[1]) + (d[2] + d[3]) if terms == 4 else sum(d[1:], d[0])
    write_outer(total, refs[terms], refs[terms + 1], refs[-4:], groups)


def outer_tiles(deltas, outer, w, held, start, groups):
    total, cols = deltas[0].shape
    rows = total // ROW_BLOCKS
    state = pl.BlockSpec((rows, TILE), lambda i, j: (i, start + j))
    full = jax.ShapeDtypeStruct(w.shape, f32)
    ops = [*deltas, outer, w]
    specs = [pl.BlockSpec((rows, TILE), lambda i, j: (i, j))] * len(deltas) + [state] * 2
    aliases = {}
    if held is not None:
        aliases = {len(ops) + k: k for k in range(4)}
        ops += list(held)
        specs += [pl.BlockSpec(memory_space=pl.ANY)] * 4
    return pl.pallas_call(
        functools.partial(outer_kernel, terms=len(deltas), groups=groups),
        grid=(ROW_BLOCKS, cols // TILE),
        in_specs=specs,
        out_specs=[state] * 4,
        out_shape=[full, full, full, jax.ShapeDtypeStruct(w.shape, bf16)],
        input_output_aliases=aliases,
        compiler_params=params(),
        cost_estimate=pl.CostEstimate(flops=0, bytes_accessed=total * cols * 24, transcendentals=0),
        name="outer",
    )(*ops)


def to_group(a, k, rep):
    return lax.ppermute(a, "rep", [(i, i ^ k) for i in range(rep)])


def groups_terms(delta, rep):
    if rep != 4:
        return [delta] + [to_group(delta, k, rep) for k in range(1, rep)]
    near, far = to_group(delta, 1, rep), to_group(delta, 2, rep)
    return [delta, near, far, to_group(far, 1, rep)]


def by_neighbours(n, rep):
    return n == 8 and rep == 4


def all_weights(w_in, w_out, gains):
    split = H * HD + 2 * KVH * HD
    low_in, low_out = w_in.astype(bf16), w_out.astype(bf16)
    low_gains = jnp.pad(gains.astype(bf16), ((0, 62), (0, 0)))
    shards = [low_gains, low_in[:, :split], low_out[0], low_in[:, split:], low_out[1]]
    full = [lax.all_gather(a, "fsdp") for a in shards]
    gain_full = full[0][:, :8].astype(f32).transpose(1, 0, 2).reshape(8, -1)
    return [gain_full] + [a.reshape(-1, a.shape[-1]) for a in full[1:]]


CHUNKS = ("q", "kv", "proj", "gate", "up", "down")
IN_COLUMNS = {"q": (0, H * HD), "kv": (H * HD, 2 * KVH * HD), "gate": (H * HD + 2 * KVH * HD, FF), "up": (H * HD + 2 * KVH * HD + FF, FF)}
CHIP_SHARE = {"q": 48, "kv": 48, "proj": 32, "gate": 48, "up": 48, "down": 16}
PLAN = {
    "begin": (
        (("z", "q", 0), ("z", "kv", 0), ("z", "q", 1), ("y", "q", 0), ("z", "kv", 1), ("y", "kv", 0), ("z", "proj", 0), ("y", "q", 1), ("z", "kv", 2), ("z", "q", 2),),
    ),
    "dy": (
        (("y", "kv", 2), ("z", "q", 3), ("x", "kv", 0), ("z", "kv", 3), ("z", "proj", 1), ("x", "q", 1), ("z", "gate", 0), ("y", "q", 2), ("y", "q", 3), ("y", "kv", 1),),
    ),
    "norm": (
        (("y", "kv", 3), ("x", "q", 0), ("z", "proj", 2), ("x", "kv", 2),),
        (("x", "q", 2), ("z", "gate", 1),),
        (("x", "q", 3), ("c", "q", 1),),
        (("c", "q", 2), ("x", "kv", 1), ("z", "proj", 3), ("y", "proj", 0), ("z", "up", 0), ("x", "kv", 3), ("y", "gate", 0), ("z", "down", 0), ("c", "kv", 2), ("c", "kv", 0), ("z", "gate", 2), ("y", "proj", 2), ("c", "q", 0), ("c", "q", 3), ("y", "proj", 1), ("c", "kv", 1), ("c", "kv", 3),),
    ),
    "qkv": (
        (),
        (),
        (("y", "up", 0),),
        (("y", "gate", 1), ("x", "proj", 2), ("z", "up", 1), ("z", "gate", 3), ("y", "proj", 3),),
    ),
    "attn": (
        (("z", "down", 1),),
        (("z", "up", 2),),
        (("y", "up", 1), ("x", "up", 0),),
        (("z", "down", 2), ("x", "proj", 0), ("x", "proj", 3), ("c", "up", 0), ("y", "gate", 2), ("y", "down", 0),),
        (("x", "gate", 1),),
        (("c", "proj", 0), ("z", "up", 3), ("y", "up", 2), ("c", "gate", 1), ("x", "proj", 1), ("c", "proj", 3),),
        (),
        (("y", "gate", 3), ("x", "up", 1), ("x", "down", 0), ("y", "up", 3), ("z", "down", 3), ("c", "proj", 1), ("c", "proj", 2), ("y", "down", 2),),
    ),
    "proj": (
        (("x", "gate", 2),),
        (("x", "gate", 3), ("y", "down", 3), ("y", "down", 1),),
        (("c", "gate", 2), ("c", "down", 0), ("x", "gate", 0), ("c", "up", 1),),
        (("x", "up", 2), ("x", "down", 2), ("c", "gate", 0), ("c", "gate", 3),),
    ),
    "gate": (
        (),
        (("x", "up", 3), ("x", "down", 1), ("c", "up", 2),),
        (("x", "down", 3),),
        (("c", "up", 3),),
    ),
    "up": (
        (("c", "down", 1),),
        (),
        (),
        (("c", "down", 2), ("c", "down", 3),),
    ),
}


def forward_kernel(*refs, names, line):
    R = dict(zip(names, refs))
    r, f = lax.axis_index("rep"), lax.axis_index("fsdp")
    x, core, z, y = r // 2, r % 2, f // 2, f % 2
    n = 2 * line
    to_y = (r, f + 1 - 2 * y)
    to_x = (r + 2 - 4 * x, f)
    to_core = (r + 1 - 2 * core, f)
    barrier = pltpu.get_barrier_semaphore()
    peers = [(r, lax.rem(f + step, n)) for step in range(1, n)]
    for to in (*peers, to_x, to_core):
        pl.semaphore_signal(barrier, inc=1, device_id=to, device_id_type=pl.DeviceIdType.MESH)
    pl.semaphore_wait(barrier, n + 1)

    def remote(src, dst, send, recv, to):
        return pltpu.make_async_remote_copy(
            src_ref=src, dst_ref=dst, send_sem=send, recv_sem=recv, device_id=to, device_id_type=pl.DeviceIdType.MESH
        )

    held = {c: R["v_" + c] if "v_" + c in R else R["full_" + c] for c in CHUNKS}
    low = {c: R["low_in"].at[:, pl.ds(at, cols)] for c, (at, cols) in IN_COLUMNS.items()}
    low |= {"proj": R["low_out"].at[0], "down": R["low_out"].at[1]}
    rows_of = {c: R["low_out"].shape[1] if c in ("proj", "down") else R["low_in"].shape[0] for c in CHUNKS}
    item = lambda side, d: 0 if d == 0 else 2 * d - 1 + (side > 0)
    exists = lambda side, d: None if d == 0 else (z - d >= 0 if side < 0 else z + d < line)

    def guard(cond, fn):
        if cond is None:
            fn()
        else:
            pl.when(cond)(fn)

    def copy(src, dst, stage, c, side, d, to):
        m, k = CHUNKS.index(c), item(side, d)
        return remote(src, dst, R["f_send"].at[stage, m, k], R["f_recv"].at[stage, m, k], to)

    def portion(c):
        half, share = rows_of[c] // 2, CHIP_SHARE[c]
        return pl.ds(pl.multiple_of(core * half + x * share, 16), half - share)

    def line_copy(c, side, d):
        plane = z + side * (d - 1)
        dst = held[c].at[plane * 2 + y, portion(c), :]
        src = low[c].at[portion(c), :] if d == 1 else dst
        return copy(src, dst, 0, c, side, d, (r, f - 2 * side))

    def line_arrival(c, side, d):
        dst = held[c].at[(z + side * d) * 2 + y, portion(c), :]
        return copy(dst, dst, 0, c, side, d, to_y)

    def y_copy(c, side, d):
        dst = held[c].at[(z + side * d) * 2 + y, portion(c), :]
        return copy(low[c].at[portion(c), :] if d == 0 else dst, dst, 1, c, side, d, to_y)

    def both_copy(c, side, d, start, rows, stage, to):
        planes = pl.ds(z * 2 + 1 - y, 1) if d == 0 else pl.ds((z + side * d) * 2, 2)
        ref = held[c].at[planes, pl.ds(pl.multiple_of(start, 16), rows), :]
        return copy(ref, ref, stage, c, side, d, to)

    def x_copy(c, side, d):
        half, share = rows_of[c] // 2, CHIP_SHARE[c]
        return both_copy(c, side, d, core * half + x * (half - share), share, 2, to_x)

    def core_copy(c, side, d):
        half = rows_of[c] // 2
        return both_copy(c, side, d, core * half, half, 3, to_core)

    def onward(side):
        return z < line - 1 if side < 0 else z > 0

    def line_stage(c, side, d):
        if d == 0:
            for way in (-1, 1):
                pl.when(onward(way))(lambda way=way: line_copy(c, way, 1).start())
        else:
            line_arrival(c, side, d).wait_recv()
            if d < line - 1:
                pl.when(onward(side))(lambda: line_copy(c, side, d + 1).start())
        y_copy(c, side, d).start()

    def y_stage(c, side, d):
        y_copy(c, side, d).wait_recv()
        x_copy(c, side, d).start()

    def x_stage(c, side, d):
        x_copy(c, side, d).wait_recv()
        core_copy(c, side, d).start()

    def core_stage(c, side, d):
        core_copy(c, side, d).wait_recv()

    stages = {"z": line_stage, "y": y_stage, "x": x_stage, "c": core_stage}
    sides = lambda d: (1,) if d == 0 else (-1, 1)

    def act(todo):
        for hop, c, d in todo:
            for side in sides(d):
                guard(exists(side, d), functools.partial(stages[hop], c, side, d))

    def serve(phase, at):
        for step, todo in enumerate(PLAN[phase]):
            if todo:

                @pl.when(at == step)
                def _():
                    act(todo)

    def keep(c):
        return pltpu.make_async_copy(R["v_" + c], R["full_" + c], R["keep_sem"].at[CHUNKS.index(c)])

    def place_own(c):
        return pltpu.make_async_copy(low[c], held[c].at[f], R["own_sem"].at[CHUNKS.index(c)])

    gain_send = lambda step: remote(R["low_gain"], R["v_gain"].at[f], R["g_send"].at[step - 1], R["g_recv"].at[step - 1], peers[step - 1])
    for step in range(1, n):
        gain_send(step).start()
    own_gain = pltpu.make_async_copy(R["low_gain"], R["v_gain"].at[f], R["g_send"].at[n - 1])
    own_gain.start()
    act(PLAN["begin"][0])
    for c in CHUNKS:
        place_own(c).start()

    rowb = lambda width: pl.BlockSpec((BQ, width), lambda i: (i, 0))
    width = R["x"].shape[1]
    steps = LEN // BQ

    def run(body, grid, ins, outs):
        pltpu.emit_pipeline(body, grid=grid, in_specs=[s for _, s in ins], out_specs=[s for _, s in outs])(
            *[R[a] for a, _ in ins], *[R[a] for a, _ in outs]
        )

    def target_step(t_ref, dy_ref, c_ref):
        at = pl.multiple_of(pl.program_id(0) * BQ, BQ)
        c = token_weight(R["table"], R["ids"][pl.ds(at, BQ), :])
        c_ref[...] = jnp.broadcast_to(c, c_ref.shape)
        dy_ref[...] = (c * t_ref[...].astype(f32)).astype(bf16)

    run(target_step, (steps,), [("target", rowb(width))], [("dy", rowb(width)), ("c", rowb(128))])
    act(PLAN["dy"][0])
    own_gain.wait()
    for step in range(1, n):
        gain_send(step).wait()
    gains = jnp.concatenate([R["v_gain"][k] for k in range(n)], axis=1).astype(f32)[0:8]
    R["gain_rows"][...] = gains
    keep_gain = pltpu.make_async_copy(R["gain_rows"], R["gain"], R["g_send"].at[n - 1])
    keep_gain.start()

    def norm_step(x_ref, first_ref):
        v = x_ref[...].astype(f32)
        inv = lax.rsqrt(jnp.mean(v * v, axis=-1, keepdims=True) + norm_eps)
        first_ref[...] = (v * inv * R["gain_rows"][0:1, :]).astype(bf16)

    def norm_body(x_ref, first_ref):
        norm_step(x_ref, first_ref)
        serve("norm", pl.program_id(0))

    run(norm_body, (steps,), [("x", rowb(width))], [("first", rowb(width))])
    for c in CHUNKS:
        place_own(c).wait()
    whole = lambda c: held[c][...].reshape(-1, held[c].shape[2])

    keep("q").start()
    keep("kv").start()

    def qkv_body(first_ref, packed_ref):
        first = first_ref[...]
        split = H * HD
        packed_ref[:, :split] = mm(first, whole("q")).astype(bf16)
        packed_ref[:, split:] = mm(first, whole("kv")).astype(bf16)
        serve("qkv", pl.program_id(0))

    run(qkv_body, (steps,), [("first", rowb(width))], [("packed", rowb(R["packed"].shape[1]))])

    qw = H // 2 * HD
    kcol = H * HD // 128
    vcol = kcol + KVH * HD // 128

    def attention_body(q_ref, k_ref, v_ref, o_ref, lse_ref):
        s = pl.program_id(0)
        i = lax.rem(s, steps)
        attention_step(R["lengths"], i, jnp.minimum(i + 1, max_blocks()), q_ref, k_ref, v_ref, o_ref, lse_ref)
        serve("attn", s)

    qspec = pl.BlockSpec((BQ, qw), lambda s: (s % steps, s // steps))
    run(
        attention_body,
        (2 * steps,),
        [
            ("packed", qspec),
            ("packed", pl.BlockSpec((LEN, 128), lambda s: (0, kcol + s // steps))),
            ("packed", pl.BlockSpec((LEN, 128), lambda s: (0, vcol + s // steps))),
        ],
        [("mixed", qspec), ("lse", pl.BlockSpec((8, BQ), lambda s: (s // steps, s % steps)))],
    )

    keep("proj").start()

    def proj_body(x_ref, mixed_ref, middle_ref, second_ref):
        middle = x_ref[...].astype(f32) + mm(mixed_ref[...], whole("proj"))
        middle_ref[...] = middle
        inv = lax.rsqrt(jnp.mean(middle * middle, axis=-1, keepdims=True) + norm_eps)
        second_ref[...] = (middle * inv * R["gain_rows"][1:2, :]).astype(bf16)
        serve("proj", pl.program_id(0))

    run(proj_body, (steps,), [("x", rowb(width)), ("mixed", rowb(H * HD))], [("middle", rowb(width)), ("second", rowb(width))])

    keep("gate").start()

    def gate_body(second_ref, gate_ref):
        gate_ref[...] = mm(second_ref[...], whole("gate"))
        serve("gate", pl.program_id(0))

    run(gate_body, (steps,), [("second", rowb(width))], [("gate", rowb(FF))])

    keep("up").start()

    def up_body(second_ref, gate_ref, up_ref, hidden_ref):
        up = mm(second_ref[...], whole("up"))
        up_ref[...] = up
        gate = gate_ref[...]
        hidden_ref[...] = (gate * jax.nn.sigmoid(gate) * up).astype(bf16)
        serve("up", pl.program_id(0))

    run(up_body, (steps,), [("second", rowb(width)), ("gate", rowb(FF))], [("up", rowb(FF)), ("hidden", rowb(FF))])

    for c in CHUNKS[:-1]:
        keep(c).wait()
    keep_gain.wait()
    for c in CHUNKS:
        for d in range(line):
            for side in sides(d):

                def finish():
                    core_copy(c, side, d).wait_send()
                    x_copy(c, side, d).wait_send()
                    y_copy(c, side, d).wait_send()

                guard(exists(side, d), finish)
                if d > 0:
                    had = z - (d - 1) >= 0 if side < 0 else z + (d - 1) < line
                    pl.when(had & onward(side))(lambda: line_copy(c, side, d).wait_send())


def forward(lengths, table, ids, arrays, low_in, low_out, gain_shard, n):
    line = n // 2
    width = arrays["x"].shape[1]
    packed = H * HD + 2 * KVH * HD
    shape = {c: (low_in.shape[0], cols) for c, (_, cols) in IN_COLUMNS.items()} | dict.fromkeys(("proj", "down"), low_out.shape[1:])
    outs = {"full_" + c: ((n, *shape[c]), bf16) for c in CHUNKS}
    outs |= {
        "gain": ((8, width), f32), "dy": ((LEN, width), bf16), "c": ((LEN, 128), f32), "first": ((LEN, width), bf16),
        "packed": ((LEN, packed), bf16), "mixed": ((LEN, H * HD), bf16), "lse": ((H, LEN), f32),
        "middle": ((LEN, width), f32), "second": ((LEN, width), bf16), "gate": ((LEN, FF), f32), "up": ((LEN, FF), f32),
        "hidden": ((LEN, FF), bf16),
    }
    dma = pltpu.SemaphoreType.DMA
    count, items = len(CHUNKS), n - 1
    scratch = {"v_" + c: pltpu.VMEM((n, *shape[c]), bf16) for c in CHUNKS[:-1]}
    scratch |= {
        "v_gain": pltpu.VMEM((n, *gain_shard.shape), bf16), "gain_rows": pltpu.VMEM((8, width), f32),
        "f_send": dma((4, count, items)), "f_recv": dma((4, count, items)), "keep_sem": dma((count,)),
        "own_sem": dma((count,)), "g_send": dma((n,)), "g_recv": dma((n,)),
    }
    inputs = dict(arrays) | {"low_in": low_in, "low_out": low_out, "low_gain": gain_shard}
    names = ["lengths", "table", "ids", *inputs, *outs, *scratch]
    anywhere = pl.BlockSpec(memory_space=pl.ANY)
    smem = pl.BlockSpec(memory_space=pltpu.SMEM)
    got = pl.pallas_call(
        functools.partial(forward_kernel, names=names, line=line),
        in_specs=[smem, smem, pl.BlockSpec(memory_space=pltpu.VMEM)] + [anywhere] * len(inputs),
        out_specs=[anywhere] * len(outs),
        out_shape=[jax.ShapeDtypeStruct(*v) for v in outs.values()],
        scratch_shapes=list(scratch.values()),
        compiler_params=pltpu.CompilerParams(collective_id=0, has_side_effects=True, vmem_limit_bytes=62 << 20),
        cost_estimate=pl.CostEstimate(flops=60 << 30, bytes_accessed=200 << 20, transcendentals=0),
        name="forward",
    )(lengths, table, ids, *inputs.values())
    return dict(zip(outs, got))


HALF = 1024
PIECES = {
    "down_y": ("y", "out", 1, HALF, HALF, "hidden", [("dy", 1, HALF)]),
    "down_z": ("z", "out", 1, 0, HALF, "hidden", [("dy", 0, HALF)]),
    "gate": ("y", "in", 0, H * HD + 2 * KVH * HD, FF, "second", [("dboth", 0, FF)]),
    "up": ("y", "in", 0, H * HD + 2 * KVH * HD + FF, FF, "second", [("dboth", 1, FF)]),
    "proj_z": ("z", "out", 0, 0, HALF, "mixed", [("dlow", 0, HALF)]),
    "proj_y": ("y", "out", 0, HALF, HALF, "mixed", [("dlow", 1, HALF)]),
    "q": ("y", "in", 0, 0, H * HD, "first", [("dq", 0, H * HD)]),
    "kv": ("y", "in", 0, H * HD, 2 * KVH * HD, "first", [("dk", 0, KVH * HD), ("dv", 0, KVH * HD)]),
}
REGIONS = {
    "down": ("out", ("down_z", "down_y"), 1, 0, 2 * HALF),
    "ffn": ("in", ("gate", "up"), 0, H * HD + 2 * KVH * HD, 2 * FF),
    "proj": ("out", ("proj_z", "proj_y"), 0, 0, 2 * HALF),
}


def back_kernel(*refs, names, line, rep, rates):
    R = dict(zip(names, refs))
    r, f = lax.axis_index("rep"), lax.axis_index("fsdp")
    z, y = f // 2, f % 2
    n = 2 * line
    other = lambda k: (r + (1 - 2 * (r % 2)) * (k % 2) + 2 * (1 - 2 * (r // 2)) * (k // 2), f)
    barrier = pltpu.get_barrier_semaphore()
    for step in range(1, n):
        pl.semaphore_signal(barrier, inc=1, device_id=(r, lax.rem(f + step, n)), device_id_type=pl.DeviceIdType.MESH)
    for k in range(1, rep):
        pl.semaphore_signal(barrier, inc=1, device_id=other(k), device_id_type=pl.DeviceIdType.MESH)
    pl.semaphore_wait(barrier, n - 1 + rep - 1)

    loads = ("down", "gate_w", "up_w", "proj", "q_w", "kv_w")
    load = lambda k: pltpu.make_async_copy(R[loads[k]], R["v_" + loads[k]], R["load_sem"].at[k])
    for k in range(len(loads)):
        load(k).start()

    def remote(src, dst, send, recv, to):
        return pltpu.make_async_remote_copy(
            src_ref=src, dst_ref=dst, send_sem=send, recv_sem=recv, device_id=(r, to), device_id_type=pl.DeviceIdType.MESH
        )

    def run(body, grid, ins, outs):
        pltpu.emit_pipeline(body, grid=grid, in_specs=[s for _, s in ins], out_specs=[s for _, s in outs])(
            *[a for a, _ in ins], *[a for a, _ in outs]
        )

    order = list(PIECES)
    middle = (z > 0) & (z < line - 1)
    low = z < line // 2
    inner = jnp.where(low, f + 2, f - 2)
    outer = jnp.where(low, f - 2, f + 2)
    to_y = f + 1 - 2 * y
    third = jnp.where(middle, 3, 2)
    far = jnp.where(low, z + 2, z - 2) * 2 + y

    def shard_rows(p):
        rows = R["own_" + PIECES[p][1]].shape[1]
        return rows // 2 if PIECES[p][1] == "out" else rows

    def span(rows, row, col, cols):
        return pl.ds(row * rows, rows), pl.ds(col, cols)

    def area(p):
        _, _, row, col, cols, _, _ = PIECES[p]
        return span(shard_rows(p), row, col, cols)

    def own(p, t):
        return R["own_" + p].at[t] if PIECES[p][0] == "z" else R["own_" + PIECES[p][1]].at[(t, *area(p))]

    def slot(p, k):
        return R["slot_" + p].at[k] if PIECES[p][0] == "z" else R["slot_" + PIECES[p][1]].at[(k, *area(p))]

    def gradient(p, side, out, add=None):
        mode, _, _, _, cols, a, bs = PIECES[p]
        rows = shard_rows(p)
        pick = lambda j: (0, j * 2 + side)
        if mode == "z":
            rows, pick = 2 * rows, lambda j: (0, j)
        block = pl.BlockSpec((1, rows, cols), lambda j: (j, 0, 0))
        ins = [(R[a], pl.BlockSpec((LEN, rows), pick))]
        for b, at, width in bs:
            ins.append((R[b], pl.BlockSpec((LEN, width), functools.partial(lambda at, j: (0, at), at))))
        if add is not None:
            ins.append((add, block))

        def step(*refs):
            out_ref, a_ref, b_refs = refs[-1], refs[0], refs[1 : 1 + len(bs)]
            col = 0
            for b_ref in b_refs:
                width = b_ref.shape[1]
                g = mm(a_ref[...], b_ref[...], TN)
                if add is not None:
                    g = g + refs[-2][0, :, col : col + width].astype(f32)
                out_ref[0, :, col : col + width] = g.astype(bf16)
                col += width

        run(step, (line,), ins, [(out, block)])

    def pair_copy(p):
        k = order.index(p)
        if PIECES[p][0] == "z":
            dst = R["slot_" + PIECES[p][1]].at[(1, *area(p))]
        else:
            dst = R["came_" + p]
        return remote(R["away_" + p], dst, R["y_send"].at[k], R["y_recv"].at[k], to_y)

    def line_copy(p, k, src, slot_at, to):
        i = order.index(p)
        return remote(src, slot(p, slot_at), R["z_send"].at[i, k], R["z_recv"].at[i, slot_at], to)

    def end_copies(p):
        t = lambda k: jnp.where(low, line - 1 - k, k)
        to = (inner, far, inner)
        return [functools.partial(line_copy, p, k, own(p, t(k)), (0, 1, 3)[k], to[k]) for k in range(3)]

    def middle_copies(p):
        return [
            functools.partial(line_copy, p, 0, R["msg_" + p], 1, far),
            functools.partial(line_copy, p, 1, own(p, 3 - z), 2, inner),
            functools.partial(line_copy, p, 2, own(p, 3 * (z - 1)), 2, outer),
        ]

    def slot_wait(p, at):
        i = order.index(p)
        remote(slot(p, at), slot(p, at), R["z_send"].at[i, 0], R["z_recv"].at[i, at], inner).wait_recv()

    def line_start(p):
        @pl.when(~middle)
        def _():
            for copy in end_copies(p):
                copy().start()

        @pl.when(middle)
        def _():
            for copy in middle_copies(p)[1:]:
                copy().start()

    def send_away(p):
        gradient(p, 1 - y, R["away_" + p])
        pair_copy(p).start()

    def keep(p):
        pair_copy(p).wait_recv()
        gradient(p, y, R["own_" + PIECES[p][1]].at[(pl.ds(0, line), *area(p))], R["came_" + p])
        line_start(p)

    def send_line(p):
        gradient(p, None, R["own_" + p])
        line_start(p)

    def serve(p):
        @pl.when(middle)
        def _():
            slot_wait(p, 0)
            rows, cols = R["msg_" + p].shape
            block = pl.BlockSpec((rows // 2, cols), lambda j: (j, 0))

            def step(a_ref, b_ref, o_ref):
                o_ref[...] = (a_ref[...].astype(f32) + b_ref[...].astype(f32)).astype(bf16)

            run(step, (2,), [(own(p, 3 * (2 - z)), block), (slot(p, 0), block)], [(R["msg_" + p], block)])
            middle_copies(p)[0]().start()

    def line_end(p):
        slot_wait(p, 1)
        slot_wait(p, 2)
        pl.when(middle)(lambda: slot_wait(p, 3))

    def total(refs):
        a, b, c, d = (ref[...].astype(f32) for ref in refs)
        return a + b + c + jnp.where(middle, d, 0.0)

    def close(p):
        line_end(p)
        rows, cols = shard_rows(p), PIECES[p][4]

        def send_step(*refs):
            refs[-1][...] = total(refs[:4]).astype(bf16)

        def stay_step(*refs):
            refs[4][...] = total(refs[:4]).astype(bf16)
            for ref in refs[5:]:
                ref[...] = jnp.zeros_like(ref)

        piece = pl.BlockSpec((rows // 2, cols), lambda j: (j, 0))
        terms = (own(p, z), slot(p, 1), slot(p, 2), slot(p, third))
        ins = lambda side: [(ref, pl.BlockSpec((rows // 2, cols), lambda j: (side * 2 + j, 0))) for ref in terms]
        run(send_step, (2,), ins(1 - y), [(R["away_" + p], piece)])
        pair_copy(p).start()
        kind = PIECES[p][1]
        outs = [R["own_" + kind].at[(z, *area(p))]] + [R["slot_" + kind].at[(k, *area(p))] for k in (2, 3)]
        run(stay_step, (2,), ins(y), [(ref, piece) for ref in outs])

    def delta_copy(name, k):
        kind, pieces, row, col, cols = REGIONS[name]
        i = list(REGIONS).index(name)
        spot = lambda at: R["delta_" + kind].at[(at, *span(shard_rows(pieces[0]), row, col, cols))]
        return pltpu.make_async_remote_copy(
            src_ref=spot(2 if k == 3 else 0), dst_ref=spot(k), send_sem=R["d_send"].at[i, k - 1], recv_sem=R["d_recv"].at[i, k - 1],
            device_id=other(1 if k == 3 else k), device_id_type=pl.DeviceIdType.MESH,
        )

    def delta(name):
        kind, pieces, row, col, cols = REGIONS[name]
        for p in pieces:
            if PIECES[p][0] == "z":
                pair_copy(p).wait_recv()
            else:
                line_end(p)
        rows = shard_rows(pieces[0])
        where = span(rows, row, col, cols)
        block = pl.BlockSpec((rows, 256), lambda j: (0, j))
        terms = [R["own_" + kind].at[(z, *where)]] + [R["slot_" + kind].at[(k, *where)] for k in (1, 2, third)]
        state = [R[k + "_" + kind].at[where] for k in ("first", "second", "w")]

        def step(*refs):
            first_ref, second_ref, w_ref, o_ref = refs[4:]
            o_ref[...] = adam_step(total(refs[:4]), first_ref[...], second_ref[...], w_ref[...], rates[kind])[2].astype(bf16)

        run(step, (cols // 256,), [(ref, block) for ref in terms + state], [(R["delta_" + kind].at[(0, *where)], block)])
        for k in (1, 2):
            delta_copy(name, k).start()

    def relay(name):
        delta_copy(name, 2).wait_recv()
        delta_copy(name, 3).start()

    rowb = lambda width: pl.BlockSpec((BQ, width), lambda i: (i, 0))
    width = R["x"].shape[1]
    R["gain_acc"][...] = jnp.zeros_like(R["gain_acc"])
    gain_rows = R["gain"][...]

    def mid_step(middle_ref, hidden_ref, dboth_ref, t_ref, c_ref, act_ref, dmid_ref, dlow_ref, dmix_ref):
        mid_v = middle_ref[...]
        act_ref[...] = (mid_v + mm(hidden_ref[...], R["v_down"][...])).astype(bf16)
        inv = lax.rsqrt(jnp.mean(mid_v * mid_v, axis=-1, keepdims=True) + norm_eps)
        n2 = mid_v * inv
        ds2 = mm(dboth_ref[:, :FF], R["v_gate_w"][...], NT) + mm(dboth_ref[:, FF:], R["v_up_w"][...], NT)
        prod = ds2 * n2
        R["gain_acc"][8:16, :] += jnp.sum(prod.reshape(BQ // 8, 8, width), axis=0)
        g = gain_rows[1:2, :]
        dy = c_ref[:, 0:1] * t_ref[...].astype(f32)
        dmid = dy + inv * (ds2 * g - n2 * jnp.mean(prod * g, axis=-1, keepdims=True))
        dmid_ref[...] = dmid
        dlow = dmid.astype(bf16)
        dlow_ref[...] = dlow
        dmix_ref[...] = mm(dlow, R["v_proj"][...], NT).astype(bf16)

    def mid_phase(part):
        count = LEN // BQ // 2
        late = lambda width: pl.BlockSpec((BQ, width), lambda i: (i + part * count, 0))
        run(
            mid_step,
            (count,),
            [(R["middle"], late(width)), (R["hidden"], late(FF)), (R["dboth"], late(2 * FF)), (R["target"], late(width)), (R["c"], late(128))],
            [(R["act"], late(width)), (R["dmid"], late(width)), (R["dlow"], late(width)), (R["dmix"], late(H * HD))],
        )

    qw = H // 2 * HD
    kcol = H * HD // 128
    vcol = kcol + KVH * HD // 128

    def attention_phase(p):
        qspec = pl.BlockSpec((BQ, qw), lambda i: (i, p))
        whole = lambda at: pl.BlockSpec((LEN, 128), lambda i: (0, at))
        R["dk_acc"][...] = jnp.zeros_like(R["dk_acc"])
        R["dv_acc"][...] = jnp.zeros_like(R["dv_acc"])

        def step(q_ref, k_ref, v_ref, d_ref, o_ref, lse_ref, dq_ref):
            attention_back_step(R["lengths"], pl.program_id(0), q_ref, k_ref, v_ref, d_ref, o_ref, lse_ref, dq_ref, R["dk_acc"], R["dv_acc"])

        pltpu.emit_pipeline(
            step, grid=(LEN // BQ,),
            in_specs=[qspec, whole(kcol + p), whole(vcol + p), qspec, qspec, pl.BlockSpec((8, BQ), lambda i: (p, i))],
            out_specs=[qspec],
        )(R["packed"], R["packed"], R["packed"], R["dmix"], R["mixed"], R["lse"], R["dq"])

        def flush(dk_ref, dv_ref):
            dk_ref[...] = R["dk_acc"][...].astype(bf16)
            dv_ref[...] = R["dv_acc"][...].astype(bf16)

        run(flush, (1,), [], [(R["dk"], pl.BlockSpec((LEN, 128), lambda i: (0, p))), (R["dv"], pl.BlockSpec((LEN, 128), lambda i: (0, p)))])

    def input_step(x_ref, dmid_ref, dq_ref, dk_ref, dv_ref, out_ref):
        x = x_ref[...].astype(f32)
        inv = lax.rsqrt(jnp.mean(x * x, axis=-1, keepdims=True) + norm_eps)
        n1 = x * inv
        kv_w, split = R["v_kv_w"], KVH * HD
        ds1 = mm(dq_ref[...], R["v_q_w"][...], NT) + mm(dk_ref[...], kv_w[:, :split], NT) + mm(dv_ref[...], kv_w[:, split:], NT)
        prod = ds1 * n1
        R["gain_acc"][0:8, :] += jnp.sum(prod.reshape(BQ // 8, 8, width), axis=0)
        g = gain_rows[0:1, :]
        out_ref[...] = (dmid_ref[...] + inv * (ds1 * g - n1 * jnp.mean(prod * g, axis=-1, keepdims=True))).astype(bf16)

    def input_phase():
        run(
            input_step,
            (LEN // BQ,),
            [(R["x"], rowb(width)), (R["dmid"], rowb(width)), (R["dq"], rowb(H * HD)), (R["dk"], rowb(KVH * HD)), (R["dv"], rowb(KVH * HD))],
            [(R["xgrad"], rowb(width))],
        )

    part = width // n

    def gain_copy(step, receive=False):
        peer = lax.rem(f + step, n)
        home = lax.rem(f + n - step, n) if receive else f
        return remote(
            R["gain_acc"].at[:, pl.ds(pl.multiple_of(peer * part, part), part)], R["gain_got"].at[home],
            R["g_send"].at[step - 1], R["g_recv"].at[step - 1], peer,
        )

    own_gain = pltpu.make_async_copy(
        R["gain_acc"].at[:, pl.ds(pl.multiple_of(f * part, part), part)], R["gain_got"].at[f], R["g_send"].at[n - 1]
    )

    def dboth_step(dy_ref, gate_ref, up_ref, dboth_ref):
        dh = mm(dy_ref[...], R["v_down"][...], NT)
        gate = gate_ref[...]
        sig = jax.nn.sigmoid(gate)
        dboth_ref[:, :FF] = (dh * up_ref[...] * sig * (1.0 + gate * (1.0 - sig))).astype(bf16)
        dboth_ref[:, FF:] = (dh * (gate * sig)).astype(bf16)

    send_line("down_z")
    send_away("down_y")
    load(0).wait()
    run(
        dboth_step,
        (LEN // BQ,),
        [(R["dy"], rowb(width)), (R["gate"], rowb(FF)), (R["up"], rowb(FF))],
        [(R["dboth"], rowb(2 * FF))],
    )
    serve("down_z")
    send_away("gate")
    for k in range(1, 4):
        load(k).wait()
    mid_phase(0)
    keep("down_y")
    mid_phase(1)
    serve("down_y")
    send_away("up")
    send_line("proj_z")
    serve("proj_z")
    attention_phase(0)
    keep("gate")
    send_away("proj_y")
    serve("gate")
    attention_phase(1)
    send_away("q")
    keep("up")
    serve("up")
    load(4).wait()
    load(5).wait()
    input_phase()
    for step in range(1, n):
        gain_copy(step).start()
    own_gain.start()
    keep("proj_y")
    serve("proj_y")
    close("proj_z")
    delta("ffn")
    keep("q")
    send_away("kv")
    delta("proj")
    close("down_z")
    serve("q")
    keep("kv")
    delta("down")
    relay("proj")
    serve("kv")
    relay("down")
    relay("ffn")

    for step in range(1, n):
        gain_copy(step, True).wait_recv()
        gain_copy(step).wait_send()
    own_gain.wait()
    for name in REGIONS:
        for k in (1, 3):
            delta_copy(name, k).wait()
        delta_copy(name, 2).wait_send()
    line_end("q")
    line_end("kv")
    for p in order:
        pair_copy(p).wait_send()

        @pl.when(middle)
        def _():
            for copy in middle_copies(p):
                copy().wait_send()

        @pl.when(~middle)
        def _():
            for copy in end_copies(p):
                copy().wait_send()


def backward(lengths, gain, arrays, n, rep, rates):
    line = n // 2
    width = arrays["x"].shape[1]
    kvw = KVH * HD
    outs = {
        "act": ((LEN, width), bf16), "dboth": ((LEN, 2 * FF), bf16), "dmid": ((LEN, width), f32), "dlow": ((LEN, width), bf16),
        "dmix": ((LEN, H * HD), bf16), "dq": ((LEN, H * HD), bf16), "dk": ((LEN, kvw), bf16), "dv": ((LEN, kvw), bf16),
        "xgrad": ((LEN, width), bf16), "gain_got": ((n, 16, width // n), f32),
    }
    for kind in ("in", "out"):
        for name, count in (("own_", line), ("slot_", 4), ("delta_", rep)):
            outs[name + kind] = ((count, *arrays["w_" + kind].shape), bf16)
    for p, (mode, kind, _, _, cols, _, _) in PIECES.items():
        rows = arrays["w_" + kind].shape[0] // (2 if kind == "out" else 1)
        if mode == "y":
            counts = (("away_", (line, rows)), ("came_", (line, rows)), ("msg_", (rows,)))
        else:
            counts = (("away_", (rows,)), ("own_", (line, 2 * rows)), ("slot_", (4, 2 * rows)), ("msg_", (2 * rows,)))
        for name, lead in counts:
            outs[name + p] = ((*lead, cols), bf16)
    dma = pltpu.SemaphoreType.DMA
    pieces = len(PIECES)
    scratch = {
        **{"v_" + k: pltpu.VMEM(arrays[k].shape, bf16) for k in ("down", "gate_w", "up_w", "proj", "q_w", "kv_w")},
        "gain_acc": pltpu.VMEM((16, width), f32), "dk_acc": pltpu.VMEM((LEN, 128), f32), "dv_acc": pltpu.VMEM((LEN, 128), f32),
        "load_sem": dma((6,)), "y_send": dma((pieces,)), "y_recv": dma((pieces,)),
        "z_send": dma((pieces, 3)), "z_recv": dma((pieces, 4)),
        "d_send": dma((len(REGIONS), rep - 1)), "d_recv": dma((len(REGIONS), rep - 1)), "g_send": dma((n,)), "g_recv": dma((n,)),
    }
    names = ["lengths", "gain", *arrays, *outs, *scratch]
    anywhere = pl.BlockSpec(memory_space=pl.ANY)
    got = pl.pallas_call(
        functools.partial(back_kernel, names=names, line=line, rep=rep, rates=rates),
        in_specs=[pl.BlockSpec(memory_space=pltpu.SMEM), pl.BlockSpec(memory_space=pltpu.VMEM)] + [anywhere] * len(arrays),
        out_specs=[anywhere] * len(outs),
        out_shape=[jax.ShapeDtypeStruct(*v) for v in outs.values()],
        scratch_shapes=list(scratch.values()),
        compiler_params=pltpu.CompilerParams(collective_id=1, has_side_effects=True, vmem_limit_bytes=62 << 20),
        cost_estimate=pl.CostEstimate(flops=200 << 30, bytes_accessed=400 << 20, transcendentals=0),
        name="backward",
    )(lengths, gain, *arrays.values())
    return dict(zip(outs, got))


rate_in = 0.02
rate_out = 0.08
rate_gains = 1.2


def body(
    tokens,
    target,
    doc_lengths,
    corpus_ids,
    corpus_weights,
    w_in,
    w_out,
    gains,
    first_in,
    first_out,
    first_gains,
    second_in,
    second_out,
    second_gains,
    outer_in,
    outer_out,
    outer_gains,
):
    n, rep = lax.axis_size("fsdp"), lax.axis_size("rep")
    line = n // 2
    f, r = lax.axis_index("fsdp"), lax.axis_index("rep")
    z, y = f // 2, f % 2
    direct = by_neighbours(n, rep)
    inside = (z > 0) & (z < line - 1)
    place = jnp.stack([z, inside]).astype(jnp.int32)
    width = w_out.shape[2]
    flat = lambda a: a.reshape(-1, a.shape[-1])
    state_in = first_in[0], second_in[0], w_in
    state_out = flat(first_out[0]), flat(second_out[0]), flat(w_out)
    moved_out = flat(outer_out)
    rates = {"in": rate_in, "out": rate_out}
    rows_in, rows_out = w_in.shape[0], w_out.shape[1]
    x, tgt, lengths = tokens[0], target[0], doc_lengths[0]
    ids = corpus_ids[0][:, None]

    if direct:
        low_gain = jnp.pad(gains.astype(bf16), ((0, 14), (0, 0)))
        fwd = forward(lengths, corpus_weights, ids, dict(x=x, target=tgt), w_in.astype(bf16), w_out.astype(bf16), low_gain, n)
        weight = lambda c: flat(fwd["full_" + c])
        kept = {k: fwd[k] for k in ("c", "middle", "hidden", "second", "gate", "up", "dy", "mixed", "packed", "lse", "first")}
        got = backward(
            lengths, fwd["gain"],
            dict(x=x, target=tgt, proj=weight("proj"), down=weight("down"), q_w=weight("q"), kv_w=weight("kv"),
                 gate_w=weight("gate"), up_w=weight("up"), first_in=state_in[0], second_in=state_in[1], w_in=w_in,
                 first_out=state_out[0], second_out=state_out[1], w_out=state_out[2], **kept),
            n, rep, rates,
        )
        activations, input_grad = got["act"], got["xgrad"]
        gain_share = jnp.sum(got["gain_got"].reshape(n, 2, 8, -1), axis=(0, 2))
        late = (H * HD + 2 * KVH * HD) // TILE
        *held, late_delta = adam_tiles(
            place, got["own_in"], got["slot_in"], *state_in, None, None, None, 0, (0, late, late, 0), rate_in, rep
        )
        near, far = to_group(late_delta, 1, rep), to_group(late_delta, 2, rep)
        rest = w_in.shape[1] // TILE - late
        in_got = adam_tiles(
            place, got["own_in"], got["slot_in"], *state_in, outer_in, got["delta_in"], held,
            0, (late, rest, rest, 0), rate_in, rep,
        )
        out_count = width // TILE
        *out_got, activations = adam_tiles(
            place, got["own_out"], got["slot_out"], *state_out, moved_out, got["delta_out"], None,
            0, (0, out_count, out_count, 0), rate_out, rep, activations,
        )
        out_got, in_got = list(out_got), list(in_got)
        far, out_got[0], in_got[0] = lax.optimization_barrier((far, out_got[0], in_got[0]))
        late_terms = [late_delta, near, far, to_group(far, 1, rep)]
        in_grads, in_steps = in_got[:3], outer_tiles(late_terms, outer_in, w_in, in_got[3:], 0, rep)
        out_grads, out_steps = out_got[:3], out_got[3:]
    else:
        gain_full, wq, proj, wf, down = all_weights(w_in, w_out, gains)
        first_low, packed = qkv(x, gain_full, wq)
        mixed, lse = attention(lengths, packed)
        middle, second_low, hidden, d_both, dy, _ = ffn(corpus_weights, x, mixed, tgt, ids, gain_full, proj, wf, down)

        def by_library(a, bs, name):
            block = 2 * BQ if a.shape[1] % (2 * BQ) == 0 else BQ
            every_row = jnp.arange(a.shape[1] // block, dtype=jnp.int32)
            total = grad_rows(every_row, a, bs, block, name=name)
            return lax.psum_scatter(total.reshape(a.shape[1], -1), "fsdp", scatter_dimension=0, tiled=True)[None]

        activations, d_mid, d_low, d_mix, gain_two = mid(
            corpus_weights, middle, hidden, d_both, tgt, ids, gain_full, proj, wf, down
        )
        dq, dk, dv = attention_back(lengths, packed, d_mix, mixed, lse)
        input_grad, gain_one = input_back(x, d_mid, dq, dk, dv, gain_full, wq)
        both = jnp.stack([jnp.sum(gain_one, axis=0), jnp.sum(gain_two, axis=0)])
        gain_share = lax.psum_scatter(both, "fsdp", scatter_dimension=1, tiled=True)
        own_in = jnp.concatenate(
            [
                by_library(first_low, [(dq, 0, H * HD), (dk, 0, KVH * HD), (dv, 0, KVH * HD)], "grad_attn"),
                by_library(second_low, [(d_both, 0, 2 * FF)], "grad_ffn"),
            ],
            axis=2,
        )
        own_out = jnp.concatenate(
            [by_library(mixed, [(d_low, 0, width)], "grad_proj"), by_library(hidden, [(dy, 0, width)], "grad_down")], axis=1
        )

        def all_tiles(own, state, outer, rate):
            count = own.shape[2] // TILE
            *grads, delta = adam_tiles(0 * place, own, None, *state, None, None, None, 0, (0, count, count, 0), rate, rep)
            return grads, outer_tiles(groups_terms(delta, rep), outer, state[2], None, 0, rep)

        in_grads, in_steps = all_tiles(own_in, state_in, outer_in, rate_in)
        out_grads, out_steps = all_tiles(own_out, state_out, moved_out, rate_out)

    first_gains_new, second_gains_new, delta = adam_step(gain_share, first_gains[0], second_gains[0], gains, rate_gains)
    terms = groups_terms(delta, rep)
    sum_gains = (terms[0] + terms[1]) + (terms[2] + terms[3]) if rep == 4 else sum(terms[1:], terms[0])
    diff_gains, outer_gains_new, new_gains = outer_step(sum_gains, outer_gains, gains, rep)

    out_shape = lambda a: a.reshape(2, rows_out, width)
    diff_in, outer_in_new, new_in, copy_in = in_steps
    diff_out, outer_out_new, new_out, copy_out = (out_shape(a) for a in out_steps)
    grad_in, first_in_new, second_in_new = in_grads
    grad_out, first_out_new, second_out_new = (out_shape(a) for a in out_grads)
    return (
        activations[None],
        input_grad[None],
        grad_in[None],
        grad_out[None],
        gain_share[None],
        first_in_new[None],
        first_out_new[None],
        first_gains_new[None],
        second_in_new[None],
        second_out_new[None],
        second_gains_new[None],
        diff_in,
        diff_out,
        diff_gains,
        outer_in_new,
        outer_out_new,
        outer_gains_new,
        new_in,
        new_out,
        new_gains,
        copy_in,
        copy_out,
        new_gains.astype(bf16),
    )


def solution(mesh):
    rows = P(("rep", "fsdp"), None, None)
    pair = P(("rep", "fsdp"), None)
    w_in, w_out, gains = P("fsdp", None), P(None, "fsdp", None), P(None, "fsdp")
    m_in, m_out, m_gains = P("rep", "fsdp", None), P("rep", None, "fsdp", None), P("rep", None, "fsdp")
    weights, moments = (w_in, w_out, gains), (m_in, m_out, m_gains)
    return jax.shard_map(
        body,
        mesh=mesh,
        in_specs=(rows, rows, pair, pair, P(), *weights, *moments, *moments, *weights),
        out_specs=(rows, rows, *moments, *moments, *moments, *weights, *weights, *weights, *weights),
        check_vma=False,
    )
```
